32 devices in a mesh: dp: 8 (over z, x), mp: 4 (over y, core).
Axes of the slice: x: 2, y: 2, z: 4, core: 2. Of those that a mesh axis runs over, the one named last changes fastest.
Arguments:
- hidden: bfloat16 [4096, 1536], P('dp'), may hold values from -6 to 6
- segment_ids: int32 [4096], replicated, may hold values from 0 to 2, as said below
- routes: int32 [4096, 6], P('dp'), may hold values from 0 to 63, all different within a row; in each aligned block of 512 rows (0 to 511, 512 to 1023, ...) at most 64 rows name the same one
- norm_gain: bfloat16 [1536], P('dp'), may hold values from 0.5 to 1.5
- mixer_in: bfloat16 [1536, 2, 3072], P('dp', None, 'mp'), may hold values from -0.15625 to 0.15625
- state_in: bfloat16 [1536, 256], P('dp'), may hold values from -0.15625 to 0.15625
- step_in: bfloat16 [1536, 48], P('dp', 'mp'), may hold values from -0.15625 to 0.15625
- conv_value: bfloat16 [4, 64, 48], P(None, 'dp', 'mp'), may hold values from -3 to 3
- conv_value_bias: bfloat16 [64, 48], P('dp', 'mp'), may hold values from -3 to 3
- conv_state: bfloat16 [4, 256], P(None, 'dp'), may hold values from -3 to 3
- conv_state_bias: bfloat16 [256], P('dp'), may hold values from -3 to 3
- head_params: bfloat16 [3, 48], P(None, 'mp')
- gated_gain: bfloat16 [64, 48], P('dp', 'mp'), may hold values from 0.5 to 1.5
- mixer_out: bfloat16 [3072, 1536], P('mp', 'dp'), may hold values from -0.109375 to 0.109375
- ffn_gain: bfloat16 [1536], P('dp'), may hold values from 0.5 to 1.5
- router: bfloat16 [1536, 64], P('dp'), may hold values from -0.078125 to 0.078125
- shared_in: bfloat16 [1536, 2, 1024], P('dp', None, 'mp'), may hold values from -0.15625 to 0.15625
- shared_out: bfloat16 [1024, 1536], P('mp', 'dp'), may hold values from -0.1875 to 0.1875
- expert_in: bfloat16 [64, 1536, 2, 512], P('dp', None, None, 'mp'), may hold values from -0.15625 to 0.15625
- expert_out: bfloat16 [64, 512, 1536], P('dp', 'mp'), may hold values from -0.25 to 0.25
- cotangent: bfloat16 [4096, 1536], P('dp'), may hold values from -6 to 6
Outputs:
- result: bfloat16 [4096, 1536], P('dp')
- grad_hidden: float32 [4096, 1536], P('dp')
- grad_norm_gain: float32 [1536], P('dp')
- grad_mixer_in: float32 [1536, 2, 3072], P('dp', None, 'mp')
- grad_state_in: float32 [1536, 256], P('dp')
- grad_step_in: float32 [1536, 48], P('dp', 'mp')
- grad_conv_value: float32 [4, 64, 48], P(None, 'dp', 'mp')
- grad_conv_value_bias: float32 [64, 48], P('dp', 'mp')
- grad_conv_state: float32 [4, 256], P(None, 'dp')
- grad_conv_state_bias: float32 [256], P('dp')
- grad_head_params: float32 [3, 48], P(None, 'mp')
- grad_gated_gain: float32 [64, 48], P('dp', 'mp')
- grad_mixer_out: float32 [3072, 1536], P('mp', 'dp')
- grad_ffn_gain: float32 [1536], P('dp')
- grad_router: float32 [1536, 64], P('dp')
- grad_shared_in: float32 [1536, 2, 1024], P('dp', None, 'mp')
- grad_shared_out: float32 [1024, 1536], P('mp', 'dp')
- grad_expert_in: float32 [64, 1536, 2, 512], P('dp', None, None, 'mp')
- grad_expert_out: float32 [64, 512, 1536], P('dp', 'mp')
The draws below stay inside these ranges and needn't reach their ends.
Inputs may be any that keep to these rules, and one draw needn't show every extreme that they name: `segment_ids`: never falling; 0 up to a position inside the first 512 tokens, 2 from a position inside the last 512 tokens, 1 between. `routes`: in each aligned block of 512 rows no expert is named by more than 64 rows, a bound that some block reaches.
All inputs are finite; a program needn't handle non-finite values.
Results may differ from the reference program's by a relative error of at most 0.02.
The reference program's roundings to bfloat16 on the way count: a program that leaves them out, or rounds other values in their place, can miss the bound.
Values may be sent and summed in bfloat16 or wider, within the bound.
A program may use at most 320 MiB of HBM per device.

```python
import math
from functools import partial
import jax
import jax.numpy as jnp
import numpy as np
from jax import lax

D = 1536
H = 48
HD = 64
NS = 128
KW = 4
BLK = 128
EXPERTS = 64
TOPK = 6
FE = 512
FS = 1024
GROUP = 512
DI = 3072
TOKENS = 4096
CAP = 64
N_DP = 8


def draw_segment_ids(key, part):
    key = jax.random.fold_in(key, 11)
    first_key, second_key = jax.random.split(key)
    opening = jax.random.randint(first_key, (), GROUP // 4, 3 * GROUP // 4)
    closing = TOKENS - jax.random.randint(second_key, (), GROUP // 4, 3 * GROUP // 4)
    places = jnp.arange(TOKENS, dtype=jnp.int32)
    return (places >= opening).astype(jnp.int32) + (places >= closing).astype(jnp.int32)


def draw_head_params(key, part):
    key = jax.random.fold_in(key, 23)
    keys = jax.random.split(key, 5)
    share = 0.5
    slow_rate = jnp.exp(jax.random.uniform(keys[1], (H,), jnp.float32, jnp.log(0.2), jnp.log(0.7)))
    fast_rate = jnp.exp(jax.random.uniform(keys[2], (H,), jnp.float32, jnp.log(2.0), jnp.log(8.0)))
    slow_heads = jax.random.uniform(keys[0], (H,), jnp.float32) < share
    log_rate = jnp.where(slow_heads, jnp.log(slow_rate / (0.01 * TOKENS)), jnp.log(fast_rate))
    step_bias = jax.random.uniform(keys[3], (H,), jnp.float32, -6.0, -4.0)
    skip_weight = jax.random.uniform(keys[4], (H,), jnp.float32, 0.5, 1.5)
    return jnp.stack([log_rate, step_bias, skip_weight], axis=0).astype(jnp.bfloat16)


def block_levels(own_key, shape, shards, smallest, top_value):
    factor_of = 1.0
    for dim, shards_of in shards:
        draws = jax.random.uniform(jax.random.fold_in(jax.random.fold_in(own_key, 6), dim), (shards_of,), jnp.float32, smallest / len(shards), top_value / len(shards))
        factor_of = factor_of * jnp.repeat(jnp.exp(draws), shape[dim] // shards_of).reshape((-1,) + (1,) * (len(shape) - 1 - dim))
    return factor_of


def assign_block(key, own, number, rows, number_of, top, most, slope):
    order = jax.random.permutation(key, number_of)
    packed, ordinary = load_shares(number_of, rows * top, most, slope, True), load_shares(number_of, rows * top, most, slope, False)
    places = jnp.arange(number_of)

    def named(sizes, rotation):
        used = int((sizes > 0).sum())
        fixed = max(1, used // 4)
        moved = fixed + (places - fixed + rotation * (used - fixed)) % max(1, number_of - fixed)
        return jnp.zeros((number_of,), jnp.int32).at[order[jnp.where(places < fixed, places, moved)]].set(jnp.asarray(sizes, jnp.int32))

    sizes = jnp.where(number % 4 == 0, named(packed, number // 4), named(ordinary, number - number // 4 - 1))
    mixed = jax.random.permutation(jax.random.fold_in(own, 3), number_of)
    source_of, receiver = mixed[0:number_of // 2 * 2:2], mixed[1:number_of // 2 * 2:2]
    margin = jnp.minimum(sizes[source_of] - 1, most - sizes[receiver]) // 2
    margin = jnp.where((source_of == order[0]) | (receiver == order[0]) | (sizes[receiver] == 0), 0, jnp.maximum(margin, 0))
    moved = jax.random.randint(jax.random.fold_in(own, 4), (number_of // 2,), 0, 1 << 20) % (margin + 1)
    sizes = sizes.at[source_of].add(-moved).at[receiver].add(moved)
    items = jnp.searchsorted(jnp.cumsum(sizes), jnp.arange(rows * top), side="right").astype(jnp.int32)
    listing = items.reshape(top, rows).T
    listing = listing[jax.random.permutation(jax.random.fold_in(own, 1), rows)]
    rotation = jax.random.randint(jax.random.fold_in(own, 2), (rows, 1), 0, top)
    return jnp.take_along_axis(listing, (jnp.arange(top)[None, :] + rotation) % top, axis=1)


def load_shares(count, total, most, lean, full):
    loads = [(1 << 20) // math.isqrt(standing ** lean) + 1 for standing in range(1, count + 1)]
    largest = most if full else min(most, max(-(-total // count), total * loads[0] // sum(loads)))
    least = 1 if total - largest >= count - 1 else 0
    holding, surplus = [largest] + [least] * (count - 1), total - largest - least * (count - 1)
    while surplus > 0:
        movable = [i for i in range(1, count) if holding[i] < largest] or [i for i in range(1, count) if holding[i] < most]
        mass, left = sum([loads[i] for i in movable]), surplus
        for i in movable:
            extra = min(most - holding[i], max(1, left * loads[i] // mass), surplus)
            holding[i] = holding[i] + extra
            surplus = surplus - extra
    return np.array(holding)


def noise(own_key, shape, deviation, bound, cuts=(), kind=jnp.bfloat16):
    loudness = block_levels(own_key, shape, cuts, -0.22, 0.18) if cuts else 1.0
    values = jax.random.normal(own_key, shape, jnp.float32) * deviation * loudness
    return jnp.minimum(jnp.maximum(values, -bound), bound).astype(kind)


def setup_inputs(seed: int = 0) -> dict:
    arg_keys = jax.random.split(jax.random.key(seed), 22)
    hidden = noise(arg_keys[0], (TOKENS, D), 1.0, 6.0, ((0, 8),))
    segment_ids = draw_segment_ids(jax.random.fold_in(arg_keys[21], 71), 0)
    routes_keys = jax.random.split(jax.random.fold_in(arg_keys[2], 1), TOKENS // GROUP)
    routes_turns = jax.random.permutation(jax.random.fold_in(arg_keys[2], 3), TOKENS // GROUP)
    routes = jax.vmap(lambda own, number: assign_block(jax.random.fold_in(arg_keys[2], 2), own, number, GROUP, EXPERTS, TOPK, CAP, 1))(routes_keys, routes_turns).reshape((TOKENS, TOPK))
    norm_gain = jnp.clip(1.0 + 0.1 * jax.random.normal(arg_keys[3], (D,), jnp.float32), 0.5, 1.5).astype(jnp.bfloat16)
    mixer_in = noise(arg_keys[4], (D, 2, DI), D ** -0.5, 0.15625, ((0, 8), (2, 4)))
    state_in = noise(arg_keys[5], (D, 2 * NS), D ** -0.5, 0.15625, ((0, 8),))
    step_in = noise(arg_keys[6], (D, H), D ** -0.5, 0.15625, ((0, 8), (1, 4)))
    conv_value = noise(arg_keys[7], (KW, HD, H), KW ** -0.5, 3.0, ((1, 8), (2, 4)))
    conv_value_bias = noise(arg_keys[8], (HD, H), 0.3, 3.0, ((0, 8), (1, 4)))
    conv_state = noise(arg_keys[9], (KW, 2 * NS), KW ** -0.5, 3.0, ((1, 8),))
    conv_state_bias = noise(arg_keys[10], (2 * NS,), 0.3, 3.0, ((0, 8),))
    head_params = draw_head_params(jax.random.fold_in(arg_keys[21], 71), 0)
    gated_gain = jnp.clip(1.0 + 0.1 * jax.random.normal(arg_keys[12], (HD, H), jnp.float32), 0.5, 1.5).astype(jnp.bfloat16)
    mixer_out = noise(arg_keys[13], (DI, D), DI ** -0.5, 0.109375, ((0, 4), (1, 8)))
    ffn_gain = jnp.clip(1.0 + 0.1 * jax.random.normal(arg_keys[14], (D,), jnp.float32), 0.5, 1.5).astype(jnp.bfloat16)
    router = noise(arg_keys[15], (D, EXPERTS), (4 * D) ** -0.5, 0.078125, ((0, 8),))
    shared_in = noise(arg_keys[16], (D, 2, FS), D ** -0.5, 0.15625, ((0, 8), (2, 4)))
    shared_out = noise(arg_keys[17], (FS, D), FS ** -0.5, 0.1875, ((0, 4), (1, 8)))
    expert_in = noise(arg_keys[18], (EXPERTS, D, 2, FE), D ** -0.5, 0.15625, ((0, 8), (3, 4)))
    expert_out = noise(arg_keys[19], (EXPERTS, FE, D), FE ** -0.5, 0.25, ((0, 8), (1, 4)))
    cotangent = noise(arg_keys[20], (TOKENS, D), 1.0, 6.0, ((0, 8),))
    return dict(hidden=hidden, segment_ids=segment_ids, routes=routes, norm_gain=norm_gain, mixer_in=mixer_in, state_in=state_in, step_in=step_in, conv_value=conv_value, conv_value_bias=conv_value_bias, conv_state=conv_state, conv_state_bias=conv_state_bias, head_params=head_params, gated_gain=gated_gain, mixer_out=mixer_out, ffn_gain=ffn_gain, router=router, shared_in=shared_in, shared_out=shared_out, expert_in=expert_in, expert_out=expert_out, cotangent=cotangent)


EPS = 1e-05
HIGH = lax.Precision.HIGHEST
MASKED = -1e+30

@jax.custom_vjp
def low(v):
    return lax.optimization_barrier(v.astype(jnp.bfloat16)).astype(jnp.float32)

@jax.custom_vjp
def low_back(v):
    return v

def low_keep(v):
    return (low(v), None)

def low_pass(kept, grad):
    return (grad,)

def back_keep(v):
    return (v, None)

def back_low(kept, grad):
    return (low(grad),)
low.defvjp(low_keep, low_pass)
low_back.defvjp(back_keep, back_low)

def matmul(left_side, right_side):
    return jnp.dot(left_side, right_side, precision=HIGH, preferred_element_type=jnp.float32)

def causal_conv(seg_ext, extended, conv_taps, conv_bias):
    tap_count = conv_taps.shape[0]
    length = extended.shape[0] - tap_count + 1
    own_seg = seg_ext[tap_count - 1:]
    summed = jnp.broadcast_to(conv_bias[None, :], (length, extended.shape[1]))
    for offset in range(tap_count):
        same_doc = (seg_ext[offset:offset + length] == own_seg).astype(jnp.float32)
        summed = summed + conv_taps[offset][None, :] * extended[offset:offset + length] * same_doc[:, None]
    return jax.nn.silu(summed)

def ssd_step(neg_rate, carried, pieces):
    states, prev_seg = carried
    values, write_vec, read_vec, step_size, seg_block = pieces
    length = values.shape[0]
    cumul = jnp.cumsum(step_size * neg_rate[None, :], axis=0)
    causal = jnp.arange(length)[:, None] >= jnp.arange(length)[None, :]
    visible = causal & (seg_block[:, None] == seg_block[None, :])
    spread = jnp.where(visible[:, :, None], cumul[:, None, :] - cumul[None, :, :], MASKED)
    inner_prod = jnp.dot(read_vec, write_vec.T, precision=HIGH, preferred_element_type=jnp.float32)
    mixing = jnp.exp(spread) * inner_prod[:, :, None] * step_size[None, :, :]
    output = jnp.einsum('tsh,shp->thp', mixing, values, precision=HIGH)
    entry_wt = jnp.exp(cumul) * (seg_block == prev_seg).astype(jnp.float32)[:, None]
    output = output + entry_wt[:, :, None] * jnp.einsum('tn,hpn->thp', read_vec, states, precision=HIGH)
    last_seg = seg_block[length - 1]
    tail_wt = jnp.exp(cumul[length - 1][None, :] - cumul) * (seg_block == last_seg).astype(jnp.float32)[:, None] * step_size
    renewed = entry_wt[length - 1][:, None, None] * states + jnp.einsum('sh,shp,sn->hpn', tail_wt, values, write_vec, precision=HIGH)
    return ((renewed, last_seg), output)

def ssd_scan(values, write_vec, read_vec, step_size, neg_rate, segments, states, prev_seg, block_len):
    total_len = values.shape[0]
    head_count = values.shape[1]
    head_width = values.shape[2]
    block_count = total_len // block_len
    pieces = (values.reshape(block_count, block_len, head_count, head_width), write_vec.reshape(block_count, block_len, write_vec.shape[1]), read_vec.reshape(block_count, block_len, read_vec.shape[1]), step_size.reshape(block_count, block_len, head_count), segments.reshape(block_count, block_len))
    step_fn = jax.checkpoint(partial(ssd_step, neg_rate))
    final_carry, outputs = lax.scan(step_fn, (states, prev_seg), pieces)
    return (outputs.reshape(total_len, head_count, head_width), final_carry[0])

def slot_table(local_routes):
    flat_routes = local_routes.reshape(-1)
    route_hits = (flat_routes[:, None] == jnp.arange(EXPERTS, dtype=jnp.int32)[None, :]).astype(jnp.int32)
    earlier = jnp.cumsum(route_hits, axis=0, dtype=jnp.int32) - route_hits
    position = lax.optimization_barrier(jnp.sum(earlier * route_hits, axis=1, dtype=jnp.int32))
    targets = flat_routes * CAP + position
    owners = jnp.arange(flat_routes.shape[0], dtype=jnp.int32) // TOPK
    sources = jnp.full((EXPERTS * CAP,), local_routes.shape[0], jnp.int32).at[targets].set(owners)
    return (targets.reshape(local_routes.shape), sources)

def layer(segment_ids, routes, hidden, norm_gain, mixer_in, state_in, step_in, conv_value, conv_value_bias, conv_state, conv_state_bias, head_params, gated_gain, mixer_out, ffn_gain, router, shared_in, shared_out, expert_in, expert_out):
    inv_first = lax.rsqrt(lax.optimization_barrier(jnp.mean(hidden * hidden, axis=1, keepdims=True)) + EPS)
    normed = low(hidden * inv_first * norm_gain[None, :])
    zx_out = low_back(matmul(normed, mixer_in.reshape(D, 2 * DI)))
    gate_z = zx_out[:, :DI]
    state_pre = low_back(matmul(normed, state_in))
    dt_raw = low_back(matmul(normed, step_in))
    pre_conv = jnp.concatenate([zx_out[:, DI:], state_pre], axis=1)
    extended = jnp.concatenate([jnp.zeros((KW - 1, DI + 2 * NS), jnp.float32), pre_conv], axis=0)
    seg_ext = jnp.concatenate([jnp.full((KW - 1,), -1, jnp.int32), segment_ids])
    conv_taps = jnp.concatenate([conv_value.transpose(0, 2, 1).reshape(KW, DI), conv_state], axis=1)
    conv_bias = jnp.concatenate([conv_value_bias.T.reshape(DI), conv_state_bias])
    conv_out = causal_conv(seg_ext, extended, conv_taps, conv_bias)
    values = conv_out[:, :DI].reshape(TOKENS, H, HD)
    write_vec = conv_out[:, DI:DI + NS]
    read_vec = conv_out[:, DI + NS:]
    step_size = jax.nn.softplus(dt_raw + head_params[1][None, :])
    neg_rate = -jnp.exp(head_params[0])
    ssd_out, final_state = ssd_scan(values, write_vec, read_vec, step_size, neg_rate, segment_ids, jnp.zeros((H, HD, NS), jnp.float32), jnp.int32(-1), BLK)
    ssd_out = ssd_out + head_params[2][None, :, None] * values
    gated = ssd_out.reshape(TOKENS, DI) * jax.nn.silu(gate_z)
    mean_square = lax.optimization_barrier(jnp.mean(gated * gated, axis=1))
    scaled = low(gated * gated_gain.T.reshape(DI)[None, :])
    mixer_proj = low_back(matmul(scaled, mixer_out))
    mixed_out = hidden + mixer_proj * lax.rsqrt(mean_square + EPS)[:, None]
    inv_second = lax.rsqrt(lax.optimization_barrier(jnp.mean(mixed_out * mixed_out, axis=1, keepdims=True)) + EPS)
    ffn_in = low(mixed_out * inv_second * ffn_gain[None, :])
    logits = low_back(matmul(ffn_in, router))
    gate_weights = jax.nn.softmax(jnp.take_along_axis(logits, routes, axis=1), axis=1)
    shared_mid = low_back(matmul(ffn_in, shared_in.reshape(D, 2 * FS)))
    shared_act = low(jax.nn.silu(shared_mid[:, :FS]) * shared_mid[:, FS:])
    shared_res = low_back(matmul(shared_act, shared_out))

    def expert_block(pieces):
        block_in, block_routes, block_gates = pieces
        targets, sources = slot_table(block_routes)
        padded = jnp.concatenate([block_in, jnp.zeros((1, D), jnp.float32)], axis=0)
        slot_rows = padded[sources].reshape(EXPERTS, CAP, D)
        expert_mid = low_back(jnp.einsum('ecd,edgf->ecgf', slot_rows, expert_in, precision=HIGH))
        expert_act = low(jax.nn.silu(expert_mid[:, :, 0]) * expert_mid[:, :, 1])
        expert_res = low_back(jnp.einsum('ecf,efd->ecd', expert_act, expert_out, precision=HIGH))
        picked = expert_res.reshape(EXPERTS * CAP, D)[targets]
        return lax.optimization_barrier(jnp.sum(block_gates[:, :, None] * picked, axis=1))
    routed = lax.map(jax.checkpoint(expert_block), (ffn_in.reshape(N_DP, GROUP, D), routes.reshape(N_DP, GROUP, TOPK), gate_weights.reshape(N_DP, GROUP, TOPK)))
    return mixed_out + shared_res + routed.reshape(TOKENS, D)

def reference(hidden, segment_ids, routes, norm_gain, mixer_in, state_in, step_in, conv_value, conv_value_bias, conv_state, conv_state_bias, head_params, gated_gain, mixer_out, ffn_gain, router, shared_in, shared_out, expert_in, expert_out, cotangent):
    forward = partial(layer, segment_ids, routes)
    output, pullback = jax.vjp(forward, hidden.astype(jnp.float32), norm_gain.astype(jnp.float32), mixer_in.astype(jnp.float32), state_in.astype(jnp.float32), step_in.astype(jnp.float32), conv_value.astype(jnp.float32), conv_value_bias.astype(jnp.float32), conv_state.astype(jnp.float32), conv_state_bias.astype(jnp.float32), head_params.astype(jnp.float32), gated_gain.astype(jnp.float32), mixer_out.astype(jnp.float32), ffn_gain.astype(jnp.float32), router.astype(jnp.float32), shared_in.astype(jnp.float32), shared_out.astype(jnp.float32), expert_in.astype(jnp.float32), expert_out.astype(jnp.float32))
    grads = pullback(cotangent.astype(jnp.float32))
    return (output.astype(jnp.bfloat16), grads[0], grads[1], grads[2], grads[3], grads[4], grads[5], grads[6], grads[7], grads[8], grads[9], grads[10], grads[11], grads[12], grads[13], grads[14], grads[15], grads[16], grads[17])
```

```python
from functools import partial

import jax
import jax.numpy as jnp
from jax import lax
from jax.experimental import pallas as pl
from jax.experimental.pallas import tpu as pltpu
from jax.sharding import PartitionSpec as P

MESH = pl.DeviceIdType.MESH
BLK = 128
EXPERTS = 64
TOPK = 6
DI = 3072
CAP = 64
LANES = 128

EPS = 1e-05
HIGH = lax.Precision.HIGHEST
MASKED = -1e30
BF = jnp.bfloat16
F32 = jnp.float32
ANY = pl.BlockSpec(memory_space=pl.ANY)
VM = pl.BlockSpec(memory_space=pltpu.VMEM)


def dot(a, b, dims=((1,), (0,)), precision=None):
    return lax.dot_general(
        a, b, (dims, ((), ())), precision=precision, preferred_element_type=F32
    )


def silu_slope(argument):
    sigmoid_val = jax.nn.sigmoid(argument)
    return sigmoid_val * (1.0 + argument * (1.0 - sigmoid_val))


def half_rows(rows):
    return (rows // 32) * 16


def ring_place(n, d):
    high, low = d // 2, d % 2
    return high * (1 - low) + (n - 1 - high) * low


def ring_device(n, p):
    back = p // (n // 2)
    return (2 * p) * (1 - back) + (2 * (n - 1 - p) + 1) * back


def greet(targets):
    barrier = pltpu.get_barrier_semaphore()
    for target in targets:
        pl.semaphore_signal(barrier, inc=1, device_id=target, device_id_type=MESH)
    pl.semaphore_wait(barrier, len(targets))


def remote(src, dst, send, recv, target):
    return pltpu.make_async_remote_copy(
        src_ref=src,
        dst_ref=dst,
        send_sem=send,
        recv_sem=recv,
        device_id=target,
        device_id_type=MESH,
    )


def mp_partners(m):
    return {"mp": m + 1 - 2 * (m % 2)}, {"mp": (m + 2) % 4}


def ring_neighbours(n):
    p = ring_place(n, lax.axis_index("dp"))
    nxt = {"dp": ring_device(n, (p + 1) % n)}
    prv = {"dp": ring_device(n, (p + n - 1) % n)}
    return p, nxt, prv


def gather_kernel(n, k, *refs):
    ins, outs = refs[:k], refs[k : 2 * k]
    local_sem, send_sem, recv_sem = refs[2 * k :]
    d = lax.axis_index("dp")
    p, nxt, prv = ring_neighbours(n)
    greet([nxt, prv])
    local = []
    for j in range(k):
        copy = pltpu.make_async_copy(ins[j], outs[j].at[d], local_sem.at[j])
        copy.start()
        local.append(copy)
    copies = {}
    for s in range(n - 1):
        for way in range(2):
            origin = ring_device(n, (p + n - s) % n if way == 0 else (p + s) % n)
            for j in range(k):
                rows = ins[j].shape[0]
                cut = half_rows(rows)
                part = pl.ds(0, cut) if way == 0 else pl.ds(cut, rows - cut)
                if s > 0:
                    copies[s - 1, way, j].wait_recv()
                copy = remote(
                    ins[j].at[part] if s == 0 else outs[j].at[origin, part],
                    outs[j].at[origin, part],
                    send_sem.at[way, s, j],
                    recv_sem.at[way, s, j],
                    nxt if way == 0 else prv,
                )
                copy.start()
                copies[s, way, j] = copy
    for way in range(2):
        for j in range(k):
            copies[n - 2, way, j].wait_recv()
    for copy in copies.values():
        copy.wait_send()
    for copy in local:
        copy.wait()


def gather_dp(arrays, cid):
    n, k = lax.axis_size("dp"), len(arrays)
    return pl.pallas_call(
        partial(gather_kernel, n, k),
        out_shape=[jax.ShapeDtypeStruct((n,) + a.shape, a.dtype) for a in arrays],
        in_specs=[ANY] * k,
        out_specs=[ANY] * k,
        scratch_shapes=[
            pltpu.SemaphoreType.DMA((k,)),
            pltpu.SemaphoreType.DMA((2, n - 1, k)),
            pltpu.SemaphoreType.DMA((2, n - 1, k)),
        ],
        compiler_params=pltpu.CompilerParams(collective_id=cid, has_side_effects=True),
    )(*arrays)


def add_rows(dst, pieces, rows, dtype):
    def body(i, carry):
        sl = pl.ds(pl.multiple_of(i * 16, 16), 16)
        total = pieces[0][sl, :].astype(F32)
        for piece in pieces[1:]:
            total = total + piece[sl, :].astype(F32)
        dst[sl, :] = total.astype(dtype)
        return carry

    lax.fori_loop(0, rows // 16, body, 0)


def scatter_kernel(n, k, *refs):
    ins, outs, slots = refs[:k], refs[k : 2 * k], refs[2 * k : 4 * k]
    send_sem, recv_sem = refs[4 * k :]
    d = lax.axis_index("dp")
    p, nxt, prv = ring_neighbours(n)
    greet([nxt, prv])
    copies = {}
    for s in range(n):
        for way in range(2):
            block = ring_device(n, (p + 2 * n - 1 - s) % n if way == 0 else (p + 1 + s) % n)
            for j in range(k):
                rows = ins[j].shape[1]
                cut = half_rows(rows)
                start, size = (0, cut) if way == 0 else (cut, rows - cut)
                mine = ins[j].at[block, pl.ds(start, size)]
                slot = slots[2 * j + way]
                if s > 0:
                    copies[s - 1, way, j].wait_recv()
                    held = slot.at[s - 1]
                    if s == n - 1:
                        add_rows(outs[j].at[pl.ds(start, size)], [held, mine], size, F32)
                        continue
                    add_rows(held, [held, mine], size, ins[j].dtype)
                    source = held
                else:
                    source = mine
                copy = remote(
                    source,
                    slot.at[s],
                    send_sem.at[way, s, j],
                    recv_sem.at[way, s, j],
                    nxt if way == 0 else prv,
                )
                copy.start()
                copies[s, way, j] = copy
    for copy in copies.values():
        copy.wait_send()


def scatter_dp(arrays, cid):
    n, k = lax.axis_size("dp"), len(arrays)
    slots = []
    for a in arrays:
        cut = half_rows(a.shape[1])
        for size in (cut, a.shape[1] - cut):
            slots.append(pltpu.VMEM((n - 1, size, a.shape[2]), a.dtype))
    return pl.pallas_call(
        partial(scatter_kernel, n, k),
        out_shape=[jax.ShapeDtypeStruct(a.shape[1:], F32) for a in arrays],
        in_specs=[VM] * k,
        out_specs=[VM] * k,
        scratch_shapes=slots
        + [
            pltpu.SemaphoreType.DMA((2, n - 1, k)),
            pltpu.SemaphoreType.DMA((2, n - 1, k)),
        ],
        compiler_params=pltpu.CompilerParams(
            collective_id=cid, has_side_effects=True, vmem_limit_bytes=48 * 1024 * 1024
        ),
    )(*arrays)


def mp_scatter_kernel(x, out, from_core, from_chip, send_sem, recv_sem):
    m = lax.axis_index("mp")
    core, chip = mp_partners(m)
    mine, far = m, (m + 2) % 4
    greet([core, chip])
    first = []
    for i in range(2):
        block = (m + 1 - 2 * (m % 2) + 2 * i) % 4
        copy = remote(x.at[block], from_core.at[i], send_sem.at[i], recv_sem.at[i], core)
        copy.start()
        first.append(copy)
    rows = out.shape[0]
    first[1].wait_recv()
    add_rows(from_core.at[1], [from_core.at[1], x.at[far]], rows, x.dtype)
    last = remote(from_core.at[1], from_chip, send_sem.at[2], recv_sem.at[2], chip)
    last.start()
    first[0].wait_recv()
    last.wait_recv()
    add_rows(out, [x.at[mine], from_core.at[0], from_chip], rows, F32)
    for copy in first + [last]:
        copy.wait_send()


def scatter_mp(x, cid):
    rows, cols = x.shape[1:]
    return pl.pallas_call(
        mp_scatter_kernel,
        out_shape=jax.ShapeDtypeStruct((rows, cols), F32),
        in_specs=[VM],
        out_specs=VM,
        scratch_shapes=[
            pltpu.VMEM((2, rows, cols), x.dtype),
            pltpu.VMEM((rows, cols), x.dtype),
            pltpu.SemaphoreType.DMA((3,)),
            pltpu.SemaphoreType.DMA((3,)),
        ],
        compiler_params=pltpu.CompilerParams(
            collective_id=cid, has_side_effects=True, vmem_limit_bytes=32 * 1024 * 1024
        ),
    )(x)


def mp_gather_kernel(k, *refs):
    ins, outs = refs[:k], refs[k : 2 * k]
    local_sem, send_sem, recv_sem = refs[2 * k :]
    m = lax.axis_index("mp")
    core, chip = mp_partners(m)
    far = (m + 2) % 4
    greet([core, chip])
    copies, local, arrive = [], [], []
    for j in range(k):
        to_chip = remote(ins[j], outs[j].at[m], send_sem.at[0, j], recv_sem.at[0, j], chip)
        to_chip.start()
        to_core = remote(ins[j], outs[j].at[m], send_sem.at[1, j], recv_sem.at[1, j], core)
        to_core.start()
        own = pltpu.make_async_copy(ins[j], outs[j].at[m], local_sem.at[j])
        own.start()
        copies += [to_chip, to_core]
        arrive.append(to_chip)
        local.append(own)
    onward = []
    for j in range(k):
        arrive[j].wait_recv()
        copy = remote(outs[j].at[far], outs[j].at[far], send_sem.at[2, j], recv_sem.at[2, j], core)
        copy.start()
        onward.append(copy)
    for j in range(k):
        copies[2 * j + 1].wait_recv()
        onward[j].wait_recv()
        local[j].wait()
    for copy in copies + onward:
        copy.wait_send()


def gather_mp(arrays, cid):
    k = len(arrays)
    return pl.pallas_call(
        partial(mp_gather_kernel, k),
        out_shape=[jax.ShapeDtypeStruct((4,) + a.shape, a.dtype) for a in arrays],
        in_specs=[ANY] * k,
        out_specs=[ANY] * k,
        scratch_shapes=[
            pltpu.SemaphoreType.DMA((k,)),
            pltpu.SemaphoreType.DMA((3, k)),
            pltpu.SemaphoreType.DMA((3, k)),
        ],
        compiler_params=pltpu.CompilerParams(collective_id=cid, has_side_effects=True),
    )(*arrays)


def token_gather_kernel(n, x, out, local_sem, send_sem, recv_sem, core_send, core_recv):
    d, m = lax.axis_index("dp"), lax.axis_index("mp")
    c = m % 2
    core, chip = mp_partners(m)
    p, nxt, prv = ring_neighbours(n)
    greet([core, chip, nxt, prv])
    own = pltpu.make_async_copy(x, out.at[d, m], local_sem)
    own.start()
    to_chip = remote(x, out.at[d, m], send_sem.at[0, n - 1], recv_sem.at[0, n - 1], chip)
    to_chip.start()
    own.wait()
    to_chip.wait_recv()
    ring, shared = {}, []
    for s in range(n):
        for way in range(2):
            origin = ring_device(n, (p + n - s) % n if way == 0 else (p + s) % n)
            place = out.at[origin, 2 * way + c]
            if s > 0:
                ring[s - 1, way].wait_recv()
            if s < n - 1:
                copy = remote(
                    place,
                    place,
                    send_sem.at[way, s],
                    recv_sem.at[way, s],
                    nxt if way == 0 else prv,
                )
                copy.start()
                ring[s, way] = copy
            over = remote(place, place, core_send.at[way, s], core_recv.at[way, s], core)
            over.start()
            shared.append(over)
    for over in shared:
        over.wait_recv()
    for copy in list(ring.values()) + shared + [to_chip]:
        copy.wait_send()


def gather_tokens(x, cid):
    n = lax.axis_size("dp")
    return pl.pallas_call(
        partial(token_gather_kernel, n),
        out_shape=jax.ShapeDtypeStruct((n, 4) + x.shape, x.dtype),
        in_specs=[ANY],
        out_specs=ANY,
        scratch_shapes=[
            pltpu.SemaphoreType.DMA,
            pltpu.SemaphoreType.DMA((2, n)),
            pltpu.SemaphoreType.DMA((2, n)),
            pltpu.SemaphoreType.DMA((2, n)),
            pltpu.SemaphoreType.DMA((2, n)),
        ],
        compiler_params=pltpu.CompilerParams(collective_id=cid, has_side_effects=True),
    )(x)


def token_scatter_kernel(
    n,
    x,
    out,
    from_core,
    slots,
    mine_buf,
    core_buf,
    first_buf,
    done_buf,
    chip_buf,
    load_sem,
    core_send,
    core_recv,
    send_sem,
    recv_sem,
):
    m = lax.axis_index("mp")
    c, y = m % 2, m // 2
    core, chip = mp_partners(m)
    p, nxt, prv = ring_neighbours(n)
    rows = out.shape[0]
    greet([core, chip, nxt, prv])

    def block_at(s, way):
        return ring_device(n, (p + 2 * n - 1 - s) % n if way == 0 else (p + 1 + s) % n)

    over = {}
    for s in range(n):
        for way in range(2):
            block = block_at(s, way)
            copy = remote(
                x.at[block, 2 * way + 1 - c],
                from_core.at[block, way],
                core_send.at[s, way],
                core_recv.at[s, way],
                core,
            )
            copy.start()
            over[s, way] = copy

    def load(s, way):
        block = block_at(s, way)
        over[s, way].wait_recv()
        a = pltpu.make_async_copy(
            x.at[block, 2 * way + c], mine_buf.at[s % 2, way], load_sem.at[0, s % 2, way]
        )
        b = pltpu.make_async_copy(
            from_core.at[block, way], core_buf.at[s % 2, way], load_sem.at[1, s % 2, way]
        )
        a.start()
        b.start()
        return a, b

    loads = {(0, way): load(0, way) for way in range(2)}
    ring = {}
    for s in range(n):
        for way in range(2):
            a, b = loads[s, way]
            a.wait()
            b.wait()
            if s < n - 1:
                loads[s + 1, way] = load(s + 1, way)
            pieces = [mine_buf.at[s % 2, way], core_buf.at[s % 2, way]]
            if s == 0:
                target = first_buf.at[way]
            else:
                ring[s - 1, way].wait_recv()
                target = slots.at[way, s - 1] if s < n - 1 else done_buf.at[way]
                pieces.append(slots.at[way, s - 1])
            add_rows(target, pieces, rows, BF)
            if s < n - 1:
                copy = remote(
                    target,
                    slots.at[way, s],
                    send_sem.at[way, s],
                    recv_sem.at[way, s],
                    nxt if way == 0 else prv,
                )
                copy.start()
                ring[s, way] = copy
    last = remote(
        done_buf.at[1 - y], chip_buf, send_sem.at[0, n - 1], recv_sem.at[0, n - 1], chip
    )
    last.start()
    last.wait_recv()
    add_rows(out, [done_buf.at[y], chip_buf], rows, F32)
    for copy in list(over.values()) + list(ring.values()) + [last]:
        copy.wait_send()


def scatter_tokens(x, cid):
    n, _, rows, cols = x.shape
    out, _ = pl.pallas_call(
        partial(token_scatter_kernel, n),
        out_shape=[
            jax.ShapeDtypeStruct((rows, cols), F32),
            jax.ShapeDtypeStruct((n, 2, rows, cols), BF),
        ],
        in_specs=[ANY],
        out_specs=[VM, ANY],
        scratch_shapes=[
            pltpu.VMEM((2, n - 1, rows, cols), BF),
            pltpu.VMEM((2, 2, rows, cols), BF),
            pltpu.VMEM((2, 2, rows, cols), BF),
            pltpu.VMEM((2, rows, cols), BF),
            pltpu.VMEM((2, rows, cols), BF),
            pltpu.VMEM((rows, cols), BF),
            pltpu.SemaphoreType.DMA((2, 2, 2)),
            pltpu.SemaphoreType.DMA((n, 2)),
            pltpu.SemaphoreType.DMA((n, 2)),
            pltpu.SemaphoreType.DMA((2, n)),
            pltpu.SemaphoreType.DMA((2, n)),
        ],
        compiler_params=pltpu.CompilerParams(
            collective_id=cid, has_side_effects=True, vmem_limit_bytes=48 * 1024 * 1024
        ),
    )(x)
    return out


def head_pair(pair, first, second):
    lane = lax.broadcasted_iota(jnp.int32, first.shape, 1)
    return jnp.where(lane < LANES // 2, first, second)


def visible_pairs(seg_col, seg_row):
    length = seg_col.shape[0]
    row = lax.broadcasted_iota(jnp.int32, (length, length), 0)
    col = lax.broadcasted_iota(jnp.int32, (length, length), 1)
    return (row >= col) & (seg_col == seg_row)


def state_decay(entry, expand):
    last = entry[entry.shape[0] - 1 :, :]
    spread = jnp.broadcast_to(last, (LANES, LANES)).T
    return dot(expand, spread, ((0,), (0,)), HIGH)


def recur_kernel(
    pairs,
    values,
    write,
    read,
    cumul,
    cumul_t,
    step_t,
    entry,
    tail,
    seg_col,
    seg_row,
    expand,
    skip,
    start,
    out,
    kept,
    state,
):
    @pl.when(pl.program_id(0) == 0)
    def _():
        state[...] = start[...]

    held = state[...]
    kept[0] = held
    v, b, c = values[...], write[...], read[...]
    scores = dot(c, b, ((1,), (1,)), HIGH)
    visible = visible_pairs(seg_col[...], seg_row[...])
    entry_full = dot(entry[...], expand[...], precision=HIGH)
    tail_full = dot(tail[...], expand[...], precision=HIGH)
    carried = entry_full * dot(c, held, ((1,), (1,)), HIGH) + skip[...] * v
    cum, cum_t, st_t = cumul[...], cumul_t[...], step_t[...]
    for pair in range(pairs):
        cols = slice(pair * LANES, (pair + 1) * LANES)
        v2 = v[:, cols]
        found = []
        for h in (2 * pair, 2 * pair + 1):
            spread = jnp.where(visible, cum[:, h : h + 1] - cum_t[h : h + 1, :], MASKED)
            mixing = jnp.exp(spread) * (scores * st_t[h : h + 1, :])
            found.append(dot(mixing, v2, precision=HIGH))
        out[:, cols] = head_pair(pair, found[0], found[1]) + carried[:, cols]
    state[...] = state_decay(entry[...], expand[...]) * held + dot(v * tail_full, b, ((0,), (0,)), HIGH)


def recur_specs(width, lengths):
    def rows(cols):
        return pl.BlockSpec((BLK, cols), lambda i: (lengths(i), 0))

    def flat(count):
        return pl.BlockSpec((count, BLK), lambda i: (0, lengths(i)))

    def whole(shape):
        return pl.BlockSpec(shape, lambda i: (0,) * len(shape))

    return rows, flat, whole


def recur_forward(v, b, c, cumul, cumul_t, step_t, entry, tail, seg_col, seg_row, expand, skip, start):
    total, width = v.shape
    blocks = total // BLK
    rows, flat, whole = recur_specs(width, lambda i: i)
    return pl.pallas_call(
        partial(recur_kernel, width // LANES),
        grid=(blocks,),
        out_shape=[
            jax.ShapeDtypeStruct((total, width), F32),
            jax.ShapeDtypeStruct((blocks, width, LANES), F32),
        ],
        in_specs=[
            rows(width),
            rows(LANES),
            rows(LANES),
            rows(LANES),
            flat(16),
            flat(16),
            rows(LANES),
            rows(LANES),
            rows(1),
            flat(1),
            whole((LANES, width)),
            whole((1, width)),
            whole((width, LANES)),
        ],
        out_specs=[
            rows(width),
            pl.BlockSpec((1, width, LANES), lambda i: (i, 0, 0)),
        ],
        scratch_shapes=[pltpu.VMEM((width, LANES), F32)],
        compiler_params=pltpu.CompilerParams(vmem_limit_bytes=48 * 1024 * 1024),
    )(v, b, c, cumul, cumul_t, step_t, entry, tail, seg_col, seg_row, expand, skip, start)


def adjoint_kernel(
    pairs,
    values,
    write,
    read,
    cumul,
    cumul_t,
    step_t,
    step,
    entry,
    tail_bare,
    seg_col,
    seg_row,
    expand,
    skip,
    kept,
    d_out,
    start,
    d_values,
    d_write,
    d_read,
    d_step,
    d_rate_step,
    d_skip,
    state,
    columns,
):
    @pl.when(pl.program_id(0) == 0)
    def _():
        state[...] = start[...]
        d_skip[...] = jnp.zeros_like(d_skip)
        columns[...] = jnp.zeros_like(columns)

    length = values.shape[0]
    lam, held = state[...], kept[0]
    v, b, c, dy = values[...], write[...], read[...], d_out[...]
    ex = expand[...]
    st = step[...]
    scores = dot(c, b, ((1,), (1,)), HIGH)
    visible = visible_pairs(seg_col[...], seg_row[...])
    entry_full = dot(entry[...], ex, precision=HIGH)
    tail = tail_bare[...] * st
    tail_full = dot(tail, ex, precision=HIGH)
    c_state = dot(c, held, ((1,), (1,)), HIGH)
    b_lam = dot(b, lam, ((1,), (1,)), HIGH)
    dy_in = dy * entry_full
    v_out = v * tail_full
    dc = dot(dy_in, held, precision=HIGH)
    db = dot(v_out, lam, precision=HIGH)
    reach = dot(dy_in * c_state, ex, ((1,), (1,)), HIGH)
    leave = dot(v * b_lam, ex, ((1,), (1,)), HIGH)
    d_skip[...] += jnp.sum(dy * v, axis=0, keepdims=True)
    dv_far = tail_full * b_lam + skip[...] * dy
    cum, cum_t, st_t = cumul[...], cumul_t[...], step_t[...]
    lane = lax.broadcasted_iota(jnp.int32, (length, LANES), 1)
    d_scores = jnp.zeros((length, length), F32)
    row_sums = jnp.zeros((length, LANES), F32)
    for pair in range(pairs):
        cols = slice(pair * LANES, (pair + 1) * LANES)
        v2, dy2 = v[:, cols], dy[:, cols]
        found = []
        for j in range(2):
            h = 2 * pair + j
            own = (lane < LANES // 2) if j == 0 else (lane >= LANES // 2)
            d_mix = dot(jnp.where(own, dy2, 0.0), v2, ((1,), (1,)), HIGH)
            spread = jnp.where(visible, cum[:, h : h + 1] - cum_t[h : h + 1, :], MASKED)
            decay = jnp.exp(spread)
            decay_step = decay * st_t[h : h + 1, :]
            weighted = d_mix * scores * decay
            d_scores = d_scores + d_mix * decay_step
            columns[h : h + 1, :] = jnp.sum(weighted, axis=0, keepdims=True)
            per_row = jnp.sum(weighted * st_t[h : h + 1, :], axis=1, keepdims=True)
            row_sums = jnp.where(lane == h, per_row, row_sums)
            found.append(dot(scores * decay_step, dy2, ((0,), (0,))))
        d_values[:, cols] = head_pair(pair, found[0], found[1]) + dv_far[:, cols]
    d_read[...] = dc + dot(d_scores, b, precision=HIGH)
    d_write[...] = db + dot(d_scores, c, ((0,), (0,)), HIGH)
    col_sums = columns[...].T
    leave_step = tail * leave
    d_step[...] = col_sums + tail_bare[...] * leave
    d_cum = row_sums - st * col_sums + reach - leave_step
    row = lax.broadcasted_iota(jnp.int32, (length, length), 0)
    col = lax.broadcasted_iota(jnp.int32, (length, length), 1)
    upper = (col >= row).astype(F32)
    met = jnp.sum(dot(lam * held, ex, ((0,), (1,)), HIGH), axis=0, keepdims=True)
    at_end = jnp.sum(leave_step, axis=0, keepdims=True) + entry[length - 1 :, :] * met
    d_rate_step[...] = dot(upper, d_cum, precision=HIGH) + at_end
    state[...] = state_decay(entry[...], ex) * lam + dot(dy_in, c, ((0,), (0,)), HIGH)


def recur_backward(
    v, b, c, cumul, cumul_t, step_t, step, entry, tail_bare, seg_col, seg_row, expand, skip, kept, dy, start
):
    total, width = v.shape
    blocks = total // BLK
    rows, flat, whole = recur_specs(width, lambda i: blocks - 1 - i)
    return pl.pallas_call(
        partial(adjoint_kernel, width // LANES),
        grid=(blocks,),
        out_shape=[
            jax.ShapeDtypeStruct((total, width), F32),
            jax.ShapeDtypeStruct((total, LANES), F32),
            jax.ShapeDtypeStruct((total, LANES), F32),
            jax.ShapeDtypeStruct((total, LANES), F32),
            jax.ShapeDtypeStruct((total, LANES), F32),
            jax.ShapeDtypeStruct((1, width), F32),
        ],
        in_specs=[
            rows(width),
            rows(LANES),
            rows(LANES),
            rows(LANES),
            flat(16),
            flat(16),
            rows(LANES),
            rows(LANES),
            rows(LANES),
            rows(1),
            flat(1),
            whole((LANES, width)),
            whole((1, width)),
            pl.BlockSpec((1, width, LANES), lambda i: (blocks - 1 - i, 0, 0)),
            rows(width),
            whole((width, LANES)),
        ],
        out_specs=[
            rows(width),
            rows(LANES),
            rows(LANES),
            rows(LANES),
            rows(LANES),
            whole((1, width)),
        ],
        scratch_shapes=[pltpu.VMEM((width, LANES), F32), pltpu.VMEM((LANES, LANES), F32)],
        compiler_params=pltpu.CompilerParams(vmem_limit_bytes=48 * 1024 * 1024),
    )(v, b, c, cumul, cumul_t, step_t, step, entry, tail_bare, seg_col, seg_row, expand, skip, kept, dy, start)


def state_scan_kernel(
    n, reverse, mine, decay, expand, out, first, second, got_first, got_second, half, send_sem, recv_sem
):
    d = lax.axis_index("dp")
    q = n - 1 - d if reverse else d
    zq, xq = q // 2, q % 2
    depth = n // 2
    rows = mine.shape[0] // 2
    xf = xq.astype(F32)

    def device(logical):
        return {"dp": n - 1 - logical if reverse else logical}

    beside = device(2 * zq + 1 - xq)
    others = [device(2 * ((zq + k) % depth) + xq) for k in range(1, depth)]
    own_rows = pl.ds(pl.multiple_of(rows * xq, 8), rows)
    other_rows = pl.ds(pl.multiple_of(rows * (1 - xq), 8), rows)
    own_lanes = pl.ds(pl.multiple_of(rows * xq, LANES), rows)

    def spread(row):
        square = jnp.broadcast_to(row, (LANES, LANES)).T
        return dot(expand[:, own_lanes], square, ((0,), (0,)), HIGH)

    for k in range(1, depth):

        @pl.when(zq < k)
        def _():
            got_second[k - 1] = jnp.zeros(got_second.shape[1:], F32)

    first[0:rows, :] = mine[other_rows, :]
    first[rows : rows + 8, :] = decay[...]
    greet([beside] + others)
    one = remote(first, got_first, send_sem.at[0], recv_sem.at[0], beside)
    one.start()
    one.wait_recv()
    own, own_decay = mine[own_rows, :], decay[...]
    got, got_decay = got_first[0:rows, :], got_first[rows : rows + 8, :]
    early = own * (1.0 - xf) + got * xf
    early_decay = own_decay * (1.0 - xf) + got_decay * xf
    late = own * xf + got * (1.0 - xf)
    late_decay = own_decay * xf + got_decay * (1.0 - xf)
    second[0:rows, :] = spread(late_decay[0:1, :]) * early + late
    second[rows : rows + 8, :] = early_decay * late_decay
    sent = []
    for k in range(1, depth):
        copy = remote(
            second, got_second.at[k - 1], send_sem.at[k], recv_sem.at[k], device(2 * ((zq + k) % depth) + xq)
        )
        sent.append(copy)

        @pl.when(zq + k < depth)
        def _():
            copy.start()

    total = jnp.zeros((rows, LANES), F32)
    for k in range(depth - 1, 0, -1):

        @pl.when(zq >= k)
        def _():
            sent[k - 1].wait_recv()

        got_k = got_second.at[k - 1]
        total = spread(got_k[rows : rows + 1, :]) * total + got_k[0:rows, :]
    after = spread(early_decay[0:1, :]) * total + early
    out[own_rows, :] = total * (1.0 - xf) + after * xf
    half[...] = total * xf + after * (1.0 - xf)
    last = remote(half, out.at[own_rows, :], send_sem.at[depth], recv_sem.at[depth], beside)
    last.start()
    last.wait_recv()
    one.wait_send()
    last.wait_send()
    for k in range(1, depth):

        @pl.when(zq + k < depth)
        def _():
            sent[k - 1].wait_send()


def state_scan(mine, decay, expand, reverse, cid):
    n = lax.axis_size("dp")
    rows = mine.shape[0]
    half = rows // 2
    depth = n // 2
    return pl.pallas_call(
        partial(state_scan_kernel, n, reverse),
        out_shape=jax.ShapeDtypeStruct(mine.shape, F32),
        in_specs=[VM] * 3,
        out_specs=VM,
        scratch_shapes=[
            pltpu.VMEM((half + 8, LANES), F32),
            pltpu.VMEM((half + 8, LANES), F32),
            pltpu.VMEM((half + 8, LANES), F32),
            pltpu.VMEM((depth - 1, half + 8, LANES), F32),
            pltpu.VMEM((half, LANES), F32),
            pltpu.SemaphoreType.DMA((depth + 1,)),
            pltpu.SemaphoreType.DMA((depth + 1,)),
        ],
        compiler_params=pltpu.CompilerParams(
            collective_id=cid, has_side_effects=True, vmem_limit_bytes=32 * 1024 * 1024
        ),
    )(mine, decay, expand)


def pick_matrix(position, own):
    length = position.shape[1]
    slot = lax.broadcasted_iota(jnp.int32, (CAP, length), 0).astype(F32)
    parts = [
        jnp.where(position[e : e + 1, :] == slot, 1.0, 0.0).astype(BF) for e in range(own)
    ]
    return jnp.concatenate(parts, axis=0)


def pick_kernel(own, x, position, out):
    pick = pick_matrix(position[0], own)
    picked = dot(pick, x[0]).astype(BF)
    out[...] = picked.reshape(out.shape)


def pick_gate_kernel(own, x, position, routes, router, out, gates, slot_gates):
    rows = x[0]
    pick = pick_matrix(position[0], own)
    picked = dot(pick, rows).astype(BF)
    out[...] = picked.reshape(out.shape)
    logits = dot(rows, router[...])
    lane = lax.broadcasted_iota(jnp.int32, logits.shape, 1).astype(F32)
    named = routes[0][:, 0:1] == lane
    for k in range(1, TOPK):
        named = named | (routes[0][:, k : k + 1] == lane)
    top = jnp.max(jnp.where(named, logits, MASKED), axis=1, keepdims=True)
    powers = jnp.where(named, jnp.exp(jnp.minimum(logits - top, 0.0)), 0.0)
    gate = powers / jnp.sum(powers, axis=1, keepdims=True)
    gates[0] = gate
    high = gate.astype(BF)
    low = (gate - high.astype(F32)).astype(BF)
    of_slot = dot(pick, high) + dot(pick, low)
    row = lax.broadcasted_iota(jnp.int32, of_slot.shape, 0)
    col = lax.broadcasted_iota(jnp.int32, of_slot.shape, 1)
    mine = col - lax.axis_index("dp") * own == row // CAP
    of_slot = jnp.sum(jnp.where(mine, of_slot, 0.0), axis=1, keepdims=True)
    slot_gates[...] = jnp.broadcast_to(of_slot, pick.shape[:1] + (LANES,)).reshape(slot_gates.shape)


def slot_spec(own, cols):
    return pl.BlockSpec((own, 1, CAP, cols), lambda s: (0, s, 0, 0))


def token_spec(rows, cols):
    return pl.BlockSpec((1, rows, cols), lambda s: (s, 0, 0))


BIG = pltpu.CompilerParams(vmem_limit_bytes=56 * 1024 * 1024)


def pick_rows(x, position):
    n, tokens, model = x.shape
    own = position.shape[1]
    return pl.pallas_call(
        partial(pick_kernel, own),
        grid=(n,),
        out_shape=jax.ShapeDtypeStruct((own, n, CAP, model), BF),
        in_specs=[token_spec(tokens, model), token_spec(own, tokens)],
        out_specs=slot_spec(own, model),
        compiler_params=BIG,
    )(x, position)


def pick_rows_gates(x, position, routes, router):
    n, tokens, model = x.shape
    own = position.shape[1]
    return pl.pallas_call(
        partial(pick_gate_kernel, own),
        grid=(n,),
        out_shape=[
            jax.ShapeDtypeStruct((own, n, CAP, model), BF),
            jax.ShapeDtypeStruct((n, tokens, LANES), F32),
            jax.ShapeDtypeStruct((own, n, CAP, LANES), F32),
        ],
        in_specs=[
            token_spec(tokens, model),
            token_spec(own, tokens),
            token_spec(tokens, TOPK),
            pl.BlockSpec((model, LANES), lambda s: (0, 0)),
        ],
        out_specs=[slot_spec(own, model), token_spec(tokens, LANES), slot_spec(own, LANES)],
        compiler_params=BIG,
    )(x, position, routes, router)


def expert_kernel(
    own, rows, cot_rows, gate, w_in, w_out, grad_in, grad_out, d_rows, res, dots, wide, both
):
    e, part = pl.program_id(0), pl.program_id(1)
    model = rows.shape[2]
    units = w_out.shape[1]

    @pl.when(part == 0)
    def _():
        wide[...] = w_in[0].astype(F32)
        both[:, 0:units] = wide[pl.ds(0, model, stride=2), :].astype(BF)
        both[:, units : 2 * units] = wide[pl.ds(1, model, stride=2), :].astype(BF)
        grad_in[...] = jnp.zeros_like(grad_in)
        grad_out[...] = jnp.zeros_like(grad_out)

    x, c, g = rows[0], cot_rows[0], gate[0]
    mid = dot(x, both[...])
    mid_gate, mid_up = mid[:, 0:units], mid[:, units : 2 * units]
    sig = jax.nn.sigmoid(mid_gate)
    mid_silu = mid_gate * sig
    act = (mid_silu * mid_up).astype(BF).astype(F32)
    back = dot(c, w_out[0], ((1,), (1,)))
    dot_sum = jnp.sum(act * back, axis=1, keepdims=True)
    lane = lax.broadcasted_iota(jnp.int32, g.shape, 1)
    dots[0] = jnp.where(lane == lax.axis_index("dp") * own + e, dot_sum, 0.0).astype(BF)
    gated = (act * g).astype(BF)
    d_act = back * g
    d_gate = (d_act * mid_up * (sig * (1.0 + mid_gate * (1.0 - sig)))).astype(BF)
    d_mid = jnp.concatenate([d_gate, (d_act * mid_silu).astype(BF)], axis=1)
    grads = dot(x, d_mid, ((0,), (0,)))
    grad_in[0, pl.ds(0, model, stride=2), :] += grads[:, 0:units]
    grad_in[0, pl.ds(1, model, stride=2), :] += grads[:, units : 2 * units]
    grad_out[0] += dot(gated, c, ((0,), (0,)))
    d_rows[0] = dot(d_mid, both[...], ((1,), (1,))).astype(BF)
    res[0] = dot(gated, w_out[0]).astype(BF)


def run_experts(rows, cot_rows, gate, w_in, w_out):
    own, slots, model = rows.shape
    units = w_out.shape[1]
    part = min(slots, 512)

    def slot(cols):
        return pl.BlockSpec((1, part, cols), lambda e, j: (e, j, 0))

    def weight(a, b):
        return pl.BlockSpec((1, a, b), lambda e, j: (e, 0, 0))

    return pl.pallas_call(
        partial(expert_kernel, own),
        grid=(own, slots // part),
        out_shape=[
            jax.ShapeDtypeStruct((own, 2 * model, units), F32),
            jax.ShapeDtypeStruct((own, units, model), F32),
            jax.ShapeDtypeStruct((own, slots, model), BF),
            jax.ShapeDtypeStruct((own, slots, model), BF),
            jax.ShapeDtypeStruct((own, slots, LANES), BF),
        ],
        in_specs=[slot(model), slot(model), slot(LANES), weight(2 * model, units), weight(units, model)],
        out_specs=[weight(2 * model, units), weight(units, model), slot(model), slot(model), slot(LANES)],
        scratch_shapes=[pltpu.VMEM((2 * model, units), F32), pltpu.VMEM((model, 2 * units), BF)],
        compiler_params=BIG,
    )(rows, cot_rows, gate, w_in, w_out)


def put_matrix(position, own):
    length = position.shape[0]
    lane = lax.broadcasted_iota(jnp.int32, (length, LANES), 1)
    slot = (lane % CAP).astype(F32)
    parts = []
    for e in range(0, own, 2):
        held = jnp.where(lane < CAP, position[:, e : e + 1], position[:, e + 1 : e + 2])
        parts.append(jnp.where(held == slot, 1.0, 0.0).astype(BF))
    return jnp.concatenate(parts, axis=1)


def put_kernel(own, position, rows, shared, *rest):
    extra, out = (rest[0], rest[1]) if len(rest) == 2 else (None, rest[0])
    model = shared.shape[1]
    put = put_matrix(position[0], own)
    total = dot(put, rows[...].reshape(own * CAP, model))
    here = jnp.where(pl.program_id(0) == lax.axis_index("dp"), 1.0, 0.0)
    out[0, :, 0:model] = (total + here * shared[...]).astype(BF)
    if extra is not None:
        out[0, :, model : model + LANES] = dot(put, extra[...].reshape(own * CAP, LANES)).astype(BF)


def put_rows(position, rows, shared, extra=None):
    n, tokens, own = position.shape
    model = shared.shape[1]
    cols = model + (0 if extra is None else LANES)
    more = [] if extra is None else [extra.reshape(own, n, CAP, LANES)]
    return pl.pallas_call(
        partial(put_kernel, own),
        grid=(n,),
        out_shape=jax.ShapeDtypeStruct((n, tokens, cols), BF),
        in_specs=[
            token_spec(tokens, own),
            slot_spec(own, model),
            pl.BlockSpec((tokens, model), lambda s: (0, 0)),
        ]
        + [slot_spec(own, LANES) for _ in more],
        out_specs=token_spec(tokens, cols),
        compiler_params=BIG,
    )(position, rows.reshape(own, n, CAP, model), shared, *more)


def grads_kernel(k, *refs):
    lefts, rights, out = refs[:k], refs[k : 2 * k], refs[2 * k]
    start = 0
    for left, right in zip(lefts, rights):
        cols = right.shape[1]
        out[:, start : start + cols] = dot(left[...], right[...], ((0,), (0,))).astype(BF)
        start += cols


def weight_grads(pairs):
    k = len(pairs)
    tokens, model = pairs[0][0].shape
    block = 256
    cols = sum(right.shape[1] for _, right in pairs)
    return pl.pallas_call(
        partial(grads_kernel, k),
        grid=(model // block,),
        out_shape=jax.ShapeDtypeStruct((model, cols), BF),
        in_specs=[pl.BlockSpec((tokens, block), lambda i: (0, i)) for _ in pairs]
        + [pl.BlockSpec(right.shape, lambda i: (0, 0)) for _, right in pairs],
        out_specs=pl.BlockSpec((block, cols), lambda i: (i, 0)),
        compiler_params=BIG,
    )(*[left for left, _ in pairs], *[right for _, right in pairs])


def combine_states(states, decays, expand, reverse):
    n = states.shape[0]
    place = lax.axis_index("dp")
    wide = dot(decays, expand, precision=HIGH)
    state = jnp.zeros(states.shape[1:], F32)
    for j in range(n):
        source = n - 1 - j if reverse else j
        use = source > place if reverse else source < place
        fresh = wide[source][:, None] * state + states[source]
        state = jnp.where(use, fresh, state)
    return state


def incoming_state(mine, decay, expand, reverse, cid):
    if lax.axis_size("dp") == 8:
        return state_scan(mine, jnp.broadcast_to(decay, (8, LANES)), expand, reverse, cid)
    rows = jnp.pad(decay, ((0, 31), (0, 0)))
    (gathered,) = gather_dp([jnp.concatenate([mine, rows], axis=0)], cid)
    width = mine.shape[0]
    return combine_states(gathered[:, :width], gathered[:, width], expand, reverse)


def per_device(
    hidden,
    segment_ids,
    routes,
    norm_gain,
    mixer_in,
    state_in,
    step_in,
    conv_value,
    conv_value_bias,
    conv_state,
    conv_state_bias,
    head_params,
    gated_gain,
    mixer_out,
    ffn_gain,
    router,
    shared_in,
    shared_out,
    expert_in,
    expert_out,
    cotangent,
):
    n = lax.axis_size("dp")
    place, mp_place = lax.axis_index("dp"), lax.axis_index("mp")
    tokens, model = hidden.shape
    shard = model // n
    inner = mixer_in.shape[2]
    state_cols = state_in.shape[1]
    taps = conv_value.shape[0]
    heads = head_params.shape[1]
    width = inner // heads
    own_experts = expert_in.shape[0]
    hidden_units = shared_out.shape[0]
    quarter = tokens // 4

    misc_parts = [
        conv_value.reshape(-1),
        conv_value_bias.reshape(-1),
        gated_gain.reshape(-1),
        conv_state.reshape(-1),
        conv_state_bias,
        norm_gain,
        ffn_gain,
    ]
    misc = jnp.concatenate(misc_parts)
    route_rows = routes.T.reshape(-1, model).astype(BF)
    small = jnp.concatenate(
        [
            hidden[tokens - 16 :],
            jnp.pad(misc, (0, model - misc.shape[0]))[None],
            route_rows,
            jnp.zeros((15 - route_rows.shape[0], model), BF),
        ],
        axis=0,
    )
    pack_a = jnp.concatenate(
        [
            mixer_in.reshape(shard, 2 * inner),
            state_in,
            jnp.pad(step_in, ((0, 0), (0, LANES - heads))),
        ],
        axis=1,
    )
    pack_b = jnp.concatenate(
        [
            mixer_out.T,
            shared_in.reshape(shard, 2 * hidden_units),
            shared_out.T,
            jnp.pad(router, ((0, 0), (0, LANES - EXPERTS))),
        ],
        axis=1,
    )
    weight_a, small_all = gather_dp([pack_a, small], 0)
    weight_a = weight_a.reshape(model, -1)
    mine_cot = lax.dynamic_slice_in_dim(cotangent, mp_place * quarter, quarter, 0)
    pack_b, small_all = lax.optimization_barrier((pack_b, small_all))
    weight_b = lax.all_gather(pack_b, "dp", axis=0, tiled=True)
    mine_cot, small_all = lax.optimization_barrier((mine_cot, small_all))
    cot_all = lax.all_gather(mine_cot, ("dp", "mp"), axis=0, tiled=True).reshape(n, tokens, model)
    out_t = weight_b[:, :inner]
    shared_w = weight_b[:, inner : inner + 2 * hidden_units]
    shared_out_t = weight_b[:, inner + 2 * hidden_units : inner + 3 * hidden_units]
    router_w = weight_b[:, inner + 3 * hidden_units :]

    pieces = []
    start = 0
    for part in misc_parts:
        pieces.append(small_all[:, 16, start : start + part.shape[0]].astype(F32))
        start += part.shape[0]
    local_p = conv_value.shape[1]
    value_rows = jnp.concatenate(pieces[:3], axis=1).reshape(n, taps + 2, local_p, heads)
    value_rows = value_rows.transpose(1, 3, 0, 2).reshape(taps + 2, inner)
    state_rows = jnp.concatenate(pieces[3:5], axis=1).reshape(n, taps + 1, state_cols // n)
    state_rows = state_rows.transpose(1, 0, 2).reshape(taps + 1, state_cols)
    gain_first = pieces[5].reshape(1, model)
    gain_second = pieces[6].reshape(1, model)
    conv_taps = jnp.concatenate([value_rows[:taps], state_rows[:taps]], axis=1)
    conv_bias = jnp.concatenate([value_rows[taps], state_rows[taps]])[None]
    gated_row = value_rows[taps + 1][None]

    group_start = place * tokens
    seg_padded = jnp.concatenate([jnp.full((taps - 1,), -1, jnp.int32), segment_ids])
    seg_ext = lax.dynamic_slice_in_dim(seg_padded, group_start, tokens + taps - 1)
    segments = seg_ext[taps - 1 :]
    prev_seg = seg_ext[taps - 2]
    same = [
        (seg_ext[k : k + tokens] == segments).astype(F32)[:, None] for k in range(taps)
    ]
    blocks = tokens // BLK
    seg_blocks = segments.reshape(blocks, BLK)
    last_segs = seg_blocks[:, BLK - 1]
    prev_segs = jnp.concatenate([prev_seg[None], last_segs[:-1]])
    entry_ok = (seg_blocks == prev_segs[:, None]).astype(F32).reshape(tokens, 1)
    tail_ok = (seg_blocks == last_segs[:, None]).astype(F32).reshape(tokens, 1)
    group_entry_ok = (segments == prev_seg).astype(F32)[:, None]
    group_tail_ok = (segments == segments[tokens - 1]).astype(F32)[:, None]
    seg_f = segments.astype(F32)
    seg_col, seg_row = seg_f[:, None], seg_f[None, :]

    behind = lax.dynamic_index_in_dim(small_all, (place + n - 1) % n, 0, False)[:16]
    hidden_ext = jnp.concatenate([behind, hidden], axis=0).astype(F32)
    inv_ext = lax.rsqrt(jnp.mean(hidden_ext * hidden_ext, axis=1, keepdims=True) + EPS)
    normed_ext = (hidden_ext * inv_ext * gain_first).astype(BF)
    normed = normed_ext[16:]
    zx_ext = dot(normed_ext, weight_a)
    gate_z = zx_ext[16:, :inner]
    pre_ext = zx_ext[16 - taps + 1 :, inner : 2 * inner + state_cols]
    head_local = head_params.astype(F32)
    dt_lanes = zx_ext[16:, 2 * inner + state_cols :]
    conv = jnp.broadcast_to(conv_bias, (tokens, inner + state_cols))
    for k in range(taps):
        conv = conv + conv_taps[k][None] * pre_ext[k : k + tokens] * same[k]
    act = jax.nn.silu(conv)
    values = act[:, :inner]
    write = act[:, inner : inner + state_cols // 2]
    read = act[:, inner + state_cols // 2 :]

    live = (jnp.arange(LANES) < heads)[None]
    head_pad = jnp.pad(head_local, ((0, 0), (0, LANES - heads)))
    rate = jnp.where(live, -jnp.exp(head_pad[0:1]), 0.0)
    step = jnp.where(live, jax.nn.softplus(dt_lanes + head_pad[1:2]), 0.0)
    rated = (step * rate).reshape(blocks, BLK, LANES)
    lower = jnp.tril(jnp.ones((BLK, BLK), F32))
    cumul_b = jnp.einsum("ts,bsh->bth", lower, rated, precision=HIGH)
    totals = cumul_b[:, BLK - 1]
    zero_row = jnp.zeros((1, LANES), F32)
    before, after = [zero_row], [zero_row]
    for i in range(blocks - 1):
        before.append(before[-1] + totals[i][None])
        after.append(after[-1] + totals[blocks - 1 - i][None])
    before = jnp.stack(before)
    after = jnp.stack(after[::-1])
    cumul = cumul_b.reshape(tokens, LANES)
    to_end = totals[:, None] - cumul_b
    entry = jnp.exp(cumul) * entry_ok
    tail_bare = jnp.exp(to_end).reshape(tokens, LANES) * tail_ok
    tail = tail_bare * step
    group_entry = jnp.exp(cumul_b + before).reshape(tokens, LANES) * group_entry_ok
    group_tail = jnp.exp(to_end + after).reshape(tokens, LANES) * group_tail_ok * step
    cumul_t = cumul[:, :16].T
    step_t = step[:, :16].T
    expand = (jnp.arange(LANES)[:, None] == jnp.arange(inner)[None, :] // width).astype(F32)
    skip = dot(head_pad[2:3], expand, precision=HIGH)
    outgoing = dot(
        values * dot(group_tail, expand, precision=HIGH), write, ((0,), (0,)), HIGH
    )
    group_decay = group_entry[tokens - 1 :]
    incoming = incoming_state(outgoing, group_decay, expand, False, 1)
    ssd, kept = recur_forward(
        values, write, read, cumul, cumul_t, step_t, entry, tail, seg_col, seg_row, expand, skip, incoming
    )

    gate_act = jax.nn.silu(gate_z)
    gated = ssd * gate_act
    scaled = (gated * gated_row).astype(BF)
    proj_part = dot(scaled, out_t, ((1,), (1,)))
    square_part = jnp.sum(gated * gated, axis=1, keepdims=True)
    proj_pack = jnp.concatenate([proj_part, jnp.broadcast_to(square_part, (tokens, LANES))], axis=1)
    proj_sum = scatter_mp(proj_pack.reshape(4, quarter, -1), 2)
    proj = proj_sum[:, :model]
    square = proj_sum[:, model : model + 1]
    inv_gated = lax.rsqrt(square / DI + EPS)
    mine_hidden = lax.dynamic_slice_in_dim(hidden, mp_place * quarter, quarter, 0).astype(F32)
    mixed = mine_hidden + proj * inv_gated
    inv_second = lax.rsqrt(jnp.mean(mixed * mixed, axis=1, keepdims=True) + EPS)
    unit_second = mixed * inv_second
    ffn_mine = (unit_second * gain_second).astype(BF)
    ffn_all = gather_tokens(ffn_mine, 3).reshape(n, tokens, model)

    routes_all = small_all[:, 17 : 17 + route_rows.shape[0]].reshape(n, TOPK, tokens)
    routes_cols = routes_all.astype(F32).transpose(0, 2, 1)
    first_expert = place * own_experts
    own_ids = (first_expert + jnp.arange(own_experts, dtype=jnp.int32)).astype(F32)
    named = jnp.any(routes_all.astype(F32)[:, None] == own_ids[None, :, None, None], axis=2)
    earlier = (jnp.arange(tokens)[:, None] < jnp.arange(tokens)[None, :]).astype(BF)
    position = jnp.einsum("set,tu->seu", named.astype(BF), earlier, preferred_element_type=F32)
    position = jnp.where(named, position, -1.0)
    position_cols = position.transpose(0, 2, 1)
    cot_rows = pick_rows(cot_all, position)

    rows, gates, slot_gates = pick_rows_gates(ffn_all, position, routes_cols, router_w)
    slots = n * CAP
    grad_in_rows, grad_expert_out, d_rows, expert_res, slot_dots = run_experts(
        rows.reshape(own_experts, slots, model),
        cot_rows.reshape(own_experts, slots, model),
        slot_gates.reshape(own_experts, slots, LANES),
        expert_in.reshape(own_experts, 2 * model, -1),
        expert_out,
    )
    grad_expert_in = grad_in_rows.reshape(expert_in.shape)

    ffn_block = lax.dynamic_index_in_dim(ffn_all, place, 0, False)
    shared_mid = dot(ffn_block, shared_w)
    shared_gate, shared_up = shared_mid[:, :hidden_units], shared_mid[:, hidden_units:]
    shared_silu = jax.nn.silu(shared_gate)
    shared_act = (shared_silu * shared_up).astype(BF)
    shared_res = dot(shared_act, shared_out_t, ((1,), (1,)))
    d_shared_act = dot(cotangent, shared_out_t)
    d_shared_mid = jnp.concatenate(
        [d_shared_act * shared_up * silu_slope(shared_gate), d_shared_act * shared_silu], axis=1
    ).astype(BF)
    d_ffn_shared = dot(d_shared_mid, shared_w, ((1,), (1,)))

    d_ffn_pack = put_rows(position_cols, d_rows, d_ffn_shared, slot_dots)
    d_ffn_sum = scatter_tokens(d_ffn_pack.reshape(n, 4, quarter, model + LANES), 4)
    expert_res, d_ffn_sum = lax.optimization_barrier((expert_res, d_ffn_sum))
    res_pack = put_rows(position_cols, expert_res, shared_res)
    if n > 8:
        res_sum = scatter_tokens(res_pack.reshape(n, 4, quarter, model), 10)
    else:
        res_sum = lax.psum_scatter(
            res_pack.reshape(n * tokens, model), ("dp", "mp"), scatter_dimension=0, tiled=True
        )
    mine_result = (mixed + res_sum.astype(F32)).astype(BF)
    result = lax.all_gather(mine_result, "mp", axis=0, tiled=True)

    own_tokens_gates = lax.dynamic_slice(
        gates, (place, mp_place * quarter, 0), (1, quarter, LANES)
    ).reshape(quarter, LANES)
    dots = d_ffn_sum[:, model : model + LANES]
    share = jnp.sum(own_tokens_gates * dots, axis=1, keepdims=True)
    d_logits = (own_tokens_gates * (dots - share)).astype(BF)
    d_ffn = d_ffn_sum[:, :model] + dot(d_logits, router_w, ((1,), (1,)))
    mine_cot_f = mine_cot.astype(F32)
    grad_gain_second = jnp.sum(d_ffn * unit_second, axis=0)
    d_unit = d_ffn * gain_second
    d_mixed = mine_cot_f + inv_second * (
        d_unit - unit_second * jnp.mean(d_unit * unit_second, axis=1, keepdims=True)
    )
    d_proj_mine = (d_mixed * inv_gated).astype(BF)
    d_inv = jnp.sum(d_mixed * proj, axis=1, keepdims=True)
    d_square = d_inv * -0.5 * inv_gated * inv_gated * inv_gated / DI
    d_square_high = d_square.astype(BF)
    d_square_low = (d_square - d_square_high.astype(F32)).astype(BF)
    sent = jnp.concatenate(
        [
            d_proj_mine,
            d_logits[:, :EXPERTS],
            d_square_high,
            d_square_low,
            jnp.zeros((quarter, LANES - EXPERTS - 2), BF),
        ],
        axis=1,
    )
    (got,) = gather_mp([sent], 5)
    got = got.reshape(tokens, model + LANES)
    d_proj = got[:, :model]
    d_logits_all = jnp.pad(got[:, model : model + EXPERTS], ((0, 0), (0, LANES - EXPERTS)))
    d_square_all = got[:, model + EXPERTS : model + EXPERTS + 1].astype(F32) + got[
        :, model + EXPERTS + 1 : model + EXPERTS + 2
    ].astype(F32)

    rows0 = ((0,), (0,))
    grad_b = weight_grads(
        [
            (d_proj, scaled),
            (ffn_block, d_shared_mid),
            (cotangent, shared_act),
            (ffn_block, d_logits_all),
        ]
    )
    grad_b, d_proj = lax.optimization_barrier((grad_b, d_proj))
    sum_b = lax.psum_scatter(grad_b, "dp", scatter_dimension=0, tiled=True).astype(F32)
    d_scaled = dot(d_proj, out_t)
    grad_gated_row = jnp.sum(d_scaled * gated, axis=0)
    d_gated = d_scaled * gated_row + 2.0 * gated * d_square_all
    d_ssd = d_gated * gate_act
    d_gate_z = d_gated * ssd * silu_slope(gate_z)

    direct = dot(d_ssd * dot(group_entry, expand, precision=HIGH), read, rows0, HIGH)
    state_grad = incoming_state(direct, group_decay, expand, True, 6)
    d_values, d_write, d_read, d_step, d_rated, d_skip_row = recur_backward(
        values,
        write,
        read,
        cumul,
        cumul_t,
        step_t,
        step,
        entry,
        tail_bare,
        seg_col,
        seg_row,
        expand,
        skip,
        kept,
        d_ssd,
        state_grad,
    )
    d_rate = jnp.sum(d_rated * step, axis=0, keepdims=True)
    d_dt = jnp.where(
        live, (d_step + rate * d_rated) * jax.nn.sigmoid(dt_lanes + head_pad[1:2]), 0.0
    )
    d_skip = dot(d_skip_row, expand, ((1,), (1,)), HIGH)
    grad_head = jnp.concatenate(
        [d_rate * rate, jnp.sum(d_dt, axis=0, keepdims=True), d_skip], axis=0
    )[:, :heads]

    d_state_act = lax.psum(jnp.concatenate([d_write, d_read], axis=1), "mp")
    d_conv = jnp.concatenate([d_values, d_state_act], axis=1) * silu_slope(conv)
    rim = d_conv[:16]
    rim_ahead = lax.ppermute(rim, "dp", [(i + 1, i) for i in range(n - 1)])
    d_conv_ext = jnp.concatenate([d_conv, rim_ahead], axis=0)
    seg_after = lax.dynamic_slice_in_dim(
        jnp.concatenate([segment_ids, jnp.full((taps - 1,), -1, jnp.int32)]),
        group_start,
        tokens + taps - 1,
    )
    d_pre = jnp.zeros_like(d_conv)
    grad_rows = []
    for k in range(taps):
        ahead = taps - 1 - k
        ok = (seg_after[ahead : ahead + tokens] == segments).astype(F32)[:, None]
        d_pre = d_pre + conv_taps[k][None] * d_conv_ext[ahead : ahead + tokens] * ok
        grad_rows.append(jnp.sum(d_conv * pre_ext[k : k + tokens] * same[k], axis=0))
    grad_rows.append(jnp.sum(d_conv, axis=0))
    d_a = jnp.concatenate([d_gate_z, d_pre, d_dt], axis=1).astype(BF)

    d_state_mine = lax.dynamic_slice_in_dim(
        d_a[:, 2 * inner : 2 * inner + state_cols], mp_place * quarter, quarter, 0
    )
    d_normed_part = dot(d_a[:, : 2 * inner], weight_a[:, : 2 * inner], ((1,), (1,))) + dot(
        d_a[:, 2 * inner + state_cols :], weight_a[:, 2 * inner + state_cols :], ((1,), (1,))
    )
    d_normed = scatter_mp(d_normed_part.astype(BF).reshape(4, quarter, model), 7)
    d_normed = d_normed + dot(
        d_state_mine, weight_a[:, 2 * inner : 2 * inner + state_cols], ((1,), (1,))
    )
    grad_a = dot(normed, d_a, rows0).astype(BF)
    inv_first = lax.rsqrt(jnp.mean(mine_hidden * mine_hidden, axis=1, keepdims=True) + EPS)
    unit_first = mine_hidden * inv_first
    grad_gain_first = jnp.sum(d_normed * unit_first, axis=0)
    d_first = d_normed * gain_first
    mine_grad_hidden = d_mixed + inv_first * (
        d_first - unit_first * jnp.mean(d_first * unit_first, axis=1, keepdims=True)
    )

    value_grads = jnp.stack([g[:inner] for g in grad_rows] + [grad_gated_row])
    value_grads = value_grads.reshape(taps + 2, heads, n, local_p).transpose(2, 0, 3, 1)
    state_grads = jnp.stack([g[inner:] for g in grad_rows])
    state_grads = state_grads.reshape(taps + 1, n, state_cols // n).transpose(1, 0, 2)
    misc_grads = [
        value_grads.reshape(n, -1),
        state_grads.reshape(n, -1),
        jnp.broadcast_to(grad_head.reshape(1, -1), (n, 3 * heads)),
        grad_gain_first.reshape(n, shard),
        grad_gain_second.reshape(n, shard),
    ]
    sizes = [g.shape[1] for g in misc_grads]
    misc_grads = jnp.concatenate(misc_grads, axis=1)
    misc_grads = jnp.pad(misc_grads, ((0, 0), (0, 32 * LANES - misc_grads.shape[1])))
    sum_a, misc_sum = scatter_dp(
        [grad_a.reshape(n, shard, -1), misc_grads.reshape(n, 32, LANES)], 8
    )
    misc_sum = misc_sum.reshape(-1)
    cut = [0]
    for size in sizes:
        cut.append(cut[-1] + size)
    value_sum = misc_sum[: cut[1]].reshape(taps + 2, local_p, heads)
    state_sum = misc_sum[cut[1] : cut[2]].reshape(taps + 1, state_cols // n)
    head_sum = misc_sum[cut[2] : cut[3]].reshape(3, heads)
    gains = jnp.pad(misc_sum[cut[3] : cut[5]], (0, 2 * model - 2 * shard)).reshape(-1, LANES)
    hidden_all, gains_all = gather_mp([mine_grad_hidden.astype(BF), gains], 9)
    gains_sum = jnp.sum(gains_all.reshape(4, -1)[:, : 2 * shard], axis=0)

    b1, b2 = inner, inner + 2 * hidden_units
    b3 = b2 + hidden_units
    return (
        result,
        hidden_all.reshape(tokens, model).astype(F32),
        gains_sum[:shard],
        sum_a[:, : 2 * inner].reshape(shard, 2, inner),
        sum_a[:, 2 * inner : 2 * inner + state_cols],
        sum_a[:, 2 * inner + state_cols : 2 * inner + state_cols + heads],
        value_sum[:taps],
        value_sum[taps],
        state_sum[:taps],
        state_sum[taps],
        head_sum,
        value_sum[taps + 1],
        sum_b[:, :b1].T,
        gains_sum[shard:],
        sum_b[:, b3 : b3 + EXPERTS],
        sum_b[:, b1:b2].reshape(shard, 2, hidden_units),
        sum_b[:, b2:b3].T,
        grad_expert_in,
        grad_expert_out,
    )


def solution(mesh):
    placed = (
        P("dp", None),
        P(),
        P("dp", None),
        P("dp"),
        P("dp", None, "mp"),
        P("dp", None),
        P("dp", "mp"),
        P(None, "dp", "mp"),
        P("dp", "mp"),
        P(None, "dp"),
        P("dp"),
        P(None, "mp"),
        P("dp", "mp"),
        P("mp", "dp"),
        P("dp"),
        P("dp", None),
        P("dp", None, "mp"),
        P("mp", "dp"),
        P("dp", None, None, "mp"),
        P("dp", "mp", None),
        P("dp", None),
    )
    return jax.shard_map(
        per_device,
        mesh=mesh,
        in_specs=placed,
        out_specs=(
            P("dp", None),
            P("dp", None),
            P("dp"),
            P("dp", None, "mp"),
            P("dp", None),
            P("dp", "mp"),
            P(None, "dp", "mp"),
            P("dp", "mp"),
            P(None, "dp"),
            P("dp"),
            P(None, "mp"),
            P("dp", "mp"),
            P("mp", "dp"),
            P("dp"),
            P("dp", None),
            P("dp", None, "mp"),
            P("mp", "dp"),
            P("dp", None, None, "mp"),
            P("dp", "mp", None),
        ),
        check_vma=False,
    )
```

```python
from functools import partial

import jax
import jax.numpy as jnp
from jax import lax
from jax.experimental import pallas as pl
from jax.experimental.pallas import tpu as pltpu
from jax.sharding import PartitionSpec as P

MESH = pl.DeviceIdType.MESH
BLK = 128
EXPERTS = 64
TOPK = 6
DI = 3072
CAP = 64
LANES = 128

EPS = 1e-05
HIGH = lax.Precision.HIGHEST
MASKED = -1e30
BF = jnp.bfloat16
F32 = jnp.float32
ANY = pl.BlockSpec(memory_space=pl.ANY)
VM = pl.BlockSpec(memory_space=pltpu.VMEM)


def dot(a, b, dims=((1,), (0,)), precision=None):
    return lax.dot_general(
        a, b, (dims, ((), ())), precision=precision, preferred_element_type=F32
    )


def silu_slope(argument):
    sigmoid_val = jax.nn.sigmoid(argument)
    return sigmoid_val * (1.0 + argument * (1.0 - sigmoid_val))


def half_rows(rows):
    return (rows // 32) * 16


def ring_place(n, d):
    high, low = d // 2, d % 2
    return high * (1 - low) + (n - 1 - high) * low


def ring_device(n, p):
    back = p // (n // 2)
    return (2 * p) * (1 - back) + (2 * (n - 1 - p) + 1) * back


def greet(targets):
    barrier = pltpu.get_barrier_semaphore()
    for target in targets:
        pl.semaphore_signal(barrier, inc=1, device_id=target, device_id_type=MESH)
    pl.semaphore_wait(barrier, len(targets))


def remote(src, dst, send, recv, target):
    return pltpu.make_async_remote_copy(
        src_ref=src,
        dst_ref=dst,
        send_sem=send,
        recv_sem=recv,
        device_id=target,
        device_id_type=MESH,
    )


def mp_partners(m):
    return {"mp": m + 1 - 2 * (m % 2)}, {"mp": (m + 2) % 4}


def ring_neighbours(n):
    p = ring_place(n, lax.axis_index("dp"))
    nxt = {"dp": ring_device(n, (p + 1) % n)}
    prv = {"dp": ring_device(n, (p + n - 1) % n)}
    return p, nxt, prv


def gather_kernel(n, k, *refs):
    ins, outs = refs[:k], refs[k : 2 * k]
    local_sem, send_sem, recv_sem = refs[2 * k :]
    d = lax.axis_index("dp")
    p, nxt, prv = ring_neighbours(n)
    greet([nxt, prv])
    local = []
    for j in range(k):
        copy = pltpu.make_async_copy(ins[j], outs[j].at[d], local_sem.at[j])
        copy.start()
        local.append(copy)
    copies = {}
    for s in range(n - 1):
        for way in range(2):
            origin = ring_device(n, (p + n - s) % n if way == 0 else (p + s) % n)
            for j in range(k):
                rows = ins[j].shape[0]
                cut = half_rows(rows)
                part = pl.ds(0, cut) if way == 0 else pl.ds(cut, rows - cut)
                if s > 0:
                    copies[s - 1, way, j].wait_recv()
                copy = remote(
                    ins[j].at[part] if s == 0 else outs[j].at[origin, part],
                    outs[j].at[origin, part],
                    send_sem.at[way, s, j],
                    recv_sem.at[way, s, j],
                    nxt if way == 0 else prv,
                )
                copy.start()
                copies[s, way, j] = copy
    for way in range(2):
        for j in range(k):
            copies[n - 2, way, j].wait_recv()
    for copy in copies.values():
        copy.wait_send()
    for copy in local:
        copy.wait()


def gather_dp(arrays, cid):
    n, k = lax.axis_size("dp"), len(arrays)
    return pl.pallas_call(
        partial(gather_kernel, n, k),
        out_shape=[jax.ShapeDtypeStruct((n,) + a.shape, a.dtype) for a in arrays],
        in_specs=[ANY] * k,
        out_specs=[ANY] * k,
        scratch_shapes=[
            pltpu.SemaphoreType.DMA((k,)),
            pltpu.SemaphoreType.DMA((2, n - 1, k)),
            pltpu.SemaphoreType.DMA((2, n - 1, k)),
        ],
        compiler_params=pltpu.CompilerParams(collective_id=cid, has_side_effects=True),
    )(*arrays)


def add_rows(dst, pieces, rows, dtype):
    def body(i, carry):
        sl = pl.ds(pl.multiple_of(i * 16, 16), 16)
        total = pieces[0][sl, :].astype(F32)
        for piece in pieces[1:]:
            total = total + piece[sl, :].astype(F32)
        dst[sl, :] = total.astype(dtype)
        return carry

    lax.fori_loop(0, rows // 16, body, 0)


def scatter_kernel(n, k, *refs):
    ins, outs, slots = refs[:k], refs[k : 2 * k], refs[2 * k : 4 * k]
    send_sem, recv_sem = refs[4 * k :]
    d = lax.axis_index("dp")
    p, nxt, prv = ring_neighbours(n)
    greet([nxt, prv])
    copies = {}
    for s in range(n):
        for way in range(2):
            block = ring_device(n, (p + 2 * n - 1 - s) % n if way == 0 else (p + 1 + s) % n)
            for j in range(k):
                rows = ins[j].shape[1]
                cut = half_rows(rows)
                start, size = (0, cut) if way == 0 else (cut, rows - cut)
                mine = ins[j].at[block, pl.ds(start, size)]
                slot = slots[2 * j + way]
                if s > 0:
                    copies[s - 1, way, j].wait_recv()
                    held = slot.at[s - 1]
                    if s == n - 1:
                        add_rows(outs[j].at[pl.ds(start, size)], [held, mine], size, F32)
                        continue
                    add_rows(held, [held, mine], size, ins[j].dtype)
                    source = held
                else:
                    source = mine
                copy = remote(
                    source,
                    slot.at[s],
                    send_sem.at[way, s, j],
                    recv_sem.at[way, s, j],
                    nxt if way == 0 else prv,
                )
                copy.start()
                copies[s, way, j] = copy
    for copy in copies.values():
        copy.wait_send()


def scatter_dp(arrays, cid):
    n, k = lax.axis_size("dp"), len(arrays)
    slots = []
    for a in arrays:
        cut = half_rows(a.shape[1])
        for size in (cut, a.shape[1] - cut):
            slots.append(pltpu.VMEM((n - 1, size, a.shape[2]), a.dtype))
    return pl.pallas_call(
        partial(scatter_kernel, n, k),
        out_shape=[jax.ShapeDtypeStruct(a.shape[1:], F32) for a in arrays],
        in_specs=[VM] * k,
        out_specs=[VM] * k,
        scratch_shapes=slots
        + [
            pltpu.SemaphoreType.DMA((2, n - 1, k)),
            pltpu.SemaphoreType.DMA((2, n - 1, k)),
        ],
        compiler_params=pltpu.CompilerParams(
            collective_id=cid, has_side_effects=True, vmem_limit_bytes=48 * 1024 * 1024
        ),
    )(*arrays)


def mp_scatter_kernel(x, out, from_core, from_chip, send_sem, recv_sem):
    m = lax.axis_index("mp")
    core, chip = mp_partners(m)
    mine, far = m, (m + 2) % 4
    greet([core, chip])
    first = []
    for i in range(2):
        block = (m + 1 - 2 * (m % 2) + 2 * i) % 4
        copy = remote(x.at[block], from_core.at[i], send_sem.at[i], recv_sem.at[i], core)
        copy.start()
        first.append(copy)
    rows = out.shape[0]
    first[1].wait_recv()
    add_rows(from_core.at[1], [from_core.at[1], x.at[far]], rows, x.dtype)
    last = remote(from_core.at[1], from_chip, send_sem.at[2], recv_sem.at[2], chip)
    last.start()
    first[0].wait_recv()
    last.wait_recv()
    add_rows(out, [x.at[mine], from_core.at[0], from_chip], rows, F32)
    for copy in first + [last]:
        copy.wait_send()


def scatter_mp(x, cid):
    rows, cols = x.shape[1:]
    return pl.pallas_call(
        mp_scatter_kernel,
        out_shape=jax.ShapeDtypeStruct((rows, cols), F32),
        in_specs=[VM],
        out_specs=VM,
        scratch_shapes=[
            pltpu.VMEM((2, rows, cols), x.dtype),
            pltpu.VMEM((rows, cols), x.dtype),
            pltpu.SemaphoreType.DMA((3,)),
            pltpu.SemaphoreType.DMA((3,)),
        ],
        compiler_params=pltpu.CompilerParams(
            collective_id=cid, has_side_effects=True, vmem_limit_bytes=32 * 1024 * 1024
        ),
    )(x)


def mp_gather_kernel(k, *refs):
    ins, outs = refs[:k], refs[k : 2 * k]
    local_sem, send_sem, recv_sem = refs[2 * k :]
    m = lax.axis_index("mp")
    core, chip = mp_partners(m)
    far = (m + 2) % 4
    greet([core, chip])
    copies, local, arrive = [], [], []
    for j in range(k):
        to_chip = remote(ins[j], outs[j].at[m], send_sem.at[0, j], recv_sem.at[0, j], chip)
        to_chip.start()
        to_core = remote(ins[j], outs[j].at[m], send_sem.at[1, j], recv_sem.at[1, j], core)
        to_core.start()
        own = pltpu.make_async_copy(ins[j], outs[j].at[m], local_sem.at[j])
        own.start()
        copies += [to_chip, to_core]
        arrive.append(to_chip)
        local.append(own)
    onward = []
    for j in range(k):
        arrive[j].wait_recv()
        copy = remote(outs[j].at[far], outs[j].at[far], send_sem.at[2, j], recv_sem.at[2, j], core)
        copy.start()
        onward.append(copy)
    for j in range(k):
        copies[2 * j + 1].wait_recv()
        onward[j].wait_recv()
        local[j].wait()
    for copy in copies + onward:
        copy.wait_send()


def gather_mp(arrays, cid):
    k = len(arrays)
    return pl.pallas_call(
        partial(mp_gather_kernel, k),
        out_shape=[jax.ShapeDtypeStruct((4,) + a.shape, a.dtype) for a in arrays],
        in_specs=[ANY] * k,
        out_specs=[ANY] * k,
        scratch_shapes=[
            pltpu.SemaphoreType.DMA((k,)),
            pltpu.SemaphoreType.DMA((3, k)),
            pltpu.SemaphoreType.DMA((3, k)),
        ],
        compiler_params=pltpu.CompilerParams(collective_id=cid, has_side_effects=True),
    )(*arrays)


class TokenGather:
    def __init__(self, n, both, x, out, sems):
        self.n, self.both, self.x, self.out = n, both, x, out
        self.local, self.ring_s, self.ring_r, self.core_s, self.core_r, self.chip_s, self.chip_r = sems
        self.d, self.m = lax.axis_index("dp"), lax.axis_index("mp")
        self.far = (self.m + 2) % 4
        self.core, self.chip = mp_partners(self.m)
        self.p, self.nxt, self.prv = ring_neighbours(n)
        self.rows = x.shape[0]
        self.sent, self.pending = [], []
        self.ring, self.chips = {}, {}

    @staticmethod
    def scratch(n):
        dma = pltpu.SemaphoreType.DMA
        return [
            dma((3,)),
            dma((2, n, 2)),
            dma((2, n, 2)),
            dma((2, n, 3)),
            dma((2, n, 3)),
            dma((2, n)),
            dma((2, n)),
        ]

    def origin(self, s, way):
        n, p = self.n, self.p
        return ring_device(n, (p + n - s) % n if way == 0 else (p + s) % n)

    def pieces(self, way):
        half, part = self.rows // 2, self.both // 2
        found = [(self.m, way * half, half)]
        if part:
            found.append((self.far, way * part, part))
        return found

    def send(self, place, s_sem, r_sem, target):
        copy = remote(place, place, s_sem, r_sem, target)
        copy.start()
        self.sent.append(copy)
        return copy

    def begin(self):
        own = self.out.at[self.d, self.m]
        load = pltpu.make_async_copy(self.x, own, self.local.at[0])
        load.start()
        self.first = None
        if self.both:
            part = pl.ds(0, self.both)
            self.first = remote(
                self.x.at[part], own.at[part], self.local.at[1], self.local.at[2], self.chip
            )
            self.first.start()
            self.sent.append(self.first)
        load.wait()

    def step(self, s):
        n = self.n
        for way in range(2):
            origin = self.origin(s, way)
            for k, (place, start, rows) in enumerate(self.pieces(way)):
                region = self.out.at[origin, place, pl.ds(start, rows)]
                if s > 0:
                    self.ring[s - 1, way, k].wait_recv()
                elif k == 1 and way == 0:
                    self.first.wait_recv()
                if s < n - 1:
                    self.ring[s, way, k] = self.send(
                        region,
                        self.ring_s.at[way, s, k],
                        self.ring_r.at[way, s, k],
                        self.nxt if way == 0 else self.prv,
                    )
                self.pending.append(
                    self.send(region, self.core_s.at[way, s, k], self.core_r.at[way, s, k], self.core)
                )
                if k == 0:
                    low = max(start, self.both)
                    size = start + rows - low
                    if size > 0:
                        part = self.out.at[origin, place, pl.ds(low, size)]
                        self.chips[s, way] = (
                            self.send(part, self.chip_s.at[way, s], self.chip_r.at[way, s], self.chip),
                            self.out.at[origin, self.far, pl.ds(low, size)],
                        )

    def pass_on(self, s):
        for way in range(2):
            if (s, way) in self.chips:
                copy, region = self.chips[s, way]
                copy.wait_recv()
                self.pending.append(
                    self.send(region, self.core_s.at[way, s, 2], self.core_r.at[way, s, 2], self.core)
                )

    def end(self):
        for copy in self.pending:
            copy.wait_recv()
        for copy in self.sent:
            copy.wait_send()


def token_gather_kernel(n, both, x, out, *sems):
    gather = TokenGather(n, both, x, out, sems)
    greet([gather.core, gather.chip, gather.nxt, gather.prv])
    gather.begin()
    for s in range(n):
        gather.step(s)
        if s > 0:
            gather.pass_on(s - 1)
    gather.pass_on(n - 1)
    gather.end()


def gather_tokens(x, cid):
    n = lax.axis_size("dp")
    return pl.pallas_call(
        partial(token_gather_kernel, n, x.shape[0] // 2),
        out_shape=jax.ShapeDtypeStruct((n, 4) + x.shape, x.dtype),
        in_specs=[ANY],
        out_specs=ANY,
        scratch_shapes=TokenGather.scratch(n),
        compiler_params=pltpu.CompilerParams(collective_id=cid, has_side_effects=True),
    )(x)


def first_kernel(n, k, *refs):
    ins, x = refs[:k], refs[k]
    outs, x_out = refs[k + 1 : 2 * k + 1], refs[2 * k + 1]
    local_sem, send_sem, recv_sem = refs[2 * k + 2 : 2 * k + 5]
    gather = TokenGather(n, 0, x, x_out, refs[2 * k + 5 :])
    d, p, nxt, prv = gather.d, gather.p, gather.nxt, gather.prv
    greet([gather.core, gather.chip, nxt, prv])
    local = []
    for j in range(k):
        copy = pltpu.make_async_copy(ins[j], outs[j].at[d], local_sem.at[j])
        copy.start()
        local.append(copy)
    copies = {}
    for s in range(n):
        for way in range(2):
            origin = gather.origin(s, way)
            for j in range(k):
                rows = ins[j].shape[0]
                cut = half_rows(rows)
                part = pl.ds(0, cut) if way == 0 else pl.ds(cut, rows - cut)
                if s > 0:
                    copies[s - 1, way, j].wait_recv()
                if s < n - 1:
                    copy = remote(
                        ins[j].at[part] if s == 0 else outs[j].at[origin, part],
                        outs[j].at[origin, part],
                        send_sem.at[way, s, j],
                        recv_sem.at[way, s, j],
                        nxt if way == 0 else prv,
                    )
                    copy.start()
                    copies[s, way, j] = copy
        if s == 0:
            gather.begin()
        gather.step(s)
        if s > 1:
            gather.pass_on(s - 2)
    gather.pass_on(n - 2)
    gather.pass_on(n - 1)
    gather.end()
    for copy in copies.values():
        copy.wait_send()
    for copy in local:
        copy.wait()


def first_gather(arrays, x, cid):
    n, k = lax.axis_size("dp"), len(arrays)
    return pl.pallas_call(
        partial(first_kernel, n, k),
        out_shape=[jax.ShapeDtypeStruct((n,) + a.shape, a.dtype) for a in arrays]
        + [jax.ShapeDtypeStruct((n, 4) + x.shape, x.dtype)],
        in_specs=[ANY] * (k + 1),
        out_specs=[ANY] * (k + 1),
        scratch_shapes=[
            pltpu.SemaphoreType.DMA((k,)),
            pltpu.SemaphoreType.DMA((2, n - 1, k)),
            pltpu.SemaphoreType.DMA((2, n - 1, k)),
        ]
        + TokenGather.scratch(n),
        compiler_params=pltpu.CompilerParams(collective_id=cid, has_side_effects=True),
    )(*arrays, x)


def token_scatter_kernel(
    n,
    x,
    out,
    from_core,
    slots,
    loads,
    from_chip,
    to_chip,
    first,
    done,
    last_buf,
    load_sem,
    core_send,
    core_recv,
    chip_send,
    chip_recv,
    send_sem,
    recv_sem,
):
    m = lax.axis_index("mp")
    c, y = m % 2, m // 2
    core, chip = mp_partners(m)
    far = (m + 2) % 4
    p, nxt, prv = ring_neighbours(n)
    rows = out.shape[0]
    half, part = rows // 2, rows // 4
    greet([core, chip, nxt, prv])

    def block_at(s, way):
        return ring_device(n, (p + 2 * n - 1 - s) % n if way == 0 else (p + 1 + s) % n)

    def regions(way):
        found = [(0, way * half, half, 0), (1, way * part, part, half)]
        if way == 1:
            found.append((1, half, half, half + part))
        return found

    over, sent = {}, []
    for s in range(n):
        for way in range(2):
            block = block_at(s, way)
            for k, (is_far, start, size, _) in enumerate(regions(way)):
                theirs = (m + 1 - 2 * c + 2 * is_far) % 4
                y_piece = (y + is_far) % 2
                copy = remote(
                    x.at[block, theirs, pl.ds(start, size)],
                    from_core.at[block, y_piece, pl.ds(start, size)],
                    core_send.at[s, way, k],
                    core_recv.at[s, way, k],
                    core,
                )
                copy.start()
                over[s, way, k] = copy
                sent.append(copy)

    def load(s, way):
        block = block_at(s, way)
        started = []
        for k, (is_far, start, size, at) in enumerate(regions(way)):
            over[s, way, k].wait_recv()
            sources = (
                x.at[block, (m + 2 * is_far) % 4, pl.ds(start, size)],
                from_core.at[block, (y + is_far) % 2, pl.ds(start, size)],
            )
            for i, source in enumerate(sources):
                copy = pltpu.make_async_copy(
                    source, loads.at[s % 2, way, i, pl.ds(at, size)], load_sem.at[s % 2, way, k, i]
                )
                copy.start()
                started.append(copy)
        return started

    chips = {}

    def to_other_chip(s):
        for copy in started[s, 1][4:6]:
            copy.wait()
        if s > 1:
            chips[s - 2].wait_send()
        at = pl.ds(half + part, half)
        add_rows(to_chip.at[s % 2], [loads.at[s % 2, 1, 0, at], loads.at[s % 2, 1, 1, at]], half, BF)
        copy = remote(to_chip.at[s % 2], from_chip.at[s], chip_send.at[s], chip_recv.at[s], chip)
        copy.start()
        chips[s] = copy

    started = {(0, way): load(0, way) for way in range(2)}
    to_other_chip(0)
    ring = {}
    for s in range(n):
        if s < n - 1:
            for way in range(2):
                started[s + 1, way] = load(s + 1, way)
            to_other_chip(s + 1)
        for way in range(2):
            for copy in started[s, way][0:4]:
                copy.wait()
            pieces = [loads.at[s % 2, way, 0], loads.at[s % 2, way, 1]]
            if s == 0:
                target = first.at[way]
            else:
                ring[s - 1, way].wait_recv()
                held = slots.at[way, s - 1]
                target = held if s < n - 1 else done.at[way]
                pieces.append(held)
            low, high = pl.ds(0, half), pl.ds(half, part)
            more = []
            if way == 1:
                chips[s].wait_recv()
                more = [from_chip.at[s]]
            add_rows(target.at[low], [piece.at[low] for piece in pieces] + more, half, BF)
            add_rows(target.at[high], [piece.at[high] for piece in pieces], part, BF)
            if s < n - 1:
                copy = remote(
                    target,
                    slots.at[way, s],
                    send_sem.at[way, s],
                    recv_sem.at[way, s],
                    nxt if way == 0 else prv,
                )
                copy.start()
                ring[s, way] = copy
    last = []
    for way in range(2):
        copy = remote(
            done.at[way, pl.ds(half, part)],
            last_buf.at[pl.ds(way * part, part)],
            send_sem.at[way, n - 1],
            recv_sem.at[way, n - 1],
            chip,
        )
        copy.start()
        last.append(copy)
    add_rows(out.at[pl.ds(half, half)], [done.at[1, pl.ds(0, half)]], half, F32)
    for copy in last:
        copy.wait_recv()
    add_rows(out.at[pl.ds(0, half)], [done.at[0, pl.ds(0, half)], last_buf], half, F32)
    for copy in sent + list(ring.values()) + last + [chips[n - 2], chips[n - 1]]:
        copy.wait_send()


def scatter_tokens(x, cid):
    n, _, rows, cols = x.shape
    half, part = rows // 2, rows // 4
    dma = pltpu.SemaphoreType.DMA
    out, _ = pl.pallas_call(
        partial(token_scatter_kernel, n),
        out_shape=[
            jax.ShapeDtypeStruct((rows, cols), F32),
            jax.ShapeDtypeStruct((n, 2, rows, cols), BF),
        ],
        in_specs=[ANY],
        out_specs=[VM, ANY],
        scratch_shapes=[
            pltpu.VMEM((2, n - 1, half + part, cols), BF),
            pltpu.VMEM((2, 2, 2, 2 * half + part, cols), BF),
            pltpu.VMEM((n, half, cols), BF),
            pltpu.VMEM((2, half, cols), BF),
            pltpu.VMEM((2, half + part, cols), BF),
            pltpu.VMEM((2, half + part, cols), BF),
            pltpu.VMEM((half, cols), BF),
            dma((2, 2, 3, 2)),
            dma((n, 2, 3)),
            dma((n, 2, 3)),
            dma((n,)),
            dma((n,)),
            dma((2, n)),
            dma((2, n)),
        ],
        compiler_params=pltpu.CompilerParams(
            collective_id=cid, has_side_effects=True, vmem_limit_bytes=56 * 1024 * 1024
        ),
    )(x)
    return out


def edge_kernel(n, part, slope, rim, total, ahead, mine, from_core, from_chip, edge, send_sem, recv_sem):
    d, m = lax.axis_index("dp"), lax.axis_index("mp")
    core, chip = mp_partners(m)
    before, after = {"dp": (d + n - 1) % n}, {"dp": (d + 1) % n}
    rows, cols = part.shape
    edge_rows, rim_cols = rim.shape
    greet([core, chip, before, after])

    def add(dst, pieces, dtype):
        add_rows(dst, pieces, rows, dtype)

    one = remote(part, from_core, send_sem.at[0], recv_sem.at[0], core)
    one.start()
    one.wait()
    add(mine, [part, from_core], BF)
    two = remote(mine, from_chip, send_sem.at[1], recv_sem.at[1], chip)
    two.start()
    two.wait_recv()
    add(total, [mine, from_chip], F32)
    edge[:, 0:rim_cols] = rim[...]
    edge[:, rim_cols : rim_cols + cols] = total[0:edge_rows, :] * slope[...]
    three = remote(edge, ahead, send_sem.at[2], recv_sem.at[2], before)

    @pl.when(d > 0)
    def _():
        three.start()

    @pl.when(d == n - 1)
    def _():
        ahead[...] = jnp.zeros_like(ahead)

    @pl.when(d < n - 1)
    def _():
        three.wait_recv()

    @pl.when(d > 0)
    def _():
        three.wait_send()

    two.wait_send()


def sum_and_edge(part, slope, rim, cid):
    rows, cols = part.shape
    edge_shape = (rim.shape[0], rim.shape[1] + cols)
    return pl.pallas_call(
        partial(edge_kernel, lax.axis_size("dp")),
        out_shape=[
            jax.ShapeDtypeStruct(part.shape, F32),
            jax.ShapeDtypeStruct(edge_shape, F32),
        ],
        in_specs=[VM] * 3,
        out_specs=[VM] * 2,
        scratch_shapes=[
            pltpu.VMEM((rows, cols), BF),
            pltpu.VMEM((rows, cols), F32),
            pltpu.VMEM((rows, cols), BF),
            pltpu.VMEM(edge_shape, F32),
            pltpu.SemaphoreType.DMA((3,)),
            pltpu.SemaphoreType.DMA((3,)),
        ],
        compiler_params=pltpu.CompilerParams(
            collective_id=cid, has_side_effects=True, vmem_limit_bytes=32 * 1024 * 1024
        ),
    )(part, slope, rim)


def head_pair(pair, first, second):
    lane = lax.broadcasted_iota(jnp.int32, first.shape, 1)
    return jnp.where(lane < LANES // 2, first, second)


def visible_pairs(seg_col, seg_row):
    length = seg_col.shape[0]
    row = lax.broadcasted_iota(jnp.int32, (length, length), 0)
    col = lax.broadcasted_iota(jnp.int32, (length, length), 1)
    return (row >= col) & (seg_col == seg_row)


def state_decay(entry, expand):
    last = entry[entry.shape[0] - 1 :, :]
    spread = jnp.broadcast_to(last, (LANES, LANES)).T
    return dot(expand, spread, ((0,), (0,)), HIGH)


def recur_kernel(
    pairs,
    values,
    write,
    read,
    cumul,
    cumul_t,
    step_t,
    entry,
    tail,
    seg_col,
    seg_row,
    expand,
    skip,
    start,
    out,
    kept,
    state,
):
    @pl.when(pl.program_id(0) == 0)
    def _():
        state[...] = start[...]

    held = state[...]
    kept[0] = held
    v, b, c = values[...], write[...], read[...]
    scores = dot(c, b, ((1,), (1,)), HIGH)
    visible = visible_pairs(seg_col[...], seg_row[...])
    entry_full = dot(entry[...], expand[...], precision=HIGH)
    tail_full = dot(tail[...], expand[...], precision=HIGH)
    carried = entry_full * dot(c, held, ((1,), (1,)), HIGH) + skip[...] * v
    cum, cum_t, st_t = cumul[...], cumul_t[...], step_t[...]
    for pair in range(pairs):
        cols = slice(pair * LANES, (pair + 1) * LANES)
        v2 = v[:, cols]
        found = []
        for h in (2 * pair, 2 * pair + 1):
            spread = jnp.where(visible, cum[:, h : h + 1] - cum_t[h : h + 1, :], MASKED)
            mixing = jnp.exp(spread) * (scores * st_t[h : h + 1, :])
            found.append(dot(mixing, v2, precision=HIGH))
        out[:, cols] = head_pair(pair, found[0], found[1]) + carried[:, cols]
    state[...] = state_decay(entry[...], expand[...]) * held + dot(v * tail_full, b, ((0,), (0,)), HIGH)


def recur_specs(width, lengths):
    def rows(cols):
        return pl.BlockSpec((BLK, cols), lambda i: (lengths(i), 0))

    def flat(count):
        return pl.BlockSpec((count, BLK), lambda i: (0, lengths(i)))

    def whole(shape):
        return pl.BlockSpec(shape, lambda i: (0,) * len(shape))

    return rows, flat, whole


def recur_forward(v, b, c, cumul, cumul_t, step_t, entry, tail, seg_col, seg_row, expand, skip, start):
    total, width = v.shape
    blocks = total // BLK
    rows, flat, whole = recur_specs(width, lambda i: i)
    return pl.pallas_call(
        partial(recur_kernel, width // LANES),
        grid=(blocks,),
        out_shape=[
            jax.ShapeDtypeStruct((total, width), F32),
            jax.ShapeDtypeStruct((blocks, width, LANES), F32),
        ],
        in_specs=[
            rows(width),
            rows(LANES),
            rows(LANES),
            rows(LANES),
            flat(16),
            flat(16),
            rows(LANES),
            rows(LANES),
            rows(1),
            flat(1),
            whole((LANES, width)),
            whole((1, width)),
            whole((width, LANES)),
        ],
        out_specs=[
            rows(width),
            pl.BlockSpec((1, width, LANES), lambda i: (i, 0, 0)),
        ],
        scratch_shapes=[pltpu.VMEM((width, LANES), F32)],
        compiler_params=pltpu.CompilerParams(vmem_limit_bytes=48 * 1024 * 1024),
    )(v, b, c, cumul, cumul_t, step_t, entry, tail, seg_col, seg_row, expand, skip, start)


def adjoint_kernel(
    pairs,
    values,
    write,
    read,
    cumul,
    cumul_t,
    step_t,
    step,
    entry,
    tail_bare,
    seg_col,
    seg_row,
    expand,
    skip,
    kept,
    d_out,
    start,
    d_values,
    d_write,
    d_read,
    d_step,
    d_rate_step,
    d_skip,
    state,
    columns,
):
    @pl.when(pl.program_id(0) == 0)
    def _():
        state[...] = start[...]
        d_skip[...] = jnp.zeros_like(d_skip)
        columns[...] = jnp.zeros_like(columns)

    length = values.shape[0]
    lam, held = state[...], kept[0]
    v, b, c, dy = values[...], write[...], read[...], d_out[...]
    ex = expand[...]
    st = step[...]
    scores = dot(c, b, ((1,), (1,)), HIGH)
    visible = visible_pairs(seg_col[...], seg_row[...])
    entry_full = dot(entry[...], ex, precision=HIGH)
    tail = tail_bare[...] * st
    tail_full = dot(tail, ex, precision=HIGH)
    c_state = dot(c, held, ((1,), (1,)), HIGH)
    b_lam = dot(b, lam, ((1,), (1,)), HIGH)
    dy_in = dy * entry_full
    v_out = v * tail_full
    dc = dot(dy_in, held, precision=HIGH)
    db = dot(v_out, lam, precision=HIGH)
    reach = dot(dy_in * c_state, ex, ((1,), (1,)), HIGH)
    leave = dot(v * b_lam, ex, ((1,), (1,)), HIGH)
    d_skip[...] += jnp.sum(dy * v, axis=0, keepdims=True)
    dv_far = tail_full * b_lam + skip[...] * dy
    cum, cum_t, st_t = cumul[...], cumul_t[...], step_t[...]
    lane = lax.broadcasted_iota(jnp.int32, (length, LANES), 1)
    d_scores = jnp.zeros((length, length), F32)
    row_sums = jnp.zeros((length, LANES), F32)
    for pair in range(pairs):
        cols = slice(pair * LANES, (pair + 1) * LANES)
        v2, dy2 = v[:, cols], dy[:, cols]
        found = []
        for j in range(2):
            h = 2 * pair + j
            own = (lane < LANES // 2) if j == 0 else (lane >= LANES // 2)
            d_mix = dot(jnp.where(own, dy2, 0.0), v2, ((1,), (1,)), HIGH)
            spread = jnp.where(visible, cum[:, h : h + 1] - cum_t[h : h + 1, :], MASKED)
            decay = jnp.exp(spread)
            decay_step = decay * st_t[h : h + 1, :]
            weighted = d_mix * scores * decay
            d_scores = d_scores + d_mix * decay_step
            columns[h : h + 1, :] = jnp.sum(weighted, axis=0, keepdims=True)
            per_row = jnp.sum(weighted * st_t[h : h + 1, :], axis=1, keepdims=True)
            row_sums = jnp.where(lane == h, per_row, row_sums)
            found.append(dot(scores * decay_step, dy2, ((0,), (0,))))
        d_values[:, cols] = head_pair(pair, found[0], found[1]) + dv_far[:, cols]
    d_read[...] = dc + dot(d_scores, b, precision=HIGH)
    d_write[...] = db + dot(d_scores, c, ((0,), (0,)), HIGH)
    col_sums = columns[...].T
    leave_step = tail * leave
    d_step[...] = col_sums + tail_bare[...] * leave
    d_cum = row_sums - st * col_sums + reach - leave_step
    row = lax.broadcasted_iota(jnp.int32, (length, length), 0)
    col = lax.broadcasted_iota(jnp.int32, (length, length), 1)
    upper = (col >= row).astype(F32)
    met = jnp.sum(dot(lam * held, ex, ((0,), (1,)), HIGH), axis=0, keepdims=True)
    at_end = jnp.sum(leave_step, axis=0, keepdims=True) + entry[length - 1 :, :] * met
    d_rate_step[...] = dot(upper, d_cum, precision=HIGH) + at_end
    state[...] = state_decay(entry[...], ex) * lam + dot(dy_in, c, ((0,), (0,)), HIGH)


def recur_backward(
    v, b, c, cumul, cumul_t, step_t, step, entry, tail_bare, seg_col, seg_row, expand, skip, kept, dy, start
):
    total, width = v.shape
    blocks = total // BLK
    rows, flat, whole = recur_specs(width, lambda i: blocks - 1 - i)
    return pl.pallas_call(
        partial(adjoint_kernel, width // LANES),
        grid=(blocks,),
        out_shape=[
            jax.ShapeDtypeStruct((total, width), F32),
            jax.ShapeDtypeStruct((total, LANES), F32),
            jax.ShapeDtypeStruct((total, LANES), F32),
            jax.ShapeDtypeStruct((total, LANES), F32),
            jax.ShapeDtypeStruct((total, LANES), F32),
            jax.ShapeDtypeStruct((1, width), F32),
        ],
        in_specs=[
            rows(width),
            rows(LANES),
            rows(LANES),
            rows(LANES),
            flat(16),
            flat(16),
            rows(LANES),
            rows(LANES),
            rows(LANES),
            rows(1),
            flat(1),
            whole((LANES, width)),
            whole((1, width)),
            pl.BlockSpec((1, width, LANES), lambda i: (blocks - 1 - i, 0, 0)),
            rows(width),
            whole((width, LANES)),
        ],
        out_specs=[
            rows(width),
            rows(LANES),
            rows(LANES),
            rows(LANES),
            rows(LANES),
            whole((1, width)),
        ],
        scratch_shapes=[pltpu.VMEM((width, LANES), F32), pltpu.VMEM((LANES, LANES), F32)],
        compiler_params=pltpu.CompilerParams(vmem_limit_bytes=48 * 1024 * 1024),
    )(v, b, c, cumul, cumul_t, step_t, step, entry, tail_bare, seg_col, seg_row, expand, skip, kept, dy, start)


def state_scan_kernel(
    n, reverse, mine, decay, expand, out, first, second, got_first, got_second, half, send_sem, recv_sem
):
    d = lax.axis_index("dp")
    q = n - 1 - d if reverse else d
    zq, xq = q // 2, q % 2
    depth = n // 2
    rows = mine.shape[0] // 2
    xf = xq.astype(F32)

    def device(logical):
        return {"dp": n - 1 - logical if reverse else logical}

    beside = device(2 * zq + 1 - xq)
    others = [device(2 * ((zq + k) % depth) + xq) for k in range(1, depth)]
    own_rows = pl.ds(pl.multiple_of(rows * xq, 8), rows)
    other_rows = pl.ds(pl.multiple_of(rows * (1 - xq), 8), rows)
    own_lanes = pl.ds(pl.multiple_of(rows * xq, LANES), rows)

    def spread(row):
        square = jnp.broadcast_to(row, (LANES, LANES)).T
        return dot(expand[:, own_lanes], square, ((0,), (0,)), HIGH)

    for k in range(1, depth):

        @pl.when(zq < k)
        def _():
            got_second[k - 1] = jnp.zeros(got_second.shape[1:], F32)

    first[0:rows, :] = mine[other_rows, :]
    first[rows : rows + 8, :] = decay[...]
    greet([beside] + others)
    one = remote(first, got_first, send_sem.at[0], recv_sem.at[0], beside)
    one.start()
    one.wait_recv()
    own, own_decay = mine[own_rows, :], decay[...]
    got, got_decay = got_first[0:rows, :], got_first[rows : rows + 8, :]
    early = own * (1.0 - xf) + got * xf
    early_decay = own_decay * (1.0 - xf) + got_decay * xf
    late = own * xf + got * (1.0 - xf)
    late_decay = own_decay * xf + got_decay * (1.0 - xf)
    second[0:rows, :] = spread(late_decay[0:1, :]) * early + late
    second[rows : rows + 8, :] = early_decay * late_decay
    sent = []
    for k in range(1, depth):
        copy = remote(
            second, got_second.at[k - 1], send_sem.at[k], recv_sem.at[k], device(2 * ((zq + k) % depth) + xq)
        )
        sent.append(copy)

        @pl.when(zq + k < depth)
        def _():
            copy.start()

    total = jnp.zeros((rows, LANES), F32)
    for k in range(depth - 1, 0, -1):

        @pl.when(zq >= k)
        def _():
            sent[k - 1].wait_recv()

        got_k = got_second.at[k - 1]
        total = spread(got_k[rows : rows + 1, :]) * total + got_k[0:rows, :]
    after = spread(early_decay[0:1, :]) * total + early
    out[own_rows, :] = total * (1.0 - xf) + after * xf
    half[...] = total * xf + after * (1.0 - xf)
    last = remote(half, out.at[own_rows, :], send_sem.at[depth], recv_sem.at[depth], beside)
    last.start()
    last.wait_recv()
    one.wait_send()
    last.wait_send()
    for k in range(1, depth):

        @pl.when(zq + k < depth)
        def _():
            sent[k - 1].wait_send()


def state_scan(mine, decay, expand, reverse, cid):
    n = lax.axis_size("dp")
    rows = mine.shape[0]
    half = rows // 2
    depth = n // 2
    return pl.pallas_call(
        partial(state_scan_kernel, n, reverse),
        out_shape=jax.ShapeDtypeStruct(mine.shape, F32),
        in_specs=[VM] * 3,
        out_specs=VM,
        scratch_shapes=[
            pltpu.VMEM((half + 8, LANES), F32),
            pltpu.VMEM((half + 8, LANES), F32),
            pltpu.VMEM((half + 8, LANES), F32),
            pltpu.VMEM((depth - 1, half + 8, LANES), F32),
            pltpu.VMEM((half, LANES), F32),
            pltpu.SemaphoreType.DMA((depth + 1,)),
            pltpu.SemaphoreType.DMA((depth + 1,)),
        ],
        compiler_params=pltpu.CompilerParams(
            collective_id=cid, has_side_effects=True, vmem_limit_bytes=32 * 1024 * 1024
        ),
    )(mine, decay, expand)


def pick_matrix(position, own):
    length = position.shape[1]
    slot = lax.broadcasted_iota(jnp.int32, (CAP, length), 0).astype(F32)
    parts = [
        jnp.where(position[e : e + 1, :] == slot, 1.0, 0.0).astype(BF) for e in range(own)
    ]
    return jnp.concatenate(parts, axis=0)


def pick_kernel(own, x, position, out):
    pick = pick_matrix(position[0], own)
    picked = dot(pick, x[0]).astype(BF)
    out[...] = picked.reshape(out.shape)


def pick_gate_kernel(own, x, position, routes, router, out, gates, slot_gates):
    rows = x[0]
    pick = pick_matrix(position[0], own)
    picked = dot(pick, rows).astype(BF)
    out[...] = picked.reshape(out.shape)
    logits = dot(rows, router[...])
    lane = lax.broadcasted_iota(jnp.int32, logits.shape, 1).astype(F32)
    named = routes[0][:, 0:1] == lane
    for k in range(1, TOPK):
        named = named | (routes[0][:, k : k + 1] == lane)
    top = jnp.max(jnp.where(named, logits, MASKED), axis=1, keepdims=True)
    powers = jnp.where(named, jnp.exp(jnp.minimum(logits - top, 0.0)), 0.0)
    gate = powers / jnp.sum(powers, axis=1, keepdims=True)
    gates[0] = gate
    high = gate.astype(BF)
    low = (gate - high.astype(F32)).astype(BF)
    of_slot = dot(pick, high) + dot(pick, low)
    row = lax.broadcasted_iota(jnp.int32, of_slot.shape, 0)
    col = lax.broadcasted_iota(jnp.int32, of_slot.shape, 1)
    mine = col - lax.axis_index("dp") * own == row // CAP
    of_slot = jnp.sum(jnp.where(mine, of_slot, 0.0), axis=1, keepdims=True)
    slot_gates[...] = jnp.broadcast_to(of_slot, pick.shape[:1] + (LANES,)).reshape(slot_gates.shape)


def slot_spec(own, cols):
    return pl.BlockSpec((own, 1, CAP, cols), lambda s: (0, s, 0, 0))


def token_spec(rows, cols):
    return pl.BlockSpec((1, rows, cols), lambda s: (s, 0, 0))


BIG = pltpu.CompilerParams(vmem_limit_bytes=56 * 1024 * 1024)


def pick_rows(x, position):
    n, tokens, model = x.shape
    own = position.shape[1]
    return pl.pallas_call(
        partial(pick_kernel, own),
        grid=(n,),
        out_shape=jax.ShapeDtypeStruct((own, n, CAP, model), BF),
        in_specs=[token_spec(tokens, model), token_spec(own, tokens)],
        out_specs=slot_spec(own, model),
        compiler_params=BIG,
    )(x, position)


def pick_rows_gates(x, position, routes, router):
    n, tokens, model = x.shape
    own = position.shape[1]
    return pl.pallas_call(
        partial(pick_gate_kernel, own),
        grid=(n,),
        out_shape=[
            jax.ShapeDtypeStruct((own, n, CAP, model), BF),
            jax.ShapeDtypeStruct((n, tokens, LANES), F32),
            jax.ShapeDtypeStruct((own, n, CAP, LANES), F32),
        ],
        in_specs=[
            token_spec(tokens, model),
            token_spec(own, tokens),
            token_spec(tokens, TOPK),
            pl.BlockSpec((model, LANES), lambda s: (0, 0)),
        ],
        out_specs=[slot_spec(own, model), token_spec(tokens, LANES), slot_spec(own, LANES)],
        compiler_params=BIG,
    )(x, position, routes, router)


def expert_kernel(
    own, rows, cot_rows, gate, w_in, w_out, grad_in, grad_out, d_rows, res, dots, wide, both
):
    e, part = pl.program_id(0), pl.program_id(1)
    model = rows.shape[2]
    units = w_out.shape[1]

    @pl.when(part == 0)
    def _():
        wide[...] = w_in[0].astype(F32)
        both[:, 0:units] = wide[pl.ds(0, model, stride=2), :].astype(BF)
        both[:, units : 2 * units] = wide[pl.ds(1, model, stride=2), :].astype(BF)
        grad_in[...] = jnp.zeros_like(grad_in)
        grad_out[...] = jnp.zeros_like(grad_out)

    x, c, g = rows[0], cot_rows[0], gate[0]
    mid = dot(x, both[...])
    mid_gate, mid_up = mid[:, 0:units], mid[:, units : 2 * units]
    sig = jax.nn.sigmoid(mid_gate)
    mid_silu = mid_gate * sig
    act = (mid_silu * mid_up).astype(BF).astype(F32)
    back = dot(c, w_out[0], ((1,), (1,)))
    dot_sum = jnp.sum(act * back, axis=1, keepdims=True)
    lane = lax.broadcasted_iota(jnp.int32, g.shape, 1)
    dots[0] = jnp.where(lane == lax.axis_index("dp") * own + e, dot_sum, 0.0).astype(BF)
    gated = (act * g).astype(BF)
    d_act = back * g
    d_gate = (d_act * mid_up * (sig * (1.0 + mid_gate * (1.0 - sig)))).astype(BF)
    d_mid = jnp.concatenate([d_gate, (d_act * mid_silu).astype(BF)], axis=1)
    grads = dot(x, d_mid, ((0,), (0,)))
    grad_in[0, pl.ds(0, model, stride=2), :] += grads[:, 0:units]
    grad_in[0, pl.ds(1, model, stride=2), :] += grads[:, units : 2 * units]
    grad_out[0] += dot(gated, c, ((0,), (0,)))
    d_rows[0] = dot(d_mid, both[...], ((1,), (1,))).astype(BF)
    res[0] = dot(gated, w_out[0]).astype(BF)


def run_experts(rows, cot_rows, gate, w_in, w_out):
    own, slots, model = rows.shape
    units = w_out.shape[1]
    part = min(slots, 512)

    def slot(cols):
        return pl.BlockSpec((1, part, cols), lambda e, j: (e, j, 0))

    def weight(a, b):
        return pl.BlockSpec((1, a, b), lambda e, j: (e, 0, 0))

    return pl.pallas_call(
        partial(expert_kernel, own),
        grid=(own, slots // part),
        out_shape=[
            jax.ShapeDtypeStruct((own, 2 * model, units), F32),
            jax.ShapeDtypeStruct((own, units, model), F32),
            jax.ShapeDtypeStruct((own, slots, model), BF),
            jax.ShapeDtypeStruct((own, slots, model), BF),
            jax.ShapeDtypeStruct((own, slots, LANES), BF),
        ],
        in_specs=[slot(model), slot(model), slot(LANES), weight(2 * model, units), weight(units, model)],
        out_specs=[weight(2 * model, units), weight(units, model), slot(model), slot(model), slot(LANES)],
        scratch_shapes=[pltpu.VMEM((2 * model, units), F32), pltpu.VMEM((model, 2 * units), BF)],
        compiler_params=BIG,
    )(rows, cot_rows, gate, w_in, w_out)


def put_matrix(position, own):
    length = position.shape[0]
    lane = lax.broadcasted_iota(jnp.int32, (length, LANES), 1)
    slot = (lane % CAP).astype(F32)
    parts = []
    for e in range(0, own, 2):
        held = jnp.where(lane < CAP, position[:, e : e + 1], position[:, e + 1 : e + 2])
        parts.append(jnp.where(held == slot, 1.0, 0.0).astype(BF))
    return jnp.concatenate(parts, axis=1)


def put_kernel(own, position, rows, shared, *rest):
    extra, out = (rest[0], rest[1]) if len(rest) == 2 else (None, rest[0])
    model = shared.shape[1]
    put = put_matrix(position[0], own)
    total = dot(put, rows[...].reshape(own * CAP, model))
    here = jnp.where(pl.program_id(0) == lax.axis_index("dp"), 1.0, 0.0)
    out[0, :, 0:model] = (total + here * shared[...]).astype(BF)
    if extra is not None:
        out[0, :, model : model + LANES] = dot(put, extra[...].reshape(own * CAP, LANES)).astype(BF)


def put_rows(position, rows, shared, extra=None):
    n, tokens, own = position.shape
    model = shared.shape[1]
    cols = model + (0 if extra is None else LANES)
    more = [] if extra is None else [extra.reshape(own, n, CAP, LANES)]
    return pl.pallas_call(
        partial(put_kernel, own),
        grid=(n,),
        out_shape=jax.ShapeDtypeStruct((n, tokens, cols), BF),
        in_specs=[
            token_spec(tokens, own),
            slot_spec(own, model),
            pl.BlockSpec((tokens, model), lambda s: (0, 0)),
        ]
        + [slot_spec(own, LANES) for _ in more],
        out_specs=token_spec(tokens, cols),
        compiler_params=BIG,
    )(position, rows.reshape(own, n, CAP, model), shared, *more)


def grads_kernel(k, *refs):
    lefts, rights, out = refs[:k], refs[k : 2 * k], refs[2 * k]
    start = 0
    for left, right in zip(lefts, rights):
        cols = right.shape[1]
        out[:, start : start + cols] = dot(left[...], right[...], ((0,), (0,))).astype(BF)
        start += cols


def weight_grads(pairs):
    k = len(pairs)
    tokens, model = pairs[0][0].shape
    block = 256
    cols = sum(right.shape[1] for _, right in pairs)
    return pl.pallas_call(
        partial(grads_kernel, k),
        grid=(model // block,),
        out_shape=jax.ShapeDtypeStruct((model, cols), BF),
        in_specs=[pl.BlockSpec((tokens, block), lambda i: (0, i)) for _ in pairs]
        + [pl.BlockSpec(right.shape, lambda i: (0, 0)) for _, right in pairs],
        out_specs=pl.BlockSpec((block, cols), lambda i: (i, 0)),
        compiler_params=BIG,
    )(*[left for left, _ in pairs], *[right for _, right in pairs])


def combine_states(states, decays, expand, reverse):
    n = states.shape[0]
    place = lax.axis_index("dp")
    wide = dot(decays, expand, precision=HIGH)
    state = jnp.zeros(states.shape[1:], F32)
    for j in range(n):
        source = n - 1 - j if reverse else j
        use = source > place if reverse else source < place
        fresh = wide[source][:, None] * state + states[source]
        state = jnp.where(use, fresh, state)
    return state


def incoming_state(mine, decay, expand, reverse, cid):
    if lax.axis_size("dp") == 8:
        return state_scan(mine, jnp.broadcast_to(decay, (8, LANES)), expand, reverse, cid)
    rows = jnp.pad(decay, ((0, 31), (0, 0)))
    (gathered,) = gather_dp([jnp.concatenate([mine, rows], axis=0)], cid)
    width = mine.shape[0]
    return combine_states(gathered[:, :width], gathered[:, width], expand, reverse)


def per_device(
    hidden,
    segment_ids,
    routes,
    norm_gain,
    mixer_in,
    state_in,
    step_in,
    conv_value,
    conv_value_bias,
    conv_state,
    conv_state_bias,
    head_params,
    gated_gain,
    mixer_out,
    ffn_gain,
    router,
    shared_in,
    shared_out,
    expert_in,
    expert_out,
    cotangent,
):
    n = lax.axis_size("dp")
    place, mp_place = lax.axis_index("dp"), lax.axis_index("mp")
    tokens, model = hidden.shape
    shard = model // n
    inner = mixer_in.shape[2]
    state_cols = state_in.shape[1]
    taps = conv_value.shape[0]
    heads = head_params.shape[1]
    width = inner // heads
    own_experts = expert_in.shape[0]
    hidden_units = shared_out.shape[0]
    quarter = tokens // 4

    misc_parts = [
        conv_value.reshape(-1),
        conv_value_bias.reshape(-1),
        gated_gain.reshape(-1),
        conv_state.reshape(-1),
        conv_state_bias,
        norm_gain,
        ffn_gain,
    ]
    misc = jnp.concatenate(misc_parts)
    route_rows = routes.T.reshape(-1, model).astype(BF)
    small = jnp.concatenate(
        [
            hidden[tokens - 16 :],
            jnp.pad(misc, (0, model - misc.shape[0]))[None],
            route_rows,
            jnp.zeros((15 - route_rows.shape[0], model), BF),
        ],
        axis=0,
    )
    pack_a = jnp.concatenate(
        [
            mixer_in.reshape(shard, 2 * inner),
            state_in,
            jnp.pad(step_in, ((0, 0), (0, LANES - heads))),
        ],
        axis=1,
    )
    pack_b = jnp.concatenate(
        [
            mixer_out.T,
            shared_in.reshape(shard, 2 * hidden_units),
            shared_out.T,
            jnp.pad(router, ((0, 0), (0, LANES - EXPERTS))),
        ],
        axis=1,
    )
    mine_cot = lax.dynamic_slice_in_dim(cotangent, mp_place * quarter, quarter, 0)
    weight_a, small_all, cot_all = first_gather([pack_a, small], mine_cot, 0)
    weight_a = weight_a.reshape(model, -1)
    cot_all = cot_all.reshape(n, tokens, model)
    pack_b, small_all = lax.optimization_barrier((pack_b, small_all))
    weight_b = lax.all_gather(pack_b, "dp", axis=0, tiled=True)
    out_t = weight_b[:, :inner]
    shared_w = weight_b[:, inner : inner + 2 * hidden_units]
    shared_out_t = weight_b[:, inner + 2 * hidden_units : inner + 3 * hidden_units]
    router_w = weight_b[:, inner + 3 * hidden_units :]

    pieces = []
    start = 0
    for part in misc_parts:
        pieces.append(small_all[:, 16, start : start + part.shape[0]].astype(F32))
        start += part.shape[0]
    local_p = conv_value.shape[1]
    value_rows = jnp.concatenate(pieces[:3], axis=1).reshape(n, taps + 2, local_p, heads)
    value_rows = value_rows.transpose(1, 3, 0, 2).reshape(taps + 2, inner)
    state_rows = jnp.concatenate(pieces[3:5], axis=1).reshape(n, taps + 1, state_cols // n)
    state_rows = state_rows.transpose(1, 0, 2).reshape(taps + 1, state_cols)
    gain_first = pieces[5].reshape(1, model)
    gain_second = pieces[6].reshape(1, model)
    conv_taps = jnp.concatenate([value_rows[:taps], state_rows[:taps]], axis=1)
    conv_bias = jnp.concatenate([value_rows[taps], state_rows[taps]])[None]
    gated_row = value_rows[taps + 1][None]

    group_start = place * tokens
    seg_padded = jnp.concatenate([jnp.full((taps - 1,), -1, jnp.int32), segment_ids])
    seg_ext = lax.dynamic_slice_in_dim(seg_padded, group_start, tokens + taps - 1)
    segments = seg_ext[taps - 1 :]
    prev_seg = seg_ext[taps - 2]
    same = [
        (seg_ext[k : k + tokens] == segments).astype(F32)[:, None] for k in range(taps)
    ]
    blocks = tokens // BLK
    seg_blocks = segments.reshape(blocks, BLK)
    last_segs = seg_blocks[:, BLK - 1]
    prev_segs = jnp.concatenate([prev_seg[None], last_segs[:-1]])
    entry_ok = (seg_blocks == prev_segs[:, None]).astype(F32).reshape(tokens, 1)
    tail_ok = (seg_blocks == last_segs[:, None]).astype(F32).reshape(tokens, 1)
    group_entry_ok = (segments == prev_seg).astype(F32)[:, None]
    group_tail_ok = (segments == segments[tokens - 1]).astype(F32)[:, None]
    seg_f = segments.astype(F32)
    seg_col, seg_row = seg_f[:, None], seg_f[None, :]

    behind = lax.dynamic_index_in_dim(small_all, (place + n - 1) % n, 0, False)[:16]
    hidden_ext = jnp.concatenate([behind, hidden], axis=0).astype(F32)
    inv_ext = lax.rsqrt(jnp.mean(hidden_ext * hidden_ext, axis=1, keepdims=True) + EPS)
    normed_ext = (hidden_ext * inv_ext * gain_first).astype(BF)
    normed = normed_ext[16:]
    zx_ext = dot(normed_ext, weight_a)
    gate_z = zx_ext[16:, :inner]
    pre_ext = zx_ext[16 - taps + 1 :, inner : 2 * inner + state_cols]
    head_local = head_params.astype(F32)
    dt_lanes = zx_ext[16:, 2 * inner + state_cols :]
    conv = jnp.broadcast_to(conv_bias, (tokens, inner + state_cols))
    for k in range(taps):
        conv = conv + conv_taps[k][None] * pre_ext[k : k + tokens] * same[k]
    act = jax.nn.silu(conv)
    values = act[:, :inner]
    write = act[:, inner : inner + state_cols // 2]
    read = act[:, inner + state_cols // 2 :]

    live = (jnp.arange(LANES) < heads)[None]
    head_pad = jnp.pad(head_local, ((0, 0), (0, LANES - heads)))
    rate = jnp.where(live, -jnp.exp(head_pad[0:1]), 0.0)
    step = jnp.where(live, jax.nn.softplus(dt_lanes + head_pad[1:2]), 0.0)
    rated = (step * rate).reshape(blocks, BLK, LANES)
    lower = jnp.tril(jnp.ones((BLK, BLK), F32))
    cumul_b = jnp.einsum("ts,bsh->bth", lower, rated, precision=HIGH)
    totals = cumul_b[:, BLK - 1]
    zero_row = jnp.zeros((1, LANES), F32)
    before, after = [zero_row], [zero_row]
    for i in range(blocks - 1):
        before.append(before[-1] + totals[i][None])
        after.append(after[-1] + totals[blocks - 1 - i][None])
    before = jnp.stack(before)
    after = jnp.stack(after[::-1])
    cumul = cumul_b.reshape(tokens, LANES)
    to_end = totals[:, None] - cumul_b
    entry = jnp.exp(cumul) * entry_ok
    tail_bare = jnp.exp(to_end).reshape(tokens, LANES) * tail_ok
    tail = tail_bare * step
    group_entry = jnp.exp(cumul_b + before).reshape(tokens, LANES) * group_entry_ok
    group_tail = jnp.exp(to_end + after).reshape(tokens, LANES) * group_tail_ok * step
    cumul_t = cumul[:, :16].T
    step_t = step[:, :16].T
    expand = (jnp.arange(LANES)[:, None] == jnp.arange(inner)[None, :] // width).astype(F32)
    skip = dot(head_pad[2:3], expand, precision=HIGH)
    outgoing = dot(
        values * dot(group_tail, expand, precision=HIGH), write, ((0,), (0,)), HIGH
    )
    group_decay = group_entry[tokens - 1 :]
    incoming = incoming_state(outgoing, group_decay, expand, False, 1)
    ssd, kept = recur_forward(
        values, write, read, cumul, cumul_t, step_t, entry, tail, seg_col, seg_row, expand, skip, incoming
    )

    gate_act = jax.nn.silu(gate_z)
    gated = ssd * gate_act
    scaled = (gated * gated_row).astype(BF)
    proj_part = dot(scaled, out_t, ((1,), (1,)))
    square_part = jnp.sum(gated * gated, axis=1, keepdims=True)
    proj_pack = jnp.concatenate([proj_part, jnp.broadcast_to(square_part, (tokens, LANES))], axis=1)
    proj_sum = scatter_mp(proj_pack.reshape(4, quarter, -1), 2)
    proj = proj_sum[:, :model]
    square = proj_sum[:, model : model + 1]
    inv_gated = lax.rsqrt(square / DI + EPS)
    mine_hidden = lax.dynamic_slice_in_dim(hidden, mp_place * quarter, quarter, 0).astype(F32)
    mixed = mine_hidden + proj * inv_gated
    inv_second = lax.rsqrt(jnp.mean(mixed * mixed, axis=1, keepdims=True) + EPS)
    unit_second = mixed * inv_second
    ffn_mine = (unit_second * gain_second).astype(BF)
    ffn_all = gather_tokens(ffn_mine, 3).reshape(n, tokens, model)

    routes_all = small_all[:, 17 : 17 + route_rows.shape[0]].reshape(n, TOPK, tokens)
    routes_cols = routes_all.astype(F32).transpose(0, 2, 1)
    first_expert = place * own_experts
    own_ids = (first_expert + jnp.arange(own_experts, dtype=jnp.int32)).astype(F32)
    named = jnp.any(routes_all.astype(F32)[:, None] == own_ids[None, :, None, None], axis=2)
    earlier = (jnp.arange(tokens)[:, None] < jnp.arange(tokens)[None, :]).astype(BF)
    position = jnp.einsum("set,tu->seu", named.astype(BF), earlier, preferred_element_type=F32)
    position = jnp.where(named, position, -1.0)
    position_cols = position.transpose(0, 2, 1)
    cot_rows = pick_rows(cot_all, position)

    rows, gates, slot_gates = pick_rows_gates(ffn_all, position, routes_cols, router_w)
    slots = n * CAP
    grad_in_rows, grad_expert_out, d_rows, expert_res, slot_dots = run_experts(
        rows.reshape(own_experts, slots, model),
        cot_rows.reshape(own_experts, slots, model),
        slot_gates.reshape(own_experts, slots, LANES),
        expert_in.reshape(own_experts, 2 * model, -1),
        expert_out,
    )
    grad_expert_in = grad_in_rows.reshape(expert_in.shape)

    ffn_block = lax.dynamic_index_in_dim(ffn_all, place, 0, False)
    shared_mid = dot(ffn_block, shared_w)
    shared_gate, shared_up = shared_mid[:, :hidden_units], shared_mid[:, hidden_units:]
    shared_silu = jax.nn.silu(shared_gate)
    shared_act = (shared_silu * shared_up).astype(BF)
    shared_res = dot(shared_act, shared_out_t, ((1,), (1,)))
    d_shared_act = dot(cotangent, shared_out_t)
    d_shared_mid = jnp.concatenate(
        [d_shared_act * shared_up * silu_slope(shared_gate), d_shared_act * shared_silu], axis=1
    ).astype(BF)
    d_ffn_shared = dot(d_shared_mid, shared_w, ((1,), (1,)))

    d_ffn_pack = put_rows(position_cols, d_rows, d_ffn_shared, slot_dots)
    d_ffn_sum = scatter_tokens(d_ffn_pack.reshape(n, 4, quarter, model + LANES), 4)
    expert_res, d_ffn_sum = lax.optimization_barrier((expert_res, d_ffn_sum))
    res_pack = put_rows(position_cols, expert_res, shared_res)
    if n > 8:
        res_sum = scatter_tokens(res_pack.reshape(n, 4, quarter, model), 10)
    else:
        res_sum = lax.psum_scatter(
            res_pack.reshape(n * tokens, model), ("dp", "mp"), scatter_dimension=0, tiled=True
        )

    own_tokens_gates = lax.dynamic_slice(
        gates, (place, mp_place * quarter, 0), (1, quarter, LANES)
    ).reshape(quarter, LANES)
    dots = d_ffn_sum[:, model : model + LANES]
    share = jnp.sum(own_tokens_gates * dots, axis=1, keepdims=True)
    d_logits = (own_tokens_gates * (dots - share)).astype(BF)
    d_ffn = d_ffn_sum[:, :model] + dot(d_logits, router_w, ((1,), (1,)))
    mine_cot_f = mine_cot.astype(F32)
    grad_gain_second = jnp.sum(d_ffn * unit_second, axis=0)
    d_unit = d_ffn * gain_second
    d_mixed = mine_cot_f + inv_second * (
        d_unit - unit_second * jnp.mean(d_unit * unit_second, axis=1, keepdims=True)
    )
    d_proj_mine = (d_mixed * inv_gated).astype(BF)
    d_inv = jnp.sum(d_mixed * proj, axis=1, keepdims=True)
    d_square = d_inv * -0.5 * inv_gated * inv_gated * inv_gated / DI
    d_square_high = d_square.astype(BF)
    d_square_low = (d_square - d_square_high.astype(F32)).astype(BF)
    sent = jnp.concatenate(
        [
            d_proj_mine,
            d_logits[:, :EXPERTS],
            d_square_high,
            d_square_low,
            jnp.zeros((quarter, LANES - EXPERTS - 2), BF),
        ],
        axis=1,
    )
    (got,) = gather_mp([sent], 5)
    got = got.reshape(tokens, model + LANES)
    d_proj = got[:, :model]
    d_logits_all = jnp.pad(got[:, model : model + EXPERTS], ((0, 0), (0, LANES - EXPERTS)))
    d_square_all = got[:, model + EXPERTS : model + EXPERTS + 1].astype(F32) + got[
        :, model + EXPERTS + 1 : model + EXPERTS + 2
    ].astype(F32)

    rows0 = ((0,), (0,))
    grad_b = weight_grads(
        [
            (d_proj, scaled),
            (ffn_block, d_shared_mid),
            (cotangent, shared_act),
            (ffn_block, d_logits_all),
        ]
    )
    grad_b, d_proj = lax.optimization_barrier((grad_b, d_proj))
    sum_b = lax.psum_scatter(grad_b, "dp", scatter_dimension=0, tiled=True).astype(F32)
    d_scaled = dot(d_proj, out_t)
    grad_gated_row = jnp.sum(d_scaled * gated, axis=0)
    d_gated = d_scaled * gated_row + 2.0 * gated * d_square_all
    d_ssd = d_gated * gate_act
    d_gate_z = d_gated * ssd * silu_slope(gate_z)

    direct = dot(d_ssd * dot(group_entry, expand, precision=HIGH), read, rows0, HIGH)
    state_grad = incoming_state(direct, group_decay, expand, True, 6)
    d_values, d_write, d_read, d_step, d_rated, d_skip_row = recur_backward(
        values,
        write,
        read,
        cumul,
        cumul_t,
        step_t,
        step,
        entry,
        tail_bare,
        seg_col,
        seg_row,
        expand,
        skip,
        kept,
        d_ssd,
        state_grad,
    )
    d_rate = jnp.sum(d_rated * step, axis=0, keepdims=True)
    d_dt = jnp.where(
        live, (d_step + rate * d_rated) * jax.nn.sigmoid(dt_lanes + head_pad[1:2]), 0.0
    )
    d_skip = dot(d_skip_row, expand, ((1,), (1,)), HIGH)
    grad_head = jnp.concatenate(
        [d_rate * rate, jnp.sum(d_dt, axis=0, keepdims=True), d_skip], axis=0
    )[:, :heads]

    slope = silu_slope(conv)
    d_conv_values = d_values * slope[:, :inner]
    d_state_act, rim_ahead = sum_and_edge(
        jnp.concatenate([d_write, d_read], axis=1), slope[:16, inner:], d_conv_values[:16], 11
    )
    d_conv = jnp.concatenate([d_conv_values, d_state_act * slope[:, inner:]], axis=1)
    d_conv_ext = jnp.concatenate([d_conv, rim_ahead], axis=0)
    seg_after = lax.dynamic_slice_in_dim(
        jnp.concatenate([segment_ids, jnp.full((taps - 1,), -1, jnp.int32)]),
        group_start,
        tokens + taps - 1,
    )
    d_pre = jnp.zeros_like(d_conv)
    grad_rows = []
    for k in range(taps):
        ahead = taps - 1 - k
        ok = (seg_after[ahead : ahead + tokens] == segments).astype(F32)[:, None]
        d_pre = d_pre + conv_taps[k][None] * d_conv_ext[ahead : ahead + tokens] * ok
        grad_rows.append(jnp.sum(d_conv * pre_ext[k : k + tokens] * same[k], axis=0))
    grad_rows.append(jnp.sum(d_conv, axis=0))
    d_a = jnp.concatenate([d_gate_z, d_pre, d_dt], axis=1).astype(BF)

    d_state_mine = lax.dynamic_slice_in_dim(
        d_a[:, 2 * inner : 2 * inner + state_cols], mp_place * quarter, quarter, 0
    )
    d_normed_part = dot(d_a[:, : 2 * inner], weight_a[:, : 2 * inner], ((1,), (1,))) + dot(
        d_a[:, 2 * inner + state_cols :], weight_a[:, 2 * inner + state_cols :], ((1,), (1,))
    )
    d_normed = scatter_mp(d_normed_part.astype(BF).reshape(4, quarter, model), 7)
    d_normed = d_normed + dot(
        d_state_mine, weight_a[:, 2 * inner : 2 * inner + state_cols], ((1,), (1,))
    )
    grad_a = dot(normed, d_a, rows0).astype(BF)
    inv_first = lax.rsqrt(jnp.mean(mine_hidden * mine_hidden, axis=1, keepdims=True) + EPS)
    unit_first = mine_hidden * inv_first
    grad_gain_first = jnp.sum(d_normed * unit_first, axis=0)
    d_first = d_normed * gain_first
    mine_grad_hidden = d_mixed + inv_first * (
        d_first - unit_first * jnp.mean(d_first * unit_first, axis=1, keepdims=True)
    )

    value_grads = jnp.stack([g[:inner] for g in grad_rows] + [grad_gated_row])
    value_grads = value_grads.reshape(taps + 2, heads, n, local_p).transpose(2, 0, 3, 1)
    state_grads = jnp.stack([g[inner:] for g in grad_rows])
    state_grads = state_grads.reshape(taps + 1, n, state_cols // n).transpose(1, 0, 2)
    misc_grads = [
        value_grads.reshape(n, -1),
        state_grads.reshape(n, -1),
        jnp.broadcast_to(grad_head.reshape(1, -1), (n, 3 * heads)),
        grad_gain_first.reshape(n, shard),
        grad_gain_second.reshape(n, shard),
    ]
    sizes = [g.shape[1] for g in misc_grads]
    misc_grads = jnp.concatenate(misc_grads, axis=1)
    misc_grads = jnp.pad(misc_grads, ((0, 0), (0, 32 * LANES - misc_grads.shape[1])))
    sum_a, misc_sum = scatter_dp(
        [grad_a.reshape(n, shard, -1), misc_grads.reshape(n, 32, LANES)], 8
    )
    misc_sum = misc_sum.reshape(-1)
    cut = [0]
    for size in sizes:
        cut.append(cut[-1] + size)
    value_sum = misc_sum[: cut[1]].reshape(taps + 2, local_p, heads)
    state_sum = misc_sum[cut[1] : cut[2]].reshape(taps + 1, state_cols // n)
    head_sum = misc_sum[cut[2] : cut[3]].reshape(3, heads)
    gains = jnp.pad(misc_sum[cut[3] : cut[5]], (0, 2 * model - 2 * shard)).reshape(-1, LANES)
    mine_result = (mixed + res_sum.astype(F32)).astype(BF)
    hidden_all, result, gains_all = gather_mp([mine_grad_hidden.astype(BF), mine_result, gains], 9)
    result = result.reshape(tokens, model)
    gains_sum = jnp.sum(gains_all.reshape(4, -1)[:, : 2 * shard], axis=0)

    b1, b2 = inner, inner + 2 * hidden_units
    b3 = b2 + hidden_units
    return (
        result,
        hidden_all.reshape(tokens, model).astype(F32),
        gains_sum[:shard],
        sum_a[:, : 2 * inner].reshape(shard, 2, inner),
        sum_a[:, 2 * inner : 2 * inner + state_cols],
        sum_a[:, 2 * inner + state_cols : 2 * inner + state_cols + heads],
        value_sum[:taps],
        value_sum[taps],
        state_sum[:taps],
        state_sum[taps],
        head_sum,
        value_sum[taps + 1],
        sum_b[:, :b1].T,
        gains_sum[shard:],
        sum_b[:, b3 : b3 + EXPERTS],
        sum_b[:, b1:b2].reshape(shard, 2, hidden_units),
        sum_b[:, b2:b3].T,
        grad_expert_in,
        grad_expert_out,
    )


def solution(mesh):
    placed = (
        P("dp", None),
        P(),
        P("dp", None),
        P("dp"),
        P("dp", None, "mp"),
        P("dp", None),
        P("dp", "mp"),
        P(None, "dp", "mp"),
        P("dp", "mp"),
        P(None, "dp"),
        P("dp"),
        P(None, "mp"),
        P("dp", "mp"),
        P("mp", "dp"),
        P("dp"),
        P("dp", None),
        P("dp", None, "mp"),
        P("mp", "dp"),
        P("dp", None, None, "mp"),
        P("dp", "mp", None),
        P("dp", None),
    )
    return jax.shard_map(
        per_device,
        mesh=mesh,
        in_specs=placed,
        out_specs=(
            P("dp", None),
            P("dp", None),
            P("dp"),
            P("dp", None, "mp"),
            P("dp", None),
            P("dp", "mp"),
            P(None, "dp", "mp"),
            P("dp", "mp"),
            P(None, "dp"),
            P("dp"),
            P(None, "mp"),
            P("dp", "mp"),
            P("mp", "dp"),
            P("dp"),
            P("dp", None),
            P("dp", None, "mp"),
            P("mp", "dp"),
            P("dp", None, None, "mp"),
            P("dp", "mp", None),
        ),
        check_vma=False,
    )
```

```python
from functools import partial

import jax
import jax.numpy as jnp
from jax import lax
from jax.experimental import pallas as pl
from jax.experimental.pallas import tpu as pltpu
from jax.sharding import PartitionSpec as P

MESH = pl.DeviceIdType.MESH
BLK = 128
EXPERTS = 64
TOPK = 6
DI = 3072
CAP = 64
LANES = 128

EPS = 1e-05
HIGH = lax.Precision.HIGHEST
MASKED = -1e30
BF = jnp.bfloat16
F32 = jnp.float32
ANY = pl.BlockSpec(memory_space=pl.ANY)
VM = pl.BlockSpec(memory_space=pltpu.VMEM)


def dot(a, b, dims=((1,), (0,)), precision=None):
    return lax.dot_general(
        a, b, (dims, ((), ())), precision=precision, preferred_element_type=F32
    )


def silu_slope(argument):
    sigmoid_val = jax.nn.sigmoid(argument)
    return sigmoid_val * (1.0 + argument * (1.0 - sigmoid_val))


def half_rows(rows):
    return (rows // 32) * 16


def chunk_rows(start, size):
    return [(start + i, min(32, size - i)) for i in range(0, size, 32)]


def both_ways(rows):
    cut = half_rows(rows)
    ways = [chunk_rows(0, cut), chunk_rows(cut, rows - cut)]
    order = []
    for i in range(max(len(w) for w in ways)):
        for way in range(2):
            if i < len(ways[way]):
                order.append((way, i) + ways[way][i])
    return order


def ring_place(n, d):
    high, low = d // 2, d % 2
    return high * (1 - low) + (n - 1 - high) * low


def ring_device(n, p):
    back = p // (n // 2)
    return (2 * p) * (1 - back) + (2 * (n - 1 - p) + 1) * back


def greet(targets):
    barrier = pltpu.get_barrier_semaphore()
    for target in targets:
        pl.semaphore_signal(barrier, inc=1, device_id=target, device_id_type=MESH)
    pl.semaphore_wait(barrier, len(targets))


def remote(src, dst, send, recv, target):
    return pltpu.make_async_remote_copy(
        src_ref=src,
        dst_ref=dst,
        send_sem=send,
        recv_sem=recv,
        device_id=target,
        device_id_type=MESH,
    )


def mp_partners(m):
    return {"mp": m + 1 - 2 * (m % 2)}, {"mp": (m + 2) % 4}


def ring_neighbours(n):
    p = ring_place(n, lax.axis_index("dp"))
    nxt = {"dp": ring_device(n, (p + 1) % n)}
    prv = {"dp": ring_device(n, (p + n - 1) % n)}
    return p, nxt, prv


class RingGather:
    def __init__(self, n, ins, outs, sems):
        self.n, self.ins, self.outs = n, ins, outs
        self.local_sem, self.send_sem, self.recv_sem = sems
        self.p, self.nxt, self.prv = ring_neighbours(n)
        self.order = [both_ways(a.shape[0]) for a in ins]
        self.copies = {}

    @staticmethod
    def scratch(n, arrays):
        dma = pltpu.SemaphoreType.DMA
        most = max(len(both_ways(a.shape[0])) for a in arrays)
        shape = (n - 1, len(arrays), most)
        return [dma((len(arrays),)), dma(shape), dma(shape)]

    def begin(self):
        d = lax.axis_index("dp")
        self.local = []
        for j, (a, out) in enumerate(zip(self.ins, self.outs)):
            copy = pltpu.make_async_copy(a, out.at[d], self.local_sem.at[j])
            copy.start()
            self.local.append(copy)

    def step(self, s):
        n, p = self.n, self.p
        for j, (a, out) in enumerate(zip(self.ins, self.outs)):
            for k, (way, _, start, rows) in enumerate(self.order[j]):
                origin = ring_device(n, (p + n - s) % n if way == 0 else (p + s) % n)
                part = pl.ds(start, rows)
                if s > 0:
                    self.copies[s - 1, j, k].wait_recv()
                if s < n - 1:
                    copy = remote(
                        a.at[part] if s == 0 else out.at[origin, part],
                        out.at[origin, part],
                        self.send_sem.at[s, j, k],
                        self.recv_sem.at[s, j, k],
                        self.nxt if way == 0 else self.prv,
                    )
                    copy.start()
                    self.copies[s, j, k] = copy

    def end(self):
        for copy in self.copies.values():
            copy.wait_send()
        for copy in self.local:
            copy.wait()


def gather_kernel(n, k, *refs):
    ring = RingGather(n, refs[:k], refs[k : 2 * k], refs[2 * k :])
    greet([ring.nxt, ring.prv])
    ring.begin()
    for s in range(n):
        ring.step(s)
    ring.end()


def gather_dp(arrays, cid):
    n, k = lax.axis_size("dp"), len(arrays)
    return pl.pallas_call(
        partial(gather_kernel, n, k),
        out_shape=[jax.ShapeDtypeStruct((n,) + a.shape, a.dtype) for a in arrays],
        in_specs=[ANY] * k,
        out_specs=[ANY] * k,
        scratch_shapes=RingGather.scratch(n, arrays),
        compiler_params=pltpu.CompilerParams(collective_id=cid, has_side_effects=True),
    )(*arrays)


def add_rows(dst, pieces, rows, dtype):
    def body(i, carry):
        sl = pl.ds(pl.multiple_of(i * 16, 16), 16)
        total = pieces[0][sl, :].astype(F32)
        for piece in pieces[1:]:
            total = total + piece[sl, :].astype(F32)
        dst[sl, :] = total.astype(dtype)
        return carry

    lax.fori_loop(0, rows // 16, body, 0)


def scatter_kernel(n, k, *refs):
    ins, outs, slots = refs[:k], refs[k : 2 * k], refs[2 * k : 3 * k]
    send_sem, recv_sem = refs[3 * k :]
    p, nxt, prv = ring_neighbours(n)
    greet([nxt, prv])
    copies = {}
    for s in range(n):
        for j in range(k):
            for i, (way, _, start, size) in enumerate(both_ways(ins[j].shape[1])):
                block = ring_device(n, (p + 2 * n - 1 - s) % n if way == 0 else (p + 1 + s) % n)
                part = pl.ds(start, size)
                mine = ins[j].at[block, part]
                if s > 0:
                    copies[s - 1, j, i].wait_recv()
                    held = slots[j].at[s - 1, part]
                    if s == n - 1:
                        add_rows(outs[j].at[part], [held, mine], size, F32)
                        continue
                    add_rows(held, [held, mine], size, ins[j].dtype)
                    source = held
                else:
                    source = mine
                copy = remote(
                    source,
                    slots[j].at[s, part],
                    send_sem.at[s, j, i],
                    recv_sem.at[s, j, i],
                    nxt if way == 0 else prv,
                )
                copy.start()
                copies[s, j, i] = copy
    for copy in copies.values():
        copy.wait_send()


def scatter_dp(arrays, cid):
    n, k = lax.axis_size("dp"), len(arrays)
    most = max(len(both_ways(a.shape[1])) for a in arrays)
    return pl.pallas_call(
        partial(scatter_kernel, n, k),
        out_shape=[jax.ShapeDtypeStruct(a.shape[1:], F32) for a in arrays],
        in_specs=[VM] * k,
        out_specs=[VM] * k,
        scratch_shapes=[pltpu.VMEM((n - 1,) + a.shape[1:], a.dtype) for a in arrays]
        + [
            pltpu.SemaphoreType.DMA((n - 1, k, most)),
            pltpu.SemaphoreType.DMA((n - 1, k, most)),
        ],
        compiler_params=pltpu.CompilerParams(
            collective_id=cid, has_side_effects=True, vmem_limit_bytes=48 * 1024 * 1024
        ),
    )(*arrays)


def mp_scatter_kernel(x, out, from_core, from_chip, send_sem, recv_sem):
    m = lax.axis_index("mp")
    core, chip = mp_partners(m)
    mine, far = m, (m + 2) % 4
    greet([core, chip])
    first = []
    for i in range(2):
        block = (m + 1 - 2 * (m % 2) + 2 * i) % 4
        copy = remote(x.at[block], from_core.at[i], send_sem.at[i], recv_sem.at[i], core)
        copy.start()
        first.append(copy)
    rows = out.shape[0]
    first[1].wait_recv()
    add_rows(from_core.at[1], [from_core.at[1], x.at[far]], rows, x.dtype)
    last = remote(from_core.at[1], from_chip, send_sem.at[2], recv_sem.at[2], chip)
    last.start()
    first[0].wait_recv()
    last.wait_recv()
    add_rows(out, [x.at[mine], from_core.at[0], from_chip], rows, F32)
    for copy in first + [last]:
        copy.wait_send()


def scatter_mp(x, cid):
    rows, cols = x.shape[1:]
    return pl.pallas_call(
        mp_scatter_kernel,
        out_shape=jax.ShapeDtypeStruct((rows, cols), F32),
        in_specs=[VM],
        out_specs=VM,
        scratch_shapes=[
            pltpu.VMEM((2, rows, cols), x.dtype),
            pltpu.VMEM((rows, cols), x.dtype),
            pltpu.SemaphoreType.DMA((3,)),
            pltpu.SemaphoreType.DMA((3,)),
        ],
        compiler_params=pltpu.CompilerParams(
            collective_id=cid, has_side_effects=True, vmem_limit_bytes=32 * 1024 * 1024
        ),
    )(x)


def mp_gather_kernel(k, *refs):
    ins, outs = refs[:k], refs[k : 2 * k]
    local_sem, send_sem, recv_sem = refs[2 * k :]
    m = lax.axis_index("mp")
    core, chip = mp_partners(m)
    far = (m + 2) % 4
    greet([core, chip])
    copies, local, arrive = [], [], []
    for j in range(k):
        to_chip = remote(ins[j], outs[j].at[m], send_sem.at[0, j], recv_sem.at[0, j], chip)
        to_chip.start()
        to_core = remote(ins[j], outs[j].at[m], send_sem.at[1, j], recv_sem.at[1, j], core)
        to_core.start()
        own = pltpu.make_async_copy(ins[j], outs[j].at[m], local_sem.at[j])
        own.start()
        copies += [to_chip, to_core]
        arrive.append(to_chip)
        local.append(own)
    onward = []
    for j in range(k):
        arrive[j].wait_recv()
        copy = remote(outs[j].at[far], outs[j].at[far], send_sem.at[2, j], recv_sem.at[2, j], core)
        copy.start()
        onward.append(copy)
    for j in range(k):
        copies[2 * j + 1].wait_recv()
        onward[j].wait_recv()
        local[j].wait()
    for copy in copies + onward:
        copy.wait_send()


def gather_mp(arrays, cid):
    k = len(arrays)
    return pl.pallas_call(
        partial(mp_gather_kernel, k),
        out_shape=[jax.ShapeDtypeStruct((4,) + a.shape, a.dtype) for a in arrays],
        in_specs=[ANY] * k,
        out_specs=[ANY] * k,
        scratch_shapes=[
            pltpu.SemaphoreType.DMA((k,)),
            pltpu.SemaphoreType.DMA((3, k)),
            pltpu.SemaphoreType.DMA((3, k)),
        ],
        compiler_params=pltpu.CompilerParams(collective_id=cid, has_side_effects=True),
    )(*arrays)


class TokenGather:
    def __init__(self, n, both, x, out, sems):
        self.n, self.both, self.x, self.out = n, both, x, out
        self.local, self.ring_s, self.ring_r, self.core_s, self.core_r, self.chip_s, self.chip_r = sems
        self.d, self.m = lax.axis_index("dp"), lax.axis_index("mp")
        self.far = (self.m + 2) % 4
        self.core, self.chip = mp_partners(self.m)
        self.p, self.nxt, self.prv = ring_neighbours(n)
        self.pieces = [(way, 0, start, rows) for way, _, start, rows in both_ways(x.shape[0])]
        self.pieces += [(way, 1, start, rows) for way, _, start, rows in both_ways(both)]
        self.sent, self.pending = [], []
        self.ring, self.chips = {}, {}

    @staticmethod
    def scratch(n, rows, both):
        dma = pltpu.SemaphoreType.DMA
        own, far = len(both_ways(rows)), len(both_ways(both))
        return [
            dma((3,)),
            dma((n - 1, own + far)),
            dma((n - 1, own + far)),
            dma((n, 2 * own + far)),
            dma((n, 2 * own + far)),
            dma((n, own)),
            dma((n, own)),
        ]

    def send(self, place, s_sem, r_sem, target):
        copy = remote(place, place, s_sem, r_sem, target)
        copy.start()
        self.sent.append(copy)
        return copy

    def begin(self):
        own = self.out.at[self.d, self.m]
        load = pltpu.make_async_copy(self.x, own, self.local.at[0])
        load.start()
        self.first = None
        if self.both:
            part = pl.ds(0, self.both)
            self.first = remote(
                self.x.at[part], own.at[part], self.local.at[1], self.local.at[2], self.chip
            )
            self.first.start()
            self.sent.append(self.first)
        load.wait()

    def step(self, s):
        n, p = self.n, self.p
        for k, (way, is_far, start, rows) in enumerate(self.pieces):
            origin = ring_device(n, (p + n - s) % n if way == 0 else (p + s) % n)
            place = self.far if is_far else self.m
            region = self.out.at[origin, place, pl.ds(start, rows)]
            if s > 0:
                self.ring[s - 1, k].wait_recv()
            elif is_far and self.first is not None:
                self.first.wait_recv()
                self.first = None
            if s < n - 1:
                self.ring[s, k] = self.send(
                    region, self.ring_s.at[s, k], self.ring_r.at[s, k], self.nxt if way == 0 else self.prv
                )
            self.pending.append(
                self.send(region, self.core_s.at[s, k], self.core_r.at[s, k], self.core)
            )
            if not is_far and start >= self.both:
                self.chips[s, k] = (
                    self.send(region, self.chip_s.at[s, k], self.chip_r.at[s, k], self.chip),
                    self.out.at[origin, self.far, pl.ds(start, rows)],
                )

    def pass_on(self, s):
        total = len(self.pieces)
        for k in range(total):
            if (s, k) in self.chips:
                copy, region = self.chips[s, k]
                copy.wait_recv()
                self.pending.append(
                    self.send(region, self.core_s.at[s, total + k], self.core_r.at[s, total + k], self.core)
                )

    def end(self):
        for copy in self.pending:
            copy.wait_recv()
        for copy in self.sent:
            copy.wait_send()


def token_gather_kernel(n, both, x, out, *sems):
    gather = TokenGather(n, both, x, out, sems)
    greet([gather.core, gather.chip, gather.nxt, gather.prv])
    gather.begin()
    for s in range(n):
        gather.step(s)
        if s > 0:
            gather.pass_on(s - 1)
    gather.pass_on(n - 1)
    gather.end()


def gather_tokens(x, cid):
    n = lax.axis_size("dp")
    both = x.shape[0] // 2
    return pl.pallas_call(
        partial(token_gather_kernel, n, both),
        out_shape=jax.ShapeDtypeStruct((n, 4) + x.shape, x.dtype),
        in_specs=[ANY],
        out_specs=ANY,
        scratch_shapes=TokenGather.scratch(n, x.shape[0], both),
        compiler_params=pltpu.CompilerParams(collective_id=cid, has_side_effects=True),
    )(x)


def first_kernel(n, k, *refs):
    ins, x = refs[:k], refs[k]
    outs, x_out = refs[k + 1 : 2 * k + 1], refs[2 * k + 1]
    ring = RingGather(n, ins, outs, refs[2 * k + 2 : 2 * k + 5])
    gather = TokenGather(n, 0, x, x_out, refs[2 * k + 5 :])
    greet([gather.core, gather.chip, gather.nxt, gather.prv])
    ring.begin()
    gather.begin()
    for s in range(n):
        gather.step(s)
        ring.step(s)
        if s > 1:
            gather.pass_on(s - 2)
    gather.pass_on(n - 2)
    gather.pass_on(n - 1)
    gather.end()
    ring.end()


def first_gather(arrays, x, cid):
    n, k = lax.axis_size("dp"), len(arrays)
    return pl.pallas_call(
        partial(first_kernel, n, k),
        out_shape=[jax.ShapeDtypeStruct((n,) + a.shape, a.dtype) for a in arrays]
        + [jax.ShapeDtypeStruct((n, 4) + x.shape, x.dtype)],
        in_specs=[ANY] * (k + 1),
        out_specs=[ANY] * (k + 1),
        scratch_shapes=RingGather.scratch(n, arrays) + TokenGather.scratch(n, x.shape[0], 0),
        compiler_params=pltpu.CompilerParams(collective_id=cid, has_side_effects=True),
    )(*arrays, x)


def token_scatter_kernel(
    n,
    x,
    out,
    from_core,
    slots,
    loads,
    far_loads,
    from_chip,
    to_chip,
    first,
    done,
    last_buf,
    load_sem,
    far_sem,
    core_send,
    core_recv,
    chip_send,
    chip_recv,
    send_sem,
    recv_sem,
):
    m = lax.axis_index("mp")
    c, y = m % 2, m // 2
    core, chip = mp_partners(m)
    p, nxt, prv = ring_neighbours(n)
    rows = out.shape[0]
    half, part = rows // 2, rows // 4
    greet([core, chip, nxt, prv])

    def block_at(s, way):
        return ring_device(n, (p + 2 * n - 1 - s) % n if way == 0 else (p + 1 + s) % n)

    parts = [
        (0, 0, 0, half, 0),
        (1, 0, half, half, 0),
        (0, 1, 0, part, half),
        (1, 1, part, part, half),
        (1, 1, half, half, None),
    ]
    over, sent, loading = {}, [], {}

    def core_sends(s):
        for k in (4, 0, 1, 2, 3):
            way, is_far, start, size, _ = parts[k]
            block, y_piece = block_at(s, way), (y + is_far) % 2
            copy = remote(
                x.at[block, (m + 1 - 2 * c + 2 * is_far) % 4, pl.ds(start, size)],
                from_core.at[block, y_piece, pl.ds(start, size)],
                core_send.at[s, k],
                core_recv.at[s, k],
                core,
            )
            copy.start()
            over[s, k] = copy
            sent.append(copy)

    def load(s, k):
        way, is_far, start, size, at = parts[k]
        block = block_at(s, way)
        over[s, k].wait_recv()
        sources = (
            x.at[block, (m + 2 * is_far) % 4, pl.ds(start, size)],
            from_core.at[block, (y + is_far) % 2, pl.ds(start, size)],
        )
        loading[s, k] = []
        for i, source in enumerate(sources):
            if k == 4:
                copy = pltpu.make_async_copy(source, far_loads.at[s % 2, i], far_sem.at[s % 2, i])
            else:
                copy = pltpu.make_async_copy(
                    source, loads.at[s % 2, way, i, pl.ds(at, size)], load_sem.at[s % 2, k, i]
                )
            copy.start()
            loading[s, k].append(copy)

    chips = {}

    def to_other_chip(s):
        for copy in loading[s, 4]:
            copy.wait()
        if s > 1:
            chips[s - 2].wait_send()
        add_rows(to_chip.at[s % 2], [far_loads.at[s % 2, 0], far_loads.at[s % 2, 1]], half, BF)
        copy = remote(to_chip.at[s % 2], from_chip.at[s], chip_send.at[s], chip_recv.at[s], chip)
        copy.start()
        chips[s] = copy

    core_sends(0)
    core_sends(1)
    load(0, 4)
    for k in range(4):
        load(0, k)
    load(1, 4)
    to_other_chip(0)
    to_other_chip(1)
    core_sends(2)
    for k in range(4):
        load(1, k)
    load(2, 4)
    ring = {}
    tiles = [(way, at, size) for way, _, at, size in both_ways(2 * (half + part))]
    tiles = [(way, at - way * (half + part), size) for way, at, size in tiles]
    for s in range(n):
        for k in range(4):
            for copy in loading[s, k]:
                copy.wait()
        for k, (way, at, size) in enumerate(tiles):
            area = pl.ds(at, size)
            pieces = [loads.at[s % 2, way, 0, area], loads.at[s % 2, way, 1, area]]
            if s == 0:
                target = first.at[way, area]
            else:
                ring[s - 1, k].wait_recv()
                held = slots.at[way, s - 1, area]
                target = held if s < n - 1 else done.at[way, area]
                pieces.append(held)
            if way == 1 and at < half:
                if at == 0:
                    chips[s].wait_recv()
                pieces.append(from_chip.at[s, area])
            add_rows(target, pieces, size, BF)
            if s < n - 1:
                copy = remote(
                    target,
                    slots.at[way, s, area],
                    send_sem.at[s, k],
                    recv_sem.at[s, k],
                    nxt if way == 0 else prv,
                )
                copy.start()
                ring[s, k] = copy
        if s + 2 < n:
            to_other_chip(s + 2)
            for k in range(4):
                load(s + 2, k)
        if s + 3 < n:
            core_sends(s + 3)
            load(s + 3, 4)
    last = []
    for way in range(2):
        copy = remote(
            done.at[way, pl.ds(half, part)],
            last_buf.at[pl.ds(way * part, part)],
            send_sem.at[n - 1, way],
            recv_sem.at[n - 1, way],
            chip,
        )
        copy.start()
        last.append(copy)
    add_rows(out.at[pl.ds(half, half)], [done.at[1, pl.ds(0, half)]], half, F32)
    for copy in last:
        copy.wait_recv()
    add_rows(out.at[pl.ds(0, half)], [done.at[0, pl.ds(0, half)], last_buf], half, F32)
    for copy in sent + list(ring.values()) + last + [chips[n - 2], chips[n - 1]]:
        copy.wait_send()


def scatter_tokens(x, cid):
    n, _, rows, cols = x.shape
    half, part = rows // 2, rows // 4
    dma = pltpu.SemaphoreType.DMA
    out, _ = pl.pallas_call(
        partial(token_scatter_kernel, n),
        out_shape=[
            jax.ShapeDtypeStruct((rows, cols), F32),
            jax.ShapeDtypeStruct((n, 2, rows, cols), BF),
        ],
        in_specs=[ANY],
        out_specs=[VM, ANY],
        scratch_shapes=[
            pltpu.VMEM((2, n - 1, half + part, cols), BF),
            pltpu.VMEM((2, 2, 2, half + part, cols), BF),
            pltpu.VMEM((2, 2, half, cols), BF),
            pltpu.VMEM((n, half, cols), BF),
            pltpu.VMEM((2, half, cols), BF),
            pltpu.VMEM((2, half + part, cols), BF),
            pltpu.VMEM((2, half + part, cols), BF),
            pltpu.VMEM((half, cols), BF),
            dma((2, 4, 2)),
            dma((2, 2)),
            dma((n, 5)),
            dma((n, 5)),
            dma((n,)),
            dma((n,)),
            dma((n, 6)),
            dma((n, 6)),
        ],
        compiler_params=pltpu.CompilerParams(
            collective_id=cid, has_side_effects=True, vmem_limit_bytes=56 * 1024 * 1024
        ),
    )(x)
    return out


def edge_kernel(n, part, slope, rim, total, ahead, mine, from_core, from_chip, edge, send_sem, recv_sem):
    d, m = lax.axis_index("dp"), lax.axis_index("mp")
    core, chip = mp_partners(m)
    before, after = {"dp": (d + n - 1) % n}, {"dp": (d + 1) % n}
    rows, cols = part.shape
    edge_rows, rim_cols = rim.shape
    greet([core, chip, before, after])

    def add(dst, pieces, dtype):
        add_rows(dst, pieces, rows, dtype)

    one = remote(part, from_core, send_sem.at[0], recv_sem.at[0], core)
    one.start()
    one.wait()
    add(mine, [part, from_core], BF)
    two = remote(mine, from_chip, send_sem.at[1], recv_sem.at[1], chip)
    two.start()
    two.wait_recv()
    add(total, [mine, from_chip], F32)
    edge[:, 0:rim_cols] = rim[...]
    edge[:, rim_cols : rim_cols + cols] = total[0:edge_rows, :] * slope[...]
    three = remote(edge, ahead, send_sem.at[2], recv_sem.at[2], before)

    @pl.when(d > 0)
    def _():
        three.start()

    @pl.when(d == n - 1)
    def _():
        ahead[...] = jnp.zeros_like(ahead)

    @pl.when(d < n - 1)
    def _():
        three.wait_recv()

    @pl.when(d > 0)
    def _():
        three.wait_send()

    two.wait_send()


def sum_and_edge(part, slope, rim, cid):
    rows, cols = part.shape
    edge_shape = (rim.shape[0], rim.shape[1] + cols)
    return pl.pallas_call(
        partial(edge_kernel, lax.axis_size("dp")),
        out_shape=[
            jax.ShapeDtypeStruct(part.shape, F32),
            jax.ShapeDtypeStruct(edge_shape, F32),
        ],
        in_specs=[VM] * 3,
        out_specs=[VM] * 2,
        scratch_shapes=[
            pltpu.VMEM((rows, cols), BF),
            pltpu.VMEM((rows, cols), F32),
            pltpu.VMEM((rows, cols), BF),
            pltpu.VMEM(edge_shape, F32),
            pltpu.SemaphoreType.DMA((3,)),
            pltpu.SemaphoreType.DMA((3,)),
        ],
        compiler_params=pltpu.CompilerParams(
            collective_id=cid, has_side_effects=True, vmem_limit_bytes=32 * 1024 * 1024
        ),
    )(part, slope, rim)


def head_pair(pair, first, second):
    lane = lax.broadcasted_iota(jnp.int32, first.shape, 1)
    return jnp.where(lane < LANES // 2, first, second)


def visible_pairs(seg_col, seg_row):
    length = seg_col.shape[0]
    row = lax.broadcasted_iota(jnp.int32, (length, length), 0)
    col = lax.broadcasted_iota(jnp.int32, (length, length), 1)
    return (row >= col) & (seg_col == seg_row)


def state_decay(entry, expand):
    last = entry[entry.shape[0] - 1 :, :]
    spread = jnp.broadcast_to(last, (LANES, LANES)).T
    return dot(expand, spread, ((0,), (0,)), HIGH)


def recur_kernel(
    pairs,
    values,
    write,
    read,
    cumul,
    cumul_t,
    step_t,
    entry,
    tail,
    seg_col,
    seg_row,
    expand,
    skip,
    start,
    out,
    kept,
    state,
):
    @pl.when(pl.program_id(0) == 0)
    def _():
        state[...] = start[...]

    held = state[...]
    kept[0] = held
    v, b, c = values[...], write[...], read[...]
    scores = dot(c, b, ((1,), (1,)), HIGH)
    visible = visible_pairs(seg_col[...], seg_row[...])
    entry_full = dot(entry[...], expand[...], precision=HIGH)
    tail_full = dot(tail[...], expand[...], precision=HIGH)
    carried = entry_full * dot(c, held, ((1,), (1,)), HIGH) + skip[...] * v
    cum, cum_t, st_t = cumul[...], cumul_t[...], step_t[...]
    for pair in range(pairs):
        cols = slice(pair * LANES, (pair + 1) * LANES)
        v2 = v[:, cols]
        found = []
        for h in (2 * pair, 2 * pair + 1):
            spread = jnp.where(visible, cum[:, h : h + 1] - cum_t[h : h + 1, :], MASKED)
            mixing = jnp.exp(spread) * (scores * st_t[h : h + 1, :])
            found.append(dot(mixing, v2, precision=HIGH))
        out[:, cols] = head_pair(pair, found[0], found[1]) + carried[:, cols]
    state[...] = state_decay(entry[...], expand[...]) * held + dot(v * tail_full, b, ((0,), (0,)), HIGH)


def recur_specs(width, lengths):
    def rows(cols):
        return pl.BlockSpec((BLK, cols), lambda i: (lengths(i), 0))

    def flat(count):
        return pl.BlockSpec((count, BLK), lambda i: (0, lengths(i)))

    def whole(shape):
        return pl.BlockSpec(shape, lambda i: (0,) * len(shape))

    return rows, flat, whole


def recur_forward(v, b, c, cumul, cumul_t, step_t, entry, tail, seg_col, seg_row, expand, skip, start):
    total, width = v.shape
    blocks = total // BLK
    rows, flat, whole = recur_specs(width, lambda i: i)
    return pl.pallas_call(
        partial(recur_kernel, width // LANES),
        grid=(blocks,),
        out_shape=[
            jax.ShapeDtypeStruct((total, width), F32),
            jax.ShapeDtypeStruct((blocks, width, LANES), F32),
        ],
        in_specs=[
            rows(width),
            rows(LANES),
            rows(LANES),
            rows(LANES),
            flat(16),
            flat(16),
            rows(LANES),
            rows(LANES),
            rows(1),
            flat(1),
            whole((LANES, width)),
            whole((1, width)),
            whole((width, LANES)),
        ],
        out_specs=[
            rows(width),
            pl.BlockSpec((1, width, LANES), lambda i: (i, 0, 0)),
        ],
        scratch_shapes=[pltpu.VMEM((width, LANES), F32)],
        compiler_params=pltpu.CompilerParams(vmem_limit_bytes=48 * 1024 * 1024),
    )(v, b, c, cumul, cumul_t, step_t, entry, tail, seg_col, seg_row, expand, skip, start)


def adjoint_kernel(
    pairs,
    values,
    write,
    read,
    cumul,
    cumul_t,
    step_t,
    step,
    entry,
    tail_bare,
    seg_col,
    seg_row,
    expand,
    skip,
    kept,
    d_out,
    start,
    d_values,
    d_write,
    d_read,
    d_step,
    d_rate_step,
    d_skip,
    state,
    columns,
):
    @pl.when(pl.program_id(0) == 0)
    def _():
        state[...] = start[...]
        d_skip[...] = jnp.zeros_like(d_skip)
        columns[...] = jnp.zeros_like(columns)

    length = values.shape[0]
    lam, held = state[...], kept[0]
    v, b, c, dy = values[...], write[...], read[...], d_out[...]
    ex = expand[...]
    st = step[...]
    scores = dot(c, b, ((1,), (1,)), HIGH)
    visible = visible_pairs(seg_col[...], seg_row[...])
    entry_full = dot(entry[...], ex, precision=HIGH)
    tail = tail_bare[...] * st
    tail_full = dot(tail, ex, precision=HIGH)
    c_state = dot(c, held, ((1,), (1,)), HIGH)
    b_lam = dot(b, lam, ((1,), (1,)), HIGH)
    dy_in = dy * entry_full
    v_out = v * tail_full
    dc = dot(dy_in, held, precision=HIGH)
    db = dot(v_out, lam, precision=HIGH)
    reach = dot(dy_in * c_state, ex, ((1,), (1,)), HIGH)
    leave = dot(v * b_lam, ex, ((1,), (1,)), HIGH)
    d_skip[...] += jnp.sum(dy * v, axis=0, keepdims=True)
    dv_far = tail_full * b_lam + skip[...] * dy
    cum, cum_t, st_t = cumul[...], cumul_t[...], step_t[...]
    lane = lax.broadcasted_iota(jnp.int32, (length, LANES), 1)
    d_scores = jnp.zeros((length, length), F32)
    row_sums = jnp.zeros((length, LANES), F32)
    for pair in range(pairs):
        cols = slice(pair * LANES, (pair + 1) * LANES)
        v2, dy2 = v[:, cols], dy[:, cols]
        found = []
        for j in range(2):
            h = 2 * pair + j
            own = (lane < LANES // 2) if j == 0 else (lane >= LANES // 2)
            d_mix = dot(jnp.where(own, dy2, 0.0), v2, ((1,), (1,)), HIGH)
            spread = jnp.where(visible, cum[:, h : h + 1] - cum_t[h : h + 1, :], MASKED)
            decay = jnp.exp(spread)
            decay_step = decay * st_t[h : h + 1, :]
            weighted = d_mix * scores * decay
            d_scores = d_scores + d_mix * decay_step
            columns[h : h + 1, :] = jnp.sum(weighted, axis=0, keepdims=True)
            per_row = jnp.sum(weighted * st_t[h : h + 1, :], axis=1, keepdims=True)
            row_sums = jnp.where(lane == h, per_row, row_sums)
            found.append(dot(scores * decay_step, dy2, ((0,), (0,))))
        d_values[:, cols] = head_pair(pair, found[0], found[1]) + dv_far[:, cols]
    d_read[...] = dc + dot(d_scores, b, precision=HIGH)
    d_write[...] = db + dot(d_scores, c, ((0,), (0,)), HIGH)
    col_sums = columns[...].T
    leave_step = tail * leave
    d_step[...] = col_sums + tail_bare[...] * leave
    d_cum = row_sums - st * col_sums + reach - leave_step
    row = lax.broadcasted_iota(jnp.int32, (length, length), 0)
    col = lax.broadcasted_iota(jnp.int32, (length, length), 1)
    upper = (col >= row).astype(F32)
    met = jnp.sum(dot(lam * held, ex, ((0,), (1,)), HIGH), axis=0, keepdims=True)
    at_end = jnp.sum(leave_step, axis=0, keepdims=True) + entry[length - 1 :, :] * met
    d_rate_step[...] = dot(upper, d_cum, precision=HIGH) + at_end
    state[...] = state_decay(entry[...], ex) * lam + dot(dy_in, c, ((0,), (0,)), HIGH)


def recur_backward(
    v, b, c, cumul, cumul_t, step_t, step, entry, tail_bare, seg_col, seg_row, expand, skip, kept, dy, start
):
    total, width = v.shape
    blocks = total // BLK
    rows, flat, whole = recur_specs(width, lambda i: blocks - 1 - i)
    return pl.pallas_call(
        partial(adjoint_kernel, width // LANES),
        grid=(blocks,),
        out_shape=[
            jax.ShapeDtypeStruct((total, width), F32),
            jax.ShapeDtypeStruct((total, LANES), F32),
            jax.ShapeDtypeStruct((total, LANES), F32),
            jax.ShapeDtypeStruct((total, LANES), F32),
            jax.ShapeDtypeStruct((total, LANES), F32),
            jax.ShapeDtypeStruct((1, width), F32),
        ],
        in_specs=[
            rows(width),
            rows(LANES),
            rows(LANES),
            rows(LANES),
            flat(16),
            flat(16),
            rows(LANES),
            rows(LANES),
            rows(LANES),
            rows(1),
            flat(1),
            whole((LANES, width)),
            whole((1, width)),
            pl.BlockSpec((1, width, LANES), lambda i: (blocks - 1 - i, 0, 0)),
            rows(width),
            whole((width, LANES)),
        ],
        out_specs=[
            rows(width),
            rows(LANES),
            rows(LANES),
            rows(LANES),
            rows(LANES),
            whole((1, width)),
        ],
        scratch_shapes=[pltpu.VMEM((width, LANES), F32), pltpu.VMEM((LANES, LANES), F32)],
        compiler_params=pltpu.CompilerParams(vmem_limit_bytes=48 * 1024 * 1024),
    )(v, b, c, cumul, cumul_t, step_t, step, entry, tail_bare, seg_col, seg_row, expand, skip, kept, dy, start)


def state_scan_kernel(
    n, reverse, mine, decay, expand, out, first, second, got_first, got_second, half, send_sem, recv_sem
):
    d = lax.axis_index("dp")
    q = n - 1 - d if reverse else d
    zq, xq = q // 2, q % 2
    depth = n // 2
    rows = mine.shape[0] // 2
    xf = xq.astype(F32)

    def device(logical):
        return {"dp": n - 1 - logical if reverse else logical}

    beside = device(2 * zq + 1 - xq)
    others = [device(2 * ((zq + k) % depth) + xq) for k in range(1, depth)]
    own_rows = pl.ds(pl.multiple_of(rows * xq, 8), rows)
    other_rows = pl.ds(pl.multiple_of(rows * (1 - xq), 8), rows)
    own_lanes = pl.ds(pl.multiple_of(rows * xq, LANES), rows)

    def spread(row):
        square = jnp.broadcast_to(row, (LANES, LANES)).T
        return dot(expand[:, own_lanes], square, ((0,), (0,)), HIGH)

    for k in range(1, depth):

        @pl.when(zq < k)
        def _():
            got_second[k - 1] = jnp.zeros(got_second.shape[1:], F32)

    first[0:rows, :] = mine[other_rows, :]
    first[rows : rows + 8, :] = decay[...]
    greet([beside] + others)
    one = remote(first, got_first, send_sem.at[0], recv_sem.at[0], beside)
    one.start()
    one.wait_recv()
    own, own_decay = mine[own_rows, :], decay[...]
    got, got_decay = got_first[0:rows, :], got_first[rows : rows + 8, :]
    early = own * (1.0 - xf) + got * xf
    early_decay = own_decay * (1.0 - xf) + got_decay * xf
    late = own * xf + got * (1.0 - xf)
    late_decay = own_decay * xf + got_decay * (1.0 - xf)
    second[0:rows, :] = spread(late_decay[0:1, :]) * early + late
    second[rows : rows + 8, :] = early_decay * late_decay
    sent = []
    for k in range(1, depth):
        copy = remote(
            second, got_second.at[k - 1], send_sem.at[k], recv_sem.at[k], device(2 * ((zq + k) % depth) + xq)
        )
        sent.append(copy)

        @pl.when(zq + k < depth)
        def _():
            copy.start()

    total = jnp.zeros((rows, LANES), F32)
    for k in range(depth - 1, 0, -1):

        @pl.when(zq >= k)
        def _():
            sent[k - 1].wait_recv()

        got_k = got_second.at[k - 1]
        total = spread(got_k[rows : rows + 1, :]) * total + got_k[0:rows, :]
    after = spread(early_decay[0:1, :]) * total + early
    out[own_rows, :] = total * (1.0 - xf) + after * xf
    half[...] = total * xf + after * (1.0 - xf)
    last = remote(half, out.at[own_rows, :], send_sem.at[depth], recv_sem.at[depth], beside)
    last.start()
    last.wait_recv()
    one.wait_send()
    last.wait_send()
    for k in range(1, depth):

        @pl.when(zq + k < depth)
        def _():
            sent[k - 1].wait_send()


def state_scan(mine, decay, expand, reverse, cid):
    n = lax.axis_size("dp")
    rows = mine.shape[0]
    half = rows // 2
    depth = n // 2
    return pl.pallas_call(
        partial(state_scan_kernel, n, reverse),
        out_shape=jax.ShapeDtypeStruct(mine.shape, F32),
        in_specs=[VM] * 3,
        out_specs=VM,
        scratch_shapes=[
            pltpu.VMEM((half + 8, LANES), F32),
            pltpu.VMEM((half + 8, LANES), F32),
            pltpu.VMEM((half + 8, LANES), F32),
            pltpu.VMEM((depth - 1, half + 8, LANES), F32),
            pltpu.VMEM((half, LANES), F32),
            pltpu.SemaphoreType.DMA((depth + 1,)),
            pltpu.SemaphoreType.DMA((depth + 1,)),
        ],
        compiler_params=pltpu.CompilerParams(
            collective_id=cid, has_side_effects=True, vmem_limit_bytes=32 * 1024 * 1024
        ),
    )(mine, decay, expand)


def pick_matrix(position, own):
    length = position.shape[1]
    slot = lax.broadcasted_iota(jnp.int32, (CAP, length), 0).astype(F32)
    parts = [
        jnp.where(position[e : e + 1, :] == slot, 1.0, 0.0).astype(BF) for e in range(own)
    ]
    return jnp.concatenate(parts, axis=0)


def pick_kernel(own, x, position, out):
    pick = pick_matrix(position[0], own)
    picked = dot(pick, x[0]).astype(BF)
    out[...] = picked.reshape(out.shape)


def pick_gate_kernel(own, x, position, routes, router, out, gates, slot_gates):
    rows = x[0]
    pick = pick_matrix(position[0], own)
    picked = dot(pick, rows).astype(BF)
    out[...] = picked.reshape(out.shape)
    logits = dot(rows, router[...])
    lane = lax.broadcasted_iota(jnp.int32, logits.shape, 1).astype(F32)
    named = routes[0][:, 0:1] == lane
    for k in range(1, TOPK):
        named = named | (routes[0][:, k : k + 1] == lane)
    top = jnp.max(jnp.where(named, logits, MASKED), axis=1, keepdims=True)
    powers = jnp.where(named, jnp.exp(jnp.minimum(logits - top, 0.0)), 0.0)
    gate = powers / jnp.sum(powers, axis=1, keepdims=True)
    gates[0] = gate
    high = gate.astype(BF)
    low = (gate - high.astype(F32)).astype(BF)
    of_slot = dot(pick, high) + dot(pick, low)
    row = lax.broadcasted_iota(jnp.int32, of_slot.shape, 0)
    col = lax.broadcasted_iota(jnp.int32, of_slot.shape, 1)
    mine = col - lax.axis_index("dp") * own == row // CAP
    of_slot = jnp.sum(jnp.where(mine, of_slot, 0.0), axis=1, keepdims=True)
    slot_gates[...] = jnp.broadcast_to(of_slot, pick.shape[:1] + (LANES,)).reshape(slot_gates.shape)


def slot_spec(own, cols):
    return pl.BlockSpec((own, 1, CAP, cols), lambda s: (0, s, 0, 0))


def token_spec(rows, cols):
    return pl.BlockSpec((1, rows, cols), lambda s: (s, 0, 0))


BIG = pltpu.CompilerParams(vmem_limit_bytes=56 * 1024 * 1024)


def pick_rows(x, position):
    n, tokens, model = x.shape
    own = position.shape[1]
    return pl.pallas_call(
        partial(pick_kernel, own),
        grid=(n,),
        out_shape=jax.ShapeDtypeStruct((own, n, CAP, model), BF),
        in_specs=[token_spec(tokens, model), token_spec(own, tokens)],
        out_specs=slot_spec(own, model),
        compiler_params=BIG,
    )(x, position)


def pick_rows_gates(x, position, routes, router):
    n, tokens, model = x.shape
    own = position.shape[1]
    return pl.pallas_call(
        partial(pick_gate_kernel, own),
        grid=(n,),
        out_shape=[
            jax.ShapeDtypeStruct((own, n, CAP, model), BF),
            jax.ShapeDtypeStruct((n, tokens, LANES), F32),
            jax.ShapeDtypeStruct((own, n, CAP, LANES), F32),
        ],
        in_specs=[
            token_spec(tokens, model),
            token_spec(own, tokens),
            token_spec(tokens, TOPK),
            pl.BlockSpec((model, LANES), lambda s: (0, 0)),
        ],
        out_specs=[slot_spec(own, model), token_spec(tokens, LANES), slot_spec(own, LANES)],
        compiler_params=BIG,
    )(x, position, routes, router)


def expert_kernel(
    own, rows, cot_rows, gate, w_in, w_out, grad_in, grad_out, d_rows, res, dots, wide, both
):
    e, part = pl.program_id(0), pl.program_id(1)
    model = rows.shape[2]
    units = w_out.shape[1]

    @pl.when(part == 0)
    def _():
        wide[...] = w_in[0].astype(F32)
        both[:, 0:units] = wide[pl.ds(0, model, stride=2), :].astype(BF)
        both[:, units : 2 * units] = wide[pl.ds(1, model, stride=2), :].astype(BF)
        grad_in[...] = jnp.zeros_like(grad_in)
        grad_out[...] = jnp.zeros_like(grad_out)

    x, c, g = rows[0], cot_rows[0], gate[0]
    mid = dot(x, both[...])
    mid_gate, mid_up = mid[:, 0:units], mid[:, units : 2 * units]
    sig = jax.nn.sigmoid(mid_gate)
    mid_silu = mid_gate * sig
    act = (mid_silu * mid_up).astype(BF).astype(F32)
    back = dot(c, w_out[0], ((1,), (1,)))
    dot_sum = jnp.sum(act * back, axis=1, keepdims=True)
    lane = lax.broadcasted_iota(jnp.int32, g.shape, 1)
    dots[0] = jnp.where(lane == lax.axis_index("dp") * own + e, dot_sum, 0.0).astype(BF)
    gated = (act * g).astype(BF)
    d_act = back * g
    d_gate = (d_act * mid_up * (sig * (1.0 + mid_gate * (1.0 - sig)))).astype(BF)
    d_mid = jnp.concatenate([d_gate, (d_act * mid_silu).astype(BF)], axis=1)
    grads = dot(x, d_mid, ((0,), (0,)))
    grad_in[0, pl.ds(0, model, stride=2), :] += grads[:, 0:units]
    grad_in[0, pl.ds(1, model, stride=2), :] += grads[:, units : 2 * units]
    grad_out[0] += dot(gated, c, ((0,), (0,)))
    d_rows[0] = dot(d_mid, both[...], ((1,), (1,))).astype(BF)
    res[0] = dot(gated, w_out[0]).astype(BF)


def run_experts(rows, cot_rows, gate, w_in, w_out):
    own, slots, model = rows.shape
    units = w_out.shape[1]
    part = min(slots, 512)

    def slot(cols):
        return pl.BlockSpec((1, part, cols), lambda e, j: (e, j, 0))

    def weight(a, b):
        return pl.BlockSpec((1, a, b), lambda e, j: (e, 0, 0))

    return pl.pallas_call(
        partial(expert_kernel, own),
        grid=(own, slots // part),
        out_shape=[
            jax.ShapeDtypeStruct((own, 2 * model, units), F32),
            jax.ShapeDtypeStruct((own, units, model), F32),
            jax.ShapeDtypeStruct((own, slots, model), BF),
            jax.ShapeDtypeStruct((own, slots, model), BF),
            jax.ShapeDtypeStruct((own, slots, LANES), BF),
        ],
        in_specs=[slot(model), slot(model), slot(LANES), weight(2 * model, units), weight(units, model)],
        out_specs=[weight(2 * model, units), weight(units, model), slot(model), slot(model), slot(LANES)],
        scratch_shapes=[pltpu.VMEM((2 * model, units), F32), pltpu.VMEM((model, 2 * units), BF)],
        compiler_params=BIG,
    )(rows, cot_rows, gate, w_in, w_out)


def put_matrix(position, own):
    length = position.shape[0]
    lane = lax.broadcasted_iota(jnp.int32, (length, LANES), 1)
    slot = (lane % CAP).astype(F32)
    parts = []
    for e in range(0, own, 2):
        held = jnp.where(lane < CAP, position[:, e : e + 1], position[:, e + 1 : e + 2])
        parts.append(jnp.where(held == slot, 1.0, 0.0).astype(BF))
    return jnp.concatenate(parts, axis=1)


def put_kernel(own, position, rows, shared, *rest):
    extra, out = (rest[0], rest[1]) if len(rest) == 2 else (None, rest[0])
    model = shared.shape[1]
    put = put_matrix(position[0], own)
    total = dot(put, rows[...].reshape(own * CAP, model))
    here = jnp.where(pl.program_id(0) == lax.axis_index("dp"), 1.0, 0.0)
    out[0, :, 0:model] = (total + here * shared[...]).astype(BF)
    if extra is not None:
        out[0, :, model : model + LANES] = dot(put, extra[...].reshape(own * CAP, LANES)).astype(BF)


def put_rows(position, rows, shared, extra=None):
    n, tokens, own = position.shape
    model = shared.shape[1]
    cols = model + (0 if extra is None else LANES)
    more = [] if extra is None else [extra.reshape(own, n, CAP, LANES)]
    return pl.pallas_call(
        partial(put_kernel, own),
        grid=(n,),
        out_shape=jax.ShapeDtypeStruct((n, tokens, cols), BF),
        in_specs=[
            token_spec(tokens, own),
            slot_spec(own, model),
            pl.BlockSpec((tokens, model), lambda s: (0, 0)),
        ]
        + [slot_spec(own, LANES) for _ in more],
        out_specs=token_spec(tokens, cols),
        compiler_params=BIG,
    )(position, rows.reshape(own, n, CAP, model), shared, *more)


def grads_kernel(k, *refs):
    lefts, rights, out = refs[:k], refs[k : 2 * k], refs[2 * k]
    start = 0
    for left, right in zip(lefts, rights):
        cols = right.shape[1]
        out[:, start : start + cols] = dot(left[...], right[...], ((0,), (0,))).astype(BF)
        start += cols


def weight_grads(pairs):
    k = len(pairs)
    tokens, model = pairs[0][0].shape
    block = 256
    cols = sum(right.shape[1] for _, right in pairs)
    return pl.pallas_call(
        partial(grads_kernel, k),
        grid=(model // block,),
        out_shape=jax.ShapeDtypeStruct((model, cols), BF),
        in_specs=[pl.BlockSpec((tokens, block), lambda i: (0, i)) for _ in pairs]
        + [pl.BlockSpec(right.shape, lambda i: (0, 0)) for _, right in pairs],
        out_specs=pl.BlockSpec((block, cols), lambda i: (i, 0)),
        compiler_params=BIG,
    )(*[left for left, _ in pairs], *[right for _, right in pairs])


def combine_states(states, decays, expand, reverse):
    n = states.shape[0]
    place = lax.axis_index("dp")
    wide = dot(decays, expand, precision=HIGH)
    state = jnp.zeros(states.shape[1:], F32)
    for j in range(n):
        source = n - 1 - j if reverse else j
        use = source > place if reverse else source < place
        fresh = wide[source][:, None] * state + states[source]
        state = jnp.where(use, fresh, state)
    return state


def incoming_state(mine, decay, expand, reverse, cid):
    if lax.axis_size("dp") == 8:
        return state_scan(mine, jnp.broadcast_to(decay, (8, LANES)), expand, reverse, cid)
    rows = jnp.pad(decay, ((0, 31), (0, 0)))
    (gathered,) = gather_dp([jnp.concatenate([mine, rows], axis=0)], cid)
    width = mine.shape[0]
    return combine_states(gathered[:, :width], gathered[:, width], expand, reverse)


def per_device(
    hidden,
    segment_ids,
    routes,
    norm_gain,
    mixer_in,
    state_in,
    step_in,
    conv_value,
    conv_value_bias,
    conv_state,
    conv_state_bias,
    head_params,
    gated_gain,
    mixer_out,
    ffn_gain,
    router,
    shared_in,
    shared_out,
    expert_in,
    expert_out,
    cotangent,
):
    n = lax.axis_size("dp")
    place, mp_place = lax.axis_index("dp"), lax.axis_index("mp")
    tokens, model = hidden.shape
    shard = model // n
    inner = mixer_in.shape[2]
    state_cols = state_in.shape[1]
    taps = conv_value.shape[0]
    heads = head_params.shape[1]
    width = inner // heads
    own_experts = expert_in.shape[0]
    hidden_units = shared_out.shape[0]
    quarter = tokens // 4

    misc_parts = [
        conv_value.reshape(-1),
        conv_value_bias.reshape(-1),
        gated_gain.reshape(-1),
        conv_state.reshape(-1),
        conv_state_bias,
        norm_gain,
        ffn_gain,
    ]
    misc = jnp.concatenate(misc_parts)
    route_rows = routes.T.reshape(-1, model).astype(BF)
    small = jnp.concatenate(
        [
            hidden[tokens - 16 :],
            jnp.pad(misc, (0, model - misc.shape[0]))[None],
            route_rows,
            jnp.zeros((15 - route_rows.shape[0], model), BF),
        ],
        axis=0,
    )
    pack_a = jnp.concatenate(
        [
            mixer_in.reshape(shard, 2 * inner),
            state_in,
            jnp.pad(step_in, ((0, 0), (0, LANES - heads))),
        ],
        axis=1,
    )
    pack_b = jnp.concatenate(
        [
            mixer_out.T,
            shared_in.reshape(shard, 2 * hidden_units),
            shared_out.T,
            jnp.pad(router, ((0, 0), (0, LANES - EXPERTS))),
        ],
        axis=1,
    )
    mine_cot = lax.dynamic_slice_in_dim(cotangent, mp_place * quarter, quarter, 0)
    weight_a, small_all, cot_all = first_gather([pack_a, small], mine_cot, 0)
    weight_a = weight_a.reshape(model, -1)
    cot_all = cot_all.reshape(n, tokens, model)
    pack_b, small_all = lax.optimization_barrier((pack_b, small_all))
    weight_b = lax.all_gather(pack_b, "dp", axis=0, tiled=True)
    out_t = weight_b[:, :inner]
    shared_w = weight_b[:, inner : inner + 2 * hidden_units]
    shared_out_t = weight_b[:, inner + 2 * hidden_units : inner + 3 * hidden_units]
    router_w = weight_b[:, inner + 3 * hidden_units :]

    pieces = []
    start = 0
    for part in misc_parts:
        pieces.append(small_all[:, 16, start : start + part.shape[0]].astype(F32))
        start += part.shape[0]
    local_p = conv_value.shape[1]
    value_rows = jnp.concatenate(pieces[:3], axis=1).reshape(n, taps + 2, local_p, heads)
    value_rows = value_rows.transpose(1, 3, 0, 2).reshape(taps + 2, inner)
    state_rows = jnp.concatenate(pieces[3:5], axis=1).reshape(n, taps + 1, state_cols // n)
    state_rows = state_rows.transpose(1, 0, 2).reshape(taps + 1, state_cols)
    gain_first = pieces[5].reshape(1, model)
    gain_second = pieces[6].reshape(1, model)
    conv_taps = jnp.concatenate([value_rows[:taps], state_rows[:taps]], axis=1)
    conv_bias = jnp.concatenate([value_rows[taps], state_rows[taps]])[None]
    gated_row = value_rows[taps + 1][None]

    group_start = place * tokens
    seg_padded = jnp.concatenate([jnp.full((taps - 1,), -1, jnp.int32), segment_ids])
    seg_ext = lax.dynamic_slice_in_dim(seg_padded, group_start, tokens + taps - 1)
    segments = seg_ext[taps - 1 :]
    prev_seg = seg_ext[taps - 2]
    same = [
        (seg_ext[k : k + tokens] == segments).astype(F32)[:, None] for k in range(taps)
    ]
    blocks = tokens // BLK
    seg_blocks = segments.reshape(blocks, BLK)
    last_segs = seg_blocks[:, BLK - 1]
    prev_segs = jnp.concatenate([prev_seg[None], last_segs[:-1]])
    entry_ok = (seg_blocks == prev_segs[:, None]).astype(F32).reshape(tokens, 1)
    tail_ok = (seg_blocks == last_segs[:, None]).astype(F32).reshape(tokens, 1)
    group_entry_ok = (segments == prev_seg).astype(F32)[:, None]
    group_tail_ok = (segments == segments[tokens - 1]).astype(F32)[:, None]
    seg_f = segments.astype(F32)
    seg_col, seg_row = seg_f[:, None], seg_f[None, :]

    behind = lax.dynamic_index_in_dim(small_all, (place + n - 1) % n, 0, False)[:16]
    hidden_ext = jnp.concatenate([behind, hidden], axis=0).astype(F32)
    inv_ext = lax.rsqrt(jnp.mean(hidden_ext * hidden_ext, axis=1, keepdims=True) + EPS)
    normed_ext = (hidden_ext * inv_ext * gain_first).astype(BF)
    normed = normed_ext[16:]
    zx_ext = dot(normed_ext, weight_a)
    gate_z = zx_ext[16:, :inner]
    pre_ext = zx_ext[16 - taps + 1 :, inner : 2 * inner + state_cols]
    head_local = head_params.astype(F32)
    dt_lanes = zx_ext[16:, 2 * inner + state_cols :]
    conv = jnp.broadcast_to(conv_bias, (tokens, inner + state_cols))
    for k in range(taps):
        conv = conv + conv_taps[k][None] * pre_ext[k : k + tokens] * same[k]
    act = jax.nn.silu(conv)
    values = act[:, :inner]
    write = act[:, inner : inner + state_cols // 2]
    read = act[:, inner + state_cols // 2 :]

    live = (jnp.arange(LANES) < heads)[None]
    head_pad = jnp.pad(head_local, ((0, 0), (0, LANES - heads)))
    rate = jnp.where(live, -jnp.exp(head_pad[0:1]), 0.0)
    step = jnp.where(live, jax.nn.softplus(dt_lanes + head_pad[1:2]), 0.0)
    rated = (step * rate).reshape(blocks, BLK, LANES)
    lower = jnp.tril(jnp.ones((BLK, BLK), F32))
    cumul_b = jnp.einsum("ts,bsh->bth", lower, rated, precision=HIGH)
    totals = cumul_b[:, BLK - 1]
    zero_row = jnp.zeros((1, LANES), F32)
    before, after = [zero_row], [zero_row]
    for i in range(blocks - 1):
        before.append(before[-1] + totals[i][None])
        after.append(after[-1] + totals[blocks - 1 - i][None])
    before = jnp.stack(before)
    after = jnp.stack(after[::-1])
    cumul = cumul_b.reshape(tokens, LANES)
    to_end = totals[:, None] - cumul_b
    entry = jnp.exp(cumul) * entry_ok
    tail_bare = jnp.exp(to_end).reshape(tokens, LANES) * tail_ok
    tail = tail_bare * step
    group_entry = jnp.exp(cumul_b + before).reshape(tokens, LANES) * group_entry_ok
    group_tail = jnp.exp(to_end + after).reshape(tokens, LANES) * group_tail_ok * step
    cumul_t = cumul[:, :16].T
    step_t = step[:, :16].T
    expand = (jnp.arange(LANES)[:, None] == jnp.arange(inner)[None, :] // width).astype(F32)
    skip = dot(head_pad[2:3], expand, precision=HIGH)
    outgoing = dot(
        values * dot(group_tail, expand, precision=HIGH), write, ((0,), (0,)), HIGH
    )
    group_decay = group_entry[tokens - 1 :]
    incoming = incoming_state(outgoing, group_decay, expand, False, 1)
    ssd, kept = recur_forward(
        values, write, read, cumul, cumul_t, step_t, entry, tail, seg_col, seg_row, expand, skip, incoming
    )

    gate_act = jax.nn.silu(gate_z)
    gated = ssd * gate_act
    scaled = (gated * gated_row).astype(BF)
    proj_part = dot(scaled, out_t, ((1,), (1,)))
    square_part = jnp.sum(gated * gated, axis=1, keepdims=True)
    proj_pack = jnp.concatenate([proj_part, jnp.broadcast_to(square_part, (tokens, LANES))], axis=1)
    proj_sum = scatter_mp(proj_pack.reshape(4, quarter, -1), 2)
    proj = proj_sum[:, :model]
    square = proj_sum[:, model : model + 1]
    inv_gated = lax.rsqrt(square / DI + EPS)
    mine_hidden = lax.dynamic_slice_in_dim(hidden, mp_place * quarter, quarter, 0).astype(F32)
    mixed = mine_hidden + proj * inv_gated
    inv_second = lax.rsqrt(jnp.mean(mixed * mixed, axis=1, keepdims=True) + EPS)
    unit_second = mixed * inv_second
    ffn_mine = (unit_second * gain_second).astype(BF)
    ffn_all = gather_tokens(ffn_mine, 3).reshape(n, tokens, model)

    routes_all = small_all[:, 17 : 17 + route_rows.shape[0]].reshape(n, TOPK, tokens)
    routes_cols = routes_all.astype(F32).transpose(0, 2, 1)
    first_expert = place * own_experts
    own_ids = (first_expert + jnp.arange(own_experts, dtype=jnp.int32)).astype(F32)
    named = jnp.any(routes_all.astype(F32)[:, None] == own_ids[None, :, None, None], axis=2)
    earlier = (jnp.arange(tokens)[:, None] < jnp.arange(tokens)[None, :]).astype(BF)
    position = jnp.einsum("set,tu->seu", named.astype(BF), earlier, preferred_element_type=F32)
    position = jnp.where(named, position, -1.0)
    position_cols = position.transpose(0, 2, 1)
    cot_rows = pick_rows(cot_all, position)

    rows, gates, slot_gates = pick_rows_gates(ffn_all, position, routes_cols, router_w)
    slots = n * CAP
    grad_in_rows, grad_expert_out, d_rows, expert_res, slot_dots = run_experts(
        rows.reshape(own_experts, slots, model),
        cot_rows.reshape(own_experts, slots, model),
        slot_gates.reshape(own_experts, slots, LANES),
        expert_in.reshape(own_experts, 2 * model, -1),
        expert_out,
    )
    grad_expert_in = grad_in_rows.reshape(expert_in.shape)

    ffn_block = lax.dynamic_index_in_dim(ffn_all, place, 0, False)
    shared_mid = dot(ffn_block, shared_w)
    shared_gate, shared_up = shared_mid[:, :hidden_units], shared_mid[:, hidden_units:]
    shared_silu = jax.nn.silu(shared_gate)
    shared_act = (shared_silu * shared_up).astype(BF)
    shared_res = dot(shared_act, shared_out_t, ((1,), (1,)))
    d_shared_act = dot(cotangent, shared_out_t)
    d_shared_mid = jnp.concatenate(
        [d_shared_act * shared_up * silu_slope(shared_gate), d_shared_act * shared_silu], axis=1
    ).astype(BF)
    d_ffn_shared = dot(d_shared_mid, shared_w, ((1,), (1,)))

    d_ffn_pack = put_rows(position_cols, d_rows, d_ffn_shared, slot_dots)
    d_ffn_sum = scatter_tokens(d_ffn_pack.reshape(n, 4, quarter, model + LANES), 4)
    expert_res, d_ffn_sum = lax.optimization_barrier((expert_res, d_ffn_sum))
    res_pack = put_rows(position_cols, expert_res, shared_res)
    if n > 8:
        res_sum = scatter_tokens(res_pack.reshape(n, 4, quarter, model), 10)
    else:
        res_sum = lax.psum_scatter(
            res_pack.reshape(n * tokens, model), ("dp", "mp"), scatter_dimension=0, tiled=True
        )

    own_tokens_gates = lax.dynamic_slice(
        gates, (place, mp_place * quarter, 0), (1, quarter, LANES)
    ).reshape(quarter, LANES)
    dots = d_ffn_sum[:, model : model + LANES]
    share = jnp.sum(own_tokens_gates * dots, axis=1, keepdims=True)
    d_logits = (own_tokens_gates * (dots - share)).astype(BF)
    d_ffn = d_ffn_sum[:, :model] + dot(d_logits, router_w, ((1,), (1,)))
    mine_cot_f = mine_cot.astype(F32)
    grad_gain_second = jnp.sum(d_ffn * unit_second, axis=0)
    d_unit = d_ffn * gain_second
    d_mixed = mine_cot_f + inv_second * (
        d_unit - unit_second * jnp.mean(d_unit * unit_second, axis=1, keepdims=True)
    )
    d_proj_mine = (d_mixed * inv_gated).astype(BF)
    d_inv = jnp.sum(d_mixed * proj, axis=1, keepdims=True)
    d_square = d_inv * -0.5 * inv_gated * inv_gated * inv_gated / DI
    d_square_high = d_square.astype(BF)
    d_square_low = (d_square - d_square_high.astype(F32)).astype(BF)
    sent = jnp.concatenate(
        [
            d_proj_mine,
            d_logits[:, :EXPERTS],
            d_square_high,
            d_square_low,
            jnp.zeros((quarter, LANES - EXPERTS - 2), BF),
        ],
        axis=1,
    )
    (got,) = gather_mp([sent], 5)
    got = got.reshape(tokens, model + LANES)
    d_proj = got[:, :model]
    d_logits_all = jnp.pad(got[:, model : model + EXPERTS], ((0, 0), (0, LANES - EXPERTS)))
    d_square_all = got[:, model + EXPERTS : model + EXPERTS + 1].astype(F32) + got[
        :, model + EXPERTS + 1 : model + EXPERTS + 2
    ].astype(F32)

    rows0 = ((0,), (0,))
    grad_b = weight_grads(
        [
            (d_proj, scaled),
            (ffn_block, d_shared_mid),
            (cotangent, shared_act),
            (ffn_block, d_logits_all),
        ]
    )
    grad_b, d_proj = lax.optimization_barrier((grad_b, d_proj))
    sum_b = lax.psum_scatter(grad_b, "dp", scatter_dimension=0, tiled=True).astype(F32)
    d_scaled = dot(d_proj, out_t)
    grad_gated_row = jnp.sum(d_scaled * gated, axis=0)
    d_gated = d_scaled * gated_row + 2.0 * gated * d_square_all
    d_ssd = d_gated * gate_act
    d_gate_z = d_gated * ssd * silu_slope(gate_z)

    direct = dot(d_ssd * dot(group_entry, expand, precision=HIGH), read, rows0, HIGH)
    state_grad = incoming_state(direct, group_decay, expand, True, 6)
    d_values, d_write, d_read, d_step, d_rated, d_skip_row = recur_backward(
        values,
        write,
        read,
        cumul,
        cumul_t,
        step_t,
        step,
        entry,
        tail_bare,
        seg_col,
        seg_row,
        expand,
        skip,
        kept,
        d_ssd,
        state_grad,
    )
    d_rate = jnp.sum(d_rated * step, axis=0, keepdims=True)
    d_dt = jnp.where(
        live, (d_step + rate * d_rated) * jax.nn.sigmoid(dt_lanes + head_pad[1:2]), 0.0
    )
    d_skip = dot(d_skip_row, expand, ((1,), (1,)), HIGH)
    grad_head = jnp.concatenate(
        [d_rate * rate, jnp.sum(d_dt, axis=0, keepdims=True), d_skip], axis=0
    )[:, :heads]

    slope = silu_slope(conv)
    d_conv_values = d_values * slope[:, :inner]
    d_state_act, rim_ahead = sum_and_edge(
        jnp.concatenate([d_write, d_read], axis=1), slope[:16, inner:], d_conv_values[:16], 11
    )
    d_conv = jnp.concatenate([d_conv_values, d_state_act * slope[:, inner:]], axis=1)
    d_conv_ext = jnp.concatenate([d_conv, rim_ahead], axis=0)
    seg_after = lax.dynamic_slice_in_dim(
        jnp.concatenate([segment_ids, jnp.full((taps - 1,), -1, jnp.int32)]),
        group_start,
        tokens + taps - 1,
    )
    d_pre = jnp.zeros_like(d_conv)
    grad_rows = []
    for k in range(taps):
        ahead = taps - 1 - k
        ok = (seg_after[ahead : ahead + tokens] == segments).astype(F32)[:, None]
        d_pre = d_pre + conv_taps[k][None] * d_conv_ext[ahead : ahead + tokens] * ok
        grad_rows.append(jnp.sum(d_conv * pre_ext[k : k + tokens] * same[k], axis=0))
    grad_rows.append(jnp.sum(d_conv, axis=0))
    d_a = jnp.concatenate([d_gate_z, d_pre, d_dt], axis=1).astype(BF)

    d_state_mine = lax.dynamic_slice_in_dim(
        d_a[:, 2 * inner : 2 * inner + state_cols], mp_place * quarter, quarter, 0
    )
    d_normed_part = dot(d_a[:, : 2 * inner], weight_a[:, : 2 * inner], ((1,), (1,))) + dot(
        d_a[:, 2 * inner + state_cols :], weight_a[:, 2 * inner + state_cols :], ((1,), (1,))
    )
    d_normed = scatter_mp(d_normed_part.astype(BF).reshape(4, quarter, model), 7)
    d_normed = d_normed + dot(
        d_state_mine, weight_a[:, 2 * inner : 2 * inner + state_cols], ((1,), (1,))
    )
    grad_a = dot(normed, d_a, rows0).astype(BF)
    inv_first = lax.rsqrt(jnp.mean(mine_hidden * mine_hidden, axis=1, keepdims=True) + EPS)
    unit_first = mine_hidden * inv_first
    grad_gain_first = jnp.sum(d_normed * unit_first, axis=0)
    d_first = d_normed * gain_first
    mine_grad_hidden = d_mixed + inv_first * (
        d_first - unit_first * jnp.mean(d_first * unit_first, axis=1, keepdims=True)
    )

    value_grads = jnp.stack([g[:inner] for g in grad_rows] + [grad_gated_row])
    value_grads = value_grads.reshape(taps + 2, heads, n, local_p).transpose(2, 0, 3, 1)
    state_grads = jnp.stack([g[inner:] for g in grad_rows])
    state_grads = state_grads.reshape(taps + 1, n, state_cols // n).transpose(1, 0, 2)
    misc_grads = [
        value_grads.reshape(n, -1),
        state_grads.reshape(n, -1),
        jnp.broadcast_to(grad_head.reshape(1, -1), (n, 3 * heads)),
        grad_gain_first.reshape(n, shard),
        grad_gain_second.reshape(n, shard),
    ]
    sizes = [g.shape[1] for g in misc_grads]
    misc_grads = jnp.concatenate(misc_grads, axis=1)
    misc_grads = jnp.pad(misc_grads, ((0, 0), (0, 32 * LANES - misc_grads.shape[1])))
    sum_a, misc_sum = scatter_dp(
        [grad_a.reshape(n, shard, -1), misc_grads.reshape(n, 32, LANES)], 8
    )
    misc_sum = misc_sum.reshape(-1)
    cut = [0]
    for size in sizes:
        cut.append(cut[-1] + size)
    value_sum = misc_sum[: cut[1]].reshape(taps + 2, local_p, heads)
    state_sum = misc_sum[cut[1] : cut[2]].reshape(taps + 1, state_cols // n)
    head_sum = misc_sum[cut[2] : cut[3]].reshape(3, heads)
    gains = jnp.pad(misc_sum[cut[3] : cut[5]], (0, 2 * model - 2 * shard)).reshape(-1, LANES)
    res_sum, gains = lax.optimization_barrier((res_sum, gains))
    mine_result = (mixed + res_sum.astype(F32)).astype(BF)
    hidden_all, result, gains_all = gather_mp([mine_grad_hidden.astype(BF), mine_result, gains], 9)
    result = result.reshape(tokens, model)
    gains_sum = jnp.sum(gains_all.reshape(4, -1)[:, : 2 * shard], axis=0)

    b1, b2 = inner, inner + 2 * hidden_units
    b3 = b2 + hidden_units
    return (
        result,
        hidden_all.reshape(tokens, model).astype(F32),
        gains_sum[:shard],
        sum_a[:, : 2 * inner].reshape(shard, 2, inner),
        sum_a[:, 2 * inner : 2 * inner + state_cols],
        sum_a[:, 2 * inner + state_cols : 2 * inner + state_cols + heads],
        value_sum[:taps],
        value_sum[taps],
        state_sum[:taps],
        state_sum[taps],
        head_sum,
        value_sum[taps + 1],
        sum_b[:, :b1].T,
        gains_sum[shard:],
        sum_b[:, b3 : b3 + EXPERTS],
        sum_b[:, b1:b2].reshape(shard, 2, hidden_units),
        sum_b[:, b2:b3].T,
        grad_expert_in,
        grad_expert_out,
    )


def solution(mesh):
    placed = (
        P("dp", None),
        P(),
        P("dp", None),
        P("dp"),
        P("dp", None, "mp"),
        P("dp", None),
        P("dp", "mp"),
        P(None, "dp", "mp"),
        P("dp", "mp"),
        P(None, "dp"),
        P("dp"),
        P(None, "mp"),
        P("dp", "mp"),
        P("mp", "dp"),
        P("dp"),
        P("dp", None),
        P("dp", None, "mp"),
        P("mp", "dp"),
        P("dp", None, None, "mp"),
        P("dp", "mp", None),
        P("dp", None),
    )
    return jax.shard_map(
        per_device,
        mesh=mesh,
        in_specs=placed,
        out_specs=(
            P("dp", None),
            P("dp", None),
            P("dp"),
            P("dp", None, "mp"),
            P("dp", None),
            P("dp", "mp"),
            P(None, "dp", "mp"),
            P("dp", "mp"),
            P(None, "dp"),
            P("dp"),
            P(None, "mp"),
            P("dp", "mp"),
            P("mp", "dp"),
            P("dp"),
            P("dp", None),
            P("dp", None, "mp"),
            P("mp", "dp"),
            P("dp", None, None, "mp"),
            P("dp", "mp", None),
        ),
        check_vma=False,
    )
```

```python
from functools import partial

import jax
import jax.numpy as jnp
from jax import lax
from jax.experimental import pallas as pl
from jax.experimental.pallas import tpu as pltpu
from jax.sharding import PartitionSpec as P

MESH = pl.DeviceIdType.MESH
BLK = 128
EXPERTS = 64
TOPK = 6
DI = 3072
CAP = 64
LANES = 128

EPS = 1e-05
HIGH = lax.Precision.HIGHEST
MASKED = -1e30
BF = jnp.bfloat16
F32 = jnp.float32
ANY = pl.BlockSpec(memory_space=pl.ANY)
VM = pl.BlockSpec(memory_space=pltpu.VMEM)


def dot(a, b, dims=((1,), (0,)), precision=None):
    return lax.dot_general(
        a, b, (dims, ((), ())), precision=precision, preferred_element_type=F32
    )


def silu_slope(argument):
    sigmoid_val = jax.nn.sigmoid(argument)
    return sigmoid_val * (1.0 + argument * (1.0 - sigmoid_val))


def half_rows(rows):
    return (rows // 32) * 16


def chunk_rows(start, size):
    return [(start + i, min(32, size - i)) for i in range(0, size, 32)]


def both_ways(rows):
    cut = half_rows(rows)
    ways = [chunk_rows(0, cut), chunk_rows(cut, rows - cut)]
    order = []
    for i in range(max(len(w) for w in ways)):
        for way in range(2):
            if i < len(ways[way]):
                order.append((way, i) + ways[way][i])
    return order


def ring_place(n, d):
    high, low = d // 2, d % 2
    return high * (1 - low) + (n - 1 - high) * low


def ring_device(n, p):
    back = p // (n // 2)
    return (2 * p) * (1 - back) + (2 * (n - 1 - p) + 1) * back


def greet(targets):
    barrier = pltpu.get_barrier_semaphore()
    for target in targets:
        pl.semaphore_signal(barrier, inc=1, device_id=target, device_id_type=MESH)
    pl.semaphore_wait(barrier, len(targets))


def remote(src, dst, send, recv, target):
    return pltpu.make_async_remote_copy(
        src_ref=src,
        dst_ref=dst,
        send_sem=send,
        recv_sem=recv,
        device_id=target,
        device_id_type=MESH,
    )


def mp_partners(m):
    return {"mp": m + 1 - 2 * (m % 2)}, {"mp": (m + 2) % 4}


def ring_neighbours(n):
    p = ring_place(n, lax.axis_index("dp"))
    nxt = {"dp": ring_device(n, (p + 1) % n)}
    prv = {"dp": ring_device(n, (p + n - 1) % n)}
    return p, nxt, prv


class RingGather:
    def __init__(self, n, ins, outs, sems):
        self.n, self.ins, self.outs = n, ins, outs
        self.local_sem, self.send_sem, self.recv_sem = sems
        self.p, self.nxt, self.prv = ring_neighbours(n)
        self.order = [both_ways(a.shape[0]) for a in ins]
        self.copies = {}

    @staticmethod
    def scratch(n, arrays):
        dma = pltpu.SemaphoreType.DMA
        most = max(len(both_ways(a.shape[0])) for a in arrays)
        shape = (n - 1, len(arrays), most)
        return [dma((len(arrays),)), dma(shape), dma(shape)]

    def begin(self):
        d = lax.axis_index("dp")
        self.local = []
        for j, (a, out) in enumerate(zip(self.ins, self.outs)):
            copy = pltpu.make_async_copy(a, out.at[d], self.local_sem.at[j])
            copy.start()
            self.local.append(copy)

    def step(self, s):
        n, p = self.n, self.p
        for j, (a, out) in enumerate(zip(self.ins, self.outs)):
            for k, (way, _, start, rows) in enumerate(self.order[j]):
                origin = ring_device(n, (p + n - s) % n if way == 0 else (p + s) % n)
                part = pl.ds(start, rows)
                if s > 0:
                    self.copies[s - 1, j, k].wait_recv()
                if s < n - 1:
                    copy = remote(
                        a.at[part] if s == 0 else out.at[origin, part],
                        out.at[origin, part],
                        self.send_sem.at[s, j, k],
                        self.recv_sem.at[s, j, k],
                        self.nxt if way == 0 else self.prv,
                    )
                    copy.start()
                    self.copies[s, j, k] = copy

    def end(self):
        for copy in self.copies.values():
            copy.wait_send()
        for copy in self.local:
            copy.wait()


def gather_kernel(n, k, *refs):
    ring = RingGather(n, refs[:k], refs[k : 2 * k], refs[2 * k :])
    greet([ring.nxt, ring.prv])
    ring.begin()
    for s in range(n):
        ring.step(s)
    ring.end()


def gather_dp(arrays, cid):
    n, k = lax.axis_size("dp"), len(arrays)
    return pl.pallas_call(
        partial(gather_kernel, n, k),
        out_shape=[jax.ShapeDtypeStruct((n,) + a.shape, a.dtype) for a in arrays],
        in_specs=[ANY] * k,
        out_specs=[ANY] * k,
        scratch_shapes=RingGather.scratch(n, arrays),
        compiler_params=pltpu.CompilerParams(collective_id=cid, has_side_effects=True),
    )(*arrays)


def add_rows(dst, pieces, rows, dtype):
    def body(i, carry):
        sl = pl.ds(pl.multiple_of(i * 16, 16), 16)
        total = pieces[0][sl, :].astype(F32)
        for piece in pieces[1:]:
            total = total + piece[sl, :].astype(F32)
        dst[sl, :] = total.astype(dtype)
        return carry

    lax.fori_loop(0, rows // 16, body, 0)


class RingScatter:
    def __init__(self, n, ins, outs, slots, sems):
        self.n, self.ins, self.outs, self.slots = n, ins, outs, slots
        self.send_sem, self.recv_sem = sems
        self.p, self.nxt, self.prv = ring_neighbours(n)
        self.copies = {}

    @staticmethod
    def scratch(n, arrays):
        most = max(len(both_ways(a.shape[1])) for a in arrays)
        shape = (n - 1, len(arrays), most)
        return [pltpu.VMEM((n - 1,) + a.shape[1:], a.dtype) for a in arrays] + [
            pltpu.SemaphoreType.DMA(shape),
            pltpu.SemaphoreType.DMA(shape),
        ]

    def step(self, s, j):
        n, p = self.n, self.p
        array, out, slots = self.ins[j], self.outs[j], self.slots[j]
        for i, (way, _, start, size) in enumerate(both_ways(array.shape[1])):
            block = ring_device(n, (p + 2 * n - 1 - s) % n if way == 0 else (p + 1 + s) % n)
            part = pl.ds(start, size)
            source = array.at[block, part]
            if s > 0:
                self.copies[s - 1, j, i].wait_recv()
                held = slots.at[s - 1, part]
                if s == n - 1:
                    add_rows(out.at[part], [held, source], size, F32)
                    continue
                add_rows(held, [held, source], size, array.dtype)
                source = held
            copy = remote(
                source,
                slots.at[s, part],
                self.send_sem.at[s, j, i],
                self.recv_sem.at[s, j, i],
                self.nxt if way == 0 else self.prv,
            )
            copy.start()
            self.copies[s, j, i] = copy

    def end(self):
        for copy in self.copies.values():
            copy.wait_send()


def last_kernel(
    n,
    grad_a,
    misc,
    gains,
    d_normed,
    extra,
    d_mixed,
    hidden,
    gain,
    result,
    out_a,
    out_misc,
    out_gains,
    all_hidden,
    all_result,
    gains_mine,
    gains_core,
    gains_chip,
    rows_core,
    rows_chip,
    rows_bf,
    slots_a,
    slots_misc,
    slots_gains,
    ring_send,
    ring_recv,
    mp_send,
    mp_recv,
    local_sem,
):
    m = lax.axis_index("mp")
    core, chip = mp_partners(m)
    far = (m + 2) % 4
    beside = m + 1 - 2 * (m % 2)
    ring = RingScatter(
        n,
        [grad_a, misc, gains_mine],
        [out_a, out_misc, out_gains],
        [slots_a, slots_misc, slots_gains],
        [ring_send, ring_recv],
    )
    greet([core, chip, ring.nxt, ring.prv])
    sent = []

    def over_mp(i, source, target, device):
        copy = remote(source, target, mp_send.at[i], mp_recv.at[i], device)
        copy.start()
        sent.append(copy)
        return copy

    ring.step(0, 0)
    ring.step(0, 1)
    gains_one = over_mp(0, gains, gains_core, core)
    rows_far = over_mp(1, d_normed.at[(beside + 2) % 4], rows_core.at[1], core)
    rows_near = over_mp(2, d_normed.at[beside], rows_core.at[0], core)
    own_result = pltpu.make_async_copy(result, all_result.at[m], local_sem.at[0])
    own_result.start()
    gains_one.wait_recv()
    for b in range(n):
        add_rows(gains_mine.at[b], [gains.at[b], gains_core.at[b]], 16, F32)
    gains_two = over_mp(3, gains_mine, gains_chip, chip)
    count = d_mixed.shape[0]
    rows_far.wait_recv()
    add_rows(rows_core.at[1], [rows_core.at[1], d_normed.at[far]], count, BF)
    rows_two = over_mp(4, rows_core.at[1], rows_chip, chip)
    result_chip = over_mp(5, result, all_result.at[m], chip)
    result_core = over_mp(6, result, all_result.at[m], core)
    gains_two.wait()
    for b in range(n):
        add_rows(gains_mine.at[b], [gains_mine.at[b], gains_chip.at[b]], 16, F32)
    ring.step(0, 2)
    for j in range(3):
        ring.step(1, j)
    rows_near.wait_recv()
    rows_two.wait_recv()

    def body(i, carry):
        sl = pl.ds(pl.multiple_of(i * 16, 16), 16)
        d_n = d_normed[m, sl, :].astype(F32) + rows_core[0, sl, :].astype(F32)
        d_n = d_n + rows_chip[sl, :].astype(F32) + extra[sl, :]
        x = hidden[sl, :].astype(F32)
        inv = lax.rsqrt(jnp.mean(x * x, axis=1, keepdims=True) + EPS)
        unit = x * inv
        d_unit = d_n * gain[...]
        mean = jnp.mean(d_unit * unit, axis=1, keepdims=True)
        rows_bf[sl, :] = (d_mixed[sl, :] + inv * (d_unit - unit * mean)).astype(BF)
        return carry

    lax.fori_loop(0, count // 16, body, 0)
    own_hidden = pltpu.make_async_copy(rows_bf, all_hidden.at[m], local_sem.at[1])
    own_hidden.start()
    hidden_chip = over_mp(7, rows_bf, all_hidden.at[m], chip)
    hidden_core = over_mp(8, rows_bf, all_hidden.at[m], core)
    arrive = []
    for s in range(2, n):
        for j in range(3):
            ring.step(s, j)
        if s == 4:
            result_chip.wait_recv()
            arrive.append(over_mp(9, all_result.at[far], all_result.at[far], core))
        if s == 6:
            hidden_chip.wait_recv()
            arrive.append(over_mp(10, all_hidden.at[far], all_hidden.at[far], core))
    for copy in [result_core, hidden_core] + arrive:
        copy.wait_recv()
    own_result.wait()
    own_hidden.wait()
    for copy in sent:
        if copy is not gains_two:
            copy.wait_send()
    ring.end()


def last_exchange(grad_a, misc, gains, d_normed, extra, d_mixed, hidden, gain, result, cid):
    n = lax.axis_size("dp")
    rows, model = d_mixed.shape
    dma = pltpu.SemaphoreType.DMA
    every = jax.ShapeDtypeStruct((4, rows, model), BF)
    return pl.pallas_call(
        partial(last_kernel, n),
        out_shape=[jax.ShapeDtypeStruct(a.shape[1:], F32) for a in (grad_a, misc, gains)] + [every, every],
        in_specs=[VM] * 8 + [ANY],
        out_specs=[VM] * 3 + [ANY] * 2,
        scratch_shapes=[
            pltpu.VMEM(gains.shape, F32),
            pltpu.VMEM(gains.shape, F32),
            pltpu.VMEM(gains.shape, F32),
            pltpu.VMEM((2, rows, model), BF),
            pltpu.VMEM((rows, model), BF),
            pltpu.VMEM((rows, model), BF),
        ]
        + RingScatter.scratch(n, [grad_a, misc, gains])
        + [dma((11,)), dma((11,)), dma((2,))],
        compiler_params=pltpu.CompilerParams(
            collective_id=cid, has_side_effects=True, vmem_limit_bytes=56 * 1024 * 1024
        ),
    )(grad_a, misc, gains, d_normed, extra, d_mixed, hidden, gain, result)


def mp_scatter_kernel(x, out, from_core, from_chip, send_sem, recv_sem):
    m = lax.axis_index("mp")
    core, chip = mp_partners(m)
    mine, far = m, (m + 2) % 4
    greet([core, chip])
    first = []
    for i in range(2):
        block = (m + 1 - 2 * (m % 2) + 2 * i) % 4
        copy = remote(x.at[block], from_core.at[i], send_sem.at[i], recv_sem.at[i], core)
        copy.start()
        first.append(copy)
    rows = out.shape[0]
    first[1].wait_recv()
    add_rows(from_core.at[1], [from_core.at[1], x.at[far]], rows, x.dtype)
    last = remote(from_core.at[1], from_chip, send_sem.at[2], recv_sem.at[2], chip)
    last.start()
    first[0].wait_recv()
    last.wait_recv()
    add_rows(out, [x.at[mine], from_core.at[0], from_chip], rows, F32)
    for copy in first + [last]:
        copy.wait_send()


def scatter_mp(x, cid):
    rows, cols = x.shape[1:]
    return pl.pallas_call(
        mp_scatter_kernel,
        out_shape=jax.ShapeDtypeStruct((rows, cols), F32),
        in_specs=[VM],
        out_specs=VM,
        scratch_shapes=[
            pltpu.VMEM((2, rows, cols), x.dtype),
            pltpu.VMEM((rows, cols), x.dtype),
            pltpu.SemaphoreType.DMA((3,)),
            pltpu.SemaphoreType.DMA((3,)),
        ],
        compiler_params=pltpu.CompilerParams(
            collective_id=cid, has_side_effects=True, vmem_limit_bytes=32 * 1024 * 1024
        ),
    )(x)


def mp_gather_kernel(k, *refs):
    ins, outs = refs[:k], refs[k : 2 * k]
    local_sem, send_sem, recv_sem = refs[2 * k :]
    m = lax.axis_index("mp")
    core, chip = mp_partners(m)
    far = (m + 2) % 4
    greet([core, chip])
    copies, local, arrive = [], [], []
    for j in range(k):
        to_chip = remote(ins[j], outs[j].at[m], send_sem.at[0, j], recv_sem.at[0, j], chip)
        to_chip.start()
        to_core = remote(ins[j], outs[j].at[m], send_sem.at[1, j], recv_sem.at[1, j], core)
        to_core.start()
        own = pltpu.make_async_copy(ins[j], outs[j].at[m], local_sem.at[j])
        own.start()
        copies += [to_chip, to_core]
        arrive.append(to_chip)
        local.append(own)
    onward = []
    for j in range(k):
        arrive[j].wait_recv()
        copy = remote(outs[j].at[far], outs[j].at[far], send_sem.at[2, j], recv_sem.at[2, j], core)
        copy.start()
        onward.append(copy)
    for j in range(k):
        copies[2 * j + 1].wait_recv()
        onward[j].wait_recv()
        local[j].wait()
    for copy in copies + onward:
        copy.wait_send()


def gather_mp(arrays, cid):
    k = len(arrays)
    return pl.pallas_call(
        partial(mp_gather_kernel, k),
        out_shape=[jax.ShapeDtypeStruct((4,) + a.shape, a.dtype) for a in arrays],
        in_specs=[ANY] * k,
        out_specs=[ANY] * k,
        scratch_shapes=[
            pltpu.SemaphoreType.DMA((k,)),
            pltpu.SemaphoreType.DMA((3, k)),
            pltpu.SemaphoreType.DMA((3, k)),
        ],
        compiler_params=pltpu.CompilerParams(collective_id=cid, has_side_effects=True),
    )(*arrays)


class TokenGather:
    def __init__(self, n, both, x, out, sems):
        self.n, self.both, self.x, self.out = n, both, x, out
        self.local, self.ring_s, self.ring_r, self.core_s, self.core_r, self.chip_s, self.chip_r = sems
        self.d, self.m = lax.axis_index("dp"), lax.axis_index("mp")
        self.far = (self.m + 2) % 4
        self.core, self.chip = mp_partners(self.m)
        self.p, self.nxt, self.prv = ring_neighbours(n)
        self.pieces = [(way, 0, start, rows) for way, _, start, rows in both_ways(x.shape[0])]
        self.pieces += [(way, 1, start, rows) for way, _, start, rows in both_ways(both)]
        self.sent, self.pending = [], []
        self.ring, self.chips = {}, {}

    @staticmethod
    def scratch(n, rows, both):
        dma = pltpu.SemaphoreType.DMA
        own, far = len(both_ways(rows)), len(both_ways(both))
        return [
            dma((3,)),
            dma((n - 1, own + far)),
            dma((n - 1, own + far)),
            dma((n, 2 * own + far)),
            dma((n, 2 * own + far)),
            dma((n, own)),
            dma((n, own)),
        ]

    def send(self, source, place, s_sem, r_sem, target):
        copy = remote(source, place, s_sem, r_sem, target)
        copy.start()
        self.sent.append(copy)
        return copy

    def begin(self):
        own = self.out.at[self.d, self.m]
        self.load = pltpu.make_async_copy(self.x, own, self.local.at[0])
        self.load.start()
        self.first = None
        if self.both:
            part = pl.ds(0, self.both)
            self.first = remote(
                self.x.at[part], own.at[part], self.local.at[1], self.local.at[2], self.chip
            )
            self.first.start()
            self.sent.append(self.first)

    def step(self, s):
        n, p = self.n, self.p
        for k, (way, is_far, start, rows) in enumerate(self.pieces):
            origin = ring_device(n, (p + n - s) % n if way == 0 else (p + s) % n)
            place = self.far if is_far else self.m
            region = self.out.at[origin, place, pl.ds(start, rows)]
            source = region if s > 0 or is_far else self.x.at[pl.ds(start, rows)]
            if s > 0:
                self.ring[s - 1, k].wait_recv()
            elif is_far and self.first is not None:
                self.first.wait_recv()
                self.first = None
            if s < n - 1:
                self.ring[s, k] = self.send(
                    source,
                    region,
                    self.ring_s.at[s, k],
                    self.ring_r.at[s, k],
                    self.nxt if way == 0 else self.prv,
                )
            self.pending.append(
                self.send(source, region, self.core_s.at[s, k], self.core_r.at[s, k], self.core)
            )
            if not is_far and start >= self.both:
                self.chips[s, k] = (
                    self.send(source, region, self.chip_s.at[s, k], self.chip_r.at[s, k], self.chip),
                    self.out.at[origin, self.far, pl.ds(start, rows)],
                )

    def pass_on(self, s):
        total = len(self.pieces)
        for k in range(total):
            if (s, k) in self.chips:
                copy, region = self.chips[s, k]
                copy.wait_recv()
                self.pending.append(
                    self.send(
                        region, region, self.core_s.at[s, total + k], self.core_r.at[s, total + k], self.core
                    )
                )

    def end(self):
        for copy in self.pending:
            copy.wait_recv()
        for copy in self.sent:
            copy.wait_send()
        self.load.wait()


def token_gather_kernel(n, both, x, out, *sems):
    gather = TokenGather(n, both, x, out, sems)
    greet([gather.core, gather.chip, gather.nxt, gather.prv])
    gather.begin()
    for s in range(n):
        gather.step(s)
        if s > 0:
            gather.pass_on(s - 1)
    gather.pass_on(n - 1)
    gather.end()


def gather_tokens(x, cid):
    n = lax.axis_size("dp")
    both = x.shape[0] // 2
    return pl.pallas_call(
        partial(token_gather_kernel, n, both),
        out_shape=jax.ShapeDtypeStruct((n, 4) + x.shape, x.dtype),
        in_specs=[ANY],
        out_specs=ANY,
        scratch_shapes=TokenGather.scratch(n, x.shape[0], both),
        compiler_params=pltpu.CompilerParams(collective_id=cid, has_side_effects=True),
    )(x)


def first_kernel(n, k, *refs):
    ins, x = refs[:k], refs[k]
    outs, x_out = refs[k + 1 : 2 * k + 1], refs[2 * k + 1]
    ring = RingGather(n, ins, outs, refs[2 * k + 2 : 2 * k + 5])
    gather = TokenGather(n, 0, x, x_out, refs[2 * k + 5 :])
    greet([gather.core, gather.chip, gather.nxt, gather.prv])
    ring.begin()
    gather.begin()
    for s in range(n):
        gather.step(s)
        ring.step(s)
        if s > 1:
            gather.pass_on(s - 2)
    gather.pass_on(n - 2)
    gather.pass_on(n - 1)
    gather.end()
    ring.end()


def first_gather(arrays, x, cid):
    n, k = lax.axis_size("dp"), len(arrays)
    return pl.pallas_call(
        partial(first_kernel, n, k),
        out_shape=[jax.ShapeDtypeStruct((n,) + a.shape, a.dtype) for a in arrays]
        + [jax.ShapeDtypeStruct((n, 4) + x.shape, x.dtype)],
        in_specs=[ANY] * (k + 1),
        out_specs=[ANY] * (k + 1),
        scratch_shapes=RingGather.scratch(n, arrays) + TokenGather.scratch(n, x.shape[0], 0),
        compiler_params=pltpu.CompilerParams(collective_id=cid, has_side_effects=True),
    )(*arrays, x)


def token_scatter_kernel(
    n,
    x,
    out,
    from_core,
    slots,
    loads,
    far_loads,
    from_chip,
    to_chip,
    first,
    done,
    last_buf,
    load_sem,
    far_sem,
    core_send,
    core_recv,
    chip_send,
    chip_recv,
    send_sem,
    recv_sem,
):
    m = lax.axis_index("mp")
    c, y = m % 2, m // 2
    core, chip = mp_partners(m)
    p, nxt, prv = ring_neighbours(n)
    rows = out.shape[0]
    half, part = rows // 2, rows // 4
    greet([core, chip, nxt, prv])

    def block_at(s, way):
        return ring_device(n, (p + 2 * n - 1 - s) % n if way == 0 else (p + 1 + s) % n)

    parts = [
        (0, 0, 0, half, 0),
        (1, 0, half, half, 0),
        (0, 1, 0, part, half),
        (1, 1, part, part, half),
        (1, 1, half, half, None),
    ]
    over, sent, loading = {}, [], {}

    def core_sends(s):
        for k in (4, 0, 1, 2, 3):
            way, is_far, start, size, _ = parts[k]
            block, y_piece = block_at(s, way), (y + is_far) % 2
            copy = remote(
                x.at[block, (m + 1 - 2 * c + 2 * is_far) % 4, pl.ds(start, size)],
                from_core.at[block, y_piece, pl.ds(start, size)],
                core_send.at[s, k],
                core_recv.at[s, k],
                core,
            )
            copy.start()
            over[s, k] = copy
            sent.append(copy)

    def load(s, k):
        way, is_far, start, size, at = parts[k]
        block = block_at(s, way)
        over[s, k].wait_recv()
        sources = (
            x.at[block, (m + 2 * is_far) % 4, pl.ds(start, size)],
            from_core.at[block, (y + is_far) % 2, pl.ds(start, size)],
        )
        loading[s, k] = []
        for i, source in enumerate(sources):
            if k == 4:
                copy = pltpu.make_async_copy(source, far_loads.at[s % 2, i], far_sem.at[s % 2, i])
            else:
                copy = pltpu.make_async_copy(
                    source, loads.at[s % 2, way, i, pl.ds(at, size)], load_sem.at[s % 2, k, i]
                )
            copy.start()
            loading[s, k].append(copy)

    chips = {}

    def to_other_chip(s):
        for copy in loading[s, 4]:
            copy.wait()
        if s > 1:
            chips[s - 2].wait_send()
        add_rows(to_chip.at[s % 2], [far_loads.at[s % 2, 0], far_loads.at[s % 2, 1]], half, BF)
        copy = remote(to_chip.at[s % 2], from_chip.at[s], chip_send.at[s], chip_recv.at[s], chip)
        copy.start()
        chips[s] = copy

    core_sends(0)
    core_sends(1)
    load(0, 4)
    for k in range(4):
        load(0, k)
    load(1, 4)
    to_other_chip(0)
    to_other_chip(1)
    core_sends(2)
    for k in range(4):
        load(1, k)
    load(2, 4)
    ring = {}
    tiles = [(way, at, size) for way, _, at, size in both_ways(2 * (half + part))]
    tiles = [(way, at - way * (half + part), size) for way, at, size in tiles]
    for s in range(n):
        for k in range(4):
            for copy in loading[s, k]:
                copy.wait()
        for k, (way, at, size) in enumerate(tiles):
            area = pl.ds(at, size)
            pieces = [loads.at[s % 2, way, 0, area], loads.at[s % 2, way, 1, area]]
            if s == 0:
                target = first.at[way, area]
            else:
                ring[s - 1, k].wait_recv()
                held = slots.at[way, s - 1, area]
                target = held if s < n - 1 else done.at[way, area]
                pieces.append(held)
            if way == 1 and at < half:
                if at == 0:
                    chips[s].wait_recv()
                pieces.append(from_chip.at[s, area])
            add_rows(target, pieces, size, BF)
            if s < n - 1:
                copy = remote(
                    target,
                    slots.at[way, s, area],
                    send_sem.at[s, k],
                    recv_sem.at[s, k],
                    nxt if way == 0 else prv,
                )
                copy.start()
                ring[s, k] = copy
        if s + 2 < n:
            to_other_chip(s + 2)
            for k in range(4):
                load(s + 2, k)
        if s + 3 < n:
            core_sends(s + 3)
            load(s + 3, 4)
    last = []
    for way in range(2):
        copy = remote(
            done.at[way, pl.ds(half, part)],
            last_buf.at[pl.ds(way * part, part)],
            send_sem.at[n - 1, way],
            recv_sem.at[n - 1, way],
            chip,
        )
        copy.start()
        last.append(copy)
    add_rows(out.at[pl.ds(half, half)], [done.at[1, pl.ds(0, half)]], half, F32)
    for copy in last:
        copy.wait_recv()
    add_rows(out.at[pl.ds(0, half)], [done.at[0, pl.ds(0, half)], last_buf], half, F32)
    for copy in sent + list(ring.values()) + last + [chips[n - 2], chips[n - 1]]:
        copy.wait_send()


def scatter_tokens(x, cid):
    n, _, rows, cols = x.shape
    half, part = rows // 2, rows // 4
    dma = pltpu.SemaphoreType.DMA
    out, _ = pl.pallas_call(
        partial(token_scatter_kernel, n),
        out_shape=[
            jax.ShapeDtypeStruct((rows, cols), F32),
            jax.ShapeDtypeStruct((n, 2, rows, cols), BF),
        ],
        in_specs=[ANY],
        out_specs=[VM, ANY],
        scratch_shapes=[
            pltpu.VMEM((2, n - 1, half + part, cols), BF),
            pltpu.VMEM((2, 2, 2, half + part, cols), BF),
            pltpu.VMEM((2, 2, half, cols), BF),
            pltpu.VMEM((n, half, cols), BF),
            pltpu.VMEM((2, half, cols), BF),
            pltpu.VMEM((2, half + part, cols), BF),
            pltpu.VMEM((2, half + part, cols), BF),
            pltpu.VMEM((half, cols), BF),
            dma((2, 4, 2)),
            dma((2, 2)),
            dma((n, 5)),
            dma((n, 5)),
            dma((n,)),
            dma((n,)),
            dma((n, 6)),
            dma((n, 6)),
        ],
        compiler_params=pltpu.CompilerParams(
            collective_id=cid, has_side_effects=True, vmem_limit_bytes=56 * 1024 * 1024
        ),
    )(x)
    return out


def edge_kernel(n, part, slope, rim, total, ahead, mine, from_core, from_chip, edge, send_sem, recv_sem):
    d, m = lax.axis_index("dp"), lax.axis_index("mp")
    core, chip = mp_partners(m)
    before, after = {"dp": (d + n - 1) % n}, {"dp": (d + 1) % n}
    rows, cols = part.shape
    edge_rows, rim_cols = rim.shape
    greet([core, chip, before, after])

    def add(dst, pieces, dtype):
        add_rows(dst, pieces, rows, dtype)

    one = remote(part, from_core, send_sem.at[0], recv_sem.at[0], core)
    one.start()
    one.wait()
    add(mine, [part, from_core], BF)
    two = remote(mine, from_chip, send_sem.at[1], recv_sem.at[1], chip)
    two.start()
    two.wait_recv()
    add(total, [mine, from_chip], F32)
    edge[:, 0:rim_cols] = rim[...]
    edge[:, rim_cols : rim_cols + cols] = total[0:edge_rows, :] * slope[...]
    three = remote(edge, ahead, send_sem.at[2], recv_sem.at[2], before)

    @pl.when(d > 0)
    def _():
        three.start()

    @pl.when(d == n - 1)
    def _():
        ahead[...] = jnp.zeros_like(ahead)

    @pl.when(d < n - 1)
    def _():
        three.wait_recv()

    @pl.when(d > 0)
    def _():
        three.wait_send()

    two.wait_send()


def sum_and_edge(part, slope, rim, cid):
    rows, cols = part.shape
    edge_shape = (rim.shape[0], rim.shape[1] + cols)
    return pl.pallas_call(
        partial(edge_kernel, lax.axis_size("dp")),
        out_shape=[
            jax.ShapeDtypeStruct(part.shape, F32),
            jax.ShapeDtypeStruct(edge_shape, F32),
        ],
        in_specs=[VM] * 3,
        out_specs=[VM] * 2,
        scratch_shapes=[
            pltpu.VMEM((rows, cols), BF),
            pltpu.VMEM((rows, cols), F32),
            pltpu.VMEM((rows, cols), BF),
            pltpu.VMEM(edge_shape, F32),
            pltpu.SemaphoreType.DMA((3,)),
            pltpu.SemaphoreType.DMA((3,)),
        ],
        compiler_params=pltpu.CompilerParams(
            collective_id=cid, has_side_effects=True, vmem_limit_bytes=32 * 1024 * 1024
        ),
    )(part, slope, rim)


def head_pair(pair, first, second):
    lane = lax.broadcasted_iota(jnp.int32, first.shape, 1)
    return jnp.where(lane < LANES // 2, first, second)


def visible_pairs(seg_col, seg_row):
    length = seg_col.shape[0]
    row = lax.broadcasted_iota(jnp.int32, (length, length), 0)
    col = lax.broadcasted_iota(jnp.int32, (length, length), 1)
    return (row >= col) & (seg_col == seg_row)


def state_decay(entry, expand):
    last = entry[entry.shape[0] - 1 :, :]
    spread = jnp.broadcast_to(last, (LANES, LANES)).T
    return dot(expand, spread, ((0,), (0,)), HIGH)


def recur_kernel(
    pairs,
    values,
    write,
    read,
    cumul,
    cumul_t,
    step_t,
    entry,
    tail,
    seg_col,
    seg_row,
    expand,
    skip,
    start,
    out,
    kept,
    state,
):
    @pl.when(pl.program_id(0) == 0)
    def _():
        state[...] = start[...]

    held = state[...]
    kept[0] = held
    v, b, c = values[...], write[...], read[...]
    scores = dot(c, b, ((1,), (1,)), HIGH)
    visible = visible_pairs(seg_col[...], seg_row[...])
    entry_full = dot(entry[...], expand[...], precision=HIGH)
    tail_full = dot(tail[...], expand[...], precision=HIGH)
    carried = entry_full * dot(c, held, ((1,), (1,)), HIGH) + skip[...] * v
    cum, cum_t, st_t = cumul[...], cumul_t[...], step_t[...]
    for pair in range(pairs):
        cols = slice(pair * LANES, (pair + 1) * LANES)
        v2 = v[:, cols]
        found = []
        for h in (2 * pair, 2 * pair + 1):
            spread = jnp.where(visible, cum[:, h : h + 1] - cum_t[h : h + 1, :], MASKED)
            mixing = jnp.exp(spread) * (scores * st_t[h : h + 1, :])
            found.append(dot(mixing, v2, precision=HIGH))
        out[:, cols] = head_pair(pair, found[0], found[1]) + carried[:, cols]
    state[...] = state_decay(entry[...], expand[...]) * held + dot(v * tail_full, b, ((0,), (0,)), HIGH)


def recur_specs(width, lengths):
    def rows(cols):
        return pl.BlockSpec((BLK, cols), lambda i: (lengths(i), 0))

    def flat(count):
        return pl.BlockSpec((count, BLK), lambda i: (0, lengths(i)))

    def whole(shape):
        return pl.BlockSpec(shape, lambda i: (0,) * len(shape))

    return rows, flat, whole


def recur_forward(v, b, c, cumul, cumul_t, step_t, entry, tail, seg_col, seg_row, expand, skip, start):
    total, width = v.shape
    blocks = total // BLK
    rows, flat, whole = recur_specs(width, lambda i: i)
    return pl.pallas_call(
        partial(recur_kernel, width // LANES),
        grid=(blocks,),
        out_shape=[
            jax.ShapeDtypeStruct((total, width), F32),
            jax.ShapeDtypeStruct((blocks, width, LANES), F32),
        ],
        in_specs=[
            rows(width),
            rows(LANES),
            rows(LANES),
            rows(LANES),
            flat(16),
            flat(16),
            rows(LANES),
            rows(LANES),
            rows(1),
            flat(1),
            whole((LANES, width)),
            whole((1, width)),
            whole((width, LANES)),
        ],
        out_specs=[
            rows(width),
            pl.BlockSpec((1, width, LANES), lambda i: (i, 0, 0)),
        ],
        scratch_shapes=[pltpu.VMEM((width, LANES), F32)],
        compiler_params=pltpu.CompilerParams(vmem_limit_bytes=48 * 1024 * 1024),
    )(v, b, c, cumul, cumul_t, step_t, entry, tail, seg_col, seg_row, expand, skip, start)


def adjoint_kernel(
    pairs,
    values,
    write,
    read,
    cumul,
    cumul_t,
    step_t,
    step,
    entry,
    tail_bare,
    seg_col,
    seg_row,
    expand,
    skip,
    kept,
    d_out,
    start,
    d_values,
    d_write,
    d_read,
    d_step,
    d_rate_step,
    d_skip,
    state,
    columns,
):
    @pl.when(pl.program_id(0) == 0)
    def _():
        state[...] = start[...]
        d_skip[...] = jnp.zeros_like(d_skip)
        columns[...] = jnp.zeros_like(columns)

    length = values.shape[0]
    lam, held = state[...], kept[0]
    v, b, c, dy = values[...], write[...], read[...], d_out[...]
    ex = expand[...]
    st = step[...]
    scores = dot(c, b, ((1,), (1,)), HIGH)
    visible = visible_pairs(seg_col[...], seg_row[...])
    entry_full = dot(entry[...], ex, precision=HIGH)
    tail = tail_bare[...] * st
    tail_full = dot(tail, ex, precision=HIGH)
    c_state = dot(c, held, ((1,), (1,)), HIGH)
    b_lam = dot(b, lam, ((1,), (1,)), HIGH)
    dy_in = dy * entry_full
    v_out = v * tail_full
    dc = dot(dy_in, held, precision=HIGH)
    db = dot(v_out, lam, precision=HIGH)
    reach = dot(dy_in * c_state, ex, ((1,), (1,)), HIGH)
    leave = dot(v * b_lam, ex, ((1,), (1,)), HIGH)
    d_skip[...] += jnp.sum(dy * v, axis=0, keepdims=True)
    dv_far = tail_full * b_lam + skip[...] * dy
    cum, cum_t, st_t = cumul[...], cumul_t[...], step_t[...]
    lane = lax.broadcasted_iota(jnp.int32, (length, LANES), 1)
    d_scores = jnp.zeros((length, length), F32)
    row_sums = jnp.zeros((length, LANES), F32)
    for pair in range(pairs):
        cols = slice(pair * LANES, (pair + 1) * LANES)
        v2, dy2 = v[:, cols], dy[:, cols]
        found = []
        for j in range(2):
            h = 2 * pair + j
            own = (lane < LANES // 2) if j == 0 else (lane >= LANES // 2)
            d_mix = dot(jnp.where(own, dy2, 0.0), v2, ((1,), (1,)), HIGH)
            spread = jnp.where(visible, cum[:, h : h + 1] - cum_t[h : h + 1, :], MASKED)
            decay = jnp.exp(spread)
            decay_step = decay * st_t[h : h + 1, :]
            weighted = d_mix * scores * decay
            d_scores = d_scores + d_mix * decay_step
            columns[h : h + 1, :] = jnp.sum(weighted, axis=0, keepdims=True)
            per_row = jnp.sum(weighted * st_t[h : h + 1, :], axis=1, keepdims=True)
            row_sums = jnp.where(lane == h, per_row, row_sums)
            found.append(dot(scores * decay_step, dy2, ((0,), (0,))))
        d_values[:, cols] = head_pair(pair, found[0], found[1]) + dv_far[:, cols]
    d_read[...] = dc + dot(d_scores, b, precision=HIGH)
    d_write[...] = db + dot(d_scores, c, ((0,), (0,)), HIGH)
    col_sums = columns[...].T
    leave_step = tail * leave
    d_step[...] = col_sums + tail_bare[...] * leave
    d_cum = row_sums - st * col_sums + reach - leave_step
    row = lax.broadcasted_iota(jnp.int32, (length, length), 0)
    col = lax.broadcasted_iota(jnp.int32, (length, length), 1)
    upper = (col >= row).astype(F32)
    met = jnp.sum(dot(lam * held, ex, ((0,), (1,)), HIGH), axis=0, keepdims=True)
    at_end = jnp.sum(leave_step, axis=0, keepdims=True) + entry[length - 1 :, :] * met
    d_rate_step[...] = dot(upper, d_cum, precision=HIGH) + at_end
    state[...] = state_decay(entry[...], ex) * lam + dot(dy_in, c, ((0,), (0,)), HIGH)


def recur_backward(
    v, b, c, cumul, cumul_t, step_t, step, entry, tail_bare, seg_col, seg_row, expand, skip, kept, dy, start
):
    total, width = v.shape
    blocks = total // BLK
    rows, flat, whole = recur_specs(width, lambda i: blocks - 1 - i)
    return pl.pallas_call(
        partial(adjoint_kernel, width // LANES),
        grid=(blocks,),
        out_shape=[
            jax.ShapeDtypeStruct((total, width), F32),
            jax.ShapeDtypeStruct((total, LANES), F32),
            jax.ShapeDtypeStruct((total, LANES), F32),
            jax.ShapeDtypeStruct((total, LANES), F32),
            jax.ShapeDtypeStruct((total, LANES), F32),
            jax.ShapeDtypeStruct((1, width), F32),
        ],
        in_specs=[
            rows(width),
            rows(LANES),
            rows(LANES),
            rows(LANES),
            flat(16),
            flat(16),
            rows(LANES),
            rows(LANES),
            rows(LANES),
            rows(1),
            flat(1),
            whole((LANES, width)),
            whole((1, width)),
            pl.BlockSpec((1, width, LANES), lambda i: (blocks - 1 - i, 0, 0)),
            rows(width),
            whole((width, LANES)),
        ],
        out_specs=[
            rows(width),
            rows(LANES),
            rows(LANES),
            rows(LANES),
            rows(LANES),
            whole((1, width)),
        ],
        scratch_shapes=[pltpu.VMEM((width, LANES), F32), pltpu.VMEM((LANES, LANES), F32)],
        compiler_params=pltpu.CompilerParams(vmem_limit_bytes=48 * 1024 * 1024),
    )(v, b, c, cumul, cumul_t, step_t, step, entry, tail_bare, seg_col, seg_row, expand, skip, kept, dy, start)


def state_scan_kernel(
    n,
    reverse,
    mine,
    decay,
    expand,
    out,
    first,
    second,
    got_first,
    got_second,
    half,
    got_half,
    send_sem,
    recv_sem,
):
    d = lax.axis_index("dp")
    q = n - 1 - d if reverse else d
    zq, xq = q // 2, q % 2
    depth = n // 2
    rows = mine.shape[0] // 2
    xf = xq.astype(F32)
    sent_type = first.dtype

    def device(logical):
        return {"dp": n - 1 - logical if reverse else logical}

    beside = device(2 * zq + 1 - xq)
    others = [device(2 * ((zq + k) % depth) + xq) for k in range(1, depth)]
    own_rows = pl.ds(pl.multiple_of(rows * xq, 16), rows)
    other_rows = pl.ds(pl.multiple_of(rows * (1 - xq), 16), rows)
    own_lanes = pl.ds(pl.multiple_of(rows * xq, LANES), rows)
    tail = pl.ds(rows, 16)
    body = pl.ds(0, rows)
    row = lax.broadcasted_iota(jnp.int32, (16, LANES), 0)

    def spread(values):
        square = jnp.broadcast_to(values, (LANES, LANES)).T
        return dot(expand[:, own_lanes], square, ((0,), (0,)), HIGH)

    def two_terms(values):
        high = values.astype(sent_type).astype(F32)
        wide = jnp.where(row == 0, high, jnp.where(row == 1, values - high, 0.0))
        return wide.astype(sent_type)

    def one_term(block):
        return block[0:1, :].astype(F32) + block[1:2, :].astype(F32)

    for k in range(1, depth):

        @pl.when(zq < k)
        def _():
            got_second[k - 1] = jnp.zeros(got_second.shape[1:], sent_type)

    own_decay = decay[0:1, :]
    first[body, :] = mine[other_rows, :].astype(sent_type)
    first[tail, :] = two_terms(own_decay)
    greet([beside] + others)
    one = remote(first, got_first, send_sem.at[0], recv_sem.at[0], beside)
    one.start()
    one.wait_recv()
    own = mine[own_rows, :]
    got, got_decay = got_first[body, :].astype(F32), one_term(got_first[tail, :])
    early = own * (1.0 - xf) + got * xf
    early_decay = own_decay * (1.0 - xf) + got_decay * xf
    late = own * xf + got * (1.0 - xf)
    late_decay = own_decay * xf + got_decay * (1.0 - xf)
    second[body, :] = (spread(late_decay) * early + late).astype(sent_type)
    second[tail, :] = two_terms(early_decay * late_decay)
    sent = []
    for k in range(1, depth):
        copy = remote(
            second, got_second.at[k - 1], send_sem.at[k], recv_sem.at[k], device(2 * ((zq + k) % depth) + xq)
        )
        sent.append(copy)

        @pl.when(zq + k < depth)
        def _():
            copy.start()

    early_spread = spread(early_decay)
    total = jnp.zeros((rows, LANES), F32)
    for k in range(depth - 1, 0, -1):

        @pl.when(zq >= k)
        def _():
            sent[k - 1].wait_recv()

        got_k = got_second.at[k - 1]
        total = spread(one_term(got_k[tail, :])) * total + got_k[body, :].astype(F32)
    after = early_spread * total + early
    half[...] = (total * xf + after * (1.0 - xf)).astype(sent_type)
    last = remote(half, got_half, send_sem.at[depth], recv_sem.at[depth], beside)
    last.start()
    out[own_rows, :] = total * (1.0 - xf) + after * xf
    last.wait_recv()
    out[other_rows, :] = got_half[...].astype(F32)
    one.wait_send()
    last.wait_send()
    for k in range(1, depth):

        @pl.when(zq + k < depth)
        def _():
            sent[k - 1].wait_send()


def state_scan(mine, decay, expand, reverse, cid, sent_type):
    n = lax.axis_size("dp")
    half = mine.shape[0] // 2
    depth = n // 2
    message = (half + 16, LANES)
    return pl.pallas_call(
        partial(state_scan_kernel, n, reverse),
        out_shape=jax.ShapeDtypeStruct(mine.shape, F32),
        in_specs=[VM] * 3,
        out_specs=VM,
        scratch_shapes=[
            pltpu.VMEM(message, sent_type),
            pltpu.VMEM(message, sent_type),
            pltpu.VMEM(message, sent_type),
            pltpu.VMEM((depth - 1,) + message, sent_type),
            pltpu.VMEM((half, LANES), sent_type),
            pltpu.VMEM((half, LANES), sent_type),
            pltpu.SemaphoreType.DMA((depth + 1,)),
            pltpu.SemaphoreType.DMA((depth + 1,)),
        ],
        compiler_params=pltpu.CompilerParams(
            collective_id=cid, has_side_effects=True, vmem_limit_bytes=32 * 1024 * 1024
        ),
    )(mine, decay, expand)


def pick_matrix(position, own):
    length = position.shape[1]
    slot = lax.broadcasted_iota(jnp.int32, (CAP, length), 0).astype(F32)
    parts = [
        jnp.where(position[e : e + 1, :] == slot, 1.0, 0.0).astype(BF) for e in range(own)
    ]
    return jnp.concatenate(parts, axis=0)


def pick_kernel(own, x, position, out):
    pick = pick_matrix(position[0], own)
    picked = dot(pick, x[0]).astype(BF)
    out[...] = picked.reshape(out.shape)


def pick_gate_kernel(own, x, position, routes, router, out, gates, slot_gates):
    rows = x[0]
    pick = pick_matrix(position[0], own)
    picked = dot(pick, rows).astype(BF)
    out[...] = picked.reshape(out.shape)
    logits = dot(rows, router[...])
    lane = lax.broadcasted_iota(jnp.int32, logits.shape, 1).astype(F32)
    named = routes[0][:, 0:1] == lane
    for k in range(1, TOPK):
        named = named | (routes[0][:, k : k + 1] == lane)
    top = jnp.max(jnp.where(named, logits, MASKED), axis=1, keepdims=True)
    powers = jnp.where(named, jnp.exp(jnp.minimum(logits - top, 0.0)), 0.0)
    gate = powers / jnp.sum(powers, axis=1, keepdims=True)
    gates[0] = gate
    high = gate.astype(BF)
    low = (gate - high.astype(F32)).astype(BF)
    of_slot = dot(pick, high) + dot(pick, low)
    row = lax.broadcasted_iota(jnp.int32, of_slot.shape, 0)
    col = lax.broadcasted_iota(jnp.int32, of_slot.shape, 1)
    mine = col - lax.axis_index("dp") * own == row // CAP
    of_slot = jnp.sum(jnp.where(mine, of_slot, 0.0), axis=1, keepdims=True)
    slot_gates[...] = jnp.broadcast_to(of_slot, pick.shape[:1] + (LANES,)).reshape(slot_gates.shape)


def slot_spec(own, cols):
    return pl.BlockSpec((own, 1, CAP, cols), lambda s: (0, s, 0, 0))


def token_spec(rows, cols):
    return pl.BlockSpec((1, rows, cols), lambda s: (s, 0, 0))


BIG = pltpu.CompilerParams(vmem_limit_bytes=56 * 1024 * 1024)


def pick_rows(x, position):
    n, tokens, model = x.shape
    own = position.shape[1]
    return pl.pallas_call(
        partial(pick_kernel, own),
        grid=(n,),
        out_shape=jax.ShapeDtypeStruct((own, n, CAP, model), BF),
        in_specs=[token_spec(tokens, model), token_spec(own, tokens)],
        out_specs=slot_spec(own, model),
        compiler_params=BIG,
    )(x, position)


def pick_rows_gates(x, position, routes, router):
    n, tokens, model = x.shape
    own = position.shape[1]
    return pl.pallas_call(
        partial(pick_gate_kernel, own),
        grid=(n,),
        out_shape=[
            jax.ShapeDtypeStruct((own, n, CAP, model), BF),
            jax.ShapeDtypeStruct((n, tokens, LANES), F32),
            jax.ShapeDtypeStruct((own, n, CAP, LANES), F32),
        ],
        in_specs=[
            token_spec(tokens, model),
            token_spec(own, tokens),
            token_spec(tokens, TOPK),
            pl.BlockSpec((model, LANES), lambda s: (0, 0)),
        ],
        out_specs=[slot_spec(own, model), token_spec(tokens, LANES), slot_spec(own, LANES)],
        compiler_params=BIG,
    )(x, position, routes, router)


def expert_kernel(
    own, rows, cot_rows, gate, w_in, w_out, grad_in, grad_out, d_rows, res, dots, wide, both
):
    e, part = pl.program_id(0), pl.program_id(1)
    model = rows.shape[2]
    units = w_out.shape[1]

    @pl.when(part == 0)
    def _():
        wide[...] = w_in[0].astype(F32)
        both[:, 0:units] = wide[pl.ds(0, model, stride=2), :].astype(BF)
        both[:, units : 2 * units] = wide[pl.ds(1, model, stride=2), :].astype(BF)
        grad_in[...] = jnp.zeros_like(grad_in)
        grad_out[...] = jnp.zeros_like(grad_out)

    x, c, g = rows[0], cot_rows[0], gate[0]
    mid = dot(x, both[...])
    mid_gate, mid_up = mid[:, 0:units], mid[:, units : 2 * units]
    sig = jax.nn.sigmoid(mid_gate)
    mid_silu = mid_gate * sig
    act = (mid_silu * mid_up).astype(BF).astype(F32)
    back = dot(c, w_out[0], ((1,), (1,)))
    dot_sum = jnp.sum(act * back, axis=1, keepdims=True)
    lane = lax.broadcasted_iota(jnp.int32, g.shape, 1)
    dots[0] = jnp.where(lane == lax.axis_index("dp") * own + e, dot_sum, 0.0).astype(BF)
    gated = (act * g).astype(BF)
    d_act = back * g
    d_gate = (d_act * mid_up * (sig * (1.0 + mid_gate * (1.0 - sig)))).astype(BF)
    d_mid = jnp.concatenate([d_gate, (d_act * mid_silu).astype(BF)], axis=1)
    grads = dot(x, d_mid, ((0,), (0,)))
    grad_in[0, pl.ds(0, model, stride=2), :] += grads[:, 0:units]
    grad_in[0, pl.ds(1, model, stride=2), :] += grads[:, units : 2 * units]
    grad_out[0] += dot(gated, c, ((0,), (0,)))
    d_rows[0] = dot(d_mid, both[...], ((1,), (1,))).astype(BF)
    res[0] = dot(gated, w_out[0]).astype(BF)


def run_experts(rows, cot_rows, gate, w_in, w_out):
    own, slots, model = rows.shape
    units = w_out.shape[1]
    part = min(slots, 512)

    def slot(cols):
        return pl.BlockSpec((1, part, cols), lambda e, j: (e, j, 0))

    def weight(a, b):
        return pl.BlockSpec((1, a, b), lambda e, j: (e, 0, 0))

    return pl.pallas_call(
        partial(expert_kernel, own),
        grid=(own, slots // part),
        out_shape=[
            jax.ShapeDtypeStruct((own, 2 * model, units), F32),
            jax.ShapeDtypeStruct((own, units, model), F32),
            jax.ShapeDtypeStruct((own, slots, model), BF),
            jax.ShapeDtypeStruct((own, slots, model), BF),
            jax.ShapeDtypeStruct((own, slots, LANES), BF),
        ],
        in_specs=[slot(model), slot(model), slot(LANES), weight(2 * model, units), weight(units, model)],
        out_specs=[weight(2 * model, units), weight(units, model), slot(model), slot(model), slot(LANES)],
        scratch_shapes=[pltpu.VMEM((2 * model, units), F32), pltpu.VMEM((model, 2 * units), BF)],
        compiler_params=BIG,
    )(rows, cot_rows, gate, w_in, w_out)


def put_matrix(position, own):
    length = position.shape[0]
    lane = lax.broadcasted_iota(jnp.int32, (length, LANES), 1)
    slot = (lane % CAP).astype(F32)
    parts = []
    for e in range(0, own, 2):
        held = jnp.where(lane < CAP, position[:, e : e + 1], position[:, e + 1 : e + 2])
        parts.append(jnp.where(held == slot, 1.0, 0.0).astype(BF))
    return jnp.concatenate(parts, axis=1)


def put_kernel(own, position, rows, shared, *rest):
    extra, out = (rest[0], rest[1]) if len(rest) == 2 else (None, rest[0])
    model = shared.shape[1]
    put = put_matrix(position[0], own)
    total = dot(put, rows[...].reshape(own * CAP, model))
    here = jnp.where(pl.program_id(0) == lax.axis_index("dp"), 1.0, 0.0)
    out[0, :, 0:model] = (total + here * shared[...]).astype(BF)
    if extra is not None:
        out[0, :, model : model + LANES] = dot(put, extra[...].reshape(own * CAP, LANES)).astype(BF)


def put_rows(position, rows, shared, extra=None):
    n, tokens, own = position.shape
    model = shared.shape[1]
    cols = model + (0 if extra is None else LANES)
    more = [] if extra is None else [extra.reshape(own, n, CAP, LANES)]
    return pl.pallas_call(
        partial(put_kernel, own),
        grid=(n,),
        out_shape=jax.ShapeDtypeStruct((n, tokens, cols), BF),
        in_specs=[
            token_spec(tokens, own),
            slot_spec(own, model),
            pl.BlockSpec((tokens, model), lambda s: (0, 0)),
        ]
        + [slot_spec(own, LANES) for _ in more],
        out_specs=token_spec(tokens, cols),
        compiler_params=BIG,
    )(position, rows.reshape(own, n, CAP, model), shared, *more)


def grads_kernel(k, *refs):
    lefts, rights, out = refs[:k], refs[k : 2 * k], refs[2 * k]
    start = 0
    for left, right in zip(lefts, rights):
        cols = right.shape[1]
        out[:, start : start + cols] = dot(left[...], right[...], ((0,), (0,))).astype(BF)
        start += cols


def weight_grads(pairs):
    k = len(pairs)
    tokens, model = pairs[0][0].shape
    block = 256
    cols = sum(right.shape[1] for _, right in pairs)
    return pl.pallas_call(
        partial(grads_kernel, k),
        grid=(model // block,),
        out_shape=jax.ShapeDtypeStruct((model, cols), BF),
        in_specs=[pl.BlockSpec((tokens, block), lambda i: (0, i)) for _ in pairs]
        + [pl.BlockSpec(right.shape, lambda i: (0, 0)) for _, right in pairs],
        out_specs=pl.BlockSpec((block, cols), lambda i: (i, 0)),
        compiler_params=BIG,
    )(*[left for left, _ in pairs], *[right for _, right in pairs])


def combine_states(states, decays, expand, reverse):
    n = states.shape[0]
    place = lax.axis_index("dp")
    wide = dot(decays, expand, precision=HIGH)
    state = jnp.zeros(states.shape[1:], F32)
    for j in range(n):
        source = n - 1 - j if reverse else j
        use = source > place if reverse else source < place
        fresh = wide[source][:, None] * state + states[source]
        state = jnp.where(use, fresh, state)
    return state


def incoming_state(mine, decay, expand, reverse, cid):
    if lax.axis_size("dp") == 8:
        return state_scan(
            mine, jnp.broadcast_to(decay, (8, LANES)), expand, reverse, cid, BF if reverse else F32
        )
    rows = jnp.pad(decay, ((0, 31), (0, 0)))
    (gathered,) = gather_dp([jnp.concatenate([mine, rows], axis=0)], cid)
    width = mine.shape[0]
    return combine_states(gathered[:, :width], gathered[:, width], expand, reverse)


def per_device(
    hidden,
    segment_ids,
    routes,
    norm_gain,
    mixer_in,
    state_in,
    step_in,
    conv_value,
    conv_value_bias,
    conv_state,
    conv_state_bias,
    head_params,
    gated_gain,
    mixer_out,
    ffn_gain,
    router,
    shared_in,
    shared_out,
    expert_in,
    expert_out,
    cotangent,
):
    n = lax.axis_size("dp")
    place, mp_place = lax.axis_index("dp"), lax.axis_index("mp")
    tokens, model = hidden.shape
    shard = model // n
    inner = mixer_in.shape[2]
    state_cols = state_in.shape[1]
    taps = conv_value.shape[0]
    heads = head_params.shape[1]
    width = inner // heads
    own_experts = expert_in.shape[0]
    hidden_units = shared_out.shape[0]
    quarter = tokens // 4

    misc_parts = [
        conv_value.reshape(-1),
        conv_value_bias.reshape(-1),
        gated_gain.reshape(-1),
        conv_state.reshape(-1),
        conv_state_bias,
        norm_gain,
        ffn_gain,
    ]
    misc = jnp.concatenate(misc_parts)
    route_rows = routes.T.reshape(-1, model).astype(BF)
    small = jnp.concatenate(
        [
            jnp.pad(misc, (0, model - misc.shape[0]))[None],
            route_rows,
            hidden[tokens - 15 + route_rows.shape[0] :],
        ],
        axis=0,
    )
    pack_a = jnp.concatenate(
        [
            mixer_in.reshape(shard, 2 * inner),
            state_in,
            jnp.pad(step_in, ((0, 0), (0, LANES - heads))),
        ],
        axis=1,
    )
    pack_b = jnp.concatenate(
        [
            mixer_out.T,
            shared_in.reshape(shard, 2 * hidden_units),
            shared_out.T,
            jnp.pad(router, ((0, 0), (0, LANES - EXPERTS))),
        ],
        axis=1,
    )
    mine_cot = lax.dynamic_slice_in_dim(cotangent, mp_place * quarter, quarter, 0)
    weight_a, small_all, cot_all = first_gather([pack_a, small], mine_cot, 0)
    weight_a = weight_a.reshape(model, -1)
    cot_all = cot_all.reshape(n, tokens, model)
    pack_b, small_all = lax.optimization_barrier((pack_b, small_all))
    weight_b = lax.all_gather(pack_b, "dp", axis=0, tiled=True)
    out_t = weight_b[:, :inner]
    shared_w = weight_b[:, inner : inner + 2 * hidden_units]
    shared_out_t = weight_b[:, inner + 2 * hidden_units : inner + 3 * hidden_units]
    router_w = weight_b[:, inner + 3 * hidden_units :]

    pieces = []
    start = 0
    for part in misc_parts:
        pieces.append(small_all[:, 0, start : start + part.shape[0]].astype(F32))
        start += part.shape[0]
    local_p = conv_value.shape[1]
    value_rows = jnp.concatenate(pieces[:3], axis=1).reshape(n, taps + 2, local_p, heads)
    value_rows = value_rows.transpose(1, 3, 0, 2).reshape(taps + 2, inner)
    state_rows = jnp.concatenate(pieces[3:5], axis=1).reshape(n, taps + 1, state_cols // n)
    state_rows = state_rows.transpose(1, 0, 2).reshape(taps + 1, state_cols)
    gain_first = pieces[5].reshape(1, model)
    gain_second = pieces[6].reshape(1, model)
    conv_taps = jnp.concatenate([value_rows[:taps], state_rows[:taps]], axis=1)
    conv_bias = jnp.concatenate([value_rows[taps], state_rows[taps]])[None]
    gated_row = value_rows[taps + 1][None]

    group_start = place * tokens
    seg_padded = jnp.concatenate([jnp.full((taps - 1,), -1, jnp.int32), segment_ids])
    seg_ext = lax.dynamic_slice_in_dim(seg_padded, group_start, tokens + taps - 1)
    segments = seg_ext[taps - 1 :]
    prev_seg = seg_ext[taps - 2]
    same = [
        (seg_ext[k : k + tokens] == segments).astype(F32)[:, None] for k in range(taps)
    ]
    blocks = tokens // BLK
    seg_blocks = segments.reshape(blocks, BLK)
    last_segs = seg_blocks[:, BLK - 1]
    prev_segs = jnp.concatenate([prev_seg[None], last_segs[:-1]])
    entry_ok = (seg_blocks == prev_segs[:, None]).astype(F32).reshape(tokens, 1)
    tail_ok = (seg_blocks == last_segs[:, None]).astype(F32).reshape(tokens, 1)
    group_entry_ok = (segments == prev_seg).astype(F32)[:, None]
    group_tail_ok = (segments == segments[tokens - 1]).astype(F32)[:, None]
    seg_f = segments.astype(F32)
    seg_col, seg_row = seg_f[:, None], seg_f[None, :]

    behind = lax.dynamic_index_in_dim(small_all, (place + n - 1) % n, 0, False)
    hidden_ext = jnp.concatenate([behind, hidden], axis=0).astype(F32)
    inv_ext = lax.rsqrt(jnp.mean(hidden_ext * hidden_ext, axis=1, keepdims=True) + EPS)
    normed_ext = (hidden_ext * inv_ext * gain_first).astype(BF)
    normed = normed_ext[16:]
    zx_ext = dot(normed_ext, weight_a)
    gate_z = zx_ext[16:, :inner]
    pre_ext = zx_ext[16 - taps + 1 :, inner : 2 * inner + state_cols]
    head_local = head_params.astype(F32)
    dt_lanes = zx_ext[16:, 2 * inner + state_cols :]
    conv = jnp.broadcast_to(conv_bias, (tokens, inner + state_cols))
    for k in range(taps):
        conv = conv + conv_taps[k][None] * pre_ext[k : k + tokens] * same[k]
    act = jax.nn.silu(conv)
    values = act[:, :inner]
    write = act[:, inner : inner + state_cols // 2]
    read = act[:, inner + state_cols // 2 :]

    live = (jnp.arange(LANES) < heads)[None]
    head_pad = jnp.pad(head_local, ((0, 0), (0, LANES - heads)))
    rate = jnp.where(live, -jnp.exp(head_pad[0:1]), 0.0)
    step = jnp.where(live, jax.nn.softplus(dt_lanes + head_pad[1:2]), 0.0)
    rated = (step * rate).reshape(blocks, BLK, LANES)
    lower = jnp.tril(jnp.ones((BLK, BLK), F32))
    cumul_b = jnp.einsum("ts,bsh->bth", lower, rated, precision=HIGH)
    totals = cumul_b[:, BLK - 1]
    zero_row = jnp.zeros((1, LANES), F32)
    before, after = [zero_row], [zero_row]
    for i in range(blocks - 1):
        before.append(before[-1] + totals[i][None])
        after.append(after[-1] + totals[blocks - 1 - i][None])
    before = jnp.stack(before)
    after = jnp.stack(after[::-1])
    cumul = cumul_b.reshape(tokens, LANES)
    to_end = totals[:, None] - cumul_b
    entry = jnp.exp(cumul) * entry_ok
    tail_bare = jnp.exp(to_end).reshape(tokens, LANES) * tail_ok
    tail = tail_bare * step
    group_entry = jnp.exp(cumul_b + before).reshape(tokens, LANES) * group_entry_ok
    group_tail = jnp.exp(to_end + after).reshape(tokens, LANES) * group_tail_ok * step
    cumul_t = cumul[:, :16].T
    step_t = step[:, :16].T
    expand = (jnp.arange(LANES)[:, None] == jnp.arange(inner)[None, :] // width).astype(F32)
    skip = dot(head_pad[2:3], expand, precision=HIGH)
    outgoing = dot(
        values * dot(group_tail, expand, precision=HIGH), write, ((0,), (0,)), HIGH
    )
    group_decay = group_entry[tokens - 1 :]
    incoming = incoming_state(outgoing, group_decay, expand, False, 1)
    ssd, kept = recur_forward(
        values, write, read, cumul, cumul_t, step_t, entry, tail, seg_col, seg_row, expand, skip, incoming
    )

    gate_act = jax.nn.silu(gate_z)
    gated = ssd * gate_act
    scaled = (gated * gated_row).astype(BF)
    proj_part = dot(scaled, out_t, ((1,), (1,)))
    square_part = jnp.sum(gated * gated, axis=1, keepdims=True)
    proj_pack = jnp.concatenate([proj_part, jnp.broadcast_to(square_part, (tokens, LANES))], axis=1)
    proj_sum = scatter_mp(proj_pack.reshape(4, quarter, -1), 2)
    proj = proj_sum[:, :model]
    square = proj_sum[:, model : model + 1]
    inv_gated = lax.rsqrt(square / DI + EPS)
    mine_hidden = lax.dynamic_slice_in_dim(hidden, mp_place * quarter, quarter, 0).astype(F32)
    mixed = mine_hidden + proj * inv_gated
    inv_second = lax.rsqrt(jnp.mean(mixed * mixed, axis=1, keepdims=True) + EPS)
    unit_second = mixed * inv_second
    ffn_mine = (unit_second * gain_second).astype(BF)
    ffn_all = gather_tokens(ffn_mine, 3).reshape(n, tokens, model)

    routes_all = small_all[:, 1 : 1 + route_rows.shape[0]].reshape(n, TOPK, tokens)
    routes_cols = routes_all.astype(F32).transpose(0, 2, 1)
    first_expert = place * own_experts
    own_ids = (first_expert + jnp.arange(own_experts, dtype=jnp.int32)).astype(F32)
    named = jnp.any(routes_all.astype(F32)[:, None] == own_ids[None, :, None, None], axis=2)
    earlier = (jnp.arange(tokens)[:, None] < jnp.arange(tokens)[None, :]).astype(BF)
    position = jnp.einsum("set,tu->seu", named.astype(BF), earlier, preferred_element_type=F32)
    position = jnp.where(named, position, -1.0)
    position_cols = position.transpose(0, 2, 1)
    cot_rows = pick_rows(cot_all, position)

    rows, gates, slot_gates = pick_rows_gates(ffn_all, position, routes_cols, router_w)
    slots = n * CAP
    grad_in_rows, grad_expert_out, d_rows, expert_res, slot_dots = run_experts(
        rows.reshape(own_experts, slots, model),
        cot_rows.reshape(own_experts, slots, model),
        slot_gates.reshape(own_experts, slots, LANES),
        expert_in.reshape(own_experts, 2 * model, -1),
        expert_out,
    )
    grad_expert_in = grad_in_rows.reshape(expert_in.shape)

    ffn_block = lax.dynamic_index_in_dim(ffn_all, place, 0, False)
    shared_mid = dot(ffn_block, shared_w)
    shared_gate, shared_up = shared_mid[:, :hidden_units], shared_mid[:, hidden_units:]
    shared_silu = jax.nn.silu(shared_gate)
    shared_act = (shared_silu * shared_up).astype(BF)
    shared_res = dot(shared_act, shared_out_t, ((1,), (1,)))
    d_shared_act = dot(cotangent, shared_out_t)
    d_shared_mid = jnp.concatenate(
        [d_shared_act * shared_up * silu_slope(shared_gate), d_shared_act * shared_silu], axis=1
    ).astype(BF)
    d_ffn_shared = dot(d_shared_mid, shared_w, ((1,), (1,)))

    d_ffn_pack = put_rows(position_cols, d_rows, d_ffn_shared, slot_dots)
    d_ffn_sum = scatter_tokens(d_ffn_pack.reshape(n, 4, quarter, model + LANES), 4)
    expert_res, d_ffn_sum = lax.optimization_barrier((expert_res, d_ffn_sum))
    res_pack = put_rows(position_cols, expert_res, shared_res)
    res_pack, d_ffn_sum = lax.optimization_barrier((res_pack, d_ffn_sum))
    if n > 8:
        res_sum = scatter_tokens(res_pack.reshape(n, 4, quarter, model), 10)
    else:
        res_sum = lax.psum_scatter(
            res_pack.reshape(n * tokens, model), ("dp", "mp"), scatter_dimension=0, tiled=True
        )

    own_tokens_gates = lax.dynamic_slice(
        gates, (place, mp_place * quarter, 0), (1, quarter, LANES)
    ).reshape(quarter, LANES)
    dots = d_ffn_sum[:, model : model + LANES]
    share = jnp.sum(own_tokens_gates * dots, axis=1, keepdims=True)
    d_logits = (own_tokens_gates * (dots - share)).astype(BF)
    d_ffn = d_ffn_sum[:, :model] + dot(d_logits, router_w, ((1,), (1,)))
    mine_cot_f = mine_cot.astype(F32)
    grad_gain_second = jnp.sum(d_ffn * unit_second, axis=0)
    d_unit = d_ffn * gain_second
    d_mixed = mine_cot_f + inv_second * (
        d_unit - unit_second * jnp.mean(d_unit * unit_second, axis=1, keepdims=True)
    )
    d_proj_mine = (d_mixed * inv_gated).astype(BF)
    d_inv = jnp.sum(d_mixed * proj, axis=1, keepdims=True)
    d_square = d_inv * -0.5 * inv_gated * inv_gated * inv_gated / DI
    d_square_high = d_square.astype(BF)
    d_square_low = (d_square - d_square_high.astype(F32)).astype(BF)
    sent = jnp.concatenate(
        [
            d_proj_mine,
            d_logits[:, :EXPERTS],
            d_square_high,
            d_square_low,
            jnp.zeros((quarter, LANES - EXPERTS - 2), BF),
        ],
        axis=1,
    )
    (got,) = gather_mp([sent], 5)
    got = got.reshape(tokens, model + LANES)
    d_proj = got[:, :model]
    d_logits_all = jnp.pad(got[:, model : model + EXPERTS], ((0, 0), (0, LANES - EXPERTS)))
    d_square_all = got[:, model + EXPERTS : model + EXPERTS + 1].astype(F32) + got[
        :, model + EXPERTS + 1 : model + EXPERTS + 2
    ].astype(F32)

    rows0 = ((0,), (0,))
    grad_b = weight_grads(
        [
            (d_proj, scaled),
            (ffn_block, d_shared_mid),
            (cotangent, shared_act),
            (ffn_block, d_logits_all),
        ]
    )
    grad_b, d_proj = lax.optimization_barrier((grad_b, d_proj))
    sum_b = lax.psum_scatter(grad_b, "dp", scatter_dimension=0, tiled=True).astype(F32)
    d_scaled = dot(d_proj, out_t)
    grad_gated_row = jnp.sum(d_scaled * gated, axis=0)
    d_gated = d_scaled * gated_row + 2.0 * gated * d_square_all
    d_ssd = d_gated * gate_act
    d_gate_z = d_gated * ssd * silu_slope(gate_z)

    direct = dot(d_ssd * dot(group_entry, expand, precision=HIGH), read, rows0, HIGH)
    state_grad = incoming_state(direct, group_decay, expand, True, 6)
    d_values, d_write, d_read, d_step, d_rated, d_skip_row = recur_backward(
        values,
        write,
        read,
        cumul,
        cumul_t,
        step_t,
        step,
        entry,
        tail_bare,
        seg_col,
        seg_row,
        expand,
        skip,
        kept,
        d_ssd,
        state_grad,
    )
    d_rate = jnp.sum(d_rated * step, axis=0, keepdims=True)
    d_dt = jnp.where(
        live, (d_step + rate * d_rated) * jax.nn.sigmoid(dt_lanes + head_pad[1:2]), 0.0
    )
    d_skip = dot(d_skip_row, expand, ((1,), (1,)), HIGH)
    grad_head = jnp.concatenate(
        [d_rate * rate, jnp.sum(d_dt, axis=0, keepdims=True), d_skip], axis=0
    )[:, :heads]

    slope = silu_slope(conv)
    d_conv_values = d_values * slope[:, :inner]
    d_state_act, rim_ahead = sum_and_edge(
        jnp.concatenate([d_write, d_read], axis=1), slope[:16, inner:], d_conv_values[:16], 11
    )
    d_conv = jnp.concatenate([d_conv_values, d_state_act * slope[:, inner:]], axis=1)
    d_conv_ext = jnp.concatenate([d_conv, rim_ahead], axis=0)
    seg_after = lax.dynamic_slice_in_dim(
        jnp.concatenate([segment_ids, jnp.full((taps - 1,), -1, jnp.int32)]),
        group_start,
        tokens + taps - 1,
    )
    d_pre = jnp.zeros_like(d_conv)
    grad_rows = []
    for k in range(taps):
        ahead = taps - 1 - k
        ok = (seg_after[ahead : ahead + tokens] == segments).astype(F32)[:, None]
        d_pre = d_pre + conv_taps[k][None] * d_conv_ext[ahead : ahead + tokens] * ok
        grad_rows.append(jnp.sum(d_conv * pre_ext[k : k + tokens] * same[k], axis=0))
    grad_rows.append(jnp.sum(d_conv, axis=0))
    d_a = jnp.concatenate([d_gate_z, d_pre, d_dt], axis=1).astype(BF)

    d_state_mine = lax.dynamic_slice_in_dim(
        d_a[:, 2 * inner : 2 * inner + state_cols], mp_place * quarter, quarter, 0
    )
    d_normed_part = dot(d_a[:, : 2 * inner], weight_a[:, : 2 * inner], ((1,), (1,))) + dot(
        d_a[:, 2 * inner + state_cols :], weight_a[:, 2 * inner + state_cols :], ((1,), (1,))
    )
    d_state_rows = dot(
        d_state_mine, weight_a[:, 2 * inner : 2 * inner + state_cols], ((1,), (1,))
    )
    grad_a = dot(normed, d_a, rows0).astype(BF)
    unit_first = hidden_ext[16:] * inv_ext[16:]
    mine_unit = lax.dynamic_slice_in_dim(unit_first, mp_place * quarter, quarter, 0)
    grad_gain_first = jnp.sum(d_normed_part * unit_first, axis=0) + jnp.sum(
        d_state_rows * mine_unit, axis=0
    )

    value_grads = jnp.stack([g[:inner] for g in grad_rows] + [grad_gated_row])
    value_grads = value_grads.reshape(taps + 2, heads, n, local_p).transpose(2, 0, 3, 1)
    state_grads = jnp.stack([g[inner:] for g in grad_rows])
    state_grads = state_grads.reshape(taps + 1, n, state_cols // n).transpose(1, 0, 2)
    misc_grads = [
        value_grads.reshape(n, -1),
        state_grads.reshape(n, -1),
        jnp.broadcast_to(grad_head.reshape(1, -1), (n, 3 * heads)),
    ]
    sizes = [g.shape[1] for g in misc_grads]
    misc_grads = jnp.concatenate(misc_grads, axis=1)
    misc_grads = jnp.pad(misc_grads, ((0, 0), (0, 32 * LANES - misc_grads.shape[1])))
    gains = jnp.concatenate(
        [grad_gain_first.reshape(n, shard), grad_gain_second.reshape(n, shard)], axis=1
    )
    gains = jnp.pad(gains, ((0, 0), (0, 16 * LANES - 2 * shard)))
    res_sum, d_state_rows = lax.optimization_barrier((res_sum, d_state_rows))
    mine_result = (mixed + res_sum.astype(F32)).astype(BF)
    sum_a, misc_sum, gains_sum, hidden_all, result = last_exchange(
        grad_a.reshape(n, shard, -1),
        misc_grads.reshape(n, 32, LANES),
        gains.reshape(n, 16, LANES),
        d_normed_part.astype(BF).reshape(4, quarter, model),
        d_state_rows,
        d_mixed,
        mine_hidden,
        gain_first,
        mine_result,
        8,
    )
    result = result.reshape(tokens, model)
    misc_sum = misc_sum.reshape(-1)
    gains_sum = gains_sum.reshape(-1)
    cut = [0]
    for size in sizes:
        cut.append(cut[-1] + size)
    value_sum = misc_sum[: cut[1]].reshape(taps + 2, local_p, heads)
    state_sum = misc_sum[cut[1] : cut[2]].reshape(taps + 1, state_cols // n)
    head_sum = misc_sum[cut[2] : cut[3]].reshape(3, heads)

    b1, b2 = inner, inner + 2 * hidden_units
    b3 = b2 + hidden_units
    return (
        result,
        hidden_all.reshape(tokens, model).astype(F32),
        gains_sum[:shard],
        sum_a[:, : 2 * inner].reshape(shard, 2, inner),
        sum_a[:, 2 * inner : 2 * inner + state_cols],
        sum_a[:, 2 * inner + state_cols : 2 * inner + state_cols + heads],
        value_sum[:taps],
        value_sum[taps],
        state_sum[:taps],
        state_sum[taps],
        head_sum,
        value_sum[taps + 1],
        sum_b[:, :b1].T,
        gains_sum[shard : 2 * shard],
        sum_b[:, b3 : b3 + EXPERTS],
        sum_b[:, b1:b2].reshape(shard, 2, hidden_units),
        sum_b[:, b2:b3].T,
        grad_expert_in,
        grad_expert_out,
    )


def solution(mesh):
    placed = (
        P("dp", None),
        P(),
        P("dp", None),
        P("dp"),
        P("dp", None, "mp"),
        P("dp", None),
        P("dp", "mp"),
        P(None, "dp", "mp"),
        P("dp", "mp"),
        P(None, "dp"),
        P("dp"),
        P(None, "mp"),
        P("dp", "mp"),
        P("mp", "dp"),
        P("dp"),
        P("dp", None),
        P("dp", None, "mp"),
        P("mp", "dp"),
        P("dp", None, None, "mp"),
        P("dp", "mp", None),
        P("dp", None),
    )
    return jax.shard_map(
        per_device,
        mesh=mesh,
        in_specs=placed,
        out_specs=(
            P("dp", None),
            P("dp", None),
            P("dp"),
            P("dp", None, "mp"),
            P("dp", None),
            P("dp", "mp"),
            P(None, "dp", "mp"),
            P("dp", "mp"),
            P(None, "dp"),
            P("dp"),
            P(None, "mp"),
            P("dp", "mp"),
            P("mp", "dp"),
            P("dp"),
            P("dp", None),
            P("dp", None, "mp"),
            P("mp", "dp"),
            P("dp", None, None, "mp"),
            P("dp", "mp", None),
        ),
        check_vma=False,
    )
```

```python
from functools import partial

import jax
import jax.numpy as jnp
from jax import lax
from jax.experimental import pallas as pl
from jax.experimental.pallas import tpu as pltpu
from jax.sharding import PartitionSpec as P

MESH = pl.DeviceIdType.MESH
BLK = 128
EXPERTS = 64
TOPK = 6
DI = 3072
CAP = 64
LANES = 128

EPS = 1e-05
HIGH = lax.Precision.HIGHEST
MASKED = -1e30
BF = jnp.bfloat16
F32 = jnp.float32
ANY = pl.BlockSpec(memory_space=pl.ANY)
VM = pl.BlockSpec(memory_space=pltpu.VMEM)


def dot(a, b, dims=((1,), (0,)), precision=None):
    return lax.dot_general(
        a, b, (dims, ((), ())), precision=precision, preferred_element_type=F32
    )


def two_parts(a):
    high = a.astype(BF)
    return high, (a - high.astype(F32)).astype(BF)


def dot_three(a, b, over):
    a_high, a_low = two_parts(a)
    b_high, b_low = two_parts(b)
    left = jnp.concatenate([a_high, a_low, a_high], axis=over[0])
    right = jnp.concatenate([b_high, b_high, b_low], axis=over[1])
    return dot(left, right, ((over[0],), (over[1],)))


def silu_slope(argument):
    sigmoid_val = jax.nn.sigmoid(argument)
    return sigmoid_val * (1.0 + argument * (1.0 - sigmoid_val))


def half_rows(rows):
    return (rows // 32) * 16


def chunk_rows(start, size):
    return [(start + i, min(32, size - i)) for i in range(0, size, 32)]


def both_ways(rows):
    cut = half_rows(rows)
    ways = [chunk_rows(0, cut), chunk_rows(cut, rows - cut)]
    order = []
    for i in range(max(len(w) for w in ways)):
        for way in range(2):
            if i < len(ways[way]):
                order.append((way, i) + ways[way][i])
    return order


def ring_place(n, d):
    high, low = d // 2, d % 2
    return high * (1 - low) + (n - 1 - high) * low


def ring_device(n, p):
    back = p // (n // 2)
    return (2 * p) * (1 - back) + (2 * (n - 1 - p) + 1) * back


def greet(targets):
    barrier = pltpu.get_barrier_semaphore()
    for target in targets:
        pl.semaphore_signal(barrier, inc=1, device_id=target, device_id_type=MESH)
    pl.semaphore_wait(barrier, len(targets))


def remote(src, dst, send, recv, target):
    return pltpu.make_async_remote_copy(
        src_ref=src,
        dst_ref=dst,
        send_sem=send,
        recv_sem=recv,
        device_id=target,
        device_id_type=MESH,
    )


def mp_partners(m):
    return {"mp": m + 1 - 2 * (m % 2)}, {"mp": (m + 2) % 4}


def ring_neighbours(n):
    p = ring_place(n, lax.axis_index("dp"))
    nxt = {"dp": ring_device(n, (p + 1) % n)}
    prv = {"dp": ring_device(n, (p + n - 1) % n)}
    return p, nxt, prv


class RingGather:
    def __init__(self, n, ins, outs, sems):
        self.n, self.ins, self.outs = n, ins, outs
        self.local_sem, self.send_sem, self.recv_sem = sems
        self.p, self.nxt, self.prv = ring_neighbours(n)
        self.order = [both_ways(a.shape[0]) for a in ins]
        self.copies = {}

    @staticmethod
    def scratch(n, arrays):
        dma = pltpu.SemaphoreType.DMA
        most = max(len(both_ways(a.shape[0])) for a in arrays)
        shape = (n - 1, len(arrays), most)
        return [dma((len(arrays),)), dma(shape), dma(shape)]

    def begin(self):
        d = lax.axis_index("dp")
        self.local = []
        for j, (a, out) in enumerate(zip(self.ins, self.outs)):
            copy = pltpu.make_async_copy(a, out.at[d], self.local_sem.at[j])
            copy.start()
            self.local.append(copy)

    def step(self, s):
        n, p = self.n, self.p
        for j, (a, out) in enumerate(zip(self.ins, self.outs)):
            for k, (way, _, start, rows) in enumerate(self.order[j]):
                origin = ring_device(n, (p + n - s) % n if way == 0 else (p + s) % n)
                part = pl.ds(start, rows)
                if s > 0:
                    self.copies[s - 1, j, k].wait_recv()
                if s < n - 1:
                    copy = remote(
                        a.at[part] if s == 0 else out.at[origin, part],
                        out.at[origin, part],
                        self.send_sem.at[s, j, k],
                        self.recv_sem.at[s, j, k],
                        self.nxt if way == 0 else self.prv,
                    )
                    copy.start()
                    self.copies[s, j, k] = copy

    def end(self):
        for copy in self.copies.values():
            copy.wait_send()
        for copy in self.local:
            copy.wait()


def gather_kernel(n, k, *refs):
    ring = RingGather(n, refs[:k], refs[k : 2 * k], refs[2 * k :])
    greet([ring.nxt, ring.prv])
    ring.begin()
    for s in range(n):
        ring.step(s)
    ring.end()


def gather_dp(arrays, cid):
    n, k = lax.axis_size("dp"), len(arrays)
    return pl.pallas_call(
        partial(gather_kernel, n, k),
        out_shape=[jax.ShapeDtypeStruct((n,) + a.shape, a.dtype) for a in arrays],
        in_specs=[ANY] * k,
        out_specs=[ANY] * k,
        scratch_shapes=RingGather.scratch(n, arrays),
        compiler_params=pltpu.CompilerParams(collective_id=cid, has_side_effects=True),
    )(*arrays)


def add_rows(dst, pieces, rows, dtype):
    def body(i, carry):
        sl = pl.ds(pl.multiple_of(i * 16, 16), 16)
        total = pieces[0][sl, :].astype(F32)
        for piece in pieces[1:]:
            total = total + piece[sl, :].astype(F32)
        dst[sl, :] = total.astype(dtype)
        return carry

    lax.fori_loop(0, rows // 16, body, 0)


class RingScatter:
    def __init__(self, n, ins, outs, slots, sems):
        self.n, self.ins, self.outs, self.slots = n, ins, outs, slots
        self.send_sem, self.recv_sem = sems
        self.p, self.nxt, self.prv = ring_neighbours(n)
        self.copies = {}

    @staticmethod
    def scratch(n, arrays):
        most = max(len(both_ways(a.shape[1])) for a in arrays)
        shape = (n - 1, len(arrays), most)
        return [pltpu.VMEM((n - 1,) + a.shape[1:], a.dtype) for a in arrays] + [
            pltpu.SemaphoreType.DMA(shape),
            pltpu.SemaphoreType.DMA(shape),
        ]

    def step(self, s, j):
        n, p = self.n, self.p
        array, out, slots = self.ins[j], self.outs[j], self.slots[j]
        for i, (way, _, start, size) in enumerate(both_ways(array.shape[1])):
            block = ring_device(n, (p + 2 * n - 1 - s) % n if way == 0 else (p + 1 + s) % n)
            part = pl.ds(start, size)
            source = array.at[block, part]
            if s > 0:
                self.copies[s - 1, j, i].wait_recv()
                held = slots.at[s - 1, part]
                if s == n - 1:
                    add_rows(out.at[part], [held, source], size, F32)
                    continue
                add_rows(held, [held, source], size, array.dtype)
                source = held
            copy = remote(
                source,
                slots.at[s, part],
                self.send_sem.at[s, j, i],
                self.recv_sem.at[s, j, i],
                self.nxt if way == 0 else self.prv,
            )
            copy.start()
            self.copies[s, j, i] = copy

    def end(self):
        for copy in self.copies.values():
            copy.wait_send()


def last_kernel(
    n,
    grad_a,
    misc,
    gains,
    d_normed,
    extra,
    d_mixed,
    hidden,
    gain,
    result,
    out_a,
    out_misc,
    out_gains,
    all_hidden,
    all_result,
    gains_mine,
    gains_core,
    gains_chip,
    rows_core,
    rows_chip,
    rows_bf,
    slots_a,
    slots_misc,
    slots_gains,
    ring_send,
    ring_recv,
    mp_send,
    mp_recv,
    local_sem,
):
    m = lax.axis_index("mp")
    core, chip = mp_partners(m)
    far = (m + 2) % 4
    beside = m + 1 - 2 * (m % 2)
    ring = RingScatter(
        n,
        [grad_a, misc, gains_mine],
        [out_a, out_misc, out_gains],
        [slots_a, slots_misc, slots_gains],
        [ring_send, ring_recv],
    )
    greet([core, chip, ring.nxt, ring.prv])
    sent = []

    def over_mp(i, source, target, device):
        copy = remote(source, target, mp_send.at[i], mp_recv.at[i], device)
        copy.start()
        sent.append(copy)
        return copy

    ring.step(0, 0)
    ring.step(0, 1)
    gains_one = over_mp(0, gains, gains_core, core)
    rows_far = over_mp(1, d_normed.at[(beside + 2) % 4], rows_core.at[1], core)
    rows_near = over_mp(2, d_normed.at[beside], rows_core.at[0], core)
    own_result = pltpu.make_async_copy(result, all_result.at[m], local_sem.at[0])
    own_result.start()
    gains_one.wait_recv()
    for b in range(n):
        add_rows(gains_mine.at[b], [gains.at[b], gains_core.at[b]], 16, F32)
    gains_two = over_mp(3, gains_mine, gains_chip, chip)
    count = d_mixed.shape[0]
    rows_far.wait_recv()
    add_rows(rows_core.at[1], [rows_core.at[1], d_normed.at[far]], count, BF)
    rows_two = over_mp(4, rows_core.at[1], rows_chip, chip)
    result_chip = over_mp(5, result, all_result.at[m], chip)
    result_core = over_mp(6, result, all_result.at[m], core)
    gains_two.wait()
    for b in range(n):
        add_rows(gains_mine.at[b], [gains_mine.at[b], gains_chip.at[b]], 16, F32)
    ring.step(0, 2)
    for j in range(3):
        ring.step(1, j)
    rows_near.wait_recv()
    rows_two.wait_recv()

    def body(i, carry):
        sl = pl.ds(pl.multiple_of(i * 16, 16), 16)
        d_n = d_normed[m, sl, :].astype(F32) + rows_core[0, sl, :].astype(F32)
        d_n = d_n + rows_chip[sl, :].astype(F32) + extra[sl, :]
        x = hidden[sl, :].astype(F32)
        inv = lax.rsqrt(jnp.mean(x * x, axis=1, keepdims=True) + EPS)
        unit = x * inv
        d_unit = d_n * gain[...]
        mean = jnp.mean(d_unit * unit, axis=1, keepdims=True)
        rows_bf[sl, :] = (d_mixed[sl, :] + inv * (d_unit - unit * mean)).astype(BF)
        return carry

    lax.fori_loop(0, count // 16, body, 0)
    own_hidden = pltpu.make_async_copy(rows_bf, all_hidden.at[m], local_sem.at[1])
    own_hidden.start()
    hidden_chip = over_mp(7, rows_bf, all_hidden.at[m], chip)
    hidden_core = over_mp(8, rows_bf, all_hidden.at[m], core)
    arrive = []
    for s in range(2, n):
        for j in range(3):
            ring.step(s, j)
        if s == 4:
            result_chip.wait_recv()
            arrive.append(over_mp(9, all_result.at[far], all_result.at[far], core))
        if s == 6:
            hidden_chip.wait_recv()
            arrive.append(over_mp(10, all_hidden.at[far], all_hidden.at[far], core))
    for copy in [result_core, hidden_core] + arrive:
        copy.wait_recv()
    own_result.wait()
    own_hidden.wait()
    for copy in sent:
        if copy is not gains_two:
            copy.wait_send()
    ring.end()


def last_exchange(grad_a, misc, gains, d_normed, extra, d_mixed, hidden, gain, result, cid):
    n = lax.axis_size("dp")
    rows, model = d_mixed.shape
    dma = pltpu.SemaphoreType.DMA
    every = jax.ShapeDtypeStruct((4, rows, model), BF)
    return pl.pallas_call(
        partial(last_kernel, n),
        out_shape=[jax.ShapeDtypeStruct(a.shape[1:], F32) for a in (grad_a, misc, gains)] + [every, every],
        in_specs=[VM] * 8 + [ANY],
        out_specs=[VM] * 3 + [ANY] * 2,
        scratch_shapes=[
            pltpu.VMEM(gains.shape, F32),
            pltpu.VMEM(gains.shape, F32),
            pltpu.VMEM(gains.shape, F32),
            pltpu.VMEM((2, rows, model), BF),
            pltpu.VMEM((rows, model), BF),
            pltpu.VMEM((rows, model), BF),
        ]
        + RingScatter.scratch(n, [grad_a, misc, gains])
        + [dma((11,)), dma((11,)), dma((2,))],
        compiler_params=pltpu.CompilerParams(
            collective_id=cid, has_side_effects=True, vmem_limit_bytes=56 * 1024 * 1024
        ),
    )(grad_a, misc, gains, d_normed, extra, d_mixed, hidden, gain, result)


def mp_scatter_kernel(x, out, from_core, from_chip, send_sem, recv_sem):
    m = lax.axis_index("mp")
    core, chip = mp_partners(m)
    mine, far = m, (m + 2) % 4
    beside = m + 1 - 2 * (m % 2)
    parts = [(pl.ds(start, size), size) for start, size in chunk_rows(0, out.shape[0])]
    greet([core, chip])
    first, last = [], []
    for slot, block in ((1, (beside + 2) % 4), (0, beside)):
        for i, (part, _) in enumerate(parts):
            copy = remote(
                x.at[block, part], from_core.at[slot, part], send_sem.at[slot, i], recv_sem.at[slot, i], core
            )
            copy.start()
            first.append(copy)
    for i, (part, size) in enumerate(parts):
        first[i].wait_recv()
        held = from_core.at[1, part]
        add_rows(held, [held, x.at[far, part]], size, x.dtype)
        copy = remote(held, from_chip.at[part], send_sem.at[2, i], recv_sem.at[2, i], chip)
        copy.start()
        last.append(copy)
    for i, (part, size) in enumerate(parts):
        first[len(parts) + i].wait_recv()
        last[i].wait_recv()
        add_rows(out.at[part], [x.at[mine, part], from_core.at[0, part], from_chip.at[part]], size, F32)
    for copy in first + last:
        copy.wait_send()


def scatter_mp(x, cid):
    rows, cols = x.shape[1:]
    count = len(chunk_rows(0, rows))
    return pl.pallas_call(
        mp_scatter_kernel,
        out_shape=jax.ShapeDtypeStruct((rows, cols), F32),
        in_specs=[VM],
        out_specs=VM,
        scratch_shapes=[
            pltpu.VMEM((2, rows, cols), x.dtype),
            pltpu.VMEM((rows, cols), x.dtype),
            pltpu.SemaphoreType.DMA((3, count)),
            pltpu.SemaphoreType.DMA((3, count)),
        ],
        compiler_params=pltpu.CompilerParams(
            collective_id=cid, has_side_effects=True, vmem_limit_bytes=32 * 1024 * 1024
        ),
    )(x)


def mp_gather_kernel(k, *refs):
    ins, outs = refs[:k], refs[k : 2 * k]
    local_sem, send_sem, recv_sem = refs[2 * k :]
    m = lax.axis_index("mp")
    core, chip = mp_partners(m)
    far = (m + 2) % 4
    greet([core, chip])
    copies, local, arrive = [], [], []
    for j in range(k):
        to_chip = remote(ins[j], outs[j].at[m], send_sem.at[0, j], recv_sem.at[0, j], chip)
        to_chip.start()
        to_core = remote(ins[j], outs[j].at[m], send_sem.at[1, j], recv_sem.at[1, j], core)
        to_core.start()
        own = pltpu.make_async_copy(ins[j], outs[j].at[m], local_sem.at[j])
        own.start()
        copies += [to_chip, to_core]
        arrive.append(to_chip)
        local.append(own)
    onward = []
    for j in range(k):
        arrive[j].wait_recv()
        copy = remote(outs[j].at[far], outs[j].at[far], send_sem.at[2, j], recv_sem.at[2, j], core)
        copy.start()
        onward.append(copy)
    for j in range(k):
        copies[2 * j + 1].wait_recv()
        onward[j].wait_recv()
        local[j].wait()
    for copy in copies + onward:
        copy.wait_send()


def gather_mp(arrays, cid):
    k = len(arrays)
    return pl.pallas_call(
        partial(mp_gather_kernel, k),
        out_shape=[jax.ShapeDtypeStruct((4,) + a.shape, a.dtype) for a in arrays],
        in_specs=[ANY] * k,
        out_specs=[ANY] * k,
        scratch_shapes=[
            pltpu.SemaphoreType.DMA((k,)),
            pltpu.SemaphoreType.DMA((3, k)),
            pltpu.SemaphoreType.DMA((3, k)),
        ],
        compiler_params=pltpu.CompilerParams(collective_id=cid, has_side_effects=True),
    )(*arrays)


class TokenGather:
    def __init__(self, n, both, x, out, sems):
        self.n, self.both, self.x, self.out = n, both, x, out
        self.local, self.ring_s, self.ring_r, self.core_s, self.core_r, self.chip_s, self.chip_r = sems
        self.d, self.m = lax.axis_index("dp"), lax.axis_index("mp")
        self.far = (self.m + 2) % 4
        self.core, self.chip = mp_partners(self.m)
        self.p, self.nxt, self.prv = ring_neighbours(n)
        self.pieces = [(way, 0, start, rows) for way, _, start, rows in both_ways(x.shape[0])]
        self.pieces += [(way, 1, start, rows) for way, _, start, rows in both_ways(both)]
        self.sent, self.pending = [], []
        self.ring, self.chips = {}, {}

    @staticmethod
    def scratch(n, rows, both):
        dma = pltpu.SemaphoreType.DMA
        own, far = len(both_ways(rows)), len(both_ways(both))
        return [
            dma((3,)),
            dma((n - 1, own + far)),
            dma((n - 1, own + far)),
            dma((n, 2 * own + far)),
            dma((n, 2 * own + far)),
            dma((n, own)),
            dma((n, own)),
        ]

    def send(self, source, place, s_sem, r_sem, target):
        copy = remote(source, place, s_sem, r_sem, target)
        copy.start()
        self.sent.append(copy)
        return copy

    def begin(self):
        own = self.out.at[self.d, self.m]
        self.load = pltpu.make_async_copy(self.x, own, self.local.at[0])
        self.load.start()
        self.first = None
        if self.both:
            part = pl.ds(0, self.both)
            self.first = remote(
                self.x.at[part], own.at[part], self.local.at[1], self.local.at[2], self.chip
            )
            self.first.start()
            self.sent.append(self.first)

    def step(self, s):
        n, p = self.n, self.p
        for k, (way, is_far, start, rows) in enumerate(self.pieces):
            origin = ring_device(n, (p + n - s) % n if way == 0 else (p + s) % n)
            place = self.far if is_far else self.m
            region = self.out.at[origin, place, pl.ds(start, rows)]
            source = region if s > 0 or is_far else self.x.at[pl.ds(start, rows)]
            if s > 0:
                self.ring[s - 1, k].wait_recv()
            elif is_far and self.first is not None:
                self.first.wait_recv()
                self.first = None
            if s < n - 1:
                self.ring[s, k] = self.send(
                    source,
                    region,
                    self.ring_s.at[s, k],
                    self.ring_r.at[s, k],
                    self.nxt if way == 0 else self.prv,
                )
            self.pending.append(
                self.send(source, region, self.core_s.at[s, k], self.core_r.at[s, k], self.core)
            )
            if not is_far and start >= self.both:
                self.chips[s, k] = (
                    self.send(source, region, self.chip_s.at[s, k], self.chip_r.at[s, k], self.chip),
                    self.out.at[origin, self.far, pl.ds(start, rows)],
                )

    def pass_on(self, s):
        total = len(self.pieces)
        for k in range(total):
            if (s, k) in self.chips:
                copy, region = self.chips[s, k]
                copy.wait_recv()
                self.pending.append(
                    self.send(
                        region, region, self.core_s.at[s, total + k], self.core_r.at[s, total + k], self.core
                    )
                )

    def end(self):
        for copy in self.pending:
            copy.wait_recv()
        for copy in self.sent:
            copy.wait_send()
        self.load.wait()


class PickWork:
    def __init__(self, own, x, position, out, x_buf, out_buf, sems):
        self.own, self.x, self.position, self.out = own, x, position, out
        self.x_buf, self.out_buf, self.load_sem, self.store_sem = x_buf, out_buf, sems[0], sems[1]
        self.loads, self.stores = {}, {}

    def load(self, s):
        copy = pltpu.make_async_copy(self.x.at[s], self.x_buf.at[s % 2], self.load_sem.at[s % 2])
        copy.start()
        self.loads[s] = copy

    def step(self, s):
        if s + 1 < self.x.shape[0]:
            self.load(s + 1)
        self.loads[s].wait()
        if s > 1:
            self.stores[s - 2].wait()
        pick = pick_matrix(self.position[s], self.own)
        picked = dot(pick, self.x_buf[s % 2]).astype(BF)
        self.out_buf[s % 2] = picked.reshape(self.out_buf.shape[1:])
        copy = pltpu.make_async_copy(self.out_buf.at[s % 2], self.out.at[:, s], self.store_sem.at[s % 2])
        copy.start()
        self.stores[s] = copy

    def end(self):
        count = self.x.shape[0]
        for s in (count - 2, count - 1):
            self.stores[s].wait()


def token_gather_kernel(n, both, own, x, y, position, out, picked, x_buf, out_buf, load_sem, store_sem, *sems):
    gather = TokenGather(n, both, x, out, sems)
    work = PickWork(own, y, position, picked, x_buf, out_buf, (load_sem, store_sem))
    work.load(0)
    greet([gather.core, gather.chip, gather.nxt, gather.prv])
    gather.begin()
    for s in range(n):
        gather.step(s)
        work.step(s)
        if s > 0:
            gather.pass_on(s - 1)
    gather.pass_on(n - 1)
    gather.end()
    work.end()


def gather_tokens(x, y, position, cid):
    n = lax.axis_size("dp")
    both = x.shape[0] // 2
    own, tokens = position.shape[1:]
    model = y.shape[2]
    return pl.pallas_call(
        partial(token_gather_kernel, n, both, own),
        out_shape=[
            jax.ShapeDtypeStruct((n, 4) + x.shape, x.dtype),
            jax.ShapeDtypeStruct((own, n, CAP, model), BF),
        ],
        in_specs=[ANY, ANY, VM],
        out_specs=[ANY, ANY],
        scratch_shapes=[
            pltpu.VMEM((2, tokens, model), BF),
            pltpu.VMEM((2, own, CAP, model), BF),
            pltpu.SemaphoreType.DMA((2,)),
            pltpu.SemaphoreType.DMA((2,)),
        ]
        + TokenGather.scratch(n, x.shape[0], both),
        compiler_params=pltpu.CompilerParams(
            collective_id=cid, has_side_effects=True, vmem_limit_bytes=48 * 1024 * 1024
        ),
    )(x, y, position)


def first_kernel(n, k, *refs):
    ins, x = refs[:k], refs[k]
    outs, x_out = refs[k + 1 : 2 * k + 1], refs[2 * k + 1]
    ring = RingGather(n, ins, outs, refs[2 * k + 2 : 2 * k + 5])
    gather = TokenGather(n, 0, x, x_out, refs[2 * k + 5 :])
    greet([gather.core, gather.chip, gather.nxt, gather.prv])
    ring.begin()
    gather.begin()
    for s in range(n):
        gather.step(s)
        ring.step(s)
        if s > 1:
            gather.pass_on(s - 2)
    gather.pass_on(n - 2)
    gather.pass_on(n - 1)
    gather.end()
    ring.end()


def first_gather(arrays, x, cid):
    n, k = lax.axis_size("dp"), len(arrays)
    return pl.pallas_call(
        partial(first_kernel, n, k),
        out_shape=[jax.ShapeDtypeStruct((n,) + a.shape, a.dtype) for a in arrays]
        + [jax.ShapeDtypeStruct((n, 4) + x.shape, x.dtype)],
        in_specs=[ANY] * (k + 1),
        out_specs=[ANY] * (k + 1),
        scratch_shapes=RingGather.scratch(n, arrays) + TokenGather.scratch(n, x.shape[0], 0),
        compiler_params=pltpu.CompilerParams(collective_id=cid, has_side_effects=True),
    )(*arrays, x)


def token_scatter_kernel(
    n,
    x,
    out,
    from_core,
    slots,
    loads,
    far_loads,
    from_chip,
    to_chip,
    first,
    done,
    last_buf,
    load_sem,
    far_sem,
    core_send,
    core_recv,
    chip_send,
    chip_recv,
    send_sem,
    recv_sem,
):
    m = lax.axis_index("mp")
    c, y = m % 2, m // 2
    core, chip = mp_partners(m)
    p, nxt, prv = ring_neighbours(n)
    rows = out.shape[0]
    half, part = rows // 2, rows // 4
    greet([core, chip, nxt, prv])

    def block_at(s, way):
        return ring_device(n, (p + 2 * n - 1 - s) % n if way == 0 else (p + 1 + s) % n)

    parts = [
        (0, 0, 0, half, 0),
        (1, 0, half, half, 0),
        (0, 1, 0, part, half),
        (1, 1, part, part, half),
        (1, 1, half, half, None),
    ]
    over, sent, loading = {}, [], {}

    def core_sends(s):
        for k in (4, 0, 1, 2, 3):
            way, is_far, start, size, _ = parts[k]
            block, y_piece = block_at(s, way), (y + is_far) % 2
            copy = remote(
                x.at[block, (m + 1 - 2 * c + 2 * is_far) % 4, pl.ds(start, size)],
                from_core.at[block, y_piece, pl.ds(start, size)],
                core_send.at[s, k],
                core_recv.at[s, k],
                core,
            )
            copy.start()
            over[s, k] = copy
            sent.append(copy)

    def load(s, k):
        way, is_far, start, size, at = parts[k]
        block = block_at(s, way)
        over[s, k].wait_recv()
        sources = (
            x.at[block, (m + 2 * is_far) % 4, pl.ds(start, size)],
            from_core.at[block, (y + is_far) % 2, pl.ds(start, size)],
        )
        loading[s, k] = []
        for i, source in enumerate(sources):
            if k == 4:
                copy = pltpu.make_async_copy(source, far_loads.at[s % 2, i], far_sem.at[s % 2, i])
            else:
                copy = pltpu.make_async_copy(
                    source, loads.at[s % 2, way, i, pl.ds(at, size)], load_sem.at[s % 2, k, i]
                )
            copy.start()
            loading[s, k].append(copy)

    chips = {}

    def to_other_chip(s):
        for copy in loading[s, 4]:
            copy.wait()
        if s > 1:
            chips[s - 2].wait_send()
        add_rows(to_chip.at[s % 2], [far_loads.at[s % 2, 0], far_loads.at[s % 2, 1]], half, BF)
        copy = remote(to_chip.at[s % 2], from_chip.at[s], chip_send.at[s], chip_recv.at[s], chip)
        copy.start()
        chips[s] = copy

    core_sends(0)
    core_sends(1)
    load(0, 4)
    for k in range(4):
        load(0, k)
    load(1, 4)
    to_other_chip(0)
    to_other_chip(1)
    core_sends(2)
    for k in range(4):
        load(1, k)
    load(2, 4)
    ring = {}
    tiles = [(way, at, size) for way, _, at, size in both_ways(2 * (half + part))]
    tiles = [(way, at - way * (half + part), size) for way, at, size in tiles]
    for s in range(n):
        for k in range(4):
            for copy in loading[s, k]:
                copy.wait()
        for k, (way, at, size) in enumerate(tiles):
            area = pl.ds(at, size)
            pieces = [loads.at[s % 2, way, 0, area], loads.at[s % 2, way, 1, area]]
            if s == 0:
                target = first.at[way, area]
            else:
                ring[s - 1, k].wait_recv()
                held = slots.at[way, s - 1, area]
                target = held if s < n - 1 else done.at[way, area]
                pieces.append(held)
            if way == 1 and at < half:
                if at == 0:
                    chips[s].wait_recv()
                pieces.append(from_chip.at[s, area])
            add_rows(target, pieces, size, BF)
            if s < n - 1:
                copy = remote(
                    target,
                    slots.at[way, s, area],
                    send_sem.at[s, k],
                    recv_sem.at[s, k],
                    nxt if way == 0 else prv,
                )
                copy.start()
                ring[s, k] = copy
        if s + 2 < n:
            to_other_chip(s + 2)
            for k in range(4):
                load(s + 2, k)
        if s + 3 < n:
            core_sends(s + 3)
            load(s + 3, 4)
    last = []
    for way in range(2):
        copy = remote(
            done.at[way, pl.ds(half, part)],
            last_buf.at[pl.ds(way * part, part)],
            send_sem.at[n - 1, way],
            recv_sem.at[n - 1, way],
            chip,
        )
        copy.start()
        last.append(copy)
    add_rows(out.at[pl.ds(half, half)], [done.at[1, pl.ds(0, half)]], half, F32)
    for copy in last:
        copy.wait_recv()
    add_rows(out.at[pl.ds(0, half)], [done.at[0, pl.ds(0, half)], last_buf], half, F32)
    for copy in sent + list(ring.values()) + last + [chips[n - 2], chips[n - 1]]:
        copy.wait_send()


def scatter_tokens(x, cid):
    n, _, rows, cols = x.shape
    half, part = rows // 2, rows // 4
    dma = pltpu.SemaphoreType.DMA
    out, _ = pl.pallas_call(
        partial(token_scatter_kernel, n),
        out_shape=[
            jax.ShapeDtypeStruct((rows, cols), F32),
            jax.ShapeDtypeStruct((n, 2, rows, cols), BF),
        ],
        in_specs=[ANY],
        out_specs=[VM, ANY],
        scratch_shapes=[
            pltpu.VMEM((2, n - 1, half + part, cols), BF),
            pltpu.VMEM((2, 2, 2, half + part, cols), BF),
            pltpu.VMEM((2, 2, half, cols), BF),
            pltpu.VMEM((n, half, cols), BF),
            pltpu.VMEM((2, half, cols), BF),
            pltpu.VMEM((2, half + part, cols), BF),
            pltpu.VMEM((2, half + part, cols), BF),
            pltpu.VMEM((half, cols), BF),
            dma((2, 4, 2)),
            dma((2, 2)),
            dma((n, 5)),
            dma((n, 5)),
            dma((n,)),
            dma((n,)),
            dma((n, 6)),
            dma((n, 6)),
        ],
        compiler_params=pltpu.CompilerParams(
            collective_id=cid, has_side_effects=True, vmem_limit_bytes=56 * 1024 * 1024
        ),
    )(x)
    return out


def edge_kernel(n, part, slope, rim, total, ahead, mine, from_core, from_chip, edge, send_sem, recv_sem):
    d, m = lax.axis_index("dp"), lax.axis_index("mp")
    core, chip = mp_partners(m)
    before, after = {"dp": (d + n - 1) % n}, {"dp": (d + 1) % n}
    rows, cols = part.shape
    edge_rows, rim_cols = rim.shape
    greet([core, chip, before, after])

    def add(dst, pieces, dtype):
        add_rows(dst, pieces, rows, dtype)

    one = remote(part, from_core, send_sem.at[0], recv_sem.at[0], core)
    one.start()
    one.wait()
    add(mine, [part, from_core], BF)
    two = remote(mine, from_chip, send_sem.at[1], recv_sem.at[1], chip)
    two.start()
    two.wait_recv()
    add(total, [mine, from_chip], F32)
    edge[:, 0:rim_cols] = rim[...]
    edge[:, rim_cols : rim_cols + cols] = total[0:edge_rows, :] * slope[...]
    three = remote(edge, ahead, send_sem.at[2], recv_sem.at[2], before)

    @pl.when(d > 0)
    def _():
        three.start()

    @pl.when(d == n - 1)
    def _():
        ahead[...] = jnp.zeros_like(ahead)

    @pl.when(d < n - 1)
    def _():
        three.wait_recv()

    @pl.when(d > 0)
    def _():
        three.wait_send()

    two.wait_send()


def sum_and_edge(part, slope, rim, cid):
    rows, cols = part.shape
    edge_shape = (rim.shape[0], rim.shape[1] + cols)
    return pl.pallas_call(
        partial(edge_kernel, lax.axis_size("dp")),
        out_shape=[
            jax.ShapeDtypeStruct(part.shape, F32),
            jax.ShapeDtypeStruct(edge_shape, F32),
        ],
        in_specs=[VM] * 3,
        out_specs=[VM] * 2,
        scratch_shapes=[
            pltpu.VMEM((rows, cols), BF),
            pltpu.VMEM((rows, cols), F32),
            pltpu.VMEM((rows, cols), BF),
            pltpu.VMEM(edge_shape, F32),
            pltpu.SemaphoreType.DMA((3,)),
            pltpu.SemaphoreType.DMA((3,)),
        ],
        compiler_params=pltpu.CompilerParams(
            collective_id=cid, has_side_effects=True, vmem_limit_bytes=32 * 1024 * 1024
        ),
    )(part, slope, rim)


def head_pair(pair, first, second):
    lane = lax.broadcasted_iota(jnp.int32, first.shape, 1)
    return jnp.where(lane < LANES // 2, first, second)


def visible_pairs(seg_col, seg_row):
    length = seg_col.shape[0]
    row = lax.broadcasted_iota(jnp.int32, (length, length), 0)
    col = lax.broadcasted_iota(jnp.int32, (length, length), 1)
    return (row >= col) & (seg_col == seg_row)


def state_decay(entry, expand):
    last = entry[entry.shape[0] - 1 :, :]
    spread = jnp.broadcast_to(last, (LANES, LANES)).T
    return dot(expand, spread, ((0,), (0,)), HIGH)


def recur_kernel(
    pairs,
    values,
    write,
    read,
    cumul,
    cumul_t,
    step_t,
    entry,
    tail,
    seg_col,
    seg_row,
    expand,
    skip,
    start,
    out,
    kept,
    state,
):
    @pl.when(pl.program_id(0) == 0)
    def _():
        state[...] = start[...]

    held = state[...]
    kept[0] = held
    v, b, c = values[...], write[...], read[...]
    scores = dot(c, b, ((1,), (1,)), HIGH)
    visible = visible_pairs(seg_col[...], seg_row[...])
    entry_full = dot(entry[...], expand[...], precision=HIGH)
    tail_full = dot(tail[...], expand[...], precision=HIGH)
    carried = entry_full * dot(c, held, ((1,), (1,)), HIGH) + skip[...] * v
    cum, cum_t, st_t = cumul[...], cumul_t[...], step_t[...]
    for pair in range(pairs):
        cols = slice(pair * LANES, (pair + 1) * LANES)
        v2 = v[:, cols]
        found = []
        for h in (2 * pair, 2 * pair + 1):
            spread = jnp.where(visible, cum[:, h : h + 1] - cum_t[h : h + 1, :], MASKED)
            mixing = jnp.exp(spread) * (scores * st_t[h : h + 1, :])
            found.append(dot_three(mixing, v2, (1, 0)))
        out[:, cols] = head_pair(pair, found[0], found[1]) + carried[:, cols]
    state[...] = state_decay(entry[...], expand[...]) * held + dot(v * tail_full, b, ((0,), (0,)), HIGH)


def recur_specs(width, lengths):
    def rows(cols):
        return pl.BlockSpec((BLK, cols), lambda i: (lengths(i), 0))

    def flat(count):
        return pl.BlockSpec((count, BLK), lambda i: (0, lengths(i)))

    def whole(shape):
        return pl.BlockSpec(shape, lambda i: (0,) * len(shape))

    return rows, flat, whole


def recur_forward(v, b, c, cumul, cumul_t, step_t, entry, tail, seg_col, seg_row, expand, skip, start):
    total, width = v.shape
    blocks = total // BLK
    rows, flat, whole = recur_specs(width, lambda i: i)
    return pl.pallas_call(
        partial(recur_kernel, width // LANES),
        grid=(blocks,),
        out_shape=[
            jax.ShapeDtypeStruct((total, width), F32),
            jax.ShapeDtypeStruct((blocks, width, LANES), F32),
        ],
        in_specs=[
            rows(width),
            rows(LANES),
            rows(LANES),
            rows(LANES),
            flat(16),
            flat(16),
            rows(LANES),
            rows(LANES),
            rows(1),
            flat(1),
            whole((LANES, width)),
            whole((1, width)),
            whole((width, LANES)),
        ],
        out_specs=[
            rows(width),
            pl.BlockSpec((1, width, LANES), lambda i: (i, 0, 0)),
        ],
        scratch_shapes=[pltpu.VMEM((width, LANES), F32)],
        compiler_params=pltpu.CompilerParams(vmem_limit_bytes=48 * 1024 * 1024),
    )(v, b, c, cumul, cumul_t, step_t, entry, tail, seg_col, seg_row, expand, skip, start)


def adjoint_kernel(
    pairs,
    values,
    write,
    read,
    cumul,
    cumul_t,
    step_t,
    step,
    entry,
    tail_bare,
    seg_col,
    seg_row,
    expand,
    skip,
    kept,
    d_out,
    start,
    d_values,
    d_write,
    d_read,
    d_step,
    d_rate_step,
    d_skip,
    state,
    columns,
):
    @pl.when(pl.program_id(0) == 0)
    def _():
        state[...] = start[...]
        d_skip[...] = jnp.zeros_like(d_skip)
        columns[...] = jnp.zeros_like(columns)

    length = values.shape[0]
    lam, held = state[...], kept[0]
    v, b, c, dy = values[...], write[...], read[...], d_out[...]
    ex = expand[...]
    st = step[...]
    scores = dot(c, b, ((1,), (1,)), HIGH)
    visible = visible_pairs(seg_col[...], seg_row[...])
    entry_full = dot(entry[...], ex, precision=HIGH)
    tail = tail_bare[...] * st
    tail_full = dot(tail, ex, precision=HIGH)
    c_state = dot(c, held, ((1,), (1,)), HIGH)
    b_lam = dot(b, lam, ((1,), (1,)), HIGH)
    dy_in = dy * entry_full
    v_out = v * tail_full
    dc = dot(dy_in, held, precision=HIGH)
    db = dot(v_out, lam, precision=HIGH)
    reach = dot(dy_in * c_state, ex, ((1,), (1,)), HIGH)
    leave = dot(v * b_lam, ex, ((1,), (1,)), HIGH)
    d_skip[...] += jnp.sum(dy * v, axis=0, keepdims=True)
    dv_far = tail_full * b_lam + skip[...] * dy
    cum, cum_t, st_t = cumul[...], cumul_t[...], step_t[...]
    lane = lax.broadcasted_iota(jnp.int32, (length, LANES), 1)
    d_scores = jnp.zeros((length, length), F32)
    row_sums = jnp.zeros((length, LANES), F32)
    for pair in range(pairs):
        cols = slice(pair * LANES, (pair + 1) * LANES)
        v2, dy2 = v[:, cols], dy[:, cols]
        found = []
        for j in range(2):
            h = 2 * pair + j
            own = (lane < LANES // 2) if j == 0 else (lane >= LANES // 2)
            d_mix = dot_three(jnp.where(own, dy2, 0.0), v2, (1, 1))
            spread = jnp.where(visible, cum[:, h : h + 1] - cum_t[h : h + 1, :], MASKED)
            decay = jnp.exp(spread)
            decay_step = decay * st_t[h : h + 1, :]
            weighted = d_mix * scores * decay
            d_scores = d_scores + d_mix * decay_step
            columns[h : h + 1, :] = jnp.sum(weighted, axis=0, keepdims=True)
            per_row = jnp.sum(weighted * st_t[h : h + 1, :], axis=1, keepdims=True)
            row_sums = jnp.where(lane == h, per_row, row_sums)
            found.append(dot(scores * decay_step, dy2, ((0,), (0,))))
        d_values[:, cols] = head_pair(pair, found[0], found[1]) + dv_far[:, cols]
    d_read[...] = dc + dot(d_scores, b, precision=HIGH)
    d_write[...] = db + dot(d_scores, c, ((0,), (0,)), HIGH)
    col_sums = columns[...].T
    leave_step = tail * leave
    d_step[...] = col_sums + tail_bare[...] * leave
    d_cum = row_sums - st * col_sums + reach - leave_step
    row = lax.broadcasted_iota(jnp.int32, (length, length), 0)
    col = lax.broadcasted_iota(jnp.int32, (length, length), 1)
    upper = (col >= row).astype(F32)
    met = jnp.sum(dot(lam * held, ex, ((0,), (1,)), HIGH), axis=0, keepdims=True)
    at_end = jnp.sum(leave_step, axis=0, keepdims=True) + entry[length - 1 :, :] * met
    d_rate_step[...] = dot(upper, d_cum, precision=HIGH) + at_end
    state[...] = state_decay(entry[...], ex) * lam + dot(dy_in, c, ((0,), (0,)), HIGH)


def recur_backward(
    v, b, c, cumul, cumul_t, step_t, step, entry, tail_bare, seg_col, seg_row, expand, skip, kept, dy, start
):
    total, width = v.shape
    blocks = total // BLK
    rows, flat, whole = recur_specs(width, lambda i: blocks - 1 - i)
    return pl.pallas_call(
        partial(adjoint_kernel, width // LANES),
        grid=(blocks,),
        out_shape=[
            jax.ShapeDtypeStruct((total, width), F32),
            jax.ShapeDtypeStruct((total, LANES), F32),
            jax.ShapeDtypeStruct((total, LANES), F32),
            jax.ShapeDtypeStruct((total, LANES), F32),
            jax.ShapeDtypeStruct((total, LANES), F32),
            jax.ShapeDtypeStruct((1, width), F32),
        ],
        in_specs=[
            rows(width),
            rows(LANES),
            rows(LANES),
            rows(LANES),
            flat(16),
            flat(16),
            rows(LANES),
            rows(LANES),
            rows(LANES),
            rows(1),
            flat(1),
            whole((LANES, width)),
            whole((1, width)),
            pl.BlockSpec((1, width, LANES), lambda i: (blocks - 1 - i, 0, 0)),
            rows(width),
            whole((width, LANES)),
        ],
        out_specs=[
            rows(width),
            rows(LANES),
            rows(LANES),
            rows(LANES),
            rows(LANES),
            whole((1, width)),
        ],
        scratch_shapes=[pltpu.VMEM((width, LANES), F32), pltpu.VMEM((LANES, LANES), F32)],
        compiler_params=pltpu.CompilerParams(vmem_limit_bytes=48 * 1024 * 1024),
    )(v, b, c, cumul, cumul_t, step_t, step, entry, tail_bare, seg_col, seg_row, expand, skip, kept, dy, start)


def state_scan_kernel(
    n,
    reverse,
    mine,
    decay,
    expand,
    out,
    first,
    second,
    got_first,
    got_second,
    half,
    got_half,
    send_sem,
    recv_sem,
):
    d = lax.axis_index("dp")
    q = n - 1 - d if reverse else d
    zq, xq = q // 2, q % 2
    depth = n // 2
    rows = mine.shape[0] // 2
    xf = xq.astype(F32)
    sent_type = first.dtype

    def device(logical):
        return {"dp": n - 1 - logical if reverse else logical}

    beside = device(2 * zq + 1 - xq)
    others = [device(2 * ((zq + k) % depth) + xq) for k in range(1, depth)]
    own_rows = pl.ds(pl.multiple_of(rows * xq, 16), rows)
    other_rows = pl.ds(pl.multiple_of(rows * (1 - xq), 16), rows)
    own_lanes = pl.ds(pl.multiple_of(rows * xq, LANES), rows)
    tail = pl.ds(rows, 16)
    body = pl.ds(0, rows)
    row = lax.broadcasted_iota(jnp.int32, (16, LANES), 0)

    def spread(values):
        square = jnp.broadcast_to(values, (LANES, LANES)).T
        return dot(expand[:, own_lanes], square, ((0,), (0,)), HIGH)

    def two_terms(values):
        high = values.astype(sent_type).astype(F32)
        wide = jnp.where(row == 0, high, jnp.where(row == 1, values - high, 0.0))
        return wide.astype(sent_type)

    def one_term(block):
        return block[0:1, :].astype(F32) + block[1:2, :].astype(F32)

    for k in range(1, depth):

        @pl.when(zq < k)
        def _():
            got_second[k - 1] = jnp.zeros(got_second.shape[1:], sent_type)

    own_decay = decay[0:1, :]
    first[body, :] = mine[other_rows, :].astype(sent_type)
    first[tail, :] = two_terms(own_decay)
    greet([beside] + others)
    one = remote(first, got_first, send_sem.at[0], recv_sem.at[0], beside)
    one.start()
    one.wait_recv()
    own = mine[own_rows, :]
    got, got_decay = got_first[body, :].astype(F32), one_term(got_first[tail, :])
    early = own * (1.0 - xf) + got * xf
    early_decay = own_decay * (1.0 - xf) + got_decay * xf
    late = own * xf + got * (1.0 - xf)
    late_decay = own_decay * xf + got_decay * (1.0 - xf)
    second[body, :] = (spread(late_decay) * early + late).astype(sent_type)
    second[tail, :] = two_terms(early_decay * late_decay)
    sent = []
    for k in range(1, depth):
        copy = remote(
            second, got_second.at[k - 1], send_sem.at[k], recv_sem.at[k], device(2 * ((zq + k) % depth) + xq)
        )
        sent.append(copy)

        @pl.when(zq + k < depth)
        def _():
            copy.start()

    early_spread = spread(early_decay)
    total = jnp.zeros((rows, LANES), F32)
    for k in range(depth - 1, 0, -1):

        @pl.when(zq >= k)
        def _():
            sent[k - 1].wait_recv()

        got_k = got_second.at[k - 1]
        total = spread(one_term(got_k[tail, :])) * total + got_k[body, :].astype(F32)
    after = early_spread * total + early
    half[...] = (total * xf + after * (1.0 - xf)).astype(sent_type)
    last = remote(half, got_half, send_sem.at[depth], recv_sem.at[depth], beside)
    last.start()
    out[own_rows, :] = total * (1.0 - xf) + after * xf
    last.wait_recv()
    out[other_rows, :] = got_half[...].astype(F32)
    one.wait_send()
    last.wait_send()
    for k in range(1, depth):

        @pl.when(zq + k < depth)
        def _():
            sent[k - 1].wait_send()


def state_scan(mine, decay, expand, reverse, cid, sent_type):
    n = lax.axis_size("dp")
    half = mine.shape[0] // 2
    depth = n // 2
    message = (half + 16, LANES)
    return pl.pallas_call(
        partial(state_scan_kernel, n, reverse),
        out_shape=jax.ShapeDtypeStruct(mine.shape, F32),
        in_specs=[VM] * 3,
        out_specs=VM,
        scratch_shapes=[
            pltpu.VMEM(message, sent_type),
            pltpu.VMEM(message, sent_type),
            pltpu.VMEM(message, sent_type),
            pltpu.VMEM((depth - 1,) + message, sent_type),
            pltpu.VMEM((half, LANES), sent_type),
            pltpu.VMEM((half, LANES), sent_type),
            pltpu.SemaphoreType.DMA((depth + 1,)),
            pltpu.SemaphoreType.DMA((depth + 1,)),
        ],
        compiler_params=pltpu.CompilerParams(
            collective_id=cid, has_side_effects=True, vmem_limit_bytes=32 * 1024 * 1024
        ),
    )(mine, decay, expand)


def pick_matrix(position, own):
    length = position.shape[1]
    slot = lax.broadcasted_iota(jnp.int32, (CAP, length), 0).astype(F32)
    parts = [
        jnp.where(position[e : e + 1, :] == slot, 1.0, 0.0).astype(BF) for e in range(own)
    ]
    return jnp.concatenate(parts, axis=0)


def pick_gate_kernel(own, x, position, routes, router, out, gates, slot_gates):
    rows = x[0]
    pick = pick_matrix(position[0], own)
    picked = dot(pick, rows).astype(BF)
    out[...] = picked.reshape(out.shape)
    logits = dot(rows, router[...])
    lane = lax.broadcasted_iota(jnp.int32, logits.shape, 1).astype(F32)
    named = routes[0][:, 0:1] == lane
    for k in range(1, TOPK):
        named = named | (routes[0][:, k : k + 1] == lane)
    top = jnp.max(jnp.where(named, logits, MASKED), axis=1, keepdims=True)
    powers = jnp.where(named, jnp.exp(jnp.minimum(logits - top, 0.0)), 0.0)
    gate = powers / jnp.sum(powers, axis=1, keepdims=True)
    gates[0] = gate
    high = gate.astype(BF)
    low = (gate - high.astype(F32)).astype(BF)
    of_slot = dot(pick, high) + dot(pick, low)
    row = lax.broadcasted_iota(jnp.int32, of_slot.shape, 0)
    col = lax.broadcasted_iota(jnp.int32, of_slot.shape, 1)
    mine = col - lax.axis_index("dp") * own == row // CAP
    of_slot = jnp.sum(jnp.where(mine, of_slot, 0.0), axis=1, keepdims=True)
    slot_gates[...] = jnp.broadcast_to(of_slot, pick.shape[:1] + (LANES,)).reshape(slot_gates.shape)


def slot_spec(own, cols):
    return pl.BlockSpec((own, 1, CAP, cols), lambda s: (0, s, 0, 0))


def token_spec(rows, cols):
    return pl.BlockSpec((1, rows, cols), lambda s: (s, 0, 0))


BIG = pltpu.CompilerParams(vmem_limit_bytes=56 * 1024 * 1024)


def pick_rows_gates(x, position, routes, router):
    n, tokens, model = x.shape
    own = position.shape[1]
    return pl.pallas_call(
        partial(pick_gate_kernel, own),
        grid=(n,),
        out_shape=[
            jax.ShapeDtypeStruct((own, n, CAP, model), BF),
            jax.ShapeDtypeStruct((n, tokens, LANES), F32),
            jax.ShapeDtypeStruct((own, n, CAP, LANES), F32),
        ],
        in_specs=[
            token_spec(tokens, model),
            token_spec(own, tokens),
            token_spec(tokens, TOPK),
            pl.BlockSpec((model, LANES), lambda s: (0, 0)),
        ],
        out_specs=[slot_spec(own, model), token_spec(tokens, LANES), slot_spec(own, LANES)],
        compiler_params=BIG,
    )(x, position, routes, router)


def expert_kernel(
    own, rows, cot_rows, gate, w_in, w_out, grad_in, grad_out, d_rows, res, dots, wide, both
):
    e, part = pl.program_id(0), pl.program_id(1)
    model = rows.shape[2]
    units = w_out.shape[1]

    @pl.when(part == 0)
    def _():
        wide[...] = w_in[0].astype(F32)
        both[:, 0:units] = wide[pl.ds(0, model, stride=2), :].astype(BF)
        both[:, units : 2 * units] = wide[pl.ds(1, model, stride=2), :].astype(BF)
        grad_in[...] = jnp.zeros_like(grad_in)
        grad_out[...] = jnp.zeros_like(grad_out)

    x, c, g = rows[0], cot_rows[0], gate[0]
    mid = dot(x, both[...])
    mid_gate, mid_up = mid[:, 0:units], mid[:, units : 2 * units]
    sig = jax.nn.sigmoid(mid_gate)
    mid_silu = mid_gate * sig
    act = (mid_silu * mid_up).astype(BF).astype(F32)
    back = dot(c, w_out[0], ((1,), (1,)))
    dot_sum = jnp.sum(act * back, axis=1, keepdims=True)
    lane = lax.broadcasted_iota(jnp.int32, g.shape, 1)
    dots[0] = jnp.where(lane == lax.axis_index("dp") * own + e, dot_sum, 0.0).astype(BF)
    gated = (act * g).astype(BF)
    d_act = back * g
    d_gate = (d_act * mid_up * (sig * (1.0 + mid_gate * (1.0 - sig)))).astype(BF)
    d_mid = jnp.concatenate([d_gate, (d_act * mid_silu).astype(BF)], axis=1)
    grads = dot(x, d_mid, ((0,), (0,)))
    grad_in[0, pl.ds(0, model, stride=2), :] += grads[:, 0:units]
    grad_in[0, pl.ds(1, model, stride=2), :] += grads[:, units : 2 * units]
    grad_out[0] += dot(gated, c, ((0,), (0,)))
    d_rows[0] = dot(d_mid, both[...], ((1,), (1,))).astype(BF)
    res[0] = dot(gated, w_out[0]).astype(BF)


def run_experts(rows, cot_rows, gate, w_in, w_out):
    own, slots, model = rows.shape
    units = w_out.shape[1]
    part = min(slots, 512)

    def slot(cols):
        return pl.BlockSpec((1, part, cols), lambda e, j: (e, j, 0))

    def weight(a, b):
        return pl.BlockSpec((1, a, b), lambda e, j: (e, 0, 0))

    return pl.pallas_call(
        partial(expert_kernel, own),
        grid=(own, slots // part),
        out_shape=[
            jax.ShapeDtypeStruct((own, 2 * model, units), F32),
            jax.ShapeDtypeStruct((own, units, model), F32),
            jax.ShapeDtypeStruct((own, slots, model), BF),
            jax.ShapeDtypeStruct((own, slots, model), BF),
            jax.ShapeDtypeStruct((own, slots, LANES), BF),
        ],
        in_specs=[slot(model), slot(model), slot(LANES), weight(2 * model, units), weight(units, model)],
        out_specs=[weight(2 * model, units), weight(units, model), slot(model), slot(model), slot(LANES)],
        scratch_shapes=[pltpu.VMEM((2 * model, units), F32), pltpu.VMEM((model, 2 * units), BF)],
        compiler_params=BIG,
    )(rows, cot_rows, gate, w_in, w_out)


def put_matrix(position, own):
    length = position.shape[0]
    lane = lax.broadcasted_iota(jnp.int32, (length, LANES), 1)
    slot = (lane % CAP).astype(F32)
    parts = []
    for e in range(0, own, 2):
        held = jnp.where(lane < CAP, position[:, e : e + 1], position[:, e + 1 : e + 2])
        parts.append(jnp.where(held == slot, 1.0, 0.0).astype(BF))
    return jnp.concatenate(parts, axis=1)


def put_kernel(own, k, position, *refs):
    out = refs[-1]
    put = put_matrix(position[0], own)
    here = jnp.where(pl.program_id(0) == lax.axis_index("dp"), 1.0, 0.0)
    start = 0
    for i in range(k):
        rows, shared = refs[2 * i], refs[2 * i + 1]
        cols = shared.shape[1]
        total = dot(put, rows[...].reshape(own * CAP, cols))
        out[0, :, start : start + cols] = (total + here * shared[...]).astype(BF)
        start += cols
    if len(refs) > 2 * k + 1:
        extra = refs[2 * k]
        out[0, :, start : start + LANES] = dot(put, extra[...].reshape(own * CAP, LANES)).astype(BF)


def put_rows(position, parts, extra=None):
    n, tokens, own = position.shape
    args, specs, cols = [], [], 0
    for rows, shared in parts:
        model = shared.shape[1]
        args += [rows.reshape(own, n, CAP, model), shared]
        specs += [slot_spec(own, model), pl.BlockSpec((tokens, model), lambda s: (0, 0))]
        cols += model
    if extra is not None:
        args.append(extra.reshape(own, n, CAP, LANES))
        specs.append(slot_spec(own, LANES))
        cols += LANES
    return pl.pallas_call(
        partial(put_kernel, own, len(parts)),
        grid=(n,),
        out_shape=jax.ShapeDtypeStruct((n, tokens, cols), BF),
        in_specs=[token_spec(tokens, own)] + specs,
        out_specs=token_spec(tokens, cols),
        compiler_params=BIG,
    )(position, *args)


def grads_kernel(k, *refs):
    lefts, rights, out = refs[:k], refs[k : 2 * k], refs[2 * k]
    start = 0
    for left, right in zip(lefts, rights):
        cols = right.shape[1]
        out[:, start : start + cols] = dot(left[...], right[...], ((0,), (0,))).astype(BF)
        start += cols


def weight_grads(pairs):
    k = len(pairs)
    tokens, model = pairs[0][0].shape
    block = 256
    cols = sum(right.shape[1] for _, right in pairs)
    return pl.pallas_call(
        partial(grads_kernel, k),
        grid=(model // block,),
        out_shape=jax.ShapeDtypeStruct((model, cols), BF),
        in_specs=[pl.BlockSpec((tokens, block), lambda i: (0, i)) for _ in pairs]
        + [pl.BlockSpec(right.shape, lambda i: (0, 0)) for _, right in pairs],
        out_specs=pl.BlockSpec((block, cols), lambda i: (i, 0)),
        compiler_params=BIG,
    )(*[left for left, _ in pairs], *[right for _, right in pairs])


def combine_states(states, decays, expand, reverse):
    n = states.shape[0]
    place = lax.axis_index("dp")
    wide = dot(decays, expand, precision=HIGH)
    state = jnp.zeros(states.shape[1:], F32)
    for j in range(n):
        source = n - 1 - j if reverse else j
        use = source > place if reverse else source < place
        fresh = wide[source][:, None] * state + states[source]
        state = jnp.where(use, fresh, state)
    return state


def incoming_state(mine, decay, expand, reverse, cid):
    if lax.axis_size("dp") == 8:
        return state_scan(
            mine, jnp.broadcast_to(decay, (8, LANES)), expand, reverse, cid, BF if reverse else F32
        )
    rows = jnp.pad(decay, ((0, 31), (0, 0)))
    (gathered,) = gather_dp([jnp.concatenate([mine, rows], axis=0)], cid)
    width = mine.shape[0]
    return combine_states(gathered[:, :width], gathered[:, width], expand, reverse)


def per_device(
    hidden,
    segment_ids,
    routes,
    norm_gain,
    mixer_in,
    state_in,
    step_in,
    conv_value,
    conv_value_bias,
    conv_state,
    conv_state_bias,
    head_params,
    gated_gain,
    mixer_out,
    ffn_gain,
    router,
    shared_in,
    shared_out,
    expert_in,
    expert_out,
    cotangent,
):
    n = lax.axis_size("dp")
    place, mp_place = lax.axis_index("dp"), lax.axis_index("mp")
    tokens, model = hidden.shape
    shard = model // n
    inner = mixer_in.shape[2]
    state_cols = state_in.shape[1]
    taps = conv_value.shape[0]
    heads = head_params.shape[1]
    width = inner // heads
    own_experts = expert_in.shape[0]
    hidden_units = shared_out.shape[0]
    quarter = tokens // 4

    misc_parts = [
        conv_value.reshape(-1),
        conv_value_bias.reshape(-1),
        gated_gain.reshape(-1),
        conv_state.reshape(-1),
        conv_state_bias,
        norm_gain,
        ffn_gain,
    ]
    misc = jnp.concatenate(misc_parts)
    route_rows = routes.T.reshape(-1, model).astype(BF)
    small = jnp.concatenate(
        [
            jnp.pad(misc, (0, model - misc.shape[0]))[None],
            route_rows,
            hidden[tokens - 15 + route_rows.shape[0] :],
        ],
        axis=0,
    )
    pack_a = jnp.concatenate(
        [
            mixer_in.reshape(shard, 2 * inner),
            state_in,
            jnp.pad(step_in, ((0, 0), (0, LANES - heads))),
        ],
        axis=1,
    )
    pack_b = jnp.concatenate(
        [
            mixer_out.T,
            shared_in.reshape(shard, 2 * hidden_units),
            shared_out.T,
            jnp.pad(router, ((0, 0), (0, LANES - EXPERTS))),
        ],
        axis=1,
    )
    mine_cot = lax.dynamic_slice_in_dim(cotangent, mp_place * quarter, quarter, 0)
    weight_a, small_all, cot_all = first_gather([pack_a, small], mine_cot, 0)
    weight_a = weight_a.reshape(model, -1)
    cot_all = cot_all.reshape(n, tokens, model)
    pack_b, small_all = lax.optimization_barrier((pack_b, small_all))
    weight_b = lax.all_gather(pack_b, "dp", axis=0, tiled=True)
    out_t = weight_b[:, :inner]
    shared_w = weight_b[:, inner : inner + 2 * hidden_units]
    shared_out_t = weight_b[:, inner + 2 * hidden_units : inner + 3 * hidden_units]
    router_w = weight_b[:, inner + 3 * hidden_units :]

    pieces = []
    start = 0
    for part in misc_parts:
        pieces.append(small_all[:, 0, start : start + part.shape[0]].astype(F32))
        start += part.shape[0]
    local_p = conv_value.shape[1]
    value_rows = jnp.concatenate(pieces[:3], axis=1).reshape(n, taps + 2, local_p, heads)
    value_rows = value_rows.transpose(1, 3, 0, 2).reshape(taps + 2, inner)
    state_rows = jnp.concatenate(pieces[3:5], axis=1).reshape(n, taps + 1, state_cols // n)
    state_rows = state_rows.transpose(1, 0, 2).reshape(taps + 1, state_cols)
    gain_first = pieces[5].reshape(1, model)
    gain_second = pieces[6].reshape(1, model)
    conv_taps = jnp.concatenate([value_rows[:taps], state_rows[:taps]], axis=1)
    conv_bias = jnp.concatenate([value_rows[taps], state_rows[taps]])[None]
    gated_row = value_rows[taps + 1][None]

    group_start = place * tokens
    seg_padded = jnp.concatenate([jnp.full((taps - 1,), -1, jnp.int32), segment_ids])
    seg_ext = lax.dynamic_slice_in_dim(seg_padded, group_start, tokens + taps - 1)
    segments = seg_ext[taps - 1 :]
    prev_seg = seg_ext[taps - 2]
    same = [
        (seg_ext[k : k + tokens] == segments).astype(F32)[:, None] for k in range(taps)
    ]
    blocks = tokens // BLK
    seg_blocks = segments.reshape(blocks, BLK)
    last_segs = seg_blocks[:, BLK - 1]
    prev_segs = jnp.concatenate([prev_seg[None], last_segs[:-1]])
    entry_ok = (seg_blocks == prev_segs[:, None]).astype(F32).reshape(tokens, 1)
    tail_ok = (seg_blocks == last_segs[:, None]).astype(F32).reshape(tokens, 1)
    group_entry_ok = (segments == prev_seg).astype(F32)[:, None]
    group_tail_ok = (segments == segments[tokens - 1]).astype(F32)[:, None]
    seg_f = segments.astype(F32)
    seg_col, seg_row = seg_f[:, None], seg_f[None, :]

    behind = lax.dynamic_index_in_dim(small_all, (place + n - 1) % n, 0, False)
    hidden_ext = jnp.concatenate([behind, hidden], axis=0).astype(F32)
    inv_ext = lax.rsqrt(jnp.mean(hidden_ext * hidden_ext, axis=1, keepdims=True) + EPS)
    normed_ext = (hidden_ext * inv_ext * gain_first).astype(BF)
    normed = normed_ext[16:]
    zx_ext = dot(normed_ext, weight_a)
    gate_z = zx_ext[16:, :inner]
    pre_ext = zx_ext[16 - taps + 1 :, inner : 2 * inner + state_cols]
    head_local = head_params.astype(F32)
    dt_lanes = zx_ext[16:, 2 * inner + state_cols :]
    conv = jnp.broadcast_to(conv_bias, (tokens, inner + state_cols))
    for k in range(taps):
        conv = conv + conv_taps[k][None] * pre_ext[k : k + tokens] * same[k]
    act = jax.nn.silu(conv)
    values = act[:, :inner]
    write = act[:, inner : inner + state_cols // 2]
    read = act[:, inner + state_cols // 2 :]

    live = (jnp.arange(LANES) < heads)[None]
    head_pad = jnp.pad(head_local, ((0, 0), (0, LANES - heads)))
    rate = jnp.where(live, -jnp.exp(head_pad[0:1]), 0.0)
    step = jnp.where(live, jax.nn.softplus(dt_lanes + head_pad[1:2]), 0.0)
    rated = (step * rate).reshape(blocks, BLK, LANES)
    lower = jnp.tril(jnp.ones((BLK, BLK), F32))
    cumul_b = jnp.einsum("ts,bsh->bth", lower, rated, precision=HIGH)
    totals = cumul_b[:, BLK - 1]
    zero_row = jnp.zeros((1, LANES), F32)
    before, after = [zero_row], [zero_row]
    for i in range(blocks - 1):
        before.append(before[-1] + totals[i][None])
        after.append(after[-1] + totals[blocks - 1 - i][None])
    before = jnp.stack(before)
    after = jnp.stack(after[::-1])
    cumul = cumul_b.reshape(tokens, LANES)
    to_end = totals[:, None] - cumul_b
    entry = jnp.exp(cumul) * entry_ok
    tail_bare = jnp.exp(to_end).reshape(tokens, LANES) * tail_ok
    tail = tail_bare * step
    group_entry = jnp.exp(cumul_b + before).reshape(tokens, LANES) * group_entry_ok
    group_tail = jnp.exp(to_end + after).reshape(tokens, LANES) * group_tail_ok * step
    cumul_t = cumul[:, :16].T
    step_t = step[:, :16].T
    expand = (jnp.arange(LANES)[:, None] == jnp.arange(inner)[None, :] // width).astype(F32)
    skip = dot(head_pad[2:3], expand, precision=HIGH)
    outgoing = dot(
        values * dot(group_tail, expand, precision=HIGH), write, ((0,), (0,)), HIGH
    )
    group_decay = group_entry[tokens - 1 :]
    incoming = incoming_state(outgoing, group_decay, expand, False, 1)
    ssd, kept = recur_forward(
        values, write, read, cumul, cumul_t, step_t, entry, tail, seg_col, seg_row, expand, skip, incoming
    )

    gate_act = jax.nn.silu(gate_z)
    gated = ssd * gate_act
    scaled = (gated * gated_row).astype(BF)
    proj_part = dot(scaled, out_t, ((1,), (1,)))
    square_part = jnp.sum(gated * gated, axis=1, keepdims=True)
    proj_pack = jnp.concatenate([proj_part, jnp.broadcast_to(square_part, (tokens, LANES))], axis=1)
    proj_sum = scatter_mp(proj_pack.reshape(4, quarter, -1), 2)
    proj = proj_sum[:, :model]
    square = proj_sum[:, model : model + 1]
    inv_gated = lax.rsqrt(square / DI + EPS)
    mine_hidden = lax.dynamic_slice_in_dim(hidden, mp_place * quarter, quarter, 0).astype(F32)
    mixed = mine_hidden + proj * inv_gated
    inv_second = lax.rsqrt(jnp.mean(mixed * mixed, axis=1, keepdims=True) + EPS)
    unit_second = mixed * inv_second
    ffn_mine = (unit_second * gain_second).astype(BF)

    routes_all = small_all[:, 1 : 1 + route_rows.shape[0]].reshape(n, TOPK, tokens)
    routes_cols = routes_all.astype(F32).transpose(0, 2, 1)
    first_expert = place * own_experts
    own_ids = (first_expert + jnp.arange(own_experts, dtype=jnp.int32)).astype(F32)
    named = jnp.any(routes_all.astype(F32)[:, None] == own_ids[None, :, None, None], axis=2)
    earlier = (jnp.arange(tokens)[:, None] < jnp.arange(tokens)[None, :]).astype(BF)
    position = jnp.einsum("set,tu->seu", named.astype(BF), earlier, preferred_element_type=F32)
    position = jnp.where(named, position, -1.0)
    position_cols = position.transpose(0, 2, 1)
    ffn_all, cot_rows = gather_tokens(ffn_mine, cot_all, position, 3)
    ffn_all = ffn_all.reshape(n, tokens, model)

    rows, gates, slot_gates = pick_rows_gates(ffn_all, position, routes_cols, router_w)
    slots = n * CAP
    grad_in_rows, grad_expert_out, d_rows, expert_res, slot_dots = run_experts(
        rows.reshape(own_experts, slots, model),
        cot_rows.reshape(own_experts, slots, model),
        slot_gates.reshape(own_experts, slots, LANES),
        expert_in.reshape(own_experts, 2 * model, -1),
        expert_out,
    )
    grad_expert_in = grad_in_rows.reshape(expert_in.shape)

    ffn_block = lax.dynamic_index_in_dim(ffn_all, place, 0, False)
    shared_mid = dot(ffn_block, shared_w)
    shared_gate, shared_up = shared_mid[:, :hidden_units], shared_mid[:, hidden_units:]
    shared_silu = jax.nn.silu(shared_gate)
    shared_act = (shared_silu * shared_up).astype(BF)
    shared_res = dot(shared_act, shared_out_t, ((1,), (1,)))
    d_shared_act = dot(cotangent, shared_out_t)
    d_shared_mid = jnp.concatenate(
        [d_shared_act * shared_up * silu_slope(shared_gate), d_shared_act * shared_silu], axis=1
    ).astype(BF)
    d_ffn_shared = dot(d_shared_mid, shared_w, ((1,), (1,)))

    if n > 8:
        d_ffn_pack = put_rows(position_cols, [(d_rows, d_ffn_shared)], slot_dots)
        d_ffn_sum = scatter_tokens(d_ffn_pack.reshape(n, 4, quarter, -1), 4)
        expert_res, d_ffn_sum = lax.optimization_barrier((expert_res, d_ffn_sum))
        res_pack = put_rows(position_cols, [(expert_res, shared_res)])
        res_sum = scatter_tokens(res_pack.reshape(n, 4, quarter, model), 10)
    else:
        pack = put_rows(position_cols, [(expert_res, shared_res), (d_rows, d_ffn_shared)], slot_dots)
        both_sums = scatter_tokens(pack.reshape(n, 4, quarter, -1), 4)
        res_sum, d_ffn_sum = both_sums[:, :model], both_sums[:, model:]

    own_tokens_gates = lax.dynamic_slice(
        gates, (place, mp_place * quarter, 0), (1, quarter, LANES)
    ).reshape(quarter, LANES)
    dots = d_ffn_sum[:, model : model + LANES]
    share = jnp.sum(own_tokens_gates * dots, axis=1, keepdims=True)
    d_logits = (own_tokens_gates * (dots - share)).astype(BF)
    d_ffn = d_ffn_sum[:, :model] + dot(d_logits, router_w, ((1,), (1,)))
    mine_cot_f = mine_cot.astype(F32)
    grad_gain_second = jnp.sum(d_ffn * unit_second, axis=0)
    d_unit = d_ffn * gain_second
    d_mixed = mine_cot_f + inv_second * (
        d_unit - unit_second * jnp.mean(d_unit * unit_second, axis=1, keepdims=True)
    )
    d_proj_mine = (d_mixed * inv_gated).astype(BF)
    d_inv = jnp.sum(d_mixed * proj, axis=1, keepdims=True)
    d_square = d_inv * -0.5 * inv_gated * inv_gated * inv_gated / DI
    d_square_high = d_square.astype(BF)
    d_square_low = (d_square - d_square_high.astype(F32)).astype(BF)
    sent = jnp.concatenate(
        [
            d_proj_mine,
            d_logits[:, :EXPERTS],
            d_square_high,
            d_square_low,
            jnp.zeros((quarter, LANES - EXPERTS - 2), BF),
        ],
        axis=1,
    )
    (got,) = gather_mp([sent], 5)
    got = got.reshape(tokens, model + LANES)
    d_proj = got[:, :model]
    d_logits_all = jnp.pad(got[:, model : model + EXPERTS], ((0, 0), (0, LANES - EXPERTS)))
    d_square_all = got[:, model + EXPERTS : model + EXPERTS + 1].astype(F32) + got[
        :, model + EXPERTS + 1 : model + EXPERTS + 2
    ].astype(F32)

    rows0 = ((0,), (0,))
    grad_b = weight_grads(
        [
            (d_proj, scaled),
            (ffn_block, d_shared_mid),
            (cotangent, shared_act),
            (ffn_block, d_logits_all),
        ]
    )
    grad_b, d_proj = lax.optimization_barrier((grad_b, d_proj))
    sum_b = lax.psum_scatter(grad_b, "dp", scatter_dimension=0, tiled=True).astype(F32)
    d_scaled = dot(d_proj, out_t)
    grad_gated_row = jnp.sum(d_scaled * gated, axis=0)
    d_gated = d_scaled * gated_row + 2.0 * gated * d_square_all
    d_ssd = d_gated * gate_act
    d_gate_z = d_gated * ssd * silu_slope(gate_z)

    direct = dot(d_ssd * dot(group_entry, expand, precision=HIGH), read, rows0, HIGH)
    state_grad = incoming_state(direct, group_decay, expand, True, 6)
    d_values, d_write, d_read, d_step, d_rated, d_skip_row = recur_backward(
        values,
        write,
        read,
        cumul,
        cumul_t,
        step_t,
        step,
        entry,
        tail_bare,
        seg_col,
        seg_row,
        expand,
        skip,
        kept,
        d_ssd,
        state_grad,
    )
    d_rate = jnp.sum(d_rated * step, axis=0, keepdims=True)
    d_dt = jnp.where(
        live, (d_step + rate * d_rated) * jax.nn.sigmoid(dt_lanes + head_pad[1:2]), 0.0
    )
    d_skip = dot(d_skip_row, expand, ((1,), (1,)), HIGH)
    grad_head = jnp.concatenate(
        [d_rate * rate, jnp.sum(d_dt, axis=0, keepdims=True), d_skip], axis=0
    )[:, :heads]

    slope = silu_slope(conv)
    d_conv_values = d_values * slope[:, :inner]
    d_state_act, rim_ahead = sum_and_edge(
        jnp.concatenate([d_write, d_read], axis=1), slope[:16, inner:], d_conv_values[:16], 11
    )
    d_conv = jnp.concatenate([d_conv_values, d_state_act * slope[:, inner:]], axis=1)
    d_conv_ext = jnp.concatenate([d_conv, rim_ahead], axis=0)
    seg_after = lax.dynamic_slice_in_dim(
        jnp.concatenate([segment_ids, jnp.full((taps - 1,), -1, jnp.int32)]),
        group_start,
        tokens + taps - 1,
    )
    d_pre = jnp.zeros_like(d_conv)
    grad_rows = []
    for k in range(taps):
        ahead = taps - 1 - k
        ok = (seg_after[ahead : ahead + tokens] == segments).astype(F32)[:, None]
        d_pre = d_pre + conv_taps[k][None] * d_conv_ext[ahead : ahead + tokens] * ok
        grad_rows.append(jnp.sum(d_conv * pre_ext[k : k + tokens] * same[k], axis=0))
    grad_rows.append(jnp.sum(d_conv, axis=0))
    d_a = jnp.concatenate([d_gate_z, d_pre, d_dt], axis=1).astype(BF)

    d_state_mine = lax.dynamic_slice_in_dim(
        d_a[:, 2 * inner : 2 * inner + state_cols], mp_place * quarter, quarter, 0
    )
    d_normed_part = dot(d_a[:, : 2 * inner], weight_a[:, : 2 * inner], ((1,), (1,))) + dot(
        d_a[:, 2 * inner + state_cols :], weight_a[:, 2 * inner + state_cols :], ((1,), (1,))
    )
    d_state_rows = dot(
        d_state_mine, weight_a[:, 2 * inner : 2 * inner + state_cols], ((1,), (1,))
    )
    grad_a = dot(normed, d_a, rows0).astype(BF)
    unit_first = hidden_ext[16:] * inv_ext[16:]
    mine_unit = lax.dynamic_slice_in_dim(unit_first, mp_place * quarter, quarter, 0)
    grad_gain_first = jnp.sum(d_normed_part * unit_first, axis=0) + jnp.sum(
        d_state_rows * mine_unit, axis=0
    )

    value_grads = jnp.stack([g[:inner] for g in grad_rows] + [grad_gated_row])
    value_grads = value_grads.reshape(taps + 2, heads, n, local_p).transpose(2, 0, 3, 1)
    state_grads = jnp.stack([g[inner:] for g in grad_rows])
    state_grads = state_grads.reshape(taps + 1, n, state_cols // n).transpose(1, 0, 2)
    misc_grads = [
        value_grads.reshape(n, -1),
        state_grads.reshape(n, -1),
        jnp.broadcast_to(grad_head.reshape(1, -1), (n, 3 * heads)),
    ]
    sizes = [g.shape[1] for g in misc_grads]
    misc_grads = jnp.concatenate(misc_grads, axis=1)
    misc_grads = jnp.pad(misc_grads, ((0, 0), (0, 32 * LANES - misc_grads.shape[1])))
    gains = jnp.concatenate(
        [grad_gain_first.reshape(n, shard), grad_gain_second.reshape(n, shard)], axis=1
    )
    gains = jnp.pad(gains, ((0, 0), (0, 16 * LANES - 2 * shard)))
    mine_result = (mixed + res_sum).astype(BF)
    sum_a, misc_sum, gains_sum, hidden_all, result = last_exchange(
        grad_a.reshape(n, shard, -1),
        misc_grads.reshape(n, 32, LANES),
        gains.reshape(n, 16, LANES),
        d_normed_part.astype(BF).reshape(4, quarter, model),
        d_state_rows,
        d_mixed,
        mine_hidden,
        gain_first,
        mine_result,
        8,
    )
    result = result.reshape(tokens, model)
    misc_sum = misc_sum.reshape(-1)
    gains_sum = gains_sum.reshape(-1)
    cut = [0]
    for size in sizes:
        cut.append(cut[-1] + size)
    value_sum = misc_sum[: cut[1]].reshape(taps + 2, local_p, heads)
    state_sum = misc_sum[cut[1] : cut[2]].reshape(taps + 1, state_cols // n)
    head_sum = misc_sum[cut[2] : cut[3]].reshape(3, heads)

    b1, b2 = inner, inner + 2 * hidden_units
    b3 = b2 + hidden_units
    return (
        result,
        hidden_all.reshape(tokens, model).astype(F32),
        gains_sum[:shard],
        sum_a[:, : 2 * inner].reshape(shard, 2, inner),
        sum_a[:, 2 * inner : 2 * inner + state_cols],
        sum_a[:, 2 * inner + state_cols : 2 * inner + state_cols + heads],
        value_sum[:taps],
        value_sum[taps],
        state_sum[:taps],
        state_sum[taps],
        head_sum,
        value_sum[taps + 1],
        sum_b[:, :b1].T,
        gains_sum[shard : 2 * shard],
        sum_b[:, b3 : b3 + EXPERTS],
        sum_b[:, b1:b2].reshape(shard, 2, hidden_units),
        sum_b[:, b2:b3].T,
        grad_expert_in,
        grad_expert_out,
    )


def solution(mesh):
    placed = (
        P("dp", None),
        P(),
        P("dp", None),
        P("dp"),
        P("dp", None, "mp"),
        P("dp", None),
        P("dp", "mp"),
        P(None, "dp", "mp"),
        P("dp", "mp"),
        P(None, "dp"),
        P("dp"),
        P(None, "mp"),
        P("dp", "mp"),
        P("mp", "dp"),
        P("dp"),
        P("dp", None),
        P("dp", None, "mp"),
        P("mp", "dp"),
        P("dp", None, None, "mp"),
        P("dp", "mp", None),
        P("dp", None),
    )
    return jax.shard_map(
        per_device,
        mesh=mesh,
        in_specs=placed,
        out_specs=(
            P("dp", None),
            P("dp", None),
            P("dp"),
            P("dp", None, "mp"),
            P("dp", None),
            P("dp", "mp"),
            P(None, "dp", "mp"),
            P("dp", "mp"),
            P(None, "dp"),
            P("dp"),
            P(None, "mp"),
            P("dp", "mp"),
            P("mp", "dp"),
            P("dp"),
            P("dp", None),
            P("dp", None, "mp"),
            P("mp", "dp"),
            P("dp", None, None, "mp"),
            P("dp", "mp", None),
        ),
        check_vma=False,
    )
```

```python
from functools import partial

import jax
import jax.numpy as jnp
from jax import lax
from jax.experimental import pallas as pl
from jax.experimental.pallas import tpu as pltpu
from jax.sharding import PartitionSpec as P

MESH = pl.DeviceIdType.MESH
BLK = 128
EXPERTS = 64
TOPK = 6
DI = 3072
CAP = 64
LANES = 128

EPS = 1e-05
HIGH = lax.Precision.HIGHEST
MASKED = -1e30
BF = jnp.bfloat16
F32 = jnp.float32
ANY = pl.BlockSpec(memory_space=pl.ANY)
VM = pl.BlockSpec(memory_space=pltpu.VMEM)


def dot(a, b, dims=((1,), (0,)), precision=None):
    return lax.dot_general(
        a, b, (dims, ((), ())), precision=precision, preferred_element_type=F32
    )


def two_parts(a):
    high = a.astype(BF)
    return high, (a - high.astype(F32)).astype(BF)


def dot_three(a, b, over):
    a_high, a_low = two_parts(a)
    b_high, b_low = two_parts(b)
    left = jnp.concatenate([a_high, a_low, a_high], axis=over[0])
    right = jnp.concatenate([b_high, b_high, b_low], axis=over[1])
    return dot(left, right, ((over[0],), (over[1],)))


def silu_slope(argument):
    sigmoid_val = jax.nn.sigmoid(argument)
    return sigmoid_val * (1.0 + argument * (1.0 - sigmoid_val))


def chunk_rows(start, size):
    return [(start + i, min(32, size - i)) for i in range(0, size, 32)]


def ring_place(n, d):
    high, low = d // 2, d % 2
    return high * (1 - low) + (n - 1 - high) * low


def ring_device(n, p):
    back = p // (n // 2)
    return (2 * p) * (1 - back) + (2 * (n - 1 - p) + 1) * back


def greet(targets):
    barrier = pltpu.get_barrier_semaphore()
    for target in targets:
        pl.semaphore_signal(barrier, inc=1, device_id=target, device_id_type=MESH)
    pl.semaphore_wait(barrier, len(targets))


def remote(src, dst, send, recv, target):
    return pltpu.make_async_remote_copy(
        src_ref=src,
        dst_ref=dst,
        send_sem=send,
        recv_sem=recv,
        device_id=target,
        device_id_type=MESH,
    )


def mp_partners(m):
    return {"mp": m + 1 - 2 * (m % 2)}, {"mp": (m + 2) % 4}


def ring_neighbours(n):
    p = ring_place(n, lax.axis_index("dp"))
    nxt = {"dp": ring_device(n, (p + 1) % n)}
    prv = {"dp": ring_device(n, (p + n - 1) % n)}
    return p, nxt, prv


class RingGather:
    def __init__(self, n, ins, outs, sems):
        self.n, self.ins, self.outs = n, ins, outs
        self.local_sem, self.send_sem, self.recv_sem = sems
        self.p, self.nxt, self.prv = ring_neighbours(n)
        self.copies = {}

    @staticmethod
    def scratch(n, arrays):
        dma = pltpu.SemaphoreType.DMA
        most = max(len(chunk_rows(0, a.shape[0])) for a in arrays)
        shape = (n // 2, len(arrays), most, 2)
        return [dma((len(arrays),)), dma(shape), dma(shape)]

    def begin(self):
        d = lax.axis_index("dp")
        self.local = []
        for j, (a, out) in enumerate(zip(self.ins, self.outs)):
            copy = pltpu.make_async_copy(a, out.at[d], self.local_sem.at[j])
            copy.start()
            self.local.append(copy)

    def step(self, s):
        n, p = self.n, self.p
        for j, (a, out) in enumerate(zip(self.ins, self.outs)):
            for i, (start, rows) in enumerate(chunk_rows(0, a.shape[0])):
                part = pl.ds(start, rows)
                for way in range(2):
                    origin = ring_device(n, (p + n - s) % n if way == 0 else (p + s) % n)
                    if (s - 1, j, i, way) in self.copies:
                        self.copies[s - 1, j, i, way].wait_recv()
                    if s + 1 < n // 2 or (s + 1 == n // 2 and i % 2 == way):
                        copy = remote(
                            a.at[part] if s == 0 else out.at[origin, part],
                            out.at[origin, part],
                            self.send_sem.at[s, j, i, way],
                            self.recv_sem.at[s, j, i, way],
                            self.nxt if way == 0 else self.prv,
                        )
                        copy.start()
                        self.copies[s, j, i, way] = copy

    def end(self):
        for copy in self.copies.values():
            copy.wait_send()
        for copy in self.local:
            copy.wait()


def gather_kernel(n, k, *refs):
    ring = RingGather(n, refs[:k], refs[k : 2 * k], refs[2 * k :])
    greet([ring.nxt, ring.prv])
    ring.begin()
    for s in range(n // 2 + 1):
        ring.step(s)
    ring.end()


def gather_dp(arrays, cid):
    n, k = lax.axis_size("dp"), len(arrays)
    return pl.pallas_call(
        partial(gather_kernel, n, k),
        out_shape=[jax.ShapeDtypeStruct((n,) + a.shape, a.dtype) for a in arrays],
        in_specs=[ANY] * k,
        out_specs=[ANY] * k,
        scratch_shapes=RingGather.scratch(n, arrays),
        compiler_params=pltpu.CompilerParams(collective_id=cid, has_side_effects=True),
    )(*arrays)


def add_rows(dst, pieces, rows, dtype):
    def body(i, carry):
        sl = pl.ds(pl.multiple_of(i * 16, 16), 16)
        total = pieces[0][sl, :].astype(F32)
        for piece in pieces[1:]:
            total = total + piece[sl, :].astype(F32)
        dst[sl, :] = total.astype(dtype)
        return carry

    lax.fori_loop(0, rows // 16, body, 0)


class RingScatter:
    def __init__(self, n, ins, outs, slots, sems):
        self.n, self.ins, self.outs, self.slots = n, ins, outs, slots
        self.send_sem, self.recv_sem = sems
        self.p, self.nxt, self.prv = ring_neighbours(n)
        self.copies = {}

    @staticmethod
    def scratch(n, arrays):
        most = max(len(chunk_rows(0, a.shape[1])) for a in arrays)
        shape = (n // 2, len(arrays), most, 2)
        return [pltpu.VMEM((n // 2, 2) + a.shape[1:], a.dtype) for a in arrays] + [
            pltpu.SemaphoreType.DMA(shape),
            pltpu.SemaphoreType.DMA(shape),
        ]

    def step(self, s, j):
        n, p = self.n, self.p
        array, out, slots = self.ins[j], self.outs[j], self.slots[j]
        for i, (start, size) in enumerate(chunk_rows(0, array.shape[1])):
            part = pl.ds(start, size)
            if s == n // 2:
                for way in range(2):
                    self.copies[s - 1, j, i, way].wait_recv()
                mine = array.at[ring_device(n, p), part]
                add_rows(out.at[part], [mine, slots.at[s - 1, 0, part], slots.at[s - 1, 1, part]], size, F32)
                continue
            for way in range(2):
                if s == 0 and i % 2 != way:
                    continue
                away = n // 2 - s
                block = ring_device(n, (p + away) % n if way == 0 else (p + n - away) % n)
                source = array.at[block, part]
                if (s - 1, j, i, way) in self.copies:
                    self.copies[s - 1, j, i, way].wait_recv()
                    held = slots.at[s - 1, way, part]
                    add_rows(held, [held, source], size, array.dtype)
                    source = held
                copy = remote(
                    source,
                    slots.at[s, way, part],
                    self.send_sem.at[s, j, i, way],
                    self.recv_sem.at[s, j, i, way],
                    self.nxt if way == 0 else self.prv,
                )
                copy.start()
                self.copies[s, j, i, way] = copy

    def end(self):
        for copy in self.copies.values():
            copy.wait_send()


def last_kernel(
    n,
    grad_a,
    misc,
    gains,
    d_normed,
    extra,
    d_mixed,
    hidden,
    gain,
    result,
    out_a,
    out_misc,
    out_gains,
    all_hidden,
    all_result,
    gains_mine,
    gains_core,
    gains_chip,
    rows_core,
    rows_chip,
    rows_bf,
    slots_a,
    slots_misc,
    slots_gains,
    ring_send,
    ring_recv,
    mp_send,
    mp_recv,
    local_sem,
):
    m = lax.axis_index("mp")
    core, chip = mp_partners(m)
    far = (m + 2) % 4
    beside = m + 1 - 2 * (m % 2)
    ring = RingScatter(
        n,
        [grad_a, misc, gains_mine],
        [out_a, out_misc, out_gains],
        [slots_a, slots_misc, slots_gains],
        [ring_send, ring_recv],
    )
    greet([core, chip, ring.nxt, ring.prv])
    sent = []

    def over_mp(i, source, target, device):
        copy = remote(source, target, mp_send.at[i], mp_recv.at[i], device)
        copy.start()
        sent.append(copy)
        return copy

    ring.step(0, 0)
    ring.step(0, 1)
    gains_one = over_mp(0, gains, gains_core, core)
    rows_far = over_mp(1, d_normed.at[(beside + 2) % 4], rows_core.at[1], core)
    rows_near = over_mp(2, d_normed.at[beside], rows_core.at[0], core)
    own_result = pltpu.make_async_copy(result, all_result.at[m], local_sem.at[0])
    own_result.start()
    gains_one.wait_recv()
    for b in range(n):
        add_rows(gains_mine.at[b], [gains.at[b], gains_core.at[b]], 16, F32)
    gains_two = over_mp(3, gains_mine, gains_chip, chip)
    count = d_mixed.shape[0]
    rows_far.wait_recv()
    add_rows(rows_core.at[1], [rows_core.at[1], d_normed.at[far]], count, BF)
    rows_two = over_mp(4, rows_core.at[1], rows_chip, chip)
    result_chip = over_mp(5, result, all_result.at[m], chip)
    result_core = over_mp(6, result, all_result.at[m], core)
    ring.step(1, 0)
    ring.step(1, 1)
    gains_two.wait()
    for b in range(n):
        add_rows(gains_mine.at[b], [gains_mine.at[b], gains_chip.at[b]], 16, F32)
    ring.step(0, 2)
    rows_near.wait_recv()
    rows_two.wait_recv()

    def body(i, carry):
        sl = pl.ds(pl.multiple_of(i * 16, 16), 16)
        d_n = d_normed[m, sl, :].astype(F32) + rows_core[0, sl, :].astype(F32)
        d_n = d_n + rows_chip[sl, :].astype(F32) + extra[sl, :]
        x = hidden[sl, :].astype(F32)
        inv = lax.rsqrt(jnp.mean(x * x, axis=1, keepdims=True) + EPS)
        unit = x * inv
        d_unit = d_n * gain[...]
        mean = jnp.mean(d_unit * unit, axis=1, keepdims=True)
        rows_bf[sl, :] = (d_mixed[sl, :] + inv * (d_unit - unit * mean)).astype(BF)
        return carry

    lax.fori_loop(0, count // 16, body, 0)
    own_hidden = pltpu.make_async_copy(rows_bf, all_hidden.at[m], local_sem.at[1])
    own_hidden.start()
    hidden_chip = over_mp(7, rows_bf, all_hidden.at[m], chip)
    hidden_core = over_mp(8, rows_bf, all_hidden.at[m], core)
    arrive = []
    for s in range(2, n // 2 + 1):
        ring.step(s, 0)
        ring.step(s, 1)
        ring.step(s - 1, 2)
        if s == 2:
            result_chip.wait_recv()
            arrive.append(over_mp(9, all_result.at[far], all_result.at[far], core))
        if s == n // 2 - 1:
            hidden_chip.wait_recv()
            arrive.append(over_mp(10, all_hidden.at[far], all_hidden.at[far], core))
    ring.step(n // 2, 2)
    for copy in [result_core, hidden_core] + arrive:
        copy.wait_recv()
    own_result.wait()
    own_hidden.wait()
    for copy in sent:
        if copy is not gains_two:
            copy.wait_send()
    ring.end()


def last_exchange(grad_a, misc, gains, d_normed, extra, d_mixed, hidden, gain, result, cid):
    n = lax.axis_size("dp")
    rows, model = d_mixed.shape
    dma = pltpu.SemaphoreType.DMA
    every = jax.ShapeDtypeStruct((4, rows, model), BF)
    return pl.pallas_call(
        partial(last_kernel, n),
        out_shape=[jax.ShapeDtypeStruct(a.shape[1:], F32) for a in (grad_a, misc, gains)] + [every, every],
        in_specs=[VM] * 8 + [ANY],
        out_specs=[VM] * 3 + [ANY] * 2,
        scratch_shapes=[
            pltpu.VMEM(gains.shape, F32),
            pltpu.VMEM(gains.shape, F32),
            pltpu.VMEM(gains.shape, F32),
            pltpu.VMEM((2, rows, model), BF),
            pltpu.VMEM((rows, model), BF),
            pltpu.VMEM((rows, model), BF),
        ]
        + RingScatter.scratch(n, [grad_a, misc, gains])
        + [dma((11,)), dma((11,)), dma((2,))],
        compiler_params=pltpu.CompilerParams(
            collective_id=cid, has_side_effects=True, vmem_limit_bytes=56 * 1024 * 1024
        ),
    )(grad_a, misc, gains, d_normed, extra, d_mixed, hidden, gain, result)


def mp_scatter_kernel(x, out, from_core, from_chip, send_sem, recv_sem):
    m = lax.axis_index("mp")
    core, chip = mp_partners(m)
    mine, far = m, (m + 2) % 4
    beside = m + 1 - 2 * (m % 2)
    parts = [(pl.ds(start, size), size) for start, size in chunk_rows(0, out.shape[0])]
    greet([core, chip])
    first, last = [], []
    for slot, block in ((1, (beside + 2) % 4), (0, beside)):
        for i, (part, _) in enumerate(parts):
            copy = remote(
                x.at[block, part], from_core.at[slot, part], send_sem.at[slot, i], recv_sem.at[slot, i], core
            )
            copy.start()
            first.append(copy)
    for i, (part, size) in enumerate(parts):
        first[i].wait_recv()
        held = from_core.at[1, part]
        add_rows(held, [held, x.at[far, part]], size, x.dtype)
        copy = remote(held, from_chip.at[part], send_sem.at[2, i], recv_sem.at[2, i], chip)
        copy.start()
        last.append(copy)
    for i, (part, size) in enumerate(parts):
        first[len(parts) + i].wait_recv()
        last[i].wait_recv()
        add_rows(out.at[part], [x.at[mine, part], from_core.at[0, part], from_chip.at[part]], size, F32)
    for copy in first + last:
        copy.wait_send()


def scatter_mp(x, cid):
    rows, cols = x.shape[1:]
    count = len(chunk_rows(0, rows))
    return pl.pallas_call(
        mp_scatter_kernel,
        out_shape=jax.ShapeDtypeStruct((rows, cols), F32),
        in_specs=[VM],
        out_specs=VM,
        scratch_shapes=[
            pltpu.VMEM((2, rows, cols), x.dtype),
            pltpu.VMEM((rows, cols), x.dtype),
            pltpu.SemaphoreType.DMA((3, count)),
            pltpu.SemaphoreType.DMA((3, count)),
        ],
        compiler_params=pltpu.CompilerParams(
            collective_id=cid, has_side_effects=True, vmem_limit_bytes=32 * 1024 * 1024
        ),
    )(x)


def mp_gather_kernel(k, *refs):
    ins, outs = refs[:k], refs[k : 2 * k]
    local_sem, send_sem, recv_sem = refs[2 * k :]
    m = lax.axis_index("mp")
    core, chip = mp_partners(m)
    far = (m + 2) % 4
    greet([core, chip])
    copies, local, arrive = [], [], []
    for j in range(k):
        to_chip = remote(ins[j], outs[j].at[m], send_sem.at[0, j], recv_sem.at[0, j], chip)
        to_chip.start()
        to_core = remote(ins[j], outs[j].at[m], send_sem.at[1, j], recv_sem.at[1, j], core)
        to_core.start()
        own = pltpu.make_async_copy(ins[j], outs[j].at[m], local_sem.at[j])
        own.start()
        copies += [to_chip, to_core]
        arrive.append(to_chip)
        local.append(own)
    onward = []
    for j in range(k):
        arrive[j].wait_recv()
        copy = remote(outs[j].at[far], outs[j].at[far], send_sem.at[2, j], recv_sem.at[2, j], core)
        copy.start()
        onward.append(copy)
    for j in range(k):
        copies[2 * j + 1].wait_recv()
        onward[j].wait_recv()
        local[j].wait()
    for copy in copies + onward:
        copy.wait_send()


def gather_mp(arrays, cid):
    k = len(arrays)
    return pl.pallas_call(
        partial(mp_gather_kernel, k),
        out_shape=[jax.ShapeDtypeStruct((4,) + a.shape, a.dtype) for a in arrays],
        in_specs=[ANY] * k,
        out_specs=[ANY] * k,
        scratch_shapes=[
            pltpu.SemaphoreType.DMA((k,)),
            pltpu.SemaphoreType.DMA((3, k)),
            pltpu.SemaphoreType.DMA((3, k)),
        ],
        compiler_params=pltpu.CompilerParams(collective_id=cid, has_side_effects=True),
    )(*arrays)


class TokenGather:
    def __init__(self, n, both, x, out, sems):
        self.n, self.both, self.x, self.out = n, both, x, out
        self.local, self.ring_s, self.ring_r, self.core_s, self.core_r, self.chip_s, self.chip_r = sems
        self.d, self.m = lax.axis_index("dp"), lax.axis_index("mp")
        self.far = (self.m + 2) % 4
        self.core, self.chip = mp_partners(self.m)
        self.p, self.nxt, self.prv = ring_neighbours(n)
        self.pieces = [(0,) + c for c in chunk_rows(0, x.shape[0])] + [(1,) + c for c in chunk_rows(0, both)]
        self.sent, self.pending = [], {}
        self.ring, self.chips = {}, {}

    @staticmethod
    def scratch(n, rows, both):
        dma = pltpu.SemaphoreType.DMA
        own, far = len(chunk_rows(0, rows)), len(chunk_rows(0, both))
        steps = n // 2
        return [
            dma((3,)),
            dma((steps, own + far, 2)),
            dma((steps, own + far, 2)),
            dma((steps + 1, 2 * own + far, 2)),
            dma((steps + 1, 2 * own + far, 2)),
            dma((steps + 1, own, 2)),
            dma((steps + 1, own, 2)),
        ]

    def send(self, source, place, s_sem, r_sem, target):
        copy = remote(source, place, s_sem, r_sem, target)
        copy.start()
        self.sent.append(copy)
        return copy

    def begin(self):
        own = self.out.at[self.d, self.m]
        self.load = pltpu.make_async_copy(self.x, own, self.local.at[0])
        self.load.start()
        self.first = None
        if self.both:
            part = pl.ds(0, self.both)
            self.first = remote(
                self.x.at[part], own.at[part], self.local.at[1], self.local.at[2], self.chip
            )
            self.first.start()
            self.sent.append(self.first)

    def step(self, s, between=None):
        n, p = self.n, self.p
        for k, (is_far, start, rows) in enumerate(self.pieces):
            if k > 0 and between is not None:
                between()
            for way in range(2):
                origin = ring_device(n, (p + n - s) % n if way == 0 else (p + s) % n)
                place = self.far if is_far else self.m
                region = self.out.at[origin, place, pl.ds(start, rows)]
                source = region if s > 0 or is_far else self.x.at[pl.ds(start, rows)]
                if (s - 1, k, way) in self.ring:
                    self.ring[s - 1, k, way].wait_recv()
                elif s > 0:
                    continue
                elif is_far and self.first is not None:
                    self.first.wait_recv()
                    self.first = None
                if s + 1 < n // 2 or (s + 1 == n // 2 and k % 2 == way):
                    self.ring[s, k, way] = self.send(
                        source,
                        region,
                        self.ring_s.at[s, k, way],
                        self.ring_r.at[s, k, way],
                        self.nxt if way == 0 else self.prv,
                    )
                if s == 0 and way == 1:
                    continue
                self.pending.setdefault(s, []).append(
                    self.send(source, region, self.core_s.at[s, k, way], self.core_r.at[s, k, way], self.core)
                )
                if not is_far and start >= self.both:
                    self.chips[s, k, way] = (
                        self.send(
                            source, region, self.chip_s.at[s, k, way], self.chip_r.at[s, k, way], self.chip
                        ),
                        self.out.at[origin, self.far, pl.ds(start, rows)],
                    )

    def pass_on(self, s):
        total = len(self.pieces)
        for k in range(total):
            for way in range(2):
                if (s, k, way) in self.chips:
                    copy, region = self.chips[s, k, way]
                    copy.wait_recv()
                    at = (s, total + k, way)
                    self.pending.setdefault(s, []).append(
                        self.send(region, region, self.core_s.at[at], self.core_r.at[at], self.core)
                    )

    def blocks(self, s):
        n, p = self.n, self.p
        if s in (0, n // 2):
            return [ring_device(n, (p + s) % n)]
        return [ring_device(n, (p + n - s) % n), ring_device(n, (p + s) % n)]

    def complete(self, s):
        if s == 0:
            self.load.wait()
        for copy in self.pending.pop(s):
            copy.wait_recv()

    def end(self):
        for s in sorted(self.pending):
            self.complete(s)
        for copy in self.sent:
            copy.wait_send()


class SlotWork:
    def __init__(self, own, small, router, position, gates, slot_gates, earlier):
        self.own, self.small, self.router = own, small, router
        self.position, self.gates, self.slot_gates, self.earlier = position, gates, slot_gates, earlier
        self.first = (lax.axis_index("dp") * own).astype(F32)
        length = earlier.shape[0]
        row = lax.broadcasted_iota(jnp.int32, (length, length), 0)
        col = lax.broadcasted_iota(jnp.int32, (length, length), 1)
        earlier[...] = jnp.where(row < col, 1.0, 0.0).astype(BF)

    def named(self, block, first, count):
        length = self.earlier.shape[0]
        routes = self.small[block, :, 0:length].astype(F32)
        expert = lax.broadcasted_iota(jnp.int32, (count, length), 0).astype(F32) + first
        found = routes[1:2, :] == expert
        for k in range(2, TOPK + 1):
            found = found | (routes[k : k + 1, :] == expert)
        return found

    def place(self, block):
        named = self.named(block, self.first, 8)
        count = dot(jnp.where(named, 1.0, 0.0).astype(BF), self.earlier[...])
        self.position[block] = jnp.where(named, count, -1.0)[0 : self.own, :]

    def pick(self, block):
        return pick_matrix(self.position[block], self.own)

    def gate(self, block, rows, pick):
        own = self.own
        logits = dot(rows, self.router[...])
        named = jnp.where(self.named(block, 0.0, LANES), 1.0, 0.0).T > 0.5
        top = jnp.max(jnp.where(named, logits, MASKED), axis=1, keepdims=True)
        powers = jnp.where(named, jnp.exp(jnp.minimum(logits - top, 0.0)), 0.0)
        gate = powers / jnp.sum(powers, axis=1, keepdims=True)
        self.gates[block] = gate
        of_slot = dot(pick, jnp.concatenate(two_parts(gate), axis=1))
        of_slot = of_slot[:, 0:LANES] + of_slot[:, LANES : 2 * LANES]
        row = lax.broadcasted_iota(jnp.int32, of_slot.shape, 0)
        col = lax.broadcasted_iota(jnp.int32, of_slot.shape, 1)
        mine = col - lax.axis_index("dp") * own == row // CAP
        of_slot = jnp.sum(jnp.where(mine, of_slot, 0.0), axis=1, keepdims=True)
        of_slot = jnp.broadcast_to(of_slot, (own * CAP, LANES)).reshape(own, CAP, LANES)
        for e in range(own):
            self.slot_gates[e, block] = of_slot[e]


class RowStream:
    def __init__(self, source, target, in_buf, out_buf, load_sem, store_sem):
        self.source, self.target, self.in_buf, self.out_buf = source, target, in_buf, out_buf
        self.load_sem, self.store_sem = load_sem, store_sem
        self.loads, self.stores = [], []

    def load(self, block):
        at = len(self.loads) % 2
        copy = pltpu.make_async_copy(self.source.at[block], self.in_buf.at[at], self.load_sem.at[at])
        copy.start()
        self.loads.append(copy)

    def take(self, i, wait=True):
        if wait:
            self.loads[i].wait()
        held = self.in_buf[i % 2]
        return held.reshape(-1, held.shape[-1])

    def give(self, i, block, picked):
        if i > 1:
            self.stores[i - 2].wait()
        self.out_buf[i % 2] = picked.astype(BF).reshape(self.out_buf.shape[1:])
        copy = pltpu.make_async_copy(
            self.out_buf.at[i % 2], self.target.at[:, block], self.store_sem.at[i % 2]
        )
        copy.start()
        self.stores.append(copy)

    def end(self):
        for copy in self.stores[-2:]:
            copy.wait()


def token_gather_kernel(
    n,
    both,
    own,
    x,
    y,
    small,
    router,
    out,
    y_rows,
    x_rows,
    position,
    gates,
    slot_gates,
    earlier,
    y_in,
    y_out,
    x_in,
    x_out,
    stream_sem,
    *sems,
):
    gather = TokenGather(n, both, x, out, sems)
    work = SlotWork(own, small, router, position, gates, slot_gates, earlier)
    y_stream = RowStream(y, y_rows, y_in, y_out, stream_sem.at[0], stream_sem.at[1])
    x_stream = RowStream(out, x_rows, x_in, x_out, stream_sem.at[2], stream_sem.at[3])
    half = n // 2
    y_stream.load(0)
    greet([gather.core, gather.chip, gather.nxt, gather.prv])
    gather.begin()

    tasks = []

    def pick_y(b):
        held = {}

        def start():
            if b + 1 < n:
                y_stream.load(b + 1)
            held["pick"] = work.pick(b)

        def finish():
            y_stream.give(b, b, dot(held["pick"], y_stream.take(b)))

        return [start, finish]

    def pick_x(s):
        blocks = gather.blocks(s)
        held = {}

        def start():
            gather.complete(s)
            held["at"] = len(x_stream.loads)
            for block in blocks:
                x_stream.load(block)

        found = [start]
        for i, block in enumerate(blocks):

            def pick(i=i, block=block):
                held[i] = work.pick(block)
                x_stream.give(held["at"] + i, block, dot(held[i], x_stream.take(held["at"] + i)))

            def gate(i=i, block=block):
                work.gate(block, x_stream.take(held["at"] + i, False), held[i])

            found += [pick, gate]
        return found

    def between():
        for _ in range(2):
            if tasks:
                tasks.pop(0)()

    gather.step(0)
    for b in range(n):
        work.place(b)
        tasks += pick_y(b)
    for _ in range(4):
        tasks.pop(0)()
    for s in range(1, half + 1):
        gather.step(s, between)
        gather.pass_on(s - 1)
        tasks += pick_x(s - 1)
    gather.pass_on(half)
    tasks += pick_x(half)
    while tasks:
        tasks.pop(0)()
    gather.end()
    y_stream.end()
    x_stream.end()


def gather_tokens(x, y, small, router, own, cid):
    n, tokens, model = y.shape
    both = x.shape[0] // 2
    quarter = x.shape[0]
    picked = jax.ShapeDtypeStruct((own, n, CAP, model), BF)
    return pl.pallas_call(
        partial(token_gather_kernel, n, both, own),
        out_shape=[
            jax.ShapeDtypeStruct((n, 4) + x.shape, x.dtype),
            picked,
            picked,
            jax.ShapeDtypeStruct((n, own, tokens), F32),
            jax.ShapeDtypeStruct((n, tokens, LANES), F32),
            jax.ShapeDtypeStruct((own, n, CAP, LANES), F32),
        ],
        in_specs=[ANY, ANY, VM, VM],
        out_specs=[ANY, ANY, ANY, VM, VM, VM],
        scratch_shapes=[
            pltpu.VMEM((tokens, tokens), BF),
            pltpu.VMEM((2, tokens, model), BF),
            pltpu.VMEM((2, own, CAP, model), BF),
            pltpu.VMEM((2, 4, quarter, model), BF),
            pltpu.VMEM((2, own, CAP, model), BF),
            pltpu.SemaphoreType.DMA((4, 2)),
        ]
        + TokenGather.scratch(n, quarter, both),
        compiler_params=pltpu.CompilerParams(
            collective_id=cid, has_side_effects=True, vmem_limit_bytes=56 * 1024 * 1024
        ),
    )(x, y, small, router)


def first_kernel(n, k, *refs):
    ins, x = refs[:k], refs[k]
    outs, x_out = refs[k + 1 : 2 * k + 1], refs[2 * k + 1]
    ring = RingGather(n, ins, outs, refs[2 * k + 2 : 2 * k + 5])
    gather = TokenGather(n, 0, x, x_out, refs[2 * k + 5 :])
    greet([gather.core, gather.chip, gather.nxt, gather.prv])
    ring.begin()
    gather.begin()
    for s in range(n // 2 + 1):
        gather.step(s)
        ring.step(s)
        if s > 0:
            gather.pass_on(s - 1)
    gather.pass_on(n // 2)
    gather.end()
    ring.end()


def first_gather(arrays, x, cid):
    n, k = lax.axis_size("dp"), len(arrays)
    return pl.pallas_call(
        partial(first_kernel, n, k),
        out_shape=[jax.ShapeDtypeStruct((n,) + a.shape, a.dtype) for a in arrays]
        + [jax.ShapeDtypeStruct((n, 4) + x.shape, x.dtype)],
        in_specs=[ANY] * (k + 1),
        out_specs=[ANY] * (k + 1),
        scratch_shapes=RingGather.scratch(n, arrays) + TokenGather.scratch(n, x.shape[0], 0),
        compiler_params=pltpu.CompilerParams(collective_id=cid, has_side_effects=True),
    )(*arrays, x)


def token_scatter_kernel(
    n,
    x,
    out,
    from_core,
    slots,
    loads,
    far_loads,
    from_chip,
    to_chip,
    first,
    done,
    last_buf,
    load_sem,
    far_sem,
    core_send,
    core_recv,
    chip_send,
    chip_recv,
    send_sem,
    recv_sem,
    last_send,
    last_recv,
):
    m = lax.axis_index("mp")
    c, y = m % 2, m // 2
    core, chip = mp_partners(m)
    far = (m + 2) % 4
    beside = m + 1 - 2 * c
    p, nxt, prv = ring_neighbours(n)
    rows = out.shape[0]
    half, steps = rows // 2, n // 2
    greet([core, chip, nxt, prv])

    def block_of(i):
        s = (i + 1) // 2
        return ring_device(n, (p + steps - s) % n if i % 2 or i == 0 else (p + n - steps + s) % n)

    over, sent, loading, chips = {}, [], {}, {}
    loaded, summed = set(), set()
    upper, lower, whole = pl.ds(half, half), pl.ds(0, half), pl.ds(0, rows)

    def core_sends(i):
        if i >= n:
            return
        block = block_of(i)
        moves = [((beside + 2) % 4, 1 - y, upper), (beside, y, whole), ((beside + 2) % 4, 1 - y, lower)]
        for k, (theirs, piece, part) in enumerate(moves):
            copy = remote(
                x.at[block, theirs, part],
                from_core.at[block, piece, part],
                core_send.at[i, k],
                core_recv.at[i, k],
                core,
            )
            copy.start()
            over[i, k] = copy
            sent.append(copy)

    def start_pair(name, source, other, target, sems):
        loading[name] = []
        for k, ref in enumerate((source, other)):
            copy = pltpu.make_async_copy(ref, target.at[k], sems.at[k])
            copy.start()
            loading[name].append(copy)

    def load(i):
        if i >= n:
            return
        block = block_of(i)
        at = i % 4
        over[i, 1].wait_recv()
        start_pair(
            (i, 0), x.at[block, m], from_core.at[block, y], loads.at[at, :, whole], load_sem.at[at, 0]
        )
        over[i, 2].wait_recv()
        start_pair(
            (i, 1),
            x.at[block, far, lower],
            from_core.at[block, 1 - y, lower],
            loads.at[at, :, pl.ds(rows, half)],
            load_sem.at[at, 1],
        )

    def load_far(i):
        if i >= n:
            return
        block = block_of(i)
        over[i, 0].wait_recv()
        start_pair(
            (i, 2),
            x.at[block, far, upper],
            from_core.at[block, 1 - y, upper],
            far_loads.at[i % 2],
            far_sem.at[i % 2],
        )

    def to_other_chip(i):
        if i >= n:
            return
        for copy in loading[i, 2]:
            copy.wait()
        if i > 1:
            chips[i - 2].wait_send()
        add_rows(to_chip.at[i % 2], [far_loads.at[i % 2, 0], far_loads.at[i % 2, 1]], half, BF)
        copy = remote(to_chip.at[i % 2], from_chip.at[i], chip_send.at[i], chip_recv.at[i], chip)
        copy.start()
        chips[i] = copy

    chunks = chunk_rows(0, rows + half)
    count = len(chunks)
    order = [k for k in range(count) if chunks[k][0] >= rows]
    order += [k for k in range(count) if chunks[k][0] < rows]

    def pieces_of(i, k):
        start, size = chunks[k]
        area = pl.ds(start, size)
        if i not in loaded:
            loaded.add(i)
            for copy in loading[i, 0] + loading[i, 1]:
                copy.wait()
        found = [loads.at[i % 4, 0, area], loads.at[i % 4, 1, area]]
        if half <= start < rows:
            if i not in summed:
                summed.add(i)
                chips[i].wait_recv()
            found.append(from_chip.at[i, pl.ds(start - half, size)])
        return found

    for i in range(3):
        core_sends(i)
    load_far(0)
    load(0)
    load_far(1)
    to_other_chip(0)
    load_far(2)
    to_other_chip(1)
    core_sends(3)
    core_sends(4)
    load(1)
    to_other_chip(2)
    load(2)
    ring = {}
    for s in range(steps):
        for k, way in [(k, way) for k in order for way in range(2) if s > 0 or k % 2 == way]:
            start, size = chunks[k]
            area = pl.ds(start, size)
            if s == 0:
                target, pieces = first.at[area], pieces_of(0, k)
            else:
                target, pieces = slots.at[s - 1, way, area], pieces_of(2 * s - 1 + way, k)
                if (s - 1, k, way) in ring:
                    ring[s - 1, k, way].wait_recv()
                    pieces.append(target)
            add_rows(target, pieces, size, BF)
            copy = remote(
                target,
                slots.at[s, way, area],
                send_sem.at[s, k, way],
                recv_sem.at[s, k, way],
                nxt if way == 0 else prv,
            )
            copy.start()
            ring[s, k, way] = copy
        for i in (2 * s + 3, 2 * s + 4):
            load_far(i)
            core_sends(i + 2)
            to_other_chip(i)
            load(i)
    last = []
    for k in order:
        start, size = chunks[k]
        area = pl.ds(start, size)
        pieces = pieces_of(n - 1, k)
        for way in range(2):
            ring[steps - 1, k, way].wait_recv()
            pieces.append(slots.at[steps - 1, way, area])
        if start < rows:
            add_rows(out.at[area], pieces, size, F32)
            continue
        at = pl.ds(start - rows, size)
        add_rows(done.at[at], pieces, size, BF)
        copy = remote(done.at[at], last_buf.at[at], last_send.at[k], last_recv.at[k], chip)
        copy.start()
        last.append(copy)
    for copy in last:
        copy.wait_recv()
    add_rows(out.at[lower], [out.at[lower], last_buf], half, F32)
    for copy in sent + list(ring.values()) + last + [chips[n - 2], chips[n - 1]]:
        copy.wait_send()


def scatter_tokens(x, cid):
    n, _, rows, cols = x.shape
    half, steps = rows // 2, n // 2
    count = len(chunk_rows(0, rows + half))
    dma = pltpu.SemaphoreType.DMA
    out, _ = pl.pallas_call(
        partial(token_scatter_kernel, n),
        out_shape=[
            jax.ShapeDtypeStruct((rows, cols), F32),
            jax.ShapeDtypeStruct((n, 2, rows, cols), BF),
        ],
        in_specs=[ANY],
        out_specs=[VM, ANY],
        scratch_shapes=[
            pltpu.VMEM((steps, 2, rows + half, cols), BF),
            pltpu.VMEM((4, 2, rows + half, cols), BF),
            pltpu.VMEM((2, 2, half, cols), BF),
            pltpu.VMEM((n, half, cols), BF),
            pltpu.VMEM((2, half, cols), BF),
            pltpu.VMEM((rows + half, cols), BF),
            pltpu.VMEM((half, cols), BF),
            pltpu.VMEM((half, cols), BF),
            dma((4, 2, 2)),
            dma((2, 2)),
            dma((n, 3)),
            dma((n, 3)),
            dma((n,)),
            dma((n,)),
            dma((steps, count, 2)),
            dma((steps, count, 2)),
            dma((count,)),
            dma((count,)),
        ],
        compiler_params=pltpu.CompilerParams(
            collective_id=cid, has_side_effects=True, vmem_limit_bytes=56 * 1024 * 1024
        ),
    )(x)
    return out


def edge_kernel(n, part, slope, rim, total, ahead, mine, from_core, from_chip, edge, send_sem, recv_sem):
    d, m = lax.axis_index("dp"), lax.axis_index("mp")
    core, chip = mp_partners(m)
    before, after = {"dp": (d + n - 1) % n}, {"dp": (d + 1) % n}
    rows, cols = part.shape
    edge_rows, rim_cols = rim.shape
    greet([core, chip, before, after])

    def add(dst, pieces, dtype):
        add_rows(dst, pieces, rows, dtype)

    one = remote(part, from_core, send_sem.at[0], recv_sem.at[0], core)
    one.start()
    one.wait()
    add(mine, [part, from_core], BF)
    two = remote(mine, from_chip, send_sem.at[1], recv_sem.at[1], chip)
    two.start()
    two.wait_recv()
    add(total, [mine, from_chip], F32)
    edge[:, 0:rim_cols] = rim[...]
    edge[:, rim_cols : rim_cols + cols] = total[0:edge_rows, :] * slope[...]
    three = remote(edge, ahead, send_sem.at[2], recv_sem.at[2], before)

    @pl.when(d > 0)
    def _():
        three.start()

    @pl.when(d == n - 1)
    def _():
        ahead[...] = jnp.zeros_like(ahead)

    @pl.when(d < n - 1)
    def _():
        three.wait_recv()

    @pl.when(d > 0)
    def _():
        three.wait_send()

    two.wait_send()


def sum_and_edge(part, slope, rim, cid):
    rows, cols = part.shape
    edge_shape = (rim.shape[0], rim.shape[1] + cols)
    return pl.pallas_call(
        partial(edge_kernel, lax.axis_size("dp")),
        out_shape=[
            jax.ShapeDtypeStruct(part.shape, F32),
            jax.ShapeDtypeStruct(edge_shape, F32),
        ],
        in_specs=[VM] * 3,
        out_specs=[VM] * 2,
        scratch_shapes=[
            pltpu.VMEM((rows, cols), BF),
            pltpu.VMEM((rows, cols), F32),
            pltpu.VMEM((rows, cols), BF),
            pltpu.VMEM(edge_shape, F32),
            pltpu.SemaphoreType.DMA((3,)),
            pltpu.SemaphoreType.DMA((3,)),
        ],
        compiler_params=pltpu.CompilerParams(
            collective_id=cid, has_side_effects=True, vmem_limit_bytes=32 * 1024 * 1024
        ),
    )(part, slope, rim)


def head_pair(pair, first, second):
    lane = lax.broadcasted_iota(jnp.int32, first.shape, 1)
    return jnp.where(lane < LANES // 2, first, second)


def visible_pairs(seg_col, seg_row):
    length = seg_col.shape[0]
    row = lax.broadcasted_iota(jnp.int32, (length, length), 0)
    col = lax.broadcasted_iota(jnp.int32, (length, length), 1)
    return (row >= col) & (seg_col == seg_row)


def state_decay(entry, expand):
    last = entry[entry.shape[0] - 1 :, :]
    spread = jnp.broadcast_to(last, (LANES, LANES)).T
    return dot(expand, spread, ((0,), (0,)), HIGH)


def recur_kernel(
    pairs,
    values,
    write,
    read,
    cumul,
    cumul_t,
    step_t,
    entry,
    tail,
    seg_col,
    seg_row,
    expand,
    skip,
    start,
    out,
    kept,
    state,
):
    @pl.when(pl.program_id(0) == 0)
    def _():
        state[...] = start[...]

    held = state[...]
    kept[0] = held
    v, b, c = values[...], write[...], read[...]
    scores = dot(c, b, ((1,), (1,)), HIGH)
    visible = visible_pairs(seg_col[...], seg_row[...])
    entry_full = dot(entry[...], expand[...], precision=HIGH)
    tail_full = dot(tail[...], expand[...], precision=HIGH)
    carried = entry_full * dot(c, held, ((1,), (1,)), HIGH) + skip[...] * v
    cum, cum_t, st_t = cumul[...], cumul_t[...], step_t[...]
    for pair in range(pairs):
        cols = slice(pair * LANES, (pair + 1) * LANES)
        v2 = v[:, cols]
        found = []
        for h in (2 * pair, 2 * pair + 1):
            spread = jnp.where(visible, cum[:, h : h + 1] - cum_t[h : h + 1, :], MASKED)
            mixing = jnp.exp(spread) * (scores * st_t[h : h + 1, :])
            found.append(dot_three(mixing, v2, (1, 0)))
        out[:, cols] = head_pair(pair, found[0], found[1]) + carried[:, cols]
    state[...] = state_decay(entry[...], expand[...]) * held + dot(v * tail_full, b, ((0,), (0,)), HIGH)


def recur_specs(width, lengths):
    def rows(cols):
        return pl.BlockSpec((BLK, cols), lambda i: (lengths(i), 0))

    def flat(count):
        return pl.BlockSpec((count, BLK), lambda i: (0, lengths(i)))

    def whole(shape):
        return pl.BlockSpec(shape, lambda i: (0,) * len(shape))

    return rows, flat, whole


def recur_forward(v, b, c, cumul, cumul_t, step_t, entry, tail, seg_col, seg_row, expand, skip, start):
    total, width = v.shape
    blocks = total // BLK
    rows, flat, whole = recur_specs(width, lambda i: i)
    return pl.pallas_call(
        partial(recur_kernel, width // LANES),
        grid=(blocks,),
        out_shape=[
            jax.ShapeDtypeStruct((total, width), F32),
            jax.ShapeDtypeStruct((blocks, width, LANES), F32),
        ],
        in_specs=[
            rows(width),
            rows(LANES),
            rows(LANES),
            rows(LANES),
            flat(16),
            flat(16),
            rows(LANES),
            rows(LANES),
            rows(1),
            flat(1),
            whole((LANES, width)),
            whole((1, width)),
            whole((width, LANES)),
        ],
        out_specs=[
            rows(width),
            pl.BlockSpec((1, width, LANES), lambda i: (i, 0, 0)),
        ],
        scratch_shapes=[pltpu.VMEM((width, LANES), F32)],
        compiler_params=pltpu.CompilerParams(vmem_limit_bytes=48 * 1024 * 1024),
    )(v, b, c, cumul, cumul_t, step_t, entry, tail, seg_col, seg_row, expand, skip, start)


def adjoint_kernel(
    pairs,
    values,
    write,
    read,
    cumul,
    cumul_t,
    step_t,
    step,
    entry,
    tail_bare,
    seg_col,
    seg_row,
    expand,
    skip,
    kept,
    d_out,
    start,
    d_values,
    d_write,
    d_read,
    d_step,
    d_rate_step,
    d_skip,
    state,
    columns,
):
    @pl.when(pl.program_id(0) == 0)
    def _():
        state[...] = start[...]
        d_skip[...] = jnp.zeros_like(d_skip)
        columns[...] = jnp.zeros_like(columns)

    length = values.shape[0]
    lam, held = state[...], kept[0]
    v, b, c, dy = values[...], write[...], read[...], d_out[...]
    ex = expand[...]
    st = step[...]
    scores = dot(c, b, ((1,), (1,)), HIGH)
    visible = visible_pairs(seg_col[...], seg_row[...])
    entry_full = dot(entry[...], ex, precision=HIGH)
    tail = tail_bare[...] * st
    tail_full = dot(tail, ex, precision=HIGH)
    c_state = dot(c, held, ((1,), (1,)), HIGH)
    b_lam = dot(b, lam, ((1,), (1,)), HIGH)
    dy_in = dy * entry_full
    v_out = v * tail_full
    dc = dot(dy_in, held, precision=HIGH)
    db = dot(v_out, lam, precision=HIGH)
    reach = dot(dy_in * c_state, ex, ((1,), (1,)), HIGH)
    leave = dot(v * b_lam, ex, ((1,), (1,)), HIGH)
    d_skip[...] += jnp.sum(dy * v, axis=0, keepdims=True)
    dv_far = tail_full * b_lam + skip[...] * dy
    cum, cum_t, st_t = cumul[...], cumul_t[...], step_t[...]
    lane = lax.broadcasted_iota(jnp.int32, (length, LANES), 1)
    d_scores = jnp.zeros((length, length), F32)
    row_sums = jnp.zeros((length, LANES), F32)
    for pair in range(pairs):
        cols = slice(pair * LANES, (pair + 1) * LANES)
        v2, dy2 = v[:, cols], dy[:, cols]
        found = []
        for j in range(2):
            h = 2 * pair + j
            own = (lane < LANES // 2) if j == 0 else (lane >= LANES // 2)
            d_mix = dot_three(jnp.where(own, dy2, 0.0), v2, (1, 1))
            spread = jnp.where(visible, cum[:, h : h + 1] - cum_t[h : h + 1, :], MASKED)
            decay = jnp.exp(spread)
            decay_step = decay * st_t[h : h + 1, :]
            weighted = d_mix * scores * decay
            d_scores = d_scores + d_mix * decay_step
            columns[h : h + 1, :] = jnp.sum(weighted, axis=0, keepdims=True)
            per_row = jnp.sum(weighted * st_t[h : h + 1, :], axis=1, keepdims=True)
            row_sums = jnp.where(lane == h, per_row, row_sums)
            found.append(dot(scores * decay_step, dy2, ((0,), (0,))))
        d_values[:, cols] = head_pair(pair, found[0], found[1]) + dv_far[:, cols]
    d_read[...] = dc + dot(d_scores, b, precision=HIGH)
    d_write[...] = db + dot(d_scores, c, ((0,), (0,)), HIGH)
    col_sums = columns[...].T
    leave_step = tail * leave
    d_step[...] = col_sums + tail_bare[...] * leave
    d_cum = row_sums - st * col_sums + reach - leave_step
    row = lax.broadcasted_iota(jnp.int32, (length, length), 0)
    col = lax.broadcasted_iota(jnp.int32, (length, length), 1)
    upper = (col >= row).astype(F32)
    met = jnp.sum(dot(lam * held, ex, ((0,), (1,)), HIGH), axis=0, keepdims=True)
    at_end = jnp.sum(leave_step, axis=0, keepdims=True) + entry[length - 1 :, :] * met
    d_rate_step[...] = dot(upper, d_cum, precision=HIGH) + at_end
    state[...] = state_decay(entry[...], ex) * lam + dot(dy_in, c, ((0,), (0,)), HIGH)


def recur_backward(
    v, b, c, cumul, cumul_t, step_t, step, entry, tail_bare, seg_col, seg_row, expand, skip, kept, dy, start
):
    total, width = v.shape
    blocks = total // BLK
    rows, flat, whole = recur_specs(width, lambda i: blocks - 1 - i)
    return pl.pallas_call(
        partial(adjoint_kernel, width // LANES),
        grid=(blocks,),
        out_shape=[
            jax.ShapeDtypeStruct((total, width), F32),
            jax.ShapeDtypeStruct((total, LANES), F32),
            jax.ShapeDtypeStruct((total, LANES), F32),
            jax.ShapeDtypeStruct((total, LANES), F32),
            jax.ShapeDtypeStruct((total, LANES), F32),
            jax.ShapeDtypeStruct((1, width), F32),
        ],
        in_specs=[
            rows(width),
            rows(LANES),
            rows(LANES),
            rows(LANES),
            flat(16),
            flat(16),
            rows(LANES),
            rows(LANES),
            rows(LANES),
            rows(1),
            flat(1),
            whole((LANES, width)),
            whole((1, width)),
            pl.BlockSpec((1, width, LANES), lambda i: (blocks - 1 - i, 0, 0)),
            rows(width),
            whole((width, LANES)),
        ],
        out_specs=[
            rows(width),
            rows(LANES),
            rows(LANES),
            rows(LANES),
            rows(LANES),
            whole((1, width)),
        ],
        scratch_shapes=[pltpu.VMEM((width, LANES), F32), pltpu.VMEM((LANES, LANES), F32)],
        compiler_params=pltpu.CompilerParams(vmem_limit_bytes=48 * 1024 * 1024),
    )(v, b, c, cumul, cumul_t, step_t, step, entry, tail_bare, seg_col, seg_row, expand, skip, kept, dy, start)


def state_scan_kernel(
    n,
    reverse,
    mine,
    decay,
    expand,
    out,
    first,
    second,
    got_first,
    got_second,
    half,
    got_half,
    send_sem,
    recv_sem,
):
    d = lax.axis_index("dp")
    q = n - 1 - d if reverse else d
    zq, xq = q // 2, q % 2
    depth = n // 2
    rows = mine.shape[0] // 2
    xf = xq.astype(F32)
    sent_type = first.dtype

    def device(logical):
        return {"dp": n - 1 - logical if reverse else logical}

    beside = device(2 * zq + 1 - xq)
    others = [device(2 * ((zq + k) % depth) + xq) for k in range(1, depth)]
    own_rows = pl.ds(pl.multiple_of(rows * xq, 16), rows)
    other_rows = pl.ds(pl.multiple_of(rows * (1 - xq), 16), rows)
    own_lanes = pl.ds(pl.multiple_of(rows * xq, LANES), rows)
    tail = pl.ds(rows, 16)
    body = pl.ds(0, rows)
    row = lax.broadcasted_iota(jnp.int32, (16, LANES), 0)

    def spread(values):
        square = jnp.broadcast_to(values, (LANES, LANES)).T
        return dot(expand[:, own_lanes], square, ((0,), (0,)), HIGH)

    def two_terms(values):
        high = values.astype(sent_type).astype(F32)
        wide = jnp.where(row == 0, high, jnp.where(row == 1, values - high, 0.0))
        return wide.astype(sent_type)

    def one_term(block):
        return block[0:1, :].astype(F32) + block[1:2, :].astype(F32)

    for k in range(1, depth):

        @pl.when(zq < k)
        def _():
            got_second[k - 1] = jnp.zeros(got_second.shape[1:], sent_type)

    own_decay = decay[0:1, :]
    first[body, :] = mine[other_rows, :].astype(sent_type)
    first[tail, :] = two_terms(own_decay)
    greet([beside] + others)
    one = remote(first, got_first, send_sem.at[0], recv_sem.at[0], beside)
    one.start()
    one.wait_recv()
    own = mine[own_rows, :]
    got, got_decay = got_first[body, :].astype(F32), one_term(got_first[tail, :])
    early = own * (1.0 - xf) + got * xf
    early_decay = own_decay * (1.0 - xf) + got_decay * xf
    late = own * xf + got * (1.0 - xf)
    late_decay = own_decay * xf + got_decay * (1.0 - xf)
    second[body, :] = (spread(late_decay) * early + late).astype(sent_type)
    second[tail, :] = two_terms(early_decay * late_decay)
    sent = []
    for k in range(1, depth):
        copy = remote(
            second, got_second.at[k - 1], send_sem.at[k], recv_sem.at[k], device(2 * ((zq + k) % depth) + xq)
        )
        sent.append(copy)

        @pl.when(zq + k < depth)
        def _():
            copy.start()

    early_spread = spread(early_decay)
    total = jnp.zeros((rows, LANES), F32)
    for k in range(depth - 1, 0, -1):

        @pl.when(zq >= k)
        def _():
            sent[k - 1].wait_recv()

        got_k = got_second.at[k - 1]
        total = spread(one_term(got_k[tail, :])) * total + got_k[body, :].astype(F32)
    after = early_spread * total + early
    half[...] = (total * xf + after * (1.0 - xf)).astype(sent_type)
    last = remote(half, got_half, send_sem.at[depth], recv_sem.at[depth], beside)
    last.start()
    out[own_rows, :] = total * (1.0 - xf) + after * xf
    last.wait_recv()
    out[other_rows, :] = got_half[...].astype(F32)
    one.wait_send()
    last.wait_send()
    for k in range(1, depth):

        @pl.when(zq + k < depth)
        def _():
            sent[k - 1].wait_send()


def state_scan(mine, decay, expand, reverse, cid, sent_type):
    n = lax.axis_size("dp")
    half = mine.shape[0] // 2
    depth = n // 2
    message = (half + 16, LANES)
    return pl.pallas_call(
        partial(state_scan_kernel, n, reverse),
        out_shape=jax.ShapeDtypeStruct(mine.shape, F32),
        in_specs=[VM] * 3,
        out_specs=VM,
        scratch_shapes=[
            pltpu.VMEM(message, sent_type),
            pltpu.VMEM(message, sent_type),
            pltpu.VMEM(message, sent_type),
            pltpu.VMEM((depth - 1,) + message, sent_type),
            pltpu.VMEM((half, LANES), sent_type),
            pltpu.VMEM((half, LANES), sent_type),
            pltpu.SemaphoreType.DMA((depth + 1,)),
            pltpu.SemaphoreType.DMA((depth + 1,)),
        ],
        compiler_params=pltpu.CompilerParams(
            collective_id=cid, has_side_effects=True, vmem_limit_bytes=32 * 1024 * 1024
        ),
    )(mine, decay, expand)


def pick_matrix(position, own):
    length = position.shape[1]
    slot = lax.broadcasted_iota(jnp.int32, (CAP, length), 0).astype(F32)
    parts = [
        jnp.where(position[e : e + 1, :] == slot, 1.0, 0.0).astype(BF) for e in range(own)
    ]
    return jnp.concatenate(parts, axis=0)


def slot_spec(own, cols):
    return pl.BlockSpec((own, 1, CAP, cols), lambda s: (0, s, 0, 0))


def token_spec(rows, cols):
    return pl.BlockSpec((1, rows, cols), lambda s: (s, 0, 0))


BIG = pltpu.CompilerParams(vmem_limit_bytes=56 * 1024 * 1024)


def expert_kernel(
    own, rows, cot_rows, gate, w_in, w_out, grad_in, grad_out, d_rows, res, dots, wide, both
):
    e, part = pl.program_id(0), pl.program_id(1)
    model = rows.shape[2]
    units = w_out.shape[1]

    @pl.when(part == 0)
    def _():
        wide[...] = w_in[0].astype(F32)
        both[:, 0:units] = wide[pl.ds(0, model, stride=2), :].astype(BF)
        both[:, units : 2 * units] = wide[pl.ds(1, model, stride=2), :].astype(BF)
        grad_in[...] = jnp.zeros_like(grad_in)
        grad_out[...] = jnp.zeros_like(grad_out)

    x, c, g = rows[0], cot_rows[0], gate[0]
    mid = dot(x, both[...])
    mid_gate, mid_up = mid[:, 0:units], mid[:, units : 2 * units]
    sig = jax.nn.sigmoid(mid_gate)
    mid_silu = mid_gate * sig
    act = (mid_silu * mid_up).astype(BF).astype(F32)
    back = dot(c, w_out[0], ((1,), (1,)))
    dot_sum = jnp.sum(act * back, axis=1, keepdims=True)
    lane = lax.broadcasted_iota(jnp.int32, g.shape, 1)
    dots[0] = jnp.where(lane == lax.axis_index("dp") * own + e, dot_sum, 0.0).astype(BF)
    gated = (act * g).astype(BF)
    d_act = back * g
    d_gate = (d_act * mid_up * (sig * (1.0 + mid_gate * (1.0 - sig)))).astype(BF)
    d_mid = jnp.concatenate([d_gate, (d_act * mid_silu).astype(BF)], axis=1)
    grads = dot(x, d_mid, ((0,), (0,)))
    grad_in[0, pl.ds(0, model, stride=2), :] += grads[:, 0:units]
    grad_in[0, pl.ds(1, model, stride=2), :] += grads[:, units : 2 * units]
    grad_out[0] += dot(gated, c, ((0,), (0,)))
    d_rows[0] = dot(d_mid, both[...], ((1,), (1,))).astype(BF)
    res[0] = dot(gated, w_out[0]).astype(BF)


def run_experts(rows, cot_rows, gate, w_in, w_out):
    own, slots, model = rows.shape
    units = w_out.shape[1]
    part = min(slots, 512)

    def slot(cols):
        return pl.BlockSpec((1, part, cols), lambda e, j: (e, j, 0))

    def weight(a, b):
        return pl.BlockSpec((1, a, b), lambda e, j: (e, 0, 0))

    return pl.pallas_call(
        partial(expert_kernel, own),
        grid=(own, slots // part),
        out_shape=[
            jax.ShapeDtypeStruct((own, 2 * model, units), F32),
            jax.ShapeDtypeStruct((own, units, model), F32),
            jax.ShapeDtypeStruct((own, slots, model), BF),
            jax.ShapeDtypeStruct((own, slots, model), BF),
            jax.ShapeDtypeStruct((own, slots, LANES), BF),
        ],
        in_specs=[slot(model), slot(model), slot(LANES), weight(2 * model, units), weight(units, model)],
        out_specs=[weight(2 * model, units), weight(units, model), slot(model), slot(model), slot(LANES)],
        scratch_shapes=[pltpu.VMEM((2 * model, units), F32), pltpu.VMEM((model, 2 * units), BF)],
        compiler_params=BIG,
    )(rows, cot_rows, gate, w_in, w_out)


def put_kernel(own, k, position, *refs):
    out = refs[-1]
    put = pick_matrix(position[0], own)
    here = jnp.where(pl.program_id(0) == lax.axis_index("dp"), 1.0, 0.0)
    start = 0
    for i in range(k):
        rows, shared = refs[2 * i], refs[2 * i + 1]
        cols = shared.shape[1]
        total = dot(put, rows[...].reshape(own * CAP, cols), ((0,), (0,)))
        out[0, :, start : start + cols] = (total + here * shared[...]).astype(BF)
        start += cols
    if len(refs) > 2 * k + 1:
        extra = refs[2 * k]
        out[0, :, start : start + LANES] = dot(
            put, extra[...].reshape(own * CAP, LANES), ((0,), (0,))
        ).astype(BF)


def put_rows(position, parts, extra=None):
    n, own, tokens = position.shape
    args, specs, cols = [], [], 0
    for rows, shared in parts:
        model = shared.shape[1]
        args += [rows.reshape(own, n, CAP, model), shared]
        specs += [slot_spec(own, model), pl.BlockSpec((tokens, model), lambda s: (0, 0))]
        cols += model
    if extra is not None:
        args.append(extra.reshape(own, n, CAP, LANES))
        specs.append(slot_spec(own, LANES))
        cols += LANES
    return pl.pallas_call(
        partial(put_kernel, own, len(parts)),
        grid=(n,),
        out_shape=jax.ShapeDtypeStruct((n, tokens, cols), BF),
        in_specs=[token_spec(own, tokens)] + specs,
        out_specs=token_spec(tokens, cols),
        compiler_params=BIG,
    )(position, *args)


def grads_kernel(k, *refs):
    lefts, rights, out = refs[:k], refs[k : 2 * k], refs[2 * k]
    start = 0
    for left, right in zip(lefts, rights):
        cols = right.shape[1]
        out[:, start : start + cols] = dot(left[...], right[...], ((0,), (0,))).astype(BF)
        start += cols


def weight_grads(pairs):
    k = len(pairs)
    tokens, model = pairs[0][0].shape
    block = 256
    cols = sum(right.shape[1] for _, right in pairs)
    return pl.pallas_call(
        partial(grads_kernel, k),
        grid=(model // block,),
        out_shape=jax.ShapeDtypeStruct((model, cols), BF),
        in_specs=[pl.BlockSpec((tokens, block), lambda i: (0, i)) for _ in pairs]
        + [pl.BlockSpec(right.shape, lambda i: (0, 0)) for _, right in pairs],
        out_specs=pl.BlockSpec((block, cols), lambda i: (i, 0)),
        compiler_params=BIG,
    )(*[left for left, _ in pairs], *[right for _, right in pairs])


def combine_states(states, decays, expand, reverse):
    n = states.shape[0]
    place = lax.axis_index("dp")
    wide = dot(decays, expand, precision=HIGH)
    state = jnp.zeros(states.shape[1:], F32)
    for j in range(n):
        source = n - 1 - j if reverse else j
        use = source > place if reverse else source < place
        fresh = wide[source][:, None] * state + states[source]
        state = jnp.where(use, fresh, state)
    return state


def incoming_state(mine, decay, expand, reverse, cid):
    if lax.axis_size("dp") == 8:
        return state_scan(
            mine, jnp.broadcast_to(decay, (8, LANES)), expand, reverse, cid, BF if reverse else F32
        )
    rows = jnp.pad(decay, ((0, 31), (0, 0)))
    (gathered,) = gather_dp([jnp.concatenate([mine, rows], axis=0)], cid)
    width = mine.shape[0]
    return combine_states(gathered[:, :width], gathered[:, width], expand, reverse)


def per_device(
    hidden,
    segment_ids,
    routes,
    norm_gain,
    mixer_in,
    state_in,
    step_in,
    conv_value,
    conv_value_bias,
    conv_state,
    conv_state_bias,
    head_params,
    gated_gain,
    mixer_out,
    ffn_gain,
    router,
    shared_in,
    shared_out,
    expert_in,
    expert_out,
    cotangent,
):
    n = lax.axis_size("dp")
    place, mp_place = lax.axis_index("dp"), lax.axis_index("mp")
    tokens, model = hidden.shape
    shard = model // n
    inner = mixer_in.shape[2]
    state_cols = state_in.shape[1]
    taps = conv_value.shape[0]
    heads = head_params.shape[1]
    width = inner // heads
    own_experts = expert_in.shape[0]
    hidden_units = shared_out.shape[0]
    quarter = tokens // 4

    misc_parts = [
        conv_value.reshape(-1),
        conv_value_bias.reshape(-1),
        gated_gain.reshape(-1),
        conv_state.reshape(-1),
        conv_state_bias,
        norm_gain,
        ffn_gain,
    ]
    misc = jnp.concatenate(misc_parts)
    small = jnp.concatenate(
        [
            jnp.pad(misc, (0, model - misc.shape[0]))[None],
            jnp.pad(routes.T.astype(BF), ((0, 0), (0, model - tokens))),
            hidden[tokens - 15 + TOPK :],
        ],
        axis=0,
    )
    pack_a = jnp.concatenate(
        [
            mixer_in.reshape(shard, 2 * inner),
            state_in,
            jnp.pad(step_in, ((0, 0), (0, LANES - heads))),
        ],
        axis=1,
    )
    pack_b = jnp.concatenate(
        [
            mixer_out.T,
            shared_in.reshape(shard, 2 * hidden_units),
            shared_out.T,
            jnp.pad(router, ((0, 0), (0, LANES - EXPERTS))),
        ],
        axis=1,
    )
    mine_cot = lax.dynamic_slice_in_dim(cotangent, mp_place * quarter, quarter, 0)
    weight_a, small_all, cot_all = first_gather([pack_a, small], mine_cot, 0)
    weight_a = weight_a.reshape(model, -1)
    cot_all = cot_all.reshape(n, tokens, model)
    pack_b, small_all = lax.optimization_barrier((pack_b, small_all))
    weight_b = lax.all_gather(pack_b, "dp", axis=0, tiled=True)
    out_t = weight_b[:, :inner]
    shared_w = weight_b[:, inner : inner + 2 * hidden_units]
    shared_out_t = weight_b[:, inner + 2 * hidden_units : inner + 3 * hidden_units]
    router_w = weight_b[:, inner + 3 * hidden_units :]

    pieces = []
    start = 0
    for part in misc_parts:
        pieces.append(small_all[:, 0, start : start + part.shape[0]].astype(F32))
        start += part.shape[0]
    local_p = conv_value.shape[1]
    value_rows = jnp.concatenate(pieces[:3], axis=1).reshape(n, taps + 2, local_p, heads)
    value_rows = value_rows.transpose(1, 3, 0, 2).reshape(taps + 2, inner)
    state_rows = jnp.concatenate(pieces[3:5], axis=1).reshape(n, taps + 1, state_cols // n)
    state_rows = state_rows.transpose(1, 0, 2).reshape(taps + 1, state_cols)
    gain_first = pieces[5].reshape(1, model)
    gain_second = pieces[6].reshape(1, model)
    conv_taps = jnp.concatenate([value_rows[:taps], state_rows[:taps]], axis=1)
    conv_bias = jnp.concatenate([value_rows[taps], state_rows[taps]])[None]
    gated_row = value_rows[taps + 1][None]

    group_start = place * tokens
    seg_padded = jnp.concatenate([jnp.full((taps - 1,), -1, jnp.int32), segment_ids])
    seg_ext = lax.dynamic_slice_in_dim(seg_padded, group_start, tokens + taps - 1)
    segments = seg_ext[taps - 1 :]
    prev_seg = seg_ext[taps - 2]
    same = [
        (seg_ext[k : k + tokens] == segments).astype(F32)[:, None] for k in range(taps)
    ]
    blocks = tokens // BLK
    seg_blocks = segments.reshape(blocks, BLK)
    last_segs = seg_blocks[:, BLK - 1]
    prev_segs = jnp.concatenate([prev_seg[None], last_segs[:-1]])
    entry_ok = (seg_blocks == prev_segs[:, None]).astype(F32).reshape(tokens, 1)
    tail_ok = (seg_blocks == last_segs[:, None]).astype(F32).reshape(tokens, 1)
    group_entry_ok = (segments == prev_seg).astype(F32)[:, None]
    group_tail_ok = (segments == segments[tokens - 1]).astype(F32)[:, None]
    seg_f = segments.astype(F32)
    seg_col, seg_row = seg_f[:, None], seg_f[None, :]

    behind = lax.dynamic_index_in_dim(small_all, (place + n - 1) % n, 0, False)
    hidden_ext = jnp.concatenate([behind, hidden], axis=0).astype(F32)
    inv_ext = lax.rsqrt(jnp.mean(hidden_ext * hidden_ext, axis=1, keepdims=True) + EPS)
    normed_ext = (hidden_ext * inv_ext * gain_first).astype(BF)
    normed = normed_ext[16:]
    zx_ext = dot(normed_ext, weight_a)
    gate_z = zx_ext[16:, :inner]
    pre_ext = zx_ext[16 - taps + 1 :, inner : 2 * inner + state_cols]
    head_local = head_params.astype(F32)
    dt_lanes = zx_ext[16:, 2 * inner + state_cols :]
    conv = jnp.broadcast_to(conv_bias, (tokens, inner + state_cols))
    for k in range(taps):
        conv = conv + conv_taps[k][None] * pre_ext[k : k + tokens] * same[k]
    act = jax.nn.silu(conv)
    values = act[:, :inner]
    write = act[:, inner : inner + state_cols // 2]
    read = act[:, inner + state_cols // 2 :]

    live = (jnp.arange(LANES) < heads)[None]
    head_pad = jnp.pad(head_local, ((0, 0), (0, LANES - heads)))
    rate = jnp.where(live, -jnp.exp(head_pad[0:1]), 0.0)
    step = jnp.where(live, jax.nn.softplus(dt_lanes + head_pad[1:2]), 0.0)
    rated = (step * rate).reshape(blocks, BLK, LANES)
    lower = jnp.tril(jnp.ones((BLK, BLK), F32))
    cumul_b = jnp.einsum("ts,bsh->bth", lower, rated, precision=HIGH)
    totals = cumul_b[:, BLK - 1]
    zero_row = jnp.zeros((1, LANES), F32)
    before, after = [zero_row], [zero_row]
    for i in range(blocks - 1):
        before.append(before[-1] + totals[i][None])
        after.append(after[-1] + totals[blocks - 1 - i][None])
    before = jnp.stack(before)
    after = jnp.stack(after[::-1])
    cumul = cumul_b.reshape(tokens, LANES)
    to_end = totals[:, None] - cumul_b
    entry = jnp.exp(cumul) * entry_ok
    tail_bare = jnp.exp(to_end).reshape(tokens, LANES) * tail_ok
    tail = tail_bare * step
    group_entry = jnp.exp(cumul_b + before).reshape(tokens, LANES) * group_entry_ok
    group_tail = jnp.exp(to_end + after).reshape(tokens, LANES) * group_tail_ok * step
    cumul_t = cumul[:, :16].T
    step_t = step[:, :16].T
    expand = (jnp.arange(LANES)[:, None] == jnp.arange(inner)[None, :] // width).astype(F32)
    skip = dot(head_pad[2:3], expand, precision=HIGH)
    outgoing = dot(
        values * dot(group_tail, expand, precision=HIGH), write, ((0,), (0,)), HIGH
    )
    group_decay = group_entry[tokens - 1 :]
    incoming = incoming_state(outgoing, group_decay, expand, False, 1)
    ssd, kept = recur_forward(
        values, write, read, cumul, cumul_t, step_t, entry, tail, seg_col, seg_row, expand, skip, incoming
    )

    gate_act = jax.nn.silu(gate_z)
    gated = ssd * gate_act
    scaled = (gated * gated_row).astype(BF)
    proj_part = dot(scaled, out_t, ((1,), (1,)))
    square_part = jnp.sum(gated * gated, axis=1, keepdims=True)
    proj_pack = jnp.concatenate([proj_part, jnp.broadcast_to(square_part, (tokens, LANES))], axis=1)
    proj_sum = scatter_mp(proj_pack.reshape(4, quarter, -1), 2)
    proj = proj_sum[:, :model]
    square = proj_sum[:, model : model + 1]
    inv_gated = lax.rsqrt(square / DI + EPS)
    mine_hidden = lax.dynamic_slice_in_dim(hidden, mp_place * quarter, quarter, 0).astype(F32)
    mixed = mine_hidden + proj * inv_gated
    inv_second = lax.rsqrt(jnp.mean(mixed * mixed, axis=1, keepdims=True) + EPS)
    unit_second = mixed * inv_second
    ffn_mine = (unit_second * gain_second).astype(BF)

    first_expert = place * own_experts
    ffn_all, cot_rows, rows, position, gates, slot_gates = gather_tokens(
        ffn_mine, cot_all, small_all, router_w, own_experts, 3
    )
    ffn_all = ffn_all.reshape(n, tokens, model)

    slots = n * CAP
    grad_in_rows, grad_expert_out, d_rows, expert_res, slot_dots = run_experts(
        rows.reshape(own_experts, slots, model),
        cot_rows.reshape(own_experts, slots, model),
        slot_gates.reshape(own_experts, slots, LANES),
        expert_in.reshape(own_experts, 2 * model, -1),
        expert_out,
    )
    grad_expert_in = grad_in_rows.reshape(expert_in.shape)

    ffn_block = lax.dynamic_index_in_dim(ffn_all, place, 0, False)
    shared_mid = dot(ffn_block, shared_w)
    shared_gate, shared_up = shared_mid[:, :hidden_units], shared_mid[:, hidden_units:]
    shared_silu = jax.nn.silu(shared_gate)
    shared_act = (shared_silu * shared_up).astype(BF)
    shared_res = dot(shared_act, shared_out_t, ((1,), (1,)))
    d_shared_act = dot(cotangent, shared_out_t)
    d_shared_mid = jnp.concatenate(
        [d_shared_act * shared_up * silu_slope(shared_gate), d_shared_act * shared_silu], axis=1
    ).astype(BF)
    d_ffn_shared = dot(d_shared_mid, shared_w, ((1,), (1,)))

    if n > 8:
        d_ffn_pack = put_rows(position, [(d_rows, d_ffn_shared)], slot_dots)
        d_ffn_sum = scatter_tokens(d_ffn_pack.reshape(n, 4, quarter, -1), 4)
        expert_res, d_ffn_sum = lax.optimization_barrier((expert_res, d_ffn_sum))
        res_pack = put_rows(position, [(expert_res, shared_res)])
        res_sum = scatter_tokens(res_pack.reshape(n, 4, quarter, model), 10)
    else:
        pack = put_rows(position, [(expert_res, shared_res), (d_rows, d_ffn_shared)], slot_dots)
        both_sums = scatter_tokens(pack.reshape(n, 4, quarter, -1), 4)
        res_sum, d_ffn_sum = both_sums[:, :model], both_sums[:, model:]

    own_tokens_gates = lax.dynamic_slice(
        gates, (place, mp_place * quarter, 0), (1, quarter, LANES)
    ).reshape(quarter, LANES)
    dots = d_ffn_sum[:, model : model + LANES]
    share = jnp.sum(own_tokens_gates * dots, axis=1, keepdims=True)
    d_logits = (own_tokens_gates * (dots - share)).astype(BF)
    d_ffn = d_ffn_sum[:, :model] + dot(d_logits, router_w, ((1,), (1,)))
    mine_cot_f = mine_cot.astype(F32)
    grad_gain_second = jnp.sum(d_ffn * unit_second, axis=0)
    d_unit = d_ffn * gain_second
    d_mixed = mine_cot_f + inv_second * (
        d_unit - unit_second * jnp.mean(d_unit * unit_second, axis=1, keepdims=True)
    )
    d_proj_mine = (d_mixed * inv_gated).astype(BF)
    d_inv = jnp.sum(d_mixed * proj, axis=1, keepdims=True)
    d_square = d_inv * -0.5 * inv_gated * inv_gated * inv_gated / DI
    d_square_high = d_square.astype(BF)
    d_square_low = (d_square - d_square_high.astype(F32)).astype(BF)
    sent = jnp.concatenate(
        [
            d_proj_mine,
            d_logits[:, :EXPERTS],
            d_square_high,
            d_square_low,
            jnp.zeros((quarter, LANES - EXPERTS - 2), BF),
        ],
        axis=1,
    )
    (got,) = gather_mp([sent], 5)
    got = got.reshape(tokens, model + LANES)
    d_proj = got[:, :model]
    d_logits_all = jnp.pad(got[:, model : model + EXPERTS], ((0, 0), (0, LANES - EXPERTS)))
    d_square_all = got[:, model + EXPERTS : model + EXPERTS + 1].astype(F32) + got[
        :, model + EXPERTS + 1 : model + EXPERTS + 2
    ].astype(F32)

    rows0 = ((0,), (0,))
    grad_b = weight_grads(
        [
            (d_proj, scaled),
            (ffn_block, d_shared_mid),
            (cotangent, shared_act),
            (ffn_block, d_logits_all),
        ]
    )
    grad_b, d_proj = lax.optimization_barrier((grad_b, d_proj))
    sum_b = lax.psum_scatter(grad_b, "dp", scatter_dimension=0, tiled=True).astype(F32)
    d_scaled = dot(d_proj, out_t)
    grad_gated_row = jnp.sum(d_scaled * gated, axis=0)
    d_gated = d_scaled * gated_row + 2.0 * gated * d_square_all
    d_ssd = d_gated * gate_act
    d_gate_z = d_gated * ssd * silu_slope(gate_z)

    direct = dot(d_ssd * dot(group_entry, expand, precision=HIGH), read, rows0, HIGH)
    state_grad = incoming_state(direct, group_decay, expand, True, 6)
    d_values, d_write, d_read, d_step, d_rated, d_skip_row = recur_backward(
        values,
        write,
        read,
        cumul,
        cumul_t,
        step_t,
        step,
        entry,
        tail_bare,
        seg_col,
        seg_row,
        expand,
        skip,
        kept,
        d_ssd,
        state_grad,
    )
    d_rate = jnp.sum(d_rated * step, axis=0, keepdims=True)
    d_dt = jnp.where(
        live, (d_step + rate * d_rated) * jax.nn.sigmoid(dt_lanes + head_pad[1:2]), 0.0
    )
    d_skip = dot(d_skip_row, expand, ((1,), (1,)), HIGH)
    grad_head = jnp.concatenate(
        [d_rate * rate, jnp.sum(d_dt, axis=0, keepdims=True), d_skip], axis=0
    )[:, :heads]

    slope = silu_slope(conv)
    d_conv_values = d_values * slope[:, :inner]
    d_state_act, rim_ahead = sum_and_edge(
        jnp.concatenate([d_write, d_read], axis=1), slope[:16, inner:], d_conv_values[:16], 11
    )
    d_conv = jnp.concatenate([d_conv_values, d_state_act * slope[:, inner:]], axis=1)
    d_conv_ext = jnp.concatenate([d_conv, rim_ahead], axis=0)
    seg_after = lax.dynamic_slice_in_dim(
        jnp.concatenate([segment_ids, jnp.full((taps - 1,), -1, jnp.int32)]),
        group_start,
        tokens + taps - 1,
    )
    d_pre = jnp.zeros_like(d_conv)
    grad_rows = []
    for k in range(taps):
        ahead = taps - 1 - k
        ok = (seg_after[ahead : ahead + tokens] == segments).astype(F32)[:, None]
        d_pre = d_pre + conv_taps[k][None] * d_conv_ext[ahead : ahead + tokens] * ok
        grad_rows.append(jnp.sum(d_conv * pre_ext[k : k + tokens] * same[k], axis=0))
    grad_rows.append(jnp.sum(d_conv, axis=0))
    d_a = jnp.concatenate([d_gate_z, d_pre, d_dt], axis=1).astype(BF)

    d_state_mine = lax.dynamic_slice_in_dim(
        d_a[:, 2 * inner : 2 * inner + state_cols], mp_place * quarter, quarter, 0
    )
    d_normed_part = dot(d_a[:, : 2 * inner], weight_a[:, : 2 * inner], ((1,), (1,))) + dot(
        d_a[:, 2 * inner + state_cols :], weight_a[:, 2 * inner + state_cols :], ((1,), (1,))
    )
    d_state_rows = dot(
        d_state_mine, weight_a[:, 2 * inner : 2 * inner + state_cols], ((1,), (1,))
    )
    grad_a = dot(normed, d_a, rows0).astype(BF)
    unit_first = hidden_ext[16:] * inv_ext[16:]
    mine_unit = lax.dynamic_slice_in_dim(unit_first, mp_place * quarter, quarter, 0)
    grad_gain_first = jnp.sum(d_normed_part * unit_first, axis=0) + jnp.sum(
        d_state_rows * mine_unit, axis=0
    )

    value_grads = jnp.stack([g[:inner] for g in grad_rows] + [grad_gated_row])
    value_grads = value_grads.reshape(taps + 2, heads, n, local_p).transpose(2, 0, 3, 1)
    state_grads = jnp.stack([g[inner:] for g in grad_rows])
    state_grads = state_grads.reshape(taps + 1, n, state_cols // n).transpose(1, 0, 2)
    misc_grads = [
        value_grads.reshape(n, -1),
        state_grads.reshape(n, -1),
        jnp.broadcast_to(grad_head.reshape(1, -1), (n, 3 * heads)),
    ]
    sizes = [g.shape[1] for g in misc_grads]
    misc_grads = jnp.concatenate(misc_grads, axis=1)
    misc_grads = jnp.pad(misc_grads, ((0, 0), (0, 32 * LANES - misc_grads.shape[1])))
    gains = jnp.concatenate(
        [grad_gain_first.reshape(n, shard), grad_gain_second.reshape(n, shard)], axis=1
    )
    gains = jnp.pad(gains, ((0, 0), (0, 16 * LANES - 2 * shard)))
    mine_result = (mixed + res_sum).astype(BF)
    sum_a, misc_sum, gains_sum, hidden_all, result = last_exchange(
        grad_a.reshape(n, shard, -1),
        misc_grads.reshape(n, 32, LANES),
        gains.reshape(n, 16, LANES),
        d_normed_part.astype(BF).reshape(4, quarter, model),
        d_state_rows,
        d_mixed,
        mine_hidden,
        gain_first,
        mine_result,
        8,
    )
    result = result.reshape(tokens, model)
    misc_sum = misc_sum.reshape(-1)
    gains_sum = gains_sum.reshape(-1)
    cut = [0]
    for size in sizes:
        cut.append(cut[-1] + size)
    value_sum = misc_sum[: cut[1]].reshape(taps + 2, local_p, heads)
    state_sum = misc_sum[cut[1] : cut[2]].reshape(taps + 1, state_cols // n)
    head_sum = misc_sum[cut[2] : cut[3]].reshape(3, heads)

    b1, b2 = inner, inner + 2 * hidden_units
    b3 = b2 + hidden_units
    return (
        result,
        hidden_all.reshape(tokens, model).astype(F32),
        gains_sum[:shard],
        sum_a[:, : 2 * inner].reshape(shard, 2, inner),
        sum_a[:, 2 * inner : 2 * inner + state_cols],
        sum_a[:, 2 * inner + state_cols : 2 * inner + state_cols + heads],
        value_sum[:taps],
        value_sum[taps],
        state_sum[:taps],
        state_sum[taps],
        head_sum,
        value_sum[taps + 1],
        sum_b[:, :b1].T,
        gains_sum[shard : 2 * shard],
        sum_b[:, b3 : b3 + EXPERTS],
        sum_b[:, b1:b2].reshape(shard, 2, hidden_units),
        sum_b[:, b2:b3].T,
        grad_expert_in,
        grad_expert_out,
    )


def solution(mesh):
    placed = (
        P("dp", None),
        P(),
        P("dp", None),
        P("dp"),
        P("dp", None, "mp"),
        P("dp", None),
        P("dp", "mp"),
        P(None, "dp", "mp"),
        P("dp", "mp"),
        P(None, "dp"),
        P("dp"),
        P(None, "mp"),
        P("dp", "mp"),
        P("mp", "dp"),
        P("dp"),
        P("dp", None),
        P("dp", None, "mp"),
        P("mp", "dp"),
        P("dp", None, None, "mp"),
        P("dp", "mp", None),
        P("dp", None),
    )
    return jax.shard_map(
        per_device,
        mesh=mesh,
        in_specs=placed,
        out_specs=(
            P("dp", None),
            P("dp", None),
            P("dp"),
            P("dp", None, "mp"),
            P("dp", None),
            P("dp", "mp"),
            P(None, "dp", "mp"),
            P("dp", "mp"),
            P(None, "dp"),
            P("dp"),
            P(None, "mp"),
            P("dp", "mp"),
            P("mp", "dp"),
            P("dp"),
            P("dp", None),
            P("dp", None, "mp"),
            P("mp", "dp"),
            P("dp", None, None, "mp"),
            P("dp", "mp", None),
        ),
        check_vma=False,
    )
```

```python
from functools import partial

import jax
import jax.numpy as jnp
from jax import lax
from jax.experimental import pallas as pl
from jax.experimental.pallas import tpu as pltpu
from jax.sharding import PartitionSpec as P

MESH = pl.DeviceIdType.MESH
BLK = 128
EXPERTS = 64
TOPK = 6
DI = 3072
CAP = 64
LANES = 128

EPS = 1e-05
HIGH = lax.Precision.HIGHEST
MASKED = -1e30
BF = jnp.bfloat16
F32 = jnp.float32
ANY = pl.BlockSpec(memory_space=pl.ANY)
VM = pl.BlockSpec(memory_space=pltpu.VMEM)


def dot(a, b, dims=((1,), (0,)), precision=None):
    return lax.dot_general(
        a, b, (dims, ((), ())), precision=precision, preferred_element_type=F32
    )


def two_parts(a):
    high = a.astype(BF)
    return high, (a - high.astype(F32)).astype(BF)


def dot_three(a, b, over):
    a_high, a_low = two_parts(a)
    b_high, b_low = two_parts(b)
    left = jnp.concatenate([a_high, a_low, a_high], axis=over[0])
    right = jnp.concatenate([b_high, b_high, b_low], axis=over[1])
    return dot(left, right, ((over[0],), (over[1],)))


def silu_slope(argument):
    sigmoid_val = jax.nn.sigmoid(argument)
    return sigmoid_val * (1.0 + argument * (1.0 - sigmoid_val))


def chunk_rows(start, size):
    return [(start + i, min(32, size - i)) for i in range(0, size, 32)]


def ring_place(n, d):
    high, low = d // 2, d % 2
    return high * (1 - low) + (n - 1 - high) * low


def ring_device(n, p):
    back = p // (n // 2)
    return (2 * p) * (1 - back) + (2 * (n - 1 - p) + 1) * back


def greet(targets):
    barrier = pltpu.get_barrier_semaphore()
    for target in targets:
        pl.semaphore_signal(barrier, inc=1, device_id=target, device_id_type=MESH)
    pl.semaphore_wait(barrier, len(targets))


def remote(src, dst, send, recv, target):
    return pltpu.make_async_remote_copy(
        src_ref=src,
        dst_ref=dst,
        send_sem=send,
        recv_sem=recv,
        device_id=target,
        device_id_type=MESH,
    )


def mp_partners(m):
    return {"mp": m + 1 - 2 * (m % 2)}, {"mp": (m + 2) % 4}


def ring_neighbours(n):
    p = ring_place(n, lax.axis_index("dp"))
    nxt = {"dp": ring_device(n, (p + 1) % n)}
    prv = {"dp": ring_device(n, (p + n - 1) % n)}
    return p, nxt, prv


class RingGather:
    def __init__(self, n, ins, outs, sems):
        self.n, self.ins, self.outs = n, ins, outs
        self.local_sem, self.send_sem, self.recv_sem = sems
        self.p, self.nxt, self.prv = ring_neighbours(n)
        self.copies = {}

    @staticmethod
    def scratch(n, arrays):
        dma = pltpu.SemaphoreType.DMA
        most = max(len(chunk_rows(0, a.shape[0])) for a in arrays)
        shape = (n // 2, len(arrays), most, 2)
        return [dma((len(arrays),)), dma(shape), dma(shape)]

    def begin(self):
        d = lax.axis_index("dp")
        self.local = []
        for j, (a, out) in enumerate(zip(self.ins, self.outs)):
            copy = pltpu.make_async_copy(a, out.at[d], self.local_sem.at[j])
            copy.start()
            self.local.append(copy)

    def step(self, s):
        n, p = self.n, self.p
        for j, (a, out) in enumerate(zip(self.ins, self.outs)):
            for i, (start, rows) in enumerate(chunk_rows(0, a.shape[0])):
                part = pl.ds(start, rows)
                for way in range(2):
                    origin = ring_device(n, (p + n - s) % n if way == 0 else (p + s) % n)
                    if (s - 1, j, i, way) in self.copies:
                        self.copies[s - 1, j, i, way].wait_recv()
                    if s + 1 < n // 2 or (s + 1 == n // 2 and i % 2 == way):
                        copy = remote(
                            a.at[part] if s == 0 else out.at[origin, part],
                            out.at[origin, part],
                            self.send_sem.at[s, j, i, way],
                            self.recv_sem.at[s, j, i, way],
                            self.nxt if way == 0 else self.prv,
                        )
                        copy.start()
                        self.copies[s, j, i, way] = copy

    def end(self):
        for copy in self.copies.values():
            copy.wait_send()
        for copy in self.local:
            copy.wait()


def gather_kernel(n, k, *refs):
    ring = RingGather(n, refs[:k], refs[k : 2 * k], refs[2 * k :])
    greet([ring.nxt, ring.prv])
    ring.begin()
    for s in range(n // 2 + 1):
        ring.step(s)
    ring.end()


def gather_dp(arrays, cid):
    n, k = lax.axis_size("dp"), len(arrays)
    return pl.pallas_call(
        partial(gather_kernel, n, k),
        out_shape=[jax.ShapeDtypeStruct((n,) + a.shape, a.dtype) for a in arrays],
        in_specs=[ANY] * k,
        out_specs=[ANY] * k,
        scratch_shapes=RingGather.scratch(n, arrays),
        compiler_params=pltpu.CompilerParams(collective_id=cid, has_side_effects=True),
    )(*arrays)


def add_rows(dst, pieces, rows, dtype):
    def body(i, carry):
        sl = pl.ds(pl.multiple_of(i * 16, 16), 16)
        total = pieces[0][sl, :].astype(F32)
        for piece in pieces[1:]:
            total = total + piece[sl, :].astype(F32)
        dst[sl, :] = total.astype(dtype)
        return carry

    lax.fori_loop(0, rows // 16, body, 0)


class RingScatter:
    def __init__(self, n, ins, outs, slots, sems):
        self.n, self.ins, self.outs, self.slots = n, ins, outs, slots
        self.send_sem, self.recv_sem = sems
        self.p, self.nxt, self.prv = ring_neighbours(n)
        self.copies = {}

    @staticmethod
    def scratch(n, arrays):
        most = max(len(chunk_rows(0, a.shape[1])) for a in arrays)
        shape = (n // 2, len(arrays), most, 2)
        return [pltpu.VMEM((n // 2, 2) + a.shape[1:], a.dtype) for a in arrays] + [
            pltpu.SemaphoreType.DMA(shape),
            pltpu.SemaphoreType.DMA(shape),
        ]

    def step(self, s, j):
        n, p = self.n, self.p
        array, out, slots = self.ins[j], self.outs[j], self.slots[j]
        for i, (start, size) in enumerate(chunk_rows(0, array.shape[1])):
            part = pl.ds(start, size)
            if s == n // 2:
                for way in range(2):
                    self.copies[s - 1, j, i, way].wait_recv()
                start_col = 0
                for ref in out:
                    cols = pl.ds(start_col, ref.shape[1])
                    start_col += ref.shape[1]
                    pieces = [array.at[ring_device(n, p), part, cols]]
                    pieces += [slots.at[s - 1, way, part, cols] for way in range(2)]
                    add_rows(ref.at[part], pieces, size, F32)
                continue
            for way in range(2):
                if s == 0 and i % 2 != way:
                    continue
                away = n // 2 - s
                block = ring_device(n, (p + away) % n if way == 0 else (p + n - away) % n)
                source = array.at[block, part]
                if (s - 1, j, i, way) in self.copies:
                    self.copies[s - 1, j, i, way].wait_recv()
                    held = slots.at[s - 1, way, part]
                    add_rows(held, [held, source], size, array.dtype)
                    source = held
                copy = remote(
                    source,
                    slots.at[s, way, part],
                    self.send_sem.at[s, j, i, way],
                    self.recv_sem.at[s, j, i, way],
                    self.nxt if way == 0 else self.prv,
                )
                copy.start()
                self.copies[s, j, i, way] = copy

    def end(self):
        for copy in self.copies.values():
            copy.wait_send()


def last_kernel(
    n,
    grad_a,
    misc,
    gains,
    d_normed,
    extra,
    d_mixed,
    hidden,
    gain,
    result,
    out_zx,
    out_state,
    out_dt,
    out_misc,
    out_gains,
    all_hidden,
    all_result,
    gains_mine,
    gains_core,
    gains_chip,
    rows_core,
    rows_chip,
    rows_bf,
    slots_a,
    slots_misc,
    slots_gains,
    ring_send,
    ring_recv,
    mp_send,
    mp_recv,
    local_sem,
):
    m = lax.axis_index("mp")
    core, chip = mp_partners(m)
    far = (m + 2) % 4
    beside = m + 1 - 2 * (m % 2)
    ring = RingScatter(
        n,
        [grad_a, misc, gains_mine],
        [(out_zx, out_state, out_dt), (out_misc,), (out_gains,)],
        [slots_a, slots_misc, slots_gains],
        [ring_send, ring_recv],
    )
    greet([core, chip, ring.nxt, ring.prv])
    sent = []

    def over_mp(i, source, target, device):
        copy = remote(source, target, mp_send.at[i], mp_recv.at[i], device)
        copy.start()
        sent.append(copy)
        return copy

    ring.step(0, 0)
    ring.step(0, 1)
    gains_one = over_mp(0, gains, gains_core, core)
    rows_far = over_mp(1, d_normed.at[(beside + 2) % 4], rows_core.at[1], core)
    rows_near = over_mp(2, d_normed.at[beside], rows_core.at[0], core)
    own_result = pltpu.make_async_copy(result, all_result.at[m], local_sem.at[0])
    own_result.start()
    gains_one.wait_recv()
    for b in range(n):
        add_rows(gains_mine.at[b], [gains.at[b], gains_core.at[b]], 16, F32)
    gains_two = over_mp(3, gains_mine, gains_chip, chip)
    count = d_mixed.shape[0]
    rows_far.wait_recv()
    add_rows(rows_core.at[1], [rows_core.at[1], d_normed.at[far]], count, BF)
    rows_two = over_mp(4, rows_core.at[1], rows_chip, chip)
    result_chip = over_mp(5, result, all_result.at[m], chip)
    result_core = over_mp(6, result, all_result.at[m], core)
    ring.step(1, 0)
    ring.step(1, 1)
    gains_two.wait()
    for b in range(n):
        add_rows(gains_mine.at[b], [gains_mine.at[b], gains_chip.at[b]], 16, F32)
    ring.step(0, 2)
    rows_near.wait_recv()
    rows_two.wait_recv()

    def body(i, carry):
        sl = pl.ds(pl.multiple_of(i * 16, 16), 16)
        d_n = d_normed[m, sl, :].astype(F32) + rows_core[0, sl, :].astype(F32)
        d_n = d_n + rows_chip[sl, :].astype(F32) + extra[sl, :]
        x = hidden[sl, :].astype(F32)
        inv = lax.rsqrt(jnp.mean(x * x, axis=1, keepdims=True) + EPS)
        unit = x * inv
        d_unit = d_n * gain[...]
        mean = jnp.mean(d_unit * unit, axis=1, keepdims=True)
        rows_bf[sl, :] = (d_mixed[sl, :] + inv * (d_unit - unit * mean)).astype(BF)
        return carry

    lax.fori_loop(0, count // 16, body, 0)
    own_hidden = pltpu.make_async_copy(rows_bf, all_hidden.at[m], local_sem.at[1])
    own_hidden.start()
    hidden_chip = over_mp(7, rows_bf, all_hidden.at[m], chip)
    hidden_core = over_mp(8, rows_bf, all_hidden.at[m], core)
    arrive = []
    for s in range(2, n // 2 + 1):
        ring.step(s, 0)
        ring.step(s, 1)
        ring.step(s - 1, 2)
        if s == 2:
            result_chip.wait_recv()
            arrive.append(over_mp(9, all_result.at[far], all_result.at[far], core))
        if s == n // 2 - 1:
            hidden_chip.wait_recv()
            arrive.append(over_mp(10, all_hidden.at[far], all_hidden.at[far], core))
    ring.step(n // 2, 2)
    for copy in [result_core, hidden_core] + arrive:
        copy.wait_recv()
    own_result.wait()
    own_hidden.wait()
    for copy in sent:
        if copy is not gains_two:
            copy.wait_send()
    ring.end()


def last_exchange(grad_a, misc, gains, d_normed, extra, d_mixed, hidden, gain, result, cols, cid):
    n = lax.axis_size("dp")
    shard = grad_a.shape[1]
    rows, model = d_mixed.shape
    dma = pltpu.SemaphoreType.DMA
    every = jax.ShapeDtypeStruct((4, rows, model), BF)
    return pl.pallas_call(
        partial(last_kernel, n),
        out_shape=[jax.ShapeDtypeStruct((shard, c), F32) for c in cols]
        + [jax.ShapeDtypeStruct(a.shape[1:], F32) for a in (misc, gains)]
        + [every, every],
        in_specs=[VM] * 8 + [ANY],
        out_specs=[VM] * 5 + [ANY] * 2,
        scratch_shapes=[
            pltpu.VMEM(gains.shape, F32),
            pltpu.VMEM(gains.shape, F32),
            pltpu.VMEM(gains.shape, F32),
            pltpu.VMEM((2, rows, model), BF),
            pltpu.VMEM((rows, model), BF),
            pltpu.VMEM((rows, model), BF),
        ]
        + RingScatter.scratch(n, [grad_a, misc, gains])
        + [dma((11,)), dma((11,)), dma((2,))],
        compiler_params=pltpu.CompilerParams(
            collective_id=cid, has_side_effects=True, vmem_limit_bytes=56 * 1024 * 1024
        ),
    )(grad_a, misc, gains, d_normed, extra, d_mixed, hidden, gain, result)


def mp_scatter_kernel(x, out, from_core, from_chip, send_sem, recv_sem):
    m = lax.axis_index("mp")
    core, chip = mp_partners(m)
    mine, far = m, (m + 2) % 4
    beside = m + 1 - 2 * (m % 2)
    parts = [(pl.ds(start, size), size) for start, size in chunk_rows(0, out.shape[0])]
    greet([core, chip])
    first, last = [], []
    for slot, block in ((1, (beside + 2) % 4), (0, beside)):
        for i, (part, _) in enumerate(parts):
            copy = remote(
                x.at[block, part], from_core.at[slot, part], send_sem.at[slot, i], recv_sem.at[slot, i], core
            )
            copy.start()
            first.append(copy)
    for i, (part, size) in enumerate(parts):
        first[i].wait_recv()
        held = from_core.at[1, part]
        add_rows(held, [held, x.at[far, part]], size, x.dtype)
        copy = remote(held, from_chip.at[part], send_sem.at[2, i], recv_sem.at[2, i], chip)
        copy.start()
        last.append(copy)
    for i, (part, size) in enumerate(parts):
        first[len(parts) + i].wait_recv()
        last[i].wait_recv()
        add_rows(out.at[part], [x.at[mine, part], from_core.at[0, part], from_chip.at[part]], size, F32)
    for copy in first + last:
        copy.wait_send()


def scatter_mp(x, cid):
    rows, cols = x.shape[1:]
    count = len(chunk_rows(0, rows))
    return pl.pallas_call(
        mp_scatter_kernel,
        out_shape=jax.ShapeDtypeStruct((rows, cols), F32),
        in_specs=[VM],
        out_specs=VM,
        scratch_shapes=[
            pltpu.VMEM((2, rows, cols), x.dtype),
            pltpu.VMEM((rows, cols), x.dtype),
            pltpu.SemaphoreType.DMA((3, count)),
            pltpu.SemaphoreType.DMA((3, count)),
        ],
        compiler_params=pltpu.CompilerParams(
            collective_id=cid, has_side_effects=True, vmem_limit_bytes=32 * 1024 * 1024
        ),
    )(x)


def mp_gather_kernel(k, *refs):
    ins, outs = refs[:k], refs[k : 2 * k]
    local_sem, send_sem, recv_sem = refs[2 * k :]
    m = lax.axis_index("mp")
    core, chip = mp_partners(m)
    far = (m + 2) % 4
    greet([core, chip])
    copies, local, arrive = [], [], []
    for j in range(k):
        to_chip = remote(ins[j], outs[j].at[m], send_sem.at[0, j], recv_sem.at[0, j], chip)
        to_chip.start()
        to_core = remote(ins[j], outs[j].at[m], send_sem.at[1, j], recv_sem.at[1, j], core)
        to_core.start()
        own = pltpu.make_async_copy(ins[j], outs[j].at[m], local_sem.at[j])
        own.start()
        copies += [to_chip, to_core]
        arrive.append(to_chip)
        local.append(own)
    onward = []
    for j in range(k):
        arrive[j].wait_recv()
        copy = remote(outs[j].at[far], outs[j].at[far], send_sem.at[2, j], recv_sem.at[2, j], core)
        copy.start()
        onward.append(copy)
    for j in range(k):
        copies[2 * j + 1].wait_recv()
        onward[j].wait_recv()
        local[j].wait()
    for copy in copies + onward:
        copy.wait_send()


def gather_mp(arrays, cid):
    k = len(arrays)
    return pl.pallas_call(
        partial(mp_gather_kernel, k),
        out_shape=[jax.ShapeDtypeStruct((4,) + a.shape, a.dtype) for a in arrays],
        in_specs=[ANY] * k,
        out_specs=[ANY] * k,
        scratch_shapes=[
            pltpu.SemaphoreType.DMA((k,)),
            pltpu.SemaphoreType.DMA((3, k)),
            pltpu.SemaphoreType.DMA((3, k)),
        ],
        compiler_params=pltpu.CompilerParams(collective_id=cid, has_side_effects=True),
    )(*arrays)


class TokenGather:
    def __init__(self, n, both, x, out, sems):
        self.n, self.both, self.out = n, both, out
        self.local, self.ring_s, self.ring_r, self.core_s, self.core_r, self.chip_s, self.chip_r = sems
        self.d, self.m = lax.axis_index("dp"), lax.axis_index("mp")
        self.far = (self.m + 2) % 4
        self.core, self.chip = mp_partners(self.m)
        self.p, self.nxt, self.prv = ring_neighbours(n)
        rows = out.shape[2]
        base = pl.multiple_of(self.m * rows, rows) if x.shape[0] > rows else 0
        self.x = x.at[pl.ds(base, rows)]
        self.pieces = [(0,) + c for c in chunk_rows(0, rows)] + [(1,) + c for c in chunk_rows(0, both)]
        self.sent, self.pending = [], {}
        self.ring, self.chips = {}, {}

    @staticmethod
    def scratch(n, rows, both):
        dma = pltpu.SemaphoreType.DMA
        own, far = len(chunk_rows(0, rows)), len(chunk_rows(0, both))
        steps = n // 2
        return [
            dma((3,)),
            dma((steps, own + far, 2)),
            dma((steps, own + far, 2)),
            dma((steps + 1, 2 * own + far, 2)),
            dma((steps + 1, 2 * own + far, 2)),
            dma((steps + 1, own, 2)),
            dma((steps + 1, own, 2)),
        ]

    def send(self, source, place, s_sem, r_sem, target):
        copy = remote(source, place, s_sem, r_sem, target)
        copy.start()
        self.sent.append(copy)
        return copy

    def begin(self):
        own = self.out.at[self.d, self.m]
        self.load = pltpu.make_async_copy(self.x, own, self.local.at[0])
        self.load.start()
        self.first = None
        if self.both:
            part = pl.ds(0, self.both)
            self.first = remote(
                self.x.at[part], own.at[part], self.local.at[1], self.local.at[2], self.chip
            )
            self.first.start()
            self.sent.append(self.first)

    def step(self, s, between=None):
        n, p = self.n, self.p
        for k, (is_far, start, rows) in enumerate(self.pieces):
            if k > 0 and between is not None:
                between()
            for way in range(2):
                origin = ring_device(n, (p + n - s) % n if way == 0 else (p + s) % n)
                place = self.far if is_far else self.m
                region = self.out.at[origin, place, pl.ds(start, rows)]
                source = region if s > 0 or is_far else self.x.at[pl.ds(start, rows)]
                if (s - 1, k, way) in self.ring:
                    self.ring[s - 1, k, way].wait_recv()
                elif s > 0:
                    continue
                elif is_far and self.first is not None:
                    self.first.wait_recv()
                    self.first = None
                if s + 1 < n // 2 or (s + 1 == n // 2 and k % 2 == way):
                    self.ring[s, k, way] = self.send(
                        source,
                        region,
                        self.ring_s.at[s, k, way],
                        self.ring_r.at[s, k, way],
                        self.nxt if way == 0 else self.prv,
                    )
                if s == 0 and way == 1:
                    continue
                self.pending.setdefault(s, []).append(
                    self.send(source, region, self.core_s.at[s, k, way], self.core_r.at[s, k, way], self.core)
                )
                if not is_far and start >= self.both:
                    self.chips[s, k, way] = (
                        self.send(
                            source, region, self.chip_s.at[s, k, way], self.chip_r.at[s, k, way], self.chip
                        ),
                        self.out.at[origin, self.far, pl.ds(start, rows)],
                    )

    def pass_on(self, s):
        total = len(self.pieces)
        for k in range(total):
            for way in range(2):
                if (s, k, way) in self.chips:
                    copy, region = self.chips[s, k, way]
                    copy.wait_recv()
                    at = (s, total + k, way)
                    self.pending.setdefault(s, []).append(
                        self.send(region, region, self.core_s.at[at], self.core_r.at[at], self.core)
                    )

    def blocks(self, s):
        n, p = self.n, self.p
        if s in (0, n // 2):
            return [ring_device(n, (p + s) % n)]
        return [ring_device(n, (p + n - s) % n), ring_device(n, (p + s) % n)]

    def complete(self, s):
        if s == 0:
            self.load.wait()
        for copy in self.pending.pop(s):
            copy.wait_recv()

    def end(self):
        for s in sorted(self.pending):
            self.complete(s)
        for copy in self.sent:
            copy.wait_send()


class SlotWork:
    def __init__(self, own, small, position):
        self.own, self.small, self.position = own, small, position
        self.first = (lax.axis_index("dp") * own).astype(F32)
        self.length = position.shape[2]

    def count_with(self, earlier):
        self.earlier = earlier
        row = lax.broadcasted_iota(jnp.int32, earlier.shape, 0)
        col = lax.broadcasted_iota(jnp.int32, earlier.shape, 1)
        earlier[...] = jnp.where(row < col, 1.0, 0.0).astype(BF)

    def gate_with(self, router, gates, slot_gates):
        self.router, self.gates, self.slot_gates = router, gates, slot_gates

    def named(self, block, first, count):
        length = self.length
        routes = self.small[block, :, 0:length].astype(F32)
        expert = lax.broadcasted_iota(jnp.int32, (count, length), 0).astype(F32) + first
        found = routes[1:2, :] == expert
        for k in range(2, TOPK + 1):
            found = found | (routes[k : k + 1, :] == expert)
        return found

    def place(self, block):
        named = self.named(block, self.first, 8)
        count = dot(jnp.where(named, 1.0, 0.0).astype(BF), self.earlier[...])
        self.position[block] = jnp.where(named, count, -1.0)[0 : self.own, :]

    def pick(self, block):
        return pick_matrix(self.position[block], self.own)

    def gate(self, block, rows, pick):
        own = self.own
        logits = dot(rows, self.router[...])
        named = jnp.where(self.named(block, 0.0, LANES), 1.0, 0.0).T > 0.5
        top = jnp.max(jnp.where(named, logits, MASKED), axis=1, keepdims=True)
        powers = jnp.where(named, jnp.exp(jnp.minimum(logits - top, 0.0)), 0.0)
        gate = powers / jnp.sum(powers, axis=1, keepdims=True)
        self.gates[block] = gate
        of_slot = dot(pick, jnp.concatenate(two_parts(gate), axis=1))
        of_slot = of_slot[:, 0:LANES] + of_slot[:, LANES : 2 * LANES]
        row = lax.broadcasted_iota(jnp.int32, of_slot.shape, 0)
        col = lax.broadcasted_iota(jnp.int32, of_slot.shape, 1)
        mine = col - lax.axis_index("dp") * own == row // CAP
        of_slot = jnp.sum(jnp.where(mine, of_slot, 0.0), axis=1, keepdims=True)
        of_slot = jnp.broadcast_to(of_slot, (own * CAP, LANES)).reshape(own, CAP, LANES)
        for e in range(own):
            self.slot_gates[e, block] = of_slot[e]


class RowStream:
    def __init__(self, source, target, in_buf, out_buf, load_sem, store_sem):
        self.source, self.target, self.in_buf, self.out_buf = source, target, in_buf, out_buf
        self.load_sem, self.store_sem = load_sem, store_sem
        self.loads, self.stores = [], []

    def load(self, block):
        at = len(self.loads) % self.in_buf.shape[0]
        copy = pltpu.make_async_copy(self.source.at[block], self.in_buf.at[at], self.load_sem.at[at])
        copy.start()
        self.loads.append(copy)

    def take(self, i, wait=True):
        if wait:
            self.loads[i].wait()
        held = self.in_buf[i % self.in_buf.shape[0]]
        return held.reshape(-1, held.shape[-1])

    def give(self, i, block, picked):
        if i > 1:
            self.stores[i - 2].wait()
        self.out_buf[i % 2] = picked.astype(BF).reshape(self.out_buf.shape[1:])
        copy = pltpu.make_async_copy(
            self.out_buf.at[i % 2], self.target.at[:, block], self.store_sem.at[i % 2]
        )
        copy.start()
        self.stores.append(copy)

    def end(self):
        for copy in self.stores[-2:]:
            copy.wait()


def token_gather_kernel(
    n,
    both,
    own,
    units,
    x,
    position,
    small,
    weights,
    cot,
    out,
    x_rows,
    gates,
    slot_gates,
    block,
    act,
    d_mid,
    shared_res,
    shared_d,
    x_in,
    x_out,
    mid,
    stream_sem,
    *sems,
):
    inner = weights.shape[1] - 3 * units - LANES
    shared_in = pl.ds(inner, 2 * units)
    shared_out = pl.ds(inner + 2 * units, units)
    router = weights.at[:, pl.ds(inner + 3 * units, LANES)]
    gather = TokenGather(n, both, x, out, sems)
    work = SlotWork(own, small, position)
    work.gate_with(router, gates, slot_gates)
    x_stream = RowStream(out, x_rows, x_in, x_out, stream_sem.at[0], stream_sem.at[1])
    half = n // 2
    greet([gather.core, gather.chip, gather.nxt, gather.prv])
    gather.begin()
    tasks = []

    def shared(held):
        def first():
            block[...] = x_stream.take(held["at"])
            mid[...] = dot(block[...], weights[:, shared_in])

        def second():
            gate, up = mid[:, 0:units], mid[:, units : 2 * units]
            sig = jax.nn.sigmoid(gate)
            silu = gate * sig
            act[...] = (silu * up).astype(BF)
            d_act = dot(cot[...], weights[:, shared_out])
            slope = sig * (1.0 + gate * (1.0 - sig))
            d_mid[:, 0:units] = (d_act * up * slope).astype(BF)
            d_mid[:, units : 2 * units] = (d_act * silu).astype(BF)

        def third():
            shared_res[...] = dot(act[...], weights[:, shared_out], ((1,), (1,)))

        def fourth():
            shared_d[...] = dot(d_mid[...], weights[:, shared_in], ((1,), (1,)))

        return [first, second, third, fourth]

    def pick_x(s):
        blocks = gather.blocks(s)
        held = {}

        def start():
            gather.complete(s)
            held["at"] = len(x_stream.loads)
            for block in blocks:
                x_stream.load(block)

        found = [start]
        if s == 0:
            found += shared(held)
        for i, block in enumerate(blocks):

            def pick(i=i, block=block):
                held[i] = work.pick(block)
                rows = x_stream.take(held["at"] + i, s > 0)
                x_stream.give(held["at"] + i, block, dot(held[i], rows))

            def gate(i=i, block=block):
                work.gate(block, x_stream.take(held["at"] + i, False), held[i])

            found += [pick, gate]
        return found

    def between():
        for _ in range(1 if len(tasks) < 6 else 2):
            if tasks:
                tasks.pop(0)()

    gather.step(0)
    for s in range(1, half + 1):
        gather.step(s, between)
        gather.pass_on(s - 1)
        tasks += pick_x(s - 1)
    final = pick_x(half)
    while len(tasks) > 4:
        tasks.pop(0)()
    gather.pass_on(half)
    tasks.pop(0)()
    tasks.pop(0)()
    final.pop(0)()
    for task in tasks + final:
        task()
    gather.end()
    x_stream.end()


def gather_tokens(x, position, small, weights, cot, units, cid):
    n, own, tokens = position.shape
    quarter, model = x.shape
    both = quarter // 2
    return pl.pallas_call(
        partial(token_gather_kernel, n, both, own, units),
        out_shape=[
            jax.ShapeDtypeStruct((n, 4) + x.shape, x.dtype),
            jax.ShapeDtypeStruct((own, n, CAP, model), BF),
            jax.ShapeDtypeStruct((n, tokens, LANES), F32),
            jax.ShapeDtypeStruct((own, n, CAP, LANES), F32),
            jax.ShapeDtypeStruct((tokens, model), BF),
            jax.ShapeDtypeStruct((tokens, units), BF),
            jax.ShapeDtypeStruct((tokens, 2 * units), BF),
            jax.ShapeDtypeStruct((tokens, model), F32),
            jax.ShapeDtypeStruct((tokens, model), F32),
        ],
        in_specs=[ANY, VM, VM, VM, VM],
        out_specs=[ANY, ANY] + [VM] * 7,
        scratch_shapes=[
            pltpu.VMEM((3, 4, quarter, model), BF),
            pltpu.VMEM((2, own, CAP, model), BF),
            pltpu.VMEM((tokens, 2 * units), F32),
            pltpu.SemaphoreType.DMA((2, 3)),
        ]
        + TokenGather.scratch(n, quarter, both),
        compiler_params=pltpu.CompilerParams(
            collective_id=cid, has_side_effects=True, vmem_limit_bytes=56 * 1024 * 1024
        ),
    )(x, position, small, weights, cot)


def slots_kernel(own, y, small, y_rows, position, earlier):
    work = SlotWork(own, small, position)
    work.count_with(earlier)
    work.place(0)
    y_rows[...] = dot(work.pick(0), y[0]).astype(BF).reshape(y_rows.shape)


def slots_of(y, small, own):
    n, tokens, model = y.shape
    return pl.pallas_call(
        partial(slots_kernel, own),
        grid=(n,),
        out_shape=[
            jax.ShapeDtypeStruct((own, n, CAP, model), BF),
            jax.ShapeDtypeStruct((n, own, tokens), F32),
        ],
        in_specs=[token_spec(tokens, model), token_spec(small.shape[1], small.shape[2])],
        out_specs=[slot_spec(own, model), token_spec(own, tokens)],
        scratch_shapes=[pltpu.VMEM((tokens, tokens), BF)],
        compiler_params=BIG,
    )(y, small)


def first_kernel(n, k, *refs):
    ins, x = refs[:k], refs[k]
    outs, x_out = refs[k + 1 : 2 * k + 1], refs[2 * k + 1]
    ring = RingGather(n, ins, outs, refs[2 * k + 2 : 2 * k + 5])
    gather = TokenGather(n, 0, x, x_out, refs[2 * k + 5 :])
    greet([gather.core, gather.chip, gather.nxt, gather.prv])
    ring.begin()
    gather.begin()
    for s in range(n // 2 + 1):
        gather.step(s)
        ring.step(s)
        if s > 0:
            gather.pass_on(s - 1)
    gather.pass_on(n // 2)
    gather.end()
    ring.end()


def first_gather(arrays, x, cid):
    n, k = lax.axis_size("dp"), len(arrays)
    rows, cols = x.shape[0] // 4, x.shape[1]
    return pl.pallas_call(
        partial(first_kernel, n, k),
        out_shape=[jax.ShapeDtypeStruct((n,) + a.shape, a.dtype) for a in arrays]
        + [jax.ShapeDtypeStruct((n, 4, rows, cols), x.dtype)],
        in_specs=[ANY] * (k + 1),
        out_specs=[ANY] * (k + 1),
        scratch_shapes=RingGather.scratch(n, arrays) + TokenGather.scratch(n, rows, 0),
        compiler_params=pltpu.CompilerParams(collective_id=cid, has_side_effects=True),
    )(*arrays, x)


def token_scatter_kernel(
    n,
    x,
    out,
    from_core,
    slots,
    loads,
    far_loads,
    from_chip,
    to_chip,
    first,
    done,
    last_buf,
    load_sem,
    far_sem,
    core_send,
    core_recv,
    chip_send,
    chip_recv,
    send_sem,
    recv_sem,
    last_send,
    last_recv,
):
    m = lax.axis_index("mp")
    c, y = m % 2, m // 2
    core, chip = mp_partners(m)
    far = (m + 2) % 4
    beside = m + 1 - 2 * c
    p, nxt, prv = ring_neighbours(n)
    rows = out.shape[0]
    half, steps = rows // 2, n // 2
    greet([core, chip, nxt, prv])

    def block_of(i):
        s = (i + 1) // 2
        return ring_device(n, (p + steps - s) % n if i % 2 or i == 0 else (p + n - steps + s) % n)

    over, sent, loading, chips = {}, [], {}, {}
    loaded, summed = set(), set()
    upper, lower, whole = pl.ds(half, half), pl.ds(0, half), pl.ds(0, rows)

    def core_sends(i):
        if i >= n:
            return
        block = block_of(i)
        moves = [((beside + 2) % 4, 1 - y, upper), (beside, y, whole), ((beside + 2) % 4, 1 - y, lower)]
        for k, (theirs, piece, part) in enumerate(moves):
            copy = remote(
                x.at[block, theirs, part],
                from_core.at[block, piece, part],
                core_send.at[i, k],
                core_recv.at[i, k],
                core,
            )
            copy.start()
            over[i, k] = copy
            sent.append(copy)

    def start_pair(name, source, other, target, sems):
        loading[name] = []
        for k, ref in enumerate((source, other)):
            copy = pltpu.make_async_copy(ref, target.at[k], sems.at[k])
            copy.start()
            loading[name].append(copy)

    def load(i):
        if i >= n:
            return
        block = block_of(i)
        at = i % 4
        over[i, 1].wait_recv()
        start_pair(
            (i, 0), x.at[block, m], from_core.at[block, y], loads.at[at, :, whole], load_sem.at[at, 0]
        )
        over[i, 2].wait_recv()
        start_pair(
            (i, 1),
            x.at[block, far, lower],
            from_core.at[block, 1 - y, lower],
            loads.at[at, :, pl.ds(rows, half)],
            load_sem.at[at, 1],
        )

    def load_far(i):
        if i >= n:
            return
        block = block_of(i)
        over[i, 0].wait_recv()
        start_pair(
            (i, 2),
            x.at[block, far, upper],
            from_core.at[block, 1 - y, upper],
            far_loads.at[i % 2],
            far_sem.at[i % 2],
        )

    def to_other_chip(i):
        if i >= n:
            return
        for copy in loading[i, 2]:
            copy.wait()
        if i > 1:
            chips[i - 2].wait_send()
        add_rows(to_chip.at[i % 2], [far_loads.at[i % 2, 0], far_loads.at[i % 2, 1]], half, BF)
        copy = remote(to_chip.at[i % 2], from_chip.at[i], chip_send.at[i], chip_recv.at[i], chip)
        copy.start()
        chips[i] = copy

    chunks = chunk_rows(0, rows + half)
    count = len(chunks)
    order = [k for k in range(count) if chunks[k][0] >= rows]
    order += [k for k in range(count) if chunks[k][0] < rows]

    def pieces_of(i, k):
        start, size = chunks[k]
        area = pl.ds(start, size)
        if i not in loaded:
            loaded.add(i)
            for copy in loading[i, 0] + loading[i, 1]:
                copy.wait()
        found = [loads.at[i % 4, 0, area], loads.at[i % 4, 1, area]]
        if half <= start < rows:
            if i not in summed:
                summed.add(i)
                chips[i].wait_recv()
            found.append(from_chip.at[i, pl.ds(start - half, size)])
        return found

    for i in range(3):
        core_sends(i)
    load_far(0)
    load(0)
    load_far(1)
    to_other_chip(0)
    load_far(2)
    to_other_chip(1)
    core_sends(3)
    core_sends(4)
    load(1)
    to_other_chip(2)
    load(2)
    ring = {}
    for s in range(steps):
        for k, way in [(k, way) for k in order for way in range(2) if s > 0 or k % 2 == way]:
            start, size = chunks[k]
            area = pl.ds(start, size)
            if s == 0:
                target, pieces = first.at[area], pieces_of(0, k)
            else:
                target, pieces = slots.at[s - 1, way, area], pieces_of(2 * s - 1 + way, k)
                if (s - 1, k, way) in ring:
                    ring[s - 1, k, way].wait_recv()
                    pieces.append(target)
            add_rows(target, pieces, size, BF)
            copy = remote(
                target,
                slots.at[s, way, area],
                send_sem.at[s, k, way],
                recv_sem.at[s, k, way],
                nxt if way == 0 else prv,
            )
            copy.start()
            ring[s, k, way] = copy
        for i in (2 * s + 3, 2 * s + 4):
            load_far(i)
            core_sends(i + 2)
            to_other_chip(i)
            load(i)
    last = []
    for k in order:
        start, size = chunks[k]
        area = pl.ds(start, size)
        pieces = pieces_of(n - 1, k)
        for way in range(2):
            ring[steps - 1, k, way].wait_recv()
            pieces.append(slots.at[steps - 1, way, area])
        if start < rows:
            add_rows(out.at[area], pieces, size, F32)
            continue
        at = pl.ds(start - rows, size)
        add_rows(done.at[at], pieces, size, BF)
        copy = remote(done.at[at], last_buf.at[at], last_send.at[k], last_recv.at[k], chip)
        copy.start()
        last.append(copy)
    for copy in last:
        copy.wait_recv()
    add_rows(out.at[lower], [out.at[lower], last_buf], half, F32)
    for copy in sent + list(ring.values()) + last + [chips[n - 2], chips[n - 1]]:
        copy.wait_send()


def scatter_tokens(x, cid):
    n, _, rows, cols = x.shape
    half, steps = rows // 2, n // 2
    count = len(chunk_rows(0, rows + half))
    dma = pltpu.SemaphoreType.DMA
    out, _ = pl.pallas_call(
        partial(token_scatter_kernel, n),
        out_shape=[
            jax.ShapeDtypeStruct((rows, cols), F32),
            jax.ShapeDtypeStruct((n, 2, rows, cols), BF),
        ],
        in_specs=[ANY],
        out_specs=[VM, ANY],
        scratch_shapes=[
            pltpu.VMEM((steps, 2, rows + half, cols), BF),
            pltpu.VMEM((4, 2, rows + half, cols), BF),
            pltpu.VMEM((2, 2, half, cols), BF),
            pltpu.VMEM((n, half, cols), BF),
            pltpu.VMEM((2, half, cols), BF),
            pltpu.VMEM((rows + half, cols), BF),
            pltpu.VMEM((half, cols), BF),
            pltpu.VMEM((half, cols), BF),
            dma((4, 2, 2)),
            dma((2, 2)),
            dma((n, 3)),
            dma((n, 3)),
            dma((n,)),
            dma((n,)),
            dma((steps, count, 2)),
            dma((steps, count, 2)),
            dma((count,)),
            dma((count,)),
        ],
        compiler_params=pltpu.CompilerParams(
            collective_id=cid, has_side_effects=True, vmem_limit_bytes=56 * 1024 * 1024
        ),
    )(x)
    return out


def put_scatter_kernel(
    n,
    own,
    position,
    slot_a,
    slot_b,
    slot_c,
    shared_a,
    shared_b,
    out,
    from_core,
    made,
    in_a,
    in_b,
    in_c,
    slots,
    loads,
    far_loads,
    from_chip,
    to_chip,
    first,
    done,
    last_buf,
    slot_sem,
    load_sem,
    far_sem,
    core_send,
    core_recv,
    chip_send,
    chip_recv,
    send_sem,
    recv_sem,
    last_send,
    last_recv,
):
    m = lax.axis_index("mp")
    c, y = m % 2, m // 2
    core, chip = mp_partners(m)
    far = (m + 2) % 4
    beside = m + 1 - 2 * c
    p, nxt, prv = ring_neighbours(n)
    rows = out.shape[0]
    model = shared_a.shape[1]
    half, steps = rows // 2, n // 2

    def block_of(i):
        s = (i + 1) // 2
        return ring_device(n, (p + steps - s) % n if i % 2 or i == 0 else (p + n - steps + s) % n)

    over, sent, loading, chips, arriving = {}, [], {}, {}, {}
    loaded, summed = set(), set()
    upper, lower, whole = pl.ds(half, half), pl.ds(0, half), pl.ds(0, rows)

    def slot_load(i):
        if i >= n:
            return
        arriving[i] = []
        for k, (source, target) in enumerate(((slot_a, in_a), (slot_b, in_b), (slot_c, in_c))):
            copy = pltpu.make_async_copy(source.at[:, block_of(i)], target.at[i % 2], slot_sem.at[i % 2, k])
            copy.start()
            arriving[i].append(copy)

    def make(i):
        if i >= n:
            return
        slot_load(i + 1)
        if i >= 4:
            for k in range(3):
                over[i - 4, k].wait_send()
        pick = pick_matrix(position[block_of(i)], own)
        for copy in arriving[i]:
            copy.wait()
        start = 0
        for target, shared in ((in_a, shared_a), (in_b, shared_b), (in_c, None)):
            cols = target.shape[3]
            total = dot(pick, target[i % 2].reshape(own * CAP, cols), ((0,), (0,)))
            if i == n - 1 and shared is not None:
                total = total + shared[...]
            made[i % 4, :, :, start : start + cols] = total.astype(BF).reshape(4, rows, cols)
            start += cols

    def core_sends(i):
        if i >= n:
            return
        block = block_of(i)
        moves = [((beside + 2) % 4, 1 - y, upper), (beside, y, whole), ((beside + 2) % 4, 1 - y, lower)]
        for k, (theirs, piece, part) in enumerate(moves):
            copy = remote(
                made.at[i % 4, theirs, part],
                from_core.at[block, piece, part],
                core_send.at[i, k],
                core_recv.at[i, k],
                core,
            )
            copy.start()
            over[i, k] = copy
            if i >= n - 4:
                sent.append(copy)

    def load(i):
        if i >= n:
            return
        block = block_of(i)
        loading[i] = []
        for k, (piece, part, at) in enumerate(((y, whole, 0), (1 - y, lower, rows))):
            over[i, k + 1].wait_recv()
            copy = pltpu.make_async_copy(
                from_core.at[block, piece, part],
                loads.at[i % 4, pl.ds(at, rows if k == 0 else half)],
                load_sem.at[i % 4, k],
            )
            copy.start()
            loading[i].append(copy)

    def to_other_chip(i):
        if i >= n:
            return
        over[i, 0].wait_recv()
        copy = pltpu.make_async_copy(
            from_core.at[block_of(i), 1 - y, upper], far_loads.at[i % 2], far_sem.at[i % 2]
        )
        copy.start()
        load(i)
        if i > 1:
            chips[i - 2].wait_send()
        copy.wait()
        add_rows(to_chip.at[i % 2], [far_loads.at[i % 2], made.at[i % 4, far, upper]], half, BF)
        copy = remote(to_chip.at[i % 2], from_chip.at[i], chip_send.at[i], chip_recv.at[i], chip)
        copy.start()
        chips[i] = copy

    chunks = chunk_rows(0, rows + half)
    order = [k for k in range(len(chunks)) if chunks[k][0] >= rows]
    order += [k for k in range(len(chunks)) if chunks[k][0] < rows]

    def pieces_of(i, k):
        start, size = chunks[k]
        area = pl.ds(start, size)
        if i not in loaded:
            loaded.add(i)
            for copy in loading[i]:
                copy.wait()
        found = [loads.at[i % 4, area]]
        if start < rows:
            found.append(made.at[i % 4, m, area])
        else:
            found.append(made.at[i % 4, far, pl.ds(start - rows, size)])
        if half <= start < rows:
            if i not in summed:
                summed.add(i)
                chips[i].wait_recv()
            found.append(from_chip.at[i, pl.ds(start - half, size)])
        return found

    slot_load(0)
    make(0)
    greet([core, chip, nxt, prv])
    core_sends(0)
    make(1)
    core_sends(1)
    to_other_chip(0)
    ring = {}
    for s in range(steps):
        for k, way in [(k, way) for k in order for way in range(2) if s > 0 or k % 2 == way]:
            start, size = chunks[k]
            area = pl.ds(start, size)
            if s == 0:
                if start == half:
                    make(2)
                    core_sends(2)
                target, pieces = first.at[area], pieces_of(0, k)
            else:
                target, pieces = slots.at[s - 1, way, area], pieces_of(2 * s - 1 + way, k)
                if (s - 1, k, way) in ring:
                    ring[s - 1, k, way].wait_recv()
                    pieces.append(target)
            add_rows(target, pieces, size, BF)
            copy = remote(
                target,
                slots.at[s, way, area],
                send_sem.at[s, k, way],
                recv_sem.at[s, k, way],
                nxt if way == 0 else prv,
            )
            copy.start()
            ring[s, k, way] = copy
        if s == 0:
            to_other_chip(1)
            to_other_chip(2)
        for i in (2 * s + 3, 2 * s + 4):
            make(i)
            core_sends(i)
        for i in (2 * s + 3, 2 * s + 4):
            to_other_chip(i)
    last = []
    for k in order:
        start, size = chunks[k]
        area = pl.ds(start, size)
        pieces = pieces_of(n - 1, k)
        for way in range(2):
            ring[steps - 1, k, way].wait_recv()
            pieces.append(slots.at[steps - 1, way, area])
        if start < rows:
            add_rows(out.at[area], pieces, size, F32)
            continue
        at = pl.ds(start - rows, size)
        add_rows(done.at[at], pieces, size, BF)
        copy = remote(done.at[at], last_buf.at[at], last_send.at[k], last_recv.at[k], chip)
        copy.start()
        last.append(copy)
    for copy in last:
        copy.wait_recv()
    add_rows(out.at[lower], [out.at[lower], last_buf], half, F32)
    for copy in sent + list(ring.values()) + last + [chips[n - 2], chips[n - 1]]:
        copy.wait_send()


def put_scatter(position, rows_a, rows_b, rows_c, shared_a, shared_b, cid):
    n, own, tokens = position.shape
    model = shared_a.shape[1]
    quarter = tokens // 4
    cols = 2 * model + LANES
    half, steps = quarter // 2, n // 2
    count = len(chunk_rows(0, quarter + half))
    dma = pltpu.SemaphoreType.DMA
    out, _ = pl.pallas_call(
        partial(put_scatter_kernel, n, own),
        out_shape=[
            jax.ShapeDtypeStruct((quarter, cols), F32),
            jax.ShapeDtypeStruct((n, 2, quarter, cols), BF),
        ],
        in_specs=[VM, ANY, ANY, ANY, VM, VM],
        out_specs=[VM, ANY],
        scratch_shapes=[
            pltpu.VMEM((4, 4, quarter, cols), BF),
            pltpu.VMEM((2, own, CAP, model), BF),
            pltpu.VMEM((2, own, CAP, model), BF),
            pltpu.VMEM((2, own, CAP, LANES), BF),
            pltpu.VMEM((steps, 2, quarter + half, cols), BF),
            pltpu.VMEM((4, quarter + half, cols), BF),
            pltpu.VMEM((2, half, cols), BF),
            pltpu.VMEM((n, half, cols), BF),
            pltpu.VMEM((2, half, cols), BF),
            pltpu.VMEM((quarter + half, cols), BF),
            pltpu.VMEM((half, cols), BF),
            pltpu.VMEM((half, cols), BF),
            dma((2, 3)),
            dma((4, 2)),
            dma((2,)),
            dma((n, 3)),
            dma((n, 3)),
            dma((n,)),
            dma((n,)),
            dma((steps, count, 2)),
            dma((steps, count, 2)),
            dma((count,)),
            dma((count,)),
        ],
        compiler_params=pltpu.CompilerParams(
            collective_id=cid, has_side_effects=True, vmem_limit_bytes=60 * 1024 * 1024
        ),
    )(
        position,
        rows_a.reshape(own, n, CAP, model),
        rows_b.reshape(own, n, CAP, model),
        rows_c.reshape(own, n, CAP, LANES),
        shared_a,
        shared_b,
    )
    return out


def edge_kernel(n, part, slope, rim, total, ahead, mine, from_core, from_chip, edge, send_sem, recv_sem):
    d, m = lax.axis_index("dp"), lax.axis_index("mp")
    core, chip = mp_partners(m)
    before, after = {"dp": (d + n - 1) % n}, {"dp": (d + 1) % n}
    rows, cols = part.shape
    edge_rows, rim_cols = rim.shape
    greet([core, chip, before, after])

    def add(dst, pieces, dtype):
        add_rows(dst, pieces, rows, dtype)

    one = remote(part, from_core, send_sem.at[0], recv_sem.at[0], core)
    one.start()
    one.wait()
    add(mine, [part, from_core], BF)
    two = remote(mine, from_chip, send_sem.at[1], recv_sem.at[1], chip)
    two.start()
    two.wait_recv()
    add(total, [mine, from_chip], F32)
    edge[:, 0:rim_cols] = rim[...]
    edge[:, rim_cols : rim_cols + cols] = total[0:edge_rows, :] * slope[...]
    three = remote(edge, ahead, send_sem.at[2], recv_sem.at[2], before)

    @pl.when(d > 0)
    def _():
        three.start()

    @pl.when(d == n - 1)
    def _():
        ahead[...] = jnp.zeros_like(ahead)

    @pl.when(d < n - 1)
    def _():
        three.wait_recv()

    @pl.when(d > 0)
    def _():
        three.wait_send()

    two.wait_send()


def sum_and_edge(part, slope, rim, cid):
    rows, cols = part.shape
    edge_shape = (rim.shape[0], rim.shape[1] + cols)
    return pl.pallas_call(
        partial(edge_kernel, lax.axis_size("dp")),
        out_shape=[
            jax.ShapeDtypeStruct(part.shape, F32),
            jax.ShapeDtypeStruct(edge_shape, F32),
        ],
        in_specs=[VM] * 3,
        out_specs=[VM] * 2,
        scratch_shapes=[
            pltpu.VMEM((rows, cols), BF),
            pltpu.VMEM((rows, cols), F32),
            pltpu.VMEM((rows, cols), BF),
            pltpu.VMEM(edge_shape, F32),
            pltpu.SemaphoreType.DMA((3,)),
            pltpu.SemaphoreType.DMA((3,)),
        ],
        compiler_params=pltpu.CompilerParams(
            collective_id=cid, has_side_effects=True, vmem_limit_bytes=32 * 1024 * 1024
        ),
    )(part, slope, rim)


def head_pair(pair, first, second):
    lane = lax.broadcasted_iota(jnp.int32, first.shape, 1)
    return jnp.where(lane < LANES // 2, first, second)


def visible_pairs(seg_col, seg_row):
    length = seg_col.shape[0]
    row = lax.broadcasted_iota(jnp.int32, (length, length), 0)
    col = lax.broadcasted_iota(jnp.int32, (length, length), 1)
    return (row >= col) & (seg_col == seg_row)


def state_decay(entry, expand):
    last = entry[entry.shape[0] - 1 :, :]
    spread = jnp.broadcast_to(last, (LANES, LANES)).T
    return dot(expand, spread, ((0,), (0,)), HIGH)


def recur_kernel(
    pairs,
    values,
    write,
    read,
    cumul,
    cumul_t,
    step_t,
    entry,
    tail,
    seg_col,
    seg_row,
    expand,
    skip,
    start,
    out,
    kept,
    state,
):
    @pl.when(pl.program_id(0) == 0)
    def _():
        state[...] = start[...]

    held = state[...]
    kept[0] = held
    v, b, c = values[...], write[...], read[...]
    scores = dot(c, b, ((1,), (1,)), HIGH)
    visible = visible_pairs(seg_col[...], seg_row[...])
    entry_full = dot(entry[...], expand[...], precision=HIGH)
    tail_full = dot(tail[...], expand[...], precision=HIGH)
    carried = entry_full * dot(c, held, ((1,), (1,)), HIGH) + skip[...] * v
    cum, cum_t, st_t = cumul[...], cumul_t[...], step_t[...]
    for pair in range(pairs):
        cols = slice(pair * LANES, (pair + 1) * LANES)
        v2 = v[:, cols]
        found = []
        for h in (2 * pair, 2 * pair + 1):
            spread = jnp.where(visible, cum[:, h : h + 1] - cum_t[h : h + 1, :], MASKED)
            mixing = jnp.exp(spread) * (scores * st_t[h : h + 1, :])
            found.append(dot_three(mixing, v2, (1, 0)))
        out[:, cols] = head_pair(pair, found[0], found[1]) + carried[:, cols]
    state[...] = state_decay(entry[...], expand[...]) * held + dot(v * tail_full, b, ((0,), (0,)), HIGH)


def recur_specs(width, lengths):
    def rows(cols):
        return pl.BlockSpec((BLK, cols), lambda i: (lengths(i), 0))

    def flat(count):
        return pl.BlockSpec((count, BLK), lambda i: (0, lengths(i)))

    def whole(shape):
        return pl.BlockSpec(shape, lambda i: (0,) * len(shape))

    return rows, flat, whole


def recur_forward(v, b, c, cumul, cumul_t, step_t, entry, tail, seg_col, seg_row, expand, skip, start):
    total, width = v.shape
    blocks = total // BLK
    rows, flat, whole = recur_specs(width, lambda i: i)
    return pl.pallas_call(
        partial(recur_kernel, width // LANES),
        grid=(blocks,),
        out_shape=[
            jax.ShapeDtypeStruct((total, width), F32),
            jax.ShapeDtypeStruct((blocks, width, LANES), F32),
        ],
        in_specs=[
            rows(width),
            rows(LANES),
            rows(LANES),
            rows(LANES),
            flat(16),
            flat(16),
            rows(LANES),
            rows(LANES),
            rows(1),
            flat(1),
            whole((LANES, width)),
            whole((1, width)),
            whole((width, LANES)),
        ],
        out_specs=[
            rows(width),
            pl.BlockSpec((1, width, LANES), lambda i: (i, 0, 0)),
        ],
        scratch_shapes=[pltpu.VMEM((width, LANES), F32)],
        compiler_params=pltpu.CompilerParams(vmem_limit_bytes=48 * 1024 * 1024),
    )(v, b, c, cumul, cumul_t, step_t, entry, tail, seg_col, seg_row, expand, skip, start)


def adjoint_kernel(
    pairs,
    values,
    write,
    read,
    cumul,
    cumul_t,
    step_t,
    step,
    entry,
    tail_bare,
    seg_col,
    seg_row,
    expand,
    skip,
    kept,
    d_out,
    start,
    d_values,
    d_write,
    d_read,
    d_step,
    d_rate_step,
    d_skip,
    state,
    columns,
):
    @pl.when(pl.program_id(0) == 0)
    def _():
        state[...] = start[...]
        d_skip[...] = jnp.zeros_like(d_skip)
        columns[...] = jnp.zeros_like(columns)

    length = values.shape[0]
    lam, held = state[...], kept[0]
    v, b, c, dy = values[...], write[...], read[...], d_out[...]
    ex = expand[...]
    st = step[...]
    scores = dot(c, b, ((1,), (1,)), HIGH)
    visible = visible_pairs(seg_col[...], seg_row[...])
    entry_full = dot(entry[...], ex, precision=HIGH)
    tail = tail_bare[...] * st
    tail_full = dot(tail, ex, precision=HIGH)
    c_state = dot(c, held, ((1,), (1,)), HIGH)
    b_lam = dot(b, lam, ((1,), (1,)), HIGH)
    dy_in = dy * entry_full
    v_out = v * tail_full
    dc = dot(dy_in, held, precision=HIGH)
    db = dot(v_out, lam, precision=HIGH)
    reach = dot(dy_in * c_state, ex, ((1,), (1,)), HIGH)
    leave = dot(v * b_lam, ex, ((1,), (1,)), HIGH)
    d_skip[...] += jnp.sum(dy * v, axis=0, keepdims=True)
    dv_far = tail_full * b_lam + skip[...] * dy
    cum, cum_t, st_t = cumul[...], cumul_t[...], step_t[...]
    lane = lax.broadcasted_iota(jnp.int32, (length, LANES), 1)
    d_scores = jnp.zeros((length, length), F32)
    row_sums = jnp.zeros((length, LANES), F32)
    for pair in range(pairs):
        cols = slice(pair * LANES, (pair + 1) * LANES)
        v2, dy2 = v[:, cols], dy[:, cols]
        found = []
        for j in range(2):
            h = 2 * pair + j
            own = (lane < LANES // 2) if j == 0 else (lane >= LANES // 2)
            d_mix = dot_three(jnp.where(own, dy2, 0.0), v2, (1, 1))
            spread = jnp.where(visible, cum[:, h : h + 1] - cum_t[h : h + 1, :], MASKED)
            decay = jnp.exp(spread)
            decay_step = decay * st_t[h : h + 1, :]
            weighted = d_mix * scores * decay
            d_scores = d_scores + d_mix * decay_step
            columns[h : h + 1, :] = jnp.sum(weighted, axis=0, keepdims=True)
            per_row = jnp.sum(weighted * st_t[h : h + 1, :], axis=1, keepdims=True)
            row_sums = jnp.where(lane == h, per_row, row_sums)
            found.append(dot(scores * decay_step, dy2, ((0,), (0,))))
        d_values[:, cols] = head_pair(pair, found[0], found[1]) + dv_far[:, cols]
    d_read[...] = dc + dot(d_scores, b, precision=HIGH)
    d_write[...] = db + dot(d_scores, c, ((0,), (0,)), HIGH)
    col_sums = columns[...].T
    leave_step = tail * leave
    d_step[...] = col_sums + tail_bare[...] * leave
    d_cum = row_sums - st * col_sums + reach - leave_step
    row = lax.broadcasted_iota(jnp.int32, (length, length), 0)
    col = lax.broadcasted_iota(jnp.int32, (length, length), 1)
    upper = (col >= row).astype(F32)
    met = jnp.sum(dot(lam * held, ex, ((0,), (1,)), HIGH), axis=0, keepdims=True)
    at_end = jnp.sum(leave_step, axis=0, keepdims=True) + entry[length - 1 :, :] * met
    d_rate_step[...] = dot(upper, d_cum, precision=HIGH) + at_end
    state[...] = state_decay(entry[...], ex) * lam + dot(dy_in, c, ((0,), (0,)), HIGH)


def recur_backward(
    v, b, c, cumul, cumul_t, step_t, step, entry, tail_bare, seg_col, seg_row, expand, skip, kept, dy, start
):
    total, width = v.shape
    blocks = total // BLK
    rows, flat, whole = recur_specs(width, lambda i: blocks - 1 - i)
    return pl.pallas_call(
        partial(adjoint_kernel, width // LANES),
        grid=(blocks,),
        out_shape=[
            jax.ShapeDtypeStruct((total, width), F32),
            jax.ShapeDtypeStruct((total, LANES), F32),
            jax.ShapeDtypeStruct((total, LANES), F32),
            jax.ShapeDtypeStruct((total, LANES), F32),
            jax.ShapeDtypeStruct((total, LANES), F32),
            jax.ShapeDtypeStruct((1, width), F32),
        ],
        in_specs=[
            rows(width),
            rows(LANES),
            rows(LANES),
            rows(LANES),
            flat(16),
            flat(16),
            rows(LANES),
            rows(LANES),
            rows(LANES),
            rows(1),
            flat(1),
            whole((LANES, width)),
            whole((1, width)),
            pl.BlockSpec((1, width, LANES), lambda i: (blocks - 1 - i, 0, 0)),
            rows(width),
            whole((width, LANES)),
        ],
        out_specs=[
            rows(width),
            rows(LANES),
            rows(LANES),
            rows(LANES),
            rows(LANES),
            whole((1, width)),
        ],
        scratch_shapes=[pltpu.VMEM((width, LANES), F32), pltpu.VMEM((LANES, LANES), F32)],
        compiler_params=pltpu.CompilerParams(vmem_limit_bytes=48 * 1024 * 1024),
    )(v, b, c, cumul, cumul_t, step_t, step, entry, tail_bare, seg_col, seg_row, expand, skip, kept, dy, start)


def state_scan_kernel(n, own, *refs):
    reverse = own == 0
    if reverse:
        mine, decay, expand, out = refs[:4]
        refs = refs[4:]
    else:
        mine, decay, expand, y, small, out, y_rows, position = refs[:8]
        refs = refs[8:]
    first, second, got_first, got_second, half, got_half, send_sem, recv_sem = refs[:8]

    def work(blocks):
        pass

    if not reverse:
        earlier, y_in, y_out, stream_sem = refs[8:]
        slots = SlotWork(own, small, position)
        stream = RowStream(y, y_rows, y_in, y_out, stream_sem.at[0], stream_sem.at[1])
        stream.load(0)

        def work(blocks):
            for b in blocks:
                if b + 1 < n:
                    stream.load(b + 1)
                if b == 0:
                    slots.count_with(earlier)
                    for block in range(n):
                        slots.place(block)
                stream.give(b, b, dot(slots.pick(b), stream.take(b)))

    d = lax.axis_index("dp")
    q = n - 1 - d if reverse else d
    zq, xq = q // 2, q % 2
    depth = n // 2
    rows = mine.shape[0] // 2
    xf = xq.astype(F32)
    sent_type = first.dtype

    def device(logical):
        return {"dp": n - 1 - logical if reverse else logical}

    beside = device(2 * zq + 1 - xq)
    others = [device(2 * ((zq + k) % depth) + xq) for k in range(1, depth)]
    own_rows = pl.ds(pl.multiple_of(rows * xq, 16), rows)
    other_rows = pl.ds(pl.multiple_of(rows * (1 - xq), 16), rows)
    own_lanes = pl.ds(pl.multiple_of(rows * xq, LANES), rows)
    tail = pl.ds(rows, 16)
    body = pl.ds(0, rows)
    row = lax.broadcasted_iota(jnp.int32, (16, LANES), 0)

    def spread(values):
        square = jnp.broadcast_to(values, (LANES, LANES)).T
        return dot(expand[:, own_lanes], square, ((0,), (0,)), HIGH)

    def two_terms(values):
        high = values.astype(sent_type).astype(F32)
        wide = jnp.where(row == 0, high, jnp.where(row == 1, values - high, 0.0))
        return wide.astype(sent_type)

    def one_term(block):
        return block[0:1, :].astype(F32) + block[1:2, :].astype(F32)

    for k in range(1, depth):

        @pl.when(zq < k)
        def _():
            got_second[k - 1] = jnp.zeros(got_second.shape[1:], sent_type)

    own_decay = decay[0:1, :]
    first[body, :] = mine[other_rows, :].astype(sent_type)
    first[tail, :] = two_terms(own_decay)
    greet([beside] + others)
    one = remote(first, got_first, send_sem.at[0], recv_sem.at[0], beside)
    one.start()
    work(range(0, 2))
    one.wait_recv()
    own_part = mine[own_rows, :]
    got, got_decay = got_first[body, :].astype(F32), one_term(got_first[tail, :])
    early = own_part * (1.0 - xf) + got * xf
    early_decay = own_decay * (1.0 - xf) + got_decay * xf
    late = own_part * xf + got * (1.0 - xf)
    late_decay = own_decay * xf + got_decay * (1.0 - xf)
    second[body, :] = (spread(late_decay) * early + late).astype(sent_type)
    second[tail, :] = two_terms(early_decay * late_decay)
    sent = []
    for k in range(1, depth):
        copy = remote(
            second, got_second.at[k - 1], send_sem.at[k], recv_sem.at[k], device(2 * ((zq + k) % depth) + xq)
        )
        sent.append(copy)

        @pl.when(zq + k < depth)
        def _():
            copy.start()

    early_spread = spread(early_decay)
    work(range(2, n - 1))
    total = jnp.zeros((rows, LANES), F32)
    for k in range(depth - 1, 0, -1):

        @pl.when(zq >= k)
        def _():
            sent[k - 1].wait_recv()

        got_k = got_second.at[k - 1]
        total = spread(one_term(got_k[tail, :])) * total + got_k[body, :].astype(F32)
    after = early_spread * total + early
    half[...] = (total * xf + after * (1.0 - xf)).astype(sent_type)
    last = remote(half, got_half, send_sem.at[depth], recv_sem.at[depth], beside)
    last.start()
    out[own_rows, :] = total * (1.0 - xf) + after * xf
    work(range(n - 1, n))
    last.wait_recv()
    out[other_rows, :] = got_half[...].astype(F32)
    one.wait_send()
    last.wait_send()
    for k in range(1, depth):

        @pl.when(zq + k < depth)
        def _():
            sent[k - 1].wait_send()

    if not reverse:
        stream.end()


def state_scan(mine, decay, expand, cid, sent_type, y=None, small=None, own=0):
    n = lax.axis_size("dp")
    half = mine.shape[0] // 2
    depth = n // 2
    message = (half + 16, LANES)
    out_shape, out_specs = [jax.ShapeDtypeStruct(mine.shape, F32)], [VM]
    args, in_specs, more = [mine, decay, expand], [VM] * 3, []
    if own:
        tokens, model = y.shape[1:]
        args += [y, small]
        in_specs += [ANY, VM]
        out_shape += [
            jax.ShapeDtypeStruct((own, n, CAP, model), BF),
            jax.ShapeDtypeStruct((n, own, tokens), F32),
        ]
        out_specs += [ANY, VM]
        more = [
            pltpu.VMEM((tokens, tokens), BF),
            pltpu.VMEM((2, tokens, model), BF),
            pltpu.VMEM((2, own, CAP, model), BF),
            pltpu.SemaphoreType.DMA((2, 2)),
        ]
    return pl.pallas_call(
        partial(state_scan_kernel, n, own),
        out_shape=out_shape,
        in_specs=in_specs,
        out_specs=out_specs,
        scratch_shapes=[
            pltpu.VMEM(message, sent_type),
            pltpu.VMEM(message, sent_type),
            pltpu.VMEM(message, sent_type),
            pltpu.VMEM((depth - 1,) + message, sent_type),
            pltpu.VMEM((half, LANES), sent_type),
            pltpu.VMEM((half, LANES), sent_type),
            pltpu.SemaphoreType.DMA((depth + 1,)),
            pltpu.SemaphoreType.DMA((depth + 1,)),
        ]
        + more,
        compiler_params=pltpu.CompilerParams(
            collective_id=cid, has_side_effects=True, vmem_limit_bytes=48 * 1024 * 1024
        ),
    )(*args)


def pick_matrix(position, own):
    length = position.shape[1]
    slot = lax.broadcasted_iota(jnp.int32, (CAP, length), 0).astype(F32)
    parts = [
        jnp.where(position[e : e + 1, :] == slot, 1.0, 0.0).astype(BF) for e in range(own)
    ]
    return jnp.concatenate(parts, axis=0)


def slot_spec(own, cols):
    return pl.BlockSpec((own, 1, CAP, cols), lambda s: (0, s, 0, 0))


def token_spec(rows, cols):
    return pl.BlockSpec((1, rows, cols), lambda s: (s, 0, 0))


BIG = pltpu.CompilerParams(vmem_limit_bytes=56 * 1024 * 1024)


def expert_kernel(
    own, parts, rows, cot_rows, gate, w_in, w_out, grad_in, grad_out, d_rows, res, dots, wide, both
):
    e, part = pl.program_id(0), pl.program_id(1)
    model = rows.shape[2]
    units = w_out.shape[1]

    @pl.when(part == 0)
    def _():
        wide[...] = w_in[0].astype(F32)
        both[:, 0:units] = wide[pl.ds(0, model, stride=2), :].astype(BF)
        both[:, units : 2 * units] = wide[pl.ds(1, model, stride=2), :].astype(BF)
        if parts > 1:
            grad_in[...] = jnp.zeros_like(grad_in)
            grad_out[...] = jnp.zeros_like(grad_out)

    x, c, g = rows[0], cot_rows[0], gate[0]
    mid = dot(x, both[...])
    mid_gate, mid_up = mid[:, 0:units], mid[:, units : 2 * units]
    sig = jax.nn.sigmoid(mid_gate)
    mid_silu = mid_gate * sig
    act = (mid_silu * mid_up).astype(BF).astype(F32)
    back = dot(c, w_out[0], ((1,), (1,)))
    dot_sum = jnp.sum(act * back, axis=1, keepdims=True)
    lane = lax.broadcasted_iota(jnp.int32, g.shape, 1)
    dots[0] = jnp.where(lane == lax.axis_index("dp") * own + e, dot_sum, 0.0).astype(BF)
    gated = (act * g).astype(BF)
    d_act = back * g
    d_gate = (d_act * mid_up * (sig * (1.0 + mid_gate * (1.0 - sig)))).astype(BF)
    d_mid = jnp.concatenate([d_gate, (d_act * mid_silu).astype(BF)], axis=1)
    grads = dot(x, d_mid, ((0,), (0,)))
    grads_down = dot(gated, c, ((0,), (0,)))
    if parts > 1:
        grad_in[0, pl.ds(0, model, stride=2), :] += grads[:, 0:units]
        grad_in[0, pl.ds(1, model, stride=2), :] += grads[:, units : 2 * units]
        grad_out[0] += grads_down
    else:
        grad_in[0, pl.ds(0, model, stride=2), :] = grads[:, 0:units]
        grad_in[0, pl.ds(1, model, stride=2), :] = grads[:, units : 2 * units]
        grad_out[0] = grads_down
    d_rows[0] = dot(d_mid, both[...], ((1,), (1,))).astype(BF)
    res[0] = dot(gated, w_out[0]).astype(BF)


def run_experts(rows, cot_rows, gate, w_in, w_out):
    own, slots, model = rows.shape
    units = w_out.shape[1]
    part = min(slots, 512)

    def slot(cols):
        return pl.BlockSpec((1, part, cols), lambda e, j: (e, j, 0))

    def weight(a, b):
        return pl.BlockSpec((1, a, b), lambda e, j: (e, 0, 0))

    return pl.pallas_call(
        partial(expert_kernel, own, slots // part),
        grid=(own, slots // part),
        out_shape=[
            jax.ShapeDtypeStruct((own, 2 * model, units), F32),
            jax.ShapeDtypeStruct((own, units, model), F32),
            jax.ShapeDtypeStruct((own, slots, model), BF),
            jax.ShapeDtypeStruct((own, slots, model), BF),
            jax.ShapeDtypeStruct((own, slots, LANES), BF),
        ],
        in_specs=[slot(model), slot(model), slot(LANES), weight(2 * model, units), weight(units, model)],
        out_specs=[weight(2 * model, units), weight(units, model), slot(model), slot(model), slot(LANES)],
        scratch_shapes=[pltpu.VMEM((2 * model, units), F32), pltpu.VMEM((model, 2 * units), BF)],
        compiler_params=BIG,
    )(rows, cot_rows, gate, w_in, w_out)


def put_kernel(own, k, position, *refs):
    out = refs[-1]
    put = pick_matrix(position[0], own)
    here = jnp.where(pl.program_id(0) == lax.axis_index("dp"), 1.0, 0.0)
    start = 0
    for i in range(k):
        rows, shared = refs[2 * i], refs[2 * i + 1]
        cols = shared.shape[1]
        total = dot(put, rows[...].reshape(own * CAP, cols), ((0,), (0,)))
        out[0, :, start : start + cols] = (total + here * shared[...]).astype(BF)
        start += cols
    if len(refs) > 2 * k + 1:
        extra = refs[2 * k]
        out[0, :, start : start + LANES] = dot(
            put, extra[...].reshape(own * CAP, LANES), ((0,), (0,))
        ).astype(BF)


def put_rows(position, parts, extra=None):
    n, own, tokens = position.shape
    args, specs, cols = [], [], 0
    for rows, shared in parts:
        model = shared.shape[1]
        args += [rows.reshape(own, n, CAP, model), shared]
        specs += [slot_spec(own, model), pl.BlockSpec((tokens, model), lambda s: (0, 0))]
        cols += model
    if extra is not None:
        args.append(extra.reshape(own, n, CAP, LANES))
        specs.append(slot_spec(own, LANES))
        cols += LANES
    return pl.pallas_call(
        partial(put_kernel, own, len(parts)),
        grid=(n,),
        out_shape=jax.ShapeDtypeStruct((n, tokens, cols), BF),
        in_specs=[token_spec(own, tokens)] + specs,
        out_specs=token_spec(tokens, cols),
        compiler_params=BIG,
    )(position, *args)


def grads_kernel(k, *refs):
    lefts, rights, out = refs[:k], refs[k : 2 * k], refs[2 * k]
    start = 0
    for left, right in zip(lefts, rights):
        cols = right.shape[1]
        out[:, start : start + cols] = dot(left[...], right[...], ((0,), (0,))).astype(BF)
        start += cols


def weight_grads(pairs):
    k = len(pairs)
    tokens, model = pairs[1][0].shape
    block = 256
    cols = sum(right.shape[1] for _, right in pairs)
    return pl.pallas_call(
        partial(grads_kernel, k),
        grid=(model // block,),
        out_shape=jax.ShapeDtypeStruct((model, cols), BF),
        in_specs=[pl.BlockSpec((tokens, block), lambda i: (0, i)) for _ in pairs]
        + [pl.BlockSpec(right.shape, lambda i: (0, 0)) for _, right in pairs],
        out_specs=pl.BlockSpec((block, cols), lambda i: (i, 0)),
        compiler_params=BIG,
    )(*[left for left, _ in pairs], *[right for _, right in pairs])


def combine_states(states, decays, expand, reverse):
    n = states.shape[0]
    place = lax.axis_index("dp")
    wide = dot(decays, expand, precision=HIGH)
    state = jnp.zeros(states.shape[1:], F32)
    for j in range(n):
        source = n - 1 - j if reverse else j
        use = source > place if reverse else source < place
        fresh = wide[source][:, None] * state + states[source]
        state = jnp.where(use, fresh, state)
    return state


def ring_state(mine, decay, expand, reverse, cid):
    rows = jnp.pad(decay, ((0, 31), (0, 0)))
    (gathered,) = gather_dp([jnp.concatenate([mine, rows], axis=0)], cid)
    width = mine.shape[0]
    return combine_states(gathered[:, :width], gathered[:, width], expand, reverse)


def per_device(
    hidden,
    segment_ids,
    routes,
    norm_gain,
    mixer_in,
    state_in,
    step_in,
    conv_value,
    conv_value_bias,
    conv_state,
    conv_state_bias,
    head_params,
    gated_gain,
    mixer_out,
    ffn_gain,
    router,
    shared_in,
    shared_out,
    expert_in,
    expert_out,
    cotangent,
):
    n = lax.axis_size("dp")
    place, mp_place = lax.axis_index("dp"), lax.axis_index("mp")
    tokens, model = hidden.shape
    shard = model // n
    inner = mixer_in.shape[2]
    state_cols = state_in.shape[1]
    taps = conv_value.shape[0]
    heads = head_params.shape[1]
    width = inner // heads
    own_experts = expert_in.shape[0]
    hidden_units = shared_out.shape[0]
    quarter = tokens // 4

    misc_parts = [
        conv_value.reshape(-1),
        conv_value_bias.reshape(-1),
        gated_gain.reshape(-1),
        conv_state.reshape(-1),
        conv_state_bias,
        norm_gain,
        ffn_gain,
    ]
    misc = jnp.concatenate(misc_parts)
    small = jnp.concatenate(
        [
            jnp.pad(misc, (0, model - misc.shape[0]))[None],
            jnp.pad(routes.T.astype(BF), ((0, 0), (0, model - tokens))),
            hidden[tokens - 15 + TOPK :],
        ],
        axis=0,
    )
    pack_a = jnp.concatenate(
        [
            mixer_in.reshape(shard, 2 * inner),
            state_in,
            jnp.pad(step_in, ((0, 0), (0, LANES - heads))),
        ],
        axis=1,
    )
    pack_b = jnp.concatenate(
        [
            mixer_out.T,
            shared_in.reshape(shard, 2 * hidden_units),
            shared_out.T,
            jnp.pad(router, ((0, 0), (0, LANES - EXPERTS))),
        ],
        axis=1,
    )
    mine_cot = lax.dynamic_slice_in_dim(cotangent, mp_place * quarter, quarter, 0)
    weight_a, small_all, cot_all = first_gather([pack_a, small], cotangent, 0)
    weight_a = weight_a.reshape(model, -1)
    cot_all = cot_all.reshape(n, tokens, model)
    pack_b, small_all = lax.optimization_barrier((pack_b, small_all))
    weight_b = lax.all_gather(pack_b, "dp", axis=0, tiled=True)
    out_t = weight_b[:, :inner]
    router_w = weight_b[:, inner + 3 * hidden_units :]

    pieces = []
    start = 0
    for part in misc_parts:
        pieces.append(small_all[:, 0, start : start + part.shape[0]].astype(F32))
        start += part.shape[0]
    local_p = conv_value.shape[1]
    value_rows = jnp.concatenate(pieces[:3], axis=1).reshape(n, taps + 2, local_p, heads)
    value_rows = value_rows.transpose(1, 3, 0, 2).reshape(taps + 2, inner)
    state_rows = jnp.concatenate(pieces[3:5], axis=1).reshape(n, taps + 1, state_cols // n)
    state_rows = state_rows.transpose(1, 0, 2).reshape(taps + 1, state_cols)
    gain_first = pieces[5].reshape(1, model)
    gain_second = pieces[6].reshape(1, model)
    conv_taps = jnp.concatenate([value_rows[:taps], state_rows[:taps]], axis=1)
    conv_bias = jnp.concatenate([value_rows[taps], state_rows[taps]])[None]
    gated_row = value_rows[taps + 1][None]

    group_start = place * tokens
    seg_padded = jnp.concatenate([jnp.full((taps - 1,), -1, jnp.int32), segment_ids])
    seg_ext = lax.dynamic_slice_in_dim(seg_padded, group_start, tokens + taps - 1)
    segments = seg_ext[taps - 1 :]
    prev_seg = seg_ext[taps - 2]
    same = [
        (seg_ext[k : k + tokens] == segments).astype(F32)[:, None] for k in range(taps)
    ]
    blocks = tokens // BLK
    seg_blocks = segments.reshape(blocks, BLK)
    last_segs = seg_blocks[:, BLK - 1]
    prev_segs = jnp.concatenate([prev_seg[None], last_segs[:-1]])
    entry_ok = (seg_blocks == prev_segs[:, None]).astype(F32).reshape(tokens, 1)
    tail_ok = (seg_blocks == last_segs[:, None]).astype(F32).reshape(tokens, 1)
    group_entry_ok = (segments == prev_seg).astype(F32)[:, None]
    group_tail_ok = (segments == segments[tokens - 1]).astype(F32)[:, None]
    seg_f = segments.astype(F32)
    seg_col, seg_row = seg_f[:, None], seg_f[None, :]

    behind = lax.dynamic_index_in_dim(small_all, (place + n - 1) % n, 0, False)
    hidden_ext = jnp.concatenate([behind, hidden], axis=0).astype(F32)
    inv_ext = lax.rsqrt(jnp.mean(hidden_ext * hidden_ext, axis=1, keepdims=True) + EPS)
    normed_ext = (hidden_ext * inv_ext * gain_first).astype(BF)
    normed = normed_ext[16:]
    zx_ext = dot(normed_ext, weight_a)
    gate_z = zx_ext[16:, :inner]
    pre_ext = zx_ext[16 - taps + 1 :, inner : 2 * inner + state_cols]
    head_local = head_params.astype(F32)
    dt_lanes = zx_ext[16:, 2 * inner + state_cols :]
    conv = jnp.broadcast_to(conv_bias, (tokens, inner + state_cols))
    for k in range(taps):
        conv = conv + conv_taps[k][None] * pre_ext[k : k + tokens] * same[k]
    act = jax.nn.silu(conv)
    values = act[:, :inner]
    write = act[:, inner : inner + state_cols // 2]
    read = act[:, inner + state_cols // 2 :]

    live = (jnp.arange(LANES) < heads)[None]
    head_pad = jnp.pad(head_local, ((0, 0), (0, LANES - heads)))
    rate = jnp.where(live, -jnp.exp(head_pad[0:1]), 0.0)
    step = jnp.where(live, jax.nn.softplus(dt_lanes + head_pad[1:2]), 0.0)
    rated = (step * rate).reshape(blocks, BLK, LANES)
    lower = jnp.tril(jnp.ones((BLK, BLK), F32))
    cumul_b = jnp.einsum("ts,bsh->bth", lower, rated, precision=HIGH)
    totals = cumul_b[:, BLK - 1]
    zero_row = jnp.zeros((1, LANES), F32)
    before, after = [zero_row], [zero_row]
    for i in range(blocks - 1):
        before.append(before[-1] + totals[i][None])
        after.append(after[-1] + totals[blocks - 1 - i][None])
    before = jnp.stack(before)
    after = jnp.stack(after[::-1])
    cumul = cumul_b.reshape(tokens, LANES)
    to_end = totals[:, None] - cumul_b
    entry = jnp.exp(cumul) * entry_ok
    tail_bare = jnp.exp(to_end).reshape(tokens, LANES) * tail_ok
    tail = tail_bare * step
    group_entry = jnp.exp(cumul_b + before).reshape(tokens, LANES) * group_entry_ok
    group_tail = jnp.exp(to_end + after).reshape(tokens, LANES) * group_tail_ok * step
    cumul_t = cumul[:, :16].T
    step_t = step[:, :16].T
    expand = (jnp.arange(LANES)[:, None] == jnp.arange(inner)[None, :] // width).astype(F32)
    skip = dot(head_pad[2:3], expand, precision=HIGH)
    outgoing = dot(
        values * dot(group_tail, expand, precision=HIGH), write, ((0,), (0,)), HIGH
    )
    group_decay = group_entry[tokens - 1 :]
    if n == 8:
        incoming, cot_rows, position = state_scan(
            outgoing, jnp.broadcast_to(group_decay, (8, LANES)), expand, 1, F32, cot_all, small_all, own_experts
        )
    else:
        incoming = ring_state(outgoing, group_decay, expand, False, 1)
        cot_rows, position = slots_of(cot_all, small_all, own_experts)
    ssd, kept = recur_forward(
        values, write, read, cumul, cumul_t, step_t, entry, tail, seg_col, seg_row, expand, skip, incoming
    )

    gate_act = jax.nn.silu(gate_z)
    gated = ssd * gate_act
    scaled = (gated * gated_row).astype(BF)
    proj_part = dot(scaled, out_t, ((1,), (1,)))
    square_part = jnp.sum(gated * gated, axis=1, keepdims=True)
    proj_pack = jnp.concatenate([proj_part, jnp.broadcast_to(square_part, (tokens, LANES))], axis=1)
    proj_sum = scatter_mp(proj_pack.reshape(4, quarter, -1), 2)
    proj = proj_sum[:, :model]
    square = proj_sum[:, model : model + 1]
    inv_gated = lax.rsqrt(square / DI + EPS)
    mine_hidden = lax.dynamic_slice_in_dim(hidden, mp_place * quarter, quarter, 0).astype(F32)
    mixed = mine_hidden + proj * inv_gated
    inv_second = lax.rsqrt(jnp.mean(mixed * mixed, axis=1, keepdims=True) + EPS)
    unit_second = mixed * inv_second
    ffn_mine = (unit_second * gain_second).astype(BF)

    first_expert = place * own_experts
    (
        _,
        rows,
        gates,
        slot_gates,
        ffn_block,
        shared_act,
        d_shared_mid,
        shared_res,
        d_ffn_shared,
    ) = gather_tokens(ffn_mine, position, small_all, weight_b, cotangent, hidden_units, 3)

    slots = n * CAP
    grad_in_rows, grad_expert_out, d_rows, expert_res, slot_dots = run_experts(
        rows.reshape(own_experts, slots, model),
        cot_rows.reshape(own_experts, slots, model),
        slot_gates.reshape(own_experts, slots, LANES),
        expert_in.reshape(own_experts, 2 * model, -1),
        expert_out,
    )
    grad_expert_in = grad_in_rows.reshape(expert_in.shape)

    if n > 8:
        d_ffn_pack = put_rows(position, [(d_rows, d_ffn_shared)], slot_dots)
        d_ffn_sum = scatter_tokens(d_ffn_pack.reshape(n, 4, quarter, -1), 4)
        expert_res, d_ffn_sum = lax.optimization_barrier((expert_res, d_ffn_sum))
        res_pack = put_rows(position, [(expert_res, shared_res)])
        res_sum = scatter_tokens(res_pack.reshape(n, 4, quarter, model), 10)
    else:
        both_sums = put_scatter(position, expert_res, d_rows, slot_dots, shared_res, d_ffn_shared, 4)
        res_sum, d_ffn_sum = both_sums[:, :model], both_sums[:, model:]

    own_tokens_gates = lax.dynamic_slice(
        gates, (place, mp_place * quarter, 0), (1, quarter, LANES)
    ).reshape(quarter, LANES)
    dots = d_ffn_sum[:, model : model + LANES]
    share = jnp.sum(own_tokens_gates * dots, axis=1, keepdims=True)
    d_logits = (own_tokens_gates * (dots - share)).astype(BF)
    d_ffn = d_ffn_sum[:, :model] + dot(d_logits, router_w, ((1,), (1,)))
    mine_cot_f = mine_cot.astype(F32)
    grad_gain_second = jnp.sum(d_ffn * unit_second, axis=0)
    d_unit = d_ffn * gain_second
    d_mixed = mine_cot_f + inv_second * (
        d_unit - unit_second * jnp.mean(d_unit * unit_second, axis=1, keepdims=True)
    )
    d_proj_mine = (d_mixed * inv_gated).astype(BF)
    d_inv = jnp.sum(d_mixed * proj, axis=1, keepdims=True)
    d_square = d_inv * -0.5 * inv_gated * inv_gated * inv_gated / DI
    d_square_high = d_square.astype(BF)
    d_square_low = (d_square - d_square_high.astype(F32)).astype(BF)
    sent = jnp.concatenate(
        [
            d_proj_mine,
            d_logits[:, :EXPERTS],
            d_square_high,
            d_square_low,
            jnp.zeros((quarter, LANES - EXPERTS - 2), BF),
        ],
        axis=1,
    )
    (got,) = gather_mp([sent], 5)
    got = got.reshape(tokens, model + LANES)
    d_proj = got[:, :model]
    d_logits_all = jnp.pad(got[:, model : model + EXPERTS], ((0, 0), (0, LANES - EXPERTS)))
    d_square_all = got[:, model + EXPERTS : model + EXPERTS + 1].astype(F32) + got[
        :, model + EXPERTS + 1 : model + EXPERTS + 2
    ].astype(F32)

    rows0 = ((0,), (0,))
    grad_b = weight_grads(
        [
            (got, scaled),
            (ffn_block, d_shared_mid),
            (cotangent, shared_act),
            (ffn_block, d_logits_all),
        ]
    )
    grad_b, got = lax.optimization_barrier((grad_b, got))
    d_proj = got[:, :model]
    sum_b = lax.psum_scatter(grad_b, "dp", scatter_dimension=0, tiled=True).astype(F32)
    d_scaled = dot(d_proj, out_t)
    grad_gated_row = jnp.sum(d_scaled * gated, axis=0)
    d_gated = d_scaled * gated_row + 2.0 * gated * d_square_all
    d_ssd = d_gated * gate_act
    d_gate_z = d_gated * ssd * silu_slope(gate_z)

    direct = dot(d_ssd * dot(group_entry, expand, precision=HIGH), read, rows0, HIGH)
    if n == 8:
        (state_grad,) = state_scan(direct, jnp.broadcast_to(group_decay, (8, LANES)), expand, 6, BF)
    else:
        state_grad = ring_state(direct, group_decay, expand, True, 6)
    d_values, d_write, d_read, d_step, d_rated, d_skip_row = recur_backward(
        values,
        write,
        read,
        cumul,
        cumul_t,
        step_t,
        step,
        entry,
        tail_bare,
        seg_col,
        seg_row,
        expand,
        skip,
        kept,
        d_ssd,
        state_grad,
    )
    d_rate = jnp.sum(d_rated * step, axis=0, keepdims=True)
    d_dt = jnp.where(
        live, (d_step + rate * d_rated) * jax.nn.sigmoid(dt_lanes + head_pad[1:2]), 0.0
    )
    d_skip = dot(d_skip_row, expand, ((1,), (1,)), HIGH)
    grad_head = jnp.concatenate(
        [d_rate * rate, jnp.sum(d_dt, axis=0, keepdims=True), d_skip], axis=0
    )[:, :heads]

    slope = silu_slope(conv)
    d_conv_values = d_values * slope[:, :inner]
    d_state_act, rim_ahead = sum_and_edge(
        jnp.concatenate([d_write, d_read], axis=1), slope[:16, inner:], d_conv_values[:16], 11
    )
    d_conv = jnp.concatenate([d_conv_values, d_state_act * slope[:, inner:]], axis=1)
    d_conv_ext = jnp.concatenate([d_conv, rim_ahead], axis=0)
    seg_after = lax.dynamic_slice_in_dim(
        jnp.concatenate([segment_ids, jnp.full((taps - 1,), -1, jnp.int32)]),
        group_start,
        tokens + taps - 1,
    )
    d_pre = jnp.zeros_like(d_conv)
    grad_rows = []
    for k in range(taps):
        ahead = taps - 1 - k
        ok = (seg_after[ahead : ahead + tokens] == segments).astype(F32)[:, None]
        d_pre = d_pre + conv_taps[k][None] * d_conv_ext[ahead : ahead + tokens] * ok
        grad_rows.append(jnp.sum(d_conv * pre_ext[k : k + tokens] * same[k], axis=0))
    grad_rows.append(jnp.sum(d_conv, axis=0))
    d_a = jnp.concatenate([d_gate_z, d_pre, d_dt], axis=1).astype(BF)

    d_state_mine = lax.dynamic_slice_in_dim(
        d_a[:, 2 * inner : 2 * inner + state_cols], mp_place * quarter, quarter, 0
    )
    d_normed_part = dot(d_a[:, : 2 * inner], weight_a[:, : 2 * inner], ((1,), (1,))) + dot(
        d_a[:, 2 * inner + state_cols :], weight_a[:, 2 * inner + state_cols :], ((1,), (1,))
    )
    d_state_rows = dot(
        d_state_mine, weight_a[:, 2 * inner : 2 * inner + state_cols], ((1,), (1,))
    )
    grad_a = dot(normed, d_a, rows0).astype(BF)
    unit_first = hidden_ext[16:] * inv_ext[16:]
    mine_unit = lax.dynamic_slice_in_dim(unit_first, mp_place * quarter, quarter, 0)
    grad_gain_first = jnp.sum(d_normed_part * unit_first, axis=0) + jnp.sum(
        d_state_rows * mine_unit, axis=0
    )

    value_grads = jnp.stack([g[:inner] for g in grad_rows] + [grad_gated_row])
    value_grads = value_grads.reshape(taps + 2, heads, n, local_p).transpose(2, 0, 3, 1)
    state_grads = jnp.stack([g[inner:] for g in grad_rows])
    state_grads = state_grads.reshape(taps + 1, n, state_cols // n).transpose(1, 0, 2)
    misc_grads = [
        value_grads.reshape(n, -1),
        state_grads.reshape(n, -1),
        jnp.broadcast_to(grad_head.reshape(1, -1), (n, 3 * heads)),
    ]
    sizes = [g.shape[1] for g in misc_grads]
    misc_grads = jnp.concatenate(misc_grads, axis=1)
    misc_grads = jnp.pad(misc_grads, ((0, 0), (0, 32 * LANES - misc_grads.shape[1])))
    gains = jnp.concatenate(
        [grad_gain_first.reshape(n, shard), grad_gain_second.reshape(n, shard)], axis=1
    )
    gains = jnp.pad(gains, ((0, 0), (0, 16 * LANES - 2 * shard)))
    mine_result = (mixed + res_sum).astype(BF)
    sum_zx, sum_state, sum_dt, misc_sum, gains_sum, hidden_all, result = last_exchange(
        grad_a.reshape(n, shard, -1),
        misc_grads.reshape(n, 32, LANES),
        gains.reshape(n, 16, LANES),
        d_normed_part.astype(BF).reshape(4, quarter, model),
        d_state_rows,
        d_mixed,
        mine_hidden,
        gain_first,
        mine_result,
        (2 * inner, state_cols, LANES),
        8,
    )
    result = result.reshape(tokens, model)
    misc_sum = misc_sum.reshape(-1)
    gains_sum = gains_sum.reshape(-1)
    cut = [0]
    for size in sizes:
        cut.append(cut[-1] + size)
    value_sum = misc_sum[: cut[1]].reshape(taps + 2, local_p, heads)
    state_sum = misc_sum[cut[1] : cut[2]].reshape(taps + 1, state_cols // n)
    head_sum = misc_sum[cut[2] : cut[3]].reshape(3, heads)

    b1, b2 = inner, inner + 2 * hidden_units
    b3 = b2 + hidden_units
    return (
        result,
        hidden_all.reshape(tokens, model).astype(F32),
        gains_sum[:shard],
        sum_zx.reshape(shard, 2, inner),
        sum_state,
        sum_dt[:, :heads],
        value_sum[:taps],
        value_sum[taps],
        state_sum[:taps],
        state_sum[taps],
        head_sum,
        value_sum[taps + 1],
        sum_b[:, :b1].T,
        gains_sum[shard : 2 * shard],
        sum_b[:, b3 : b3 + EXPERTS],
        sum_b[:, b1:b2].reshape(shard, 2, hidden_units),
        sum_b[:, b2:b3].T,
        grad_expert_in,
        grad_expert_out,
    )


def solution(mesh):
    placed = (
        P("dp", None),
        P(),
        P("dp", None),
        P("dp"),
        P("dp", None, "mp"),
        P("dp", None),
        P("dp", "mp"),
        P(None, "dp", "mp"),
        P("dp", "mp"),
        P(None, "dp"),
        P("dp"),
        P(None, "mp"),
        P("dp", "mp"),
        P("mp", "dp"),
        P("dp"),
        P("dp", None),
        P("dp", None, "mp"),
        P("mp", "dp"),
        P("dp", None, None, "mp"),
        P("dp", "mp", None),
        P("dp", None),
    )
    return jax.shard_map(
        per_device,
        mesh=mesh,
        in_specs=placed,
        out_specs=(
            P("dp", None),
            P("dp", None),
            P("dp"),
            P("dp", None, "mp"),
            P("dp", None),
            P("dp", "mp"),
            P(None, "dp", "mp"),
            P("dp", "mp"),
            P(None, "dp"),
            P("dp"),
            P(None, "mp"),
            P("dp", "mp"),
            P("mp", "dp"),
            P("dp"),
            P("dp", None),
            P("dp", None, "mp"),
            P("mp", "dp"),
            P("dp", None, None, "mp"),
            P("dp", "mp", None),
        ),
        check_vma=False,
    )
```

```python
from functools import partial

import jax
import jax.numpy as jnp
from jax import lax
from jax.experimental import pallas as pl
from jax.experimental.pallas import tpu as pltpu
from jax.sharding import PartitionSpec as P

MESH = pl.DeviceIdType.MESH
BLK = 128
EXPERTS = 64
TOPK = 6
DI = 3072
CAP = 64
LANES = 128

EPS = 1e-05
HIGH = lax.Precision.HIGHEST
MASKED = -1e30
BF = jnp.bfloat16
F32 = jnp.float32
ANY = pl.BlockSpec(memory_space=pl.ANY)
VM = pl.BlockSpec(memory_space=pltpu.VMEM)


def dot(a, b, dims=((1,), (0,)), precision=None):
    return lax.dot_general(
        a, b, (dims, ((), ())), precision=precision, preferred_element_type=F32
    )


def two_parts(a):
    high = a.astype(BF)
    return high, (a - high.astype(F32)).astype(BF)


def dot_three(a, b, over):
    a_high, a_low = two_parts(a)
    b_high, b_low = two_parts(b)
    left = jnp.concatenate([a_high, a_low, a_high], axis=over[0])
    right = jnp.concatenate([b_high, b_high, b_low], axis=over[1])
    return dot(left, right, ((over[0],), (over[1],)))


def silu_slope(argument):
    sigmoid_val = jax.nn.sigmoid(argument)
    return sigmoid_val * (1.0 + argument * (1.0 - sigmoid_val))


def chunk_rows(start, size):
    return [(start + i, min(32, size - i)) for i in range(0, size, 32)]


def ring_place(n, d):
    high, low = d // 2, d % 2
    return high * (1 - low) + (n - 1 - high) * low


def ring_device(n, p):
    back = p // (n // 2)
    return (2 * p) * (1 - back) + (2 * (n - 1 - p) + 1) * back


def greet(targets):
    barrier = pltpu.get_barrier_semaphore()
    for target in targets:
        pl.semaphore_signal(barrier, inc=1, device_id=target, device_id_type=MESH)
    pl.semaphore_wait(barrier, len(targets))


def remote(src, dst, send, recv, target):
    return pltpu.make_async_remote_copy(
        src_ref=src,
        dst_ref=dst,
        send_sem=send,
        recv_sem=recv,
        device_id=target,
        device_id_type=MESH,
    )


def mp_partners(m):
    return {"mp": m + 1 - 2 * (m % 2)}, {"mp": (m + 2) % 4}


def ring_neighbours(n):
    p = ring_place(n, lax.axis_index("dp"))
    nxt = {"dp": ring_device(n, (p + 1) % n)}
    prv = {"dp": ring_device(n, (p + n - 1) % n)}
    return p, nxt, prv


class RingGather:
    def __init__(self, n, ins, outs, sems):
        self.n, self.ins, self.outs = n, ins, outs
        self.local_sem, self.send_sem, self.recv_sem = sems
        self.p, self.nxt, self.prv = ring_neighbours(n)
        self.copies = {}

    @staticmethod
    def scratch(n, arrays):
        dma = pltpu.SemaphoreType.DMA
        most = max(len(chunk_rows(0, a.shape[0])) for a in arrays)
        shape = (n // 2, len(arrays), most, 2)
        return [dma((len(arrays),)), dma(shape), dma(shape)]

    def begin(self):
        d = lax.axis_index("dp")
        self.local = []
        for j, (a, out) in enumerate(zip(self.ins, self.outs)):
            copy = pltpu.make_async_copy(a, out.at[d], self.local_sem.at[j])
            copy.start()
            self.local.append(copy)

    def step(self, s):
        n, p = self.n, self.p
        for j, (a, out) in enumerate(zip(self.ins, self.outs)):
            for i, (start, rows) in enumerate(chunk_rows(0, a.shape[0])):
                part = pl.ds(start, rows)
                for way in range(2):
                    origin = ring_device(n, (p + n - s) % n if way == 0 else (p + s) % n)
                    if (s - 1, j, i, way) in self.copies:
                        self.copies[s - 1, j, i, way].wait_recv()
                    if s + 1 < n // 2 or (s + 1 == n // 2 and i % 2 == way):
                        copy = remote(
                            a.at[part] if s == 0 else out.at[origin, part],
                            out.at[origin, part],
                            self.send_sem.at[s, j, i, way],
                            self.recv_sem.at[s, j, i, way],
                            self.nxt if way == 0 else self.prv,
                        )
                        copy.start()
                        self.copies[s, j, i, way] = copy

    def end(self):
        for copy in self.copies.values():
            copy.wait_send()
        for copy in self.local:
            copy.wait()


def gather_kernel(n, k, *refs):
    ring = RingGather(n, refs[:k], refs[k : 2 * k], refs[2 * k :])
    greet([ring.nxt, ring.prv])
    ring.begin()
    for s in range(n // 2 + 1):
        ring.step(s)
    ring.end()


def gather_dp(arrays, cid):
    n, k = lax.axis_size("dp"), len(arrays)
    return pl.pallas_call(
        partial(gather_kernel, n, k),
        out_shape=[jax.ShapeDtypeStruct((n,) + a.shape, a.dtype) for a in arrays],
        in_specs=[ANY] * k,
        out_specs=[ANY] * k,
        scratch_shapes=RingGather.scratch(n, arrays),
        compiler_params=pltpu.CompilerParams(collective_id=cid, has_side_effects=True),
    )(*arrays)


def add_rows(dst, pieces, rows, dtype):
    def body(i, carry):
        sl = pl.ds(pl.multiple_of(i * 16, 16), 16)
        total = pieces[0][sl, :].astype(F32)
        for piece in pieces[1:]:
            total = total + piece[sl, :].astype(F32)
        dst[sl, :] = total.astype(dtype)
        return carry

    lax.fori_loop(0, rows // 16, body, 0)


class RingScatter:
    def __init__(self, n, ins, outs, slots, sems):
        self.n, self.ins, self.outs, self.slots = n, ins, outs, slots
        self.send_sem, self.recv_sem = sems
        self.p, self.nxt, self.prv = ring_neighbours(n)
        self.copies = {}

    @staticmethod
    def scratch(n, arrays):
        most = max(len(chunk_rows(0, a.shape[1])) for a in arrays)
        shape = (n // 2, len(arrays), most, 2)
        return [pltpu.VMEM((n // 2, 2) + a.shape[1:], a.dtype) for a in arrays] + [
            pltpu.SemaphoreType.DMA(shape),
            pltpu.SemaphoreType.DMA(shape),
        ]

    def step(self, s, j):
        n, p = self.n, self.p
        array, out, slots = self.ins[j], self.outs[j], self.slots[j]
        for i, (start, size) in enumerate(chunk_rows(0, array.shape[1])):
            part = pl.ds(start, size)
            if s == n // 2:
                for way in range(2):
                    self.copies[s - 1, j, i, way].wait_recv()
                start_col = 0
                for ref in out:
                    cols = pl.ds(start_col, ref.shape[1])
                    start_col += ref.shape[1]
                    pieces = [array.at[ring_device(n, p), part, cols]]
                    pieces += [slots.at[s - 1, way, part, cols] for way in range(2)]
                    add_rows(ref.at[part], pieces, size, F32)
                continue
            for way in range(2):
                if s == 0 and i % 2 != way:
                    continue
                away = n // 2 - s
                block = ring_device(n, (p + away) % n if way == 0 else (p + n - away) % n)
                source = array.at[block, part]
                if (s - 1, j, i, way) in self.copies:
                    self.copies[s - 1, j, i, way].wait_recv()
                    held = slots.at[s - 1, way, part]
                    add_rows(held, [held, source], size, array.dtype)
                    source = held
                copy = remote(
                    source,
                    slots.at[s, way, part],
                    self.send_sem.at[s, j, i, way],
                    self.recv_sem.at[s, j, i, way],
                    self.nxt if way == 0 else self.prv,
                )
                copy.start()
                self.copies[s, j, i, way] = copy

    def end(self):
        for copy in self.copies.values():
            copy.wait_send()


def last_kernel(
    n,
    grad_a,
    misc,
    gains,
    d_normed,
    extra,
    d_mixed,
    hidden,
    gain,
    result,
    out_zx,
    out_state,
    out_dt,
    out_misc,
    out_gains,
    all_hidden,
    all_result,
    gains_mine,
    gains_core,
    gains_chip,
    rows_core,
    rows_chip,
    rows_bf,
    slots_a,
    slots_misc,
    slots_gains,
    ring_send,
    ring_recv,
    mp_send,
    mp_recv,
    local_sem,
):
    m = lax.axis_index("mp")
    core, chip = mp_partners(m)
    far = (m + 2) % 4
    beside = m + 1 - 2 * (m % 2)
    ring = RingScatter(
        n,
        [grad_a, misc, gains_mine],
        [(out_zx, out_state, out_dt), (out_misc,), (out_gains,)],
        [slots_a, slots_misc, slots_gains],
        [ring_send, ring_recv],
    )
    greet([core, chip, ring.nxt, ring.prv])
    sent = []

    def over_mp(i, source, target, device):
        copy = remote(source, target, mp_send.at[i], mp_recv.at[i], device)
        copy.start()
        sent.append(copy)
        return copy

    ring.step(0, 0)
    ring.step(0, 1)
    gains_one = over_mp(0, gains, gains_core, core)
    rows_far = over_mp(1, d_normed.at[(beside + 2) % 4], rows_core.at[1], core)
    rows_near = over_mp(2, d_normed.at[beside], rows_core.at[0], core)
    own_result = pltpu.make_async_copy(result, all_result.at[m], local_sem.at[0])
    own_result.start()
    gains_one.wait_recv()
    for b in range(n):
        add_rows(gains_mine.at[b], [gains.at[b], gains_core.at[b]], 16, F32)
    gains_two = over_mp(3, gains_mine, gains_chip, chip)
    count = d_mixed.shape[0]
    rows_far.wait_recv()
    add_rows(rows_core.at[1], [rows_core.at[1], d_normed.at[far]], count, BF)
    rows_two = over_mp(4, rows_core.at[1], rows_chip, chip)
    result_chip = over_mp(5, result, all_result.at[m], chip)
    result_core = over_mp(6, result, all_result.at[m], core)
    ring.step(1, 0)
    ring.step(1, 1)
    gains_two.wait()
    for b in range(n):
        add_rows(gains_mine.at[b], [gains_mine.at[b], gains_chip.at[b]], 16, F32)
    ring.step(0, 2)
    rows_near.wait_recv()
    rows_two.wait_recv()

    def body(i, carry):
        sl = pl.ds(pl.multiple_of(i * 16, 16), 16)
        d_n = d_normed[m, sl, :].astype(F32) + rows_core[0, sl, :].astype(F32)
        d_n = d_n + rows_chip[sl, :].astype(F32) + extra[sl, :]
        x = hidden[sl, :].astype(F32)
        inv = lax.rsqrt(jnp.mean(x * x, axis=1, keepdims=True) + EPS)
        unit = x * inv
        d_unit = d_n * gain[...]
        mean = jnp.mean(d_unit * unit, axis=1, keepdims=True)
        rows_bf[sl, :] = (d_mixed[sl, :] + inv * (d_unit - unit * mean)).astype(BF)
        return carry

    lax.fori_loop(0, count // 16, body, 0)
    own_hidden = pltpu.make_async_copy(rows_bf, all_hidden.at[m], local_sem.at[1])
    own_hidden.start()
    hidden_chip = over_mp(7, rows_bf, all_hidden.at[m], chip)
    hidden_core = over_mp(8, rows_bf, all_hidden.at[m], core)
    arrive = []
    for s in range(2, n // 2 + 1):
        ring.step(s, 0)
        ring.step(s, 1)
        ring.step(s - 1, 2)
        if s == 2:
            result_chip.wait_recv()
            arrive.append(over_mp(9, all_result.at[far], all_result.at[far], core))
        if s == n // 2 - 1:
            hidden_chip.wait_recv()
            arrive.append(over_mp(10, all_hidden.at[far], all_hidden.at[far], core))
    ring.step(n // 2, 2)
    for copy in [result_core, hidden_core] + arrive:
        copy.wait_recv()
    own_result.wait()
    own_hidden.wait()
    for copy in sent:
        if copy is not gains_two:
            copy.wait_send()
    ring.end()


def last_exchange(grad_a, misc, gains, d_normed, extra, d_mixed, hidden, gain, result, cols, cid):
    n = lax.axis_size("dp")
    shard = grad_a.shape[1]
    rows, model = d_mixed.shape
    dma = pltpu.SemaphoreType.DMA
    every = jax.ShapeDtypeStruct((4, rows, model), BF)
    return pl.pallas_call(
        partial(last_kernel, n),
        out_shape=[jax.ShapeDtypeStruct((shard, c), F32) for c in cols]
        + [jax.ShapeDtypeStruct(a.shape[1:], F32) for a in (misc, gains)]
        + [every, every],
        in_specs=[VM] * 8 + [ANY],
        out_specs=[VM] * 5 + [ANY] * 2,
        scratch_shapes=[
            pltpu.VMEM(gains.shape, F32),
            pltpu.VMEM(gains.shape, F32),
            pltpu.VMEM(gains.shape, F32),
            pltpu.VMEM((2, rows, model), BF),
            pltpu.VMEM((rows, model), BF),
            pltpu.VMEM((rows, model), BF),
        ]
        + RingScatter.scratch(n, [grad_a, misc, gains])
        + [dma((11,)), dma((11,)), dma((2,))],
        compiler_params=pltpu.CompilerParams(
            collective_id=cid, has_side_effects=True, vmem_limit_bytes=56 * 1024 * 1024
        ),
    )(grad_a, misc, gains, d_normed, extra, d_mixed, hidden, gain, result)


def mp_scatter_kernel(x, out, from_core, from_chip, send_sem, recv_sem):
    m = lax.axis_index("mp")
    core, chip = mp_partners(m)
    mine, far = m, (m + 2) % 4
    beside = m + 1 - 2 * (m % 2)
    parts = [(pl.ds(start, size), size) for start, size in chunk_rows(0, out.shape[0])]
    greet([core, chip])
    first, last = [], []
    for slot, block in ((1, (beside + 2) % 4), (0, beside)):
        for i, (part, _) in enumerate(parts):
            copy = remote(
                x.at[block, part], from_core.at[slot, part], send_sem.at[slot, i], recv_sem.at[slot, i], core
            )
            copy.start()
            first.append(copy)
    for i, (part, size) in enumerate(parts):
        first[i].wait_recv()
        held = from_core.at[1, part]
        add_rows(held, [held, x.at[far, part]], size, x.dtype)
        copy = remote(held, from_chip.at[part], send_sem.at[2, i], recv_sem.at[2, i], chip)
        copy.start()
        last.append(copy)
    for i, (part, size) in enumerate(parts):
        first[len(parts) + i].wait_recv()
        last[i].wait_recv()
        add_rows(out.at[part], [x.at[mine, part], from_core.at[0, part], from_chip.at[part]], size, F32)
    for copy in first + last:
        copy.wait_send()


def scatter_mp(x, cid):
    rows, cols = x.shape[1:]
    count = len(chunk_rows(0, rows))
    return pl.pallas_call(
        mp_scatter_kernel,
        out_shape=jax.ShapeDtypeStruct((rows, cols), F32),
        in_specs=[VM],
        out_specs=VM,
        scratch_shapes=[
            pltpu.VMEM((2, rows, cols), x.dtype),
            pltpu.VMEM((rows, cols), x.dtype),
            pltpu.SemaphoreType.DMA((3, count)),
            pltpu.SemaphoreType.DMA((3, count)),
        ],
        compiler_params=pltpu.CompilerParams(
            collective_id=cid, has_side_effects=True, vmem_limit_bytes=32 * 1024 * 1024
        ),
    )(x)


def mp_gather_kernel(k, *refs):
    ins, outs = refs[:k], refs[k : 2 * k]
    local_sem, send_sem, recv_sem = refs[2 * k :]
    m = lax.axis_index("mp")
    core, chip = mp_partners(m)
    far = (m + 2) % 4
    greet([core, chip])
    copies, local, arrive = [], [], []
    for j in range(k):
        to_chip = remote(ins[j], outs[j].at[m], send_sem.at[0, j], recv_sem.at[0, j], chip)
        to_chip.start()
        to_core = remote(ins[j], outs[j].at[m], send_sem.at[1, j], recv_sem.at[1, j], core)
        to_core.start()
        own = pltpu.make_async_copy(ins[j], outs[j].at[m], local_sem.at[j])
        own.start()
        copies += [to_chip, to_core]
        arrive.append(to_chip)
        local.append(own)
    onward = []
    for j in range(k):
        arrive[j].wait_recv()
        copy = remote(outs[j].at[far], outs[j].at[far], send_sem.at[2, j], recv_sem.at[2, j], core)
        copy.start()
        onward.append(copy)
    for j in range(k):
        copies[2 * j + 1].wait_recv()
        onward[j].wait_recv()
        local[j].wait()
    for copy in copies + onward:
        copy.wait_send()


def gather_mp(arrays, cid):
    k = len(arrays)
    return pl.pallas_call(
        partial(mp_gather_kernel, k),
        out_shape=[jax.ShapeDtypeStruct((4,) + a.shape, a.dtype) for a in arrays],
        in_specs=[ANY] * k,
        out_specs=[ANY] * k,
        scratch_shapes=[
            pltpu.SemaphoreType.DMA((k,)),
            pltpu.SemaphoreType.DMA((3, k)),
            pltpu.SemaphoreType.DMA((3, k)),
        ],
        compiler_params=pltpu.CompilerParams(collective_id=cid, has_side_effects=True),
    )(*arrays)


class TokenGather:
    def __init__(self, n, both, x, out, sems):
        self.n, self.both, self.out = n, both, out
        self.local, self.ring_s, self.ring_r, self.core_s, self.core_r, self.chip_s, self.chip_r = sems
        self.d, self.m = lax.axis_index("dp"), lax.axis_index("mp")
        self.far = (self.m + 2) % 4
        self.core, self.chip = mp_partners(self.m)
        self.p, self.nxt, self.prv = ring_neighbours(n)
        rows = out.shape[2]
        base = pl.multiple_of(self.m * rows, rows) if x.shape[0] > rows else 0
        self.x = x.at[pl.ds(base, rows)]
        self.pieces = [(0,) + c for c in chunk_rows(0, both) + chunk_rows(both, rows - both)]
        self.pieces += [(1,) + c for c in chunk_rows(0, both)]
        self.sent, self.pending = [], {}
        self.ring, self.chips = {}, {}

    @staticmethod
    def scratch(n, rows, both):
        dma = pltpu.SemaphoreType.DMA
        far = len(chunk_rows(0, both))
        own = far + len(chunk_rows(both, rows - both))
        steps = n // 2
        return [
            dma((3,)),
            dma((steps, own + far, 2)),
            dma((steps, own + far, 2)),
            dma((steps + 1, 2 * own + far, 2)),
            dma((steps + 1, 2 * own + far, 2)),
            dma((steps + 1, own, 2)),
            dma((steps + 1, own, 2)),
        ]

    def send(self, source, place, s_sem, r_sem, target):
        copy = remote(source, place, s_sem, r_sem, target)
        copy.start()
        self.sent.append(copy)
        return copy

    def begin(self):
        own = self.out.at[self.d, self.m]
        self.load = pltpu.make_async_copy(self.x, own, self.local.at[0])
        self.load.start()
        self.first = None
        if self.both:
            part = pl.ds(0, self.both)
            self.first = remote(
                self.x.at[part], own.at[part], self.local.at[1], self.local.at[2], self.chip
            )
            self.first.start()
            self.sent.append(self.first)

    def step(self, s, between=None):
        n, p = self.n, self.p
        for k, (is_far, start, rows) in enumerate(self.pieces):
            if k > 0 and between is not None:
                between()
            for way in range(2):
                origin = ring_device(n, (p + n - s) % n if way == 0 else (p + s) % n)
                place = self.far if is_far else self.m
                region = self.out.at[origin, place, pl.ds(start, rows)]
                source = region if s > 0 or is_far else self.x.at[pl.ds(start, rows)]
                if (s - 1, k, way) in self.ring:
                    self.ring[s - 1, k, way].wait_recv()
                elif s > 0:
                    continue
                elif is_far and self.first is not None:
                    self.first.wait_recv()
                    self.first = None
                if s + 1 < n // 2 or (s + 1 == n // 2 and k % 2 == way):
                    self.ring[s, k, way] = self.send(
                        source,
                        region,
                        self.ring_s.at[s, k, way],
                        self.ring_r.at[s, k, way],
                        self.nxt if way == 0 else self.prv,
                    )
                if s == 0 and way == 1:
                    continue
                self.pending.setdefault(s, []).append(
                    self.send(source, region, self.core_s.at[s, k, way], self.core_r.at[s, k, way], self.core)
                )
                if not is_far and start >= self.both:
                    self.chips[s, k, way] = (
                        self.send(
                            source, region, self.chip_s.at[s, k, way], self.chip_r.at[s, k, way], self.chip
                        ),
                        self.out.at[origin, self.far, pl.ds(start, rows)],
                    )

    def pass_on(self, s):
        total = len(self.pieces)
        for k in range(total):
            for way in range(2):
                if (s, k, way) in self.chips:
                    copy, region = self.chips[s, k, way]
                    copy.wait_recv()
                    at = (s, total + k, way)
                    self.pending.setdefault(s, []).append(
                        self.send(region, region, self.core_s.at[at], self.core_r.at[at], self.core)
                    )

    def blocks(self, s):
        n, p = self.n, self.p
        if s in (0, n // 2):
            return [ring_device(n, (p + s) % n)]
        return [ring_device(n, (p + n - s) % n), ring_device(n, (p + s) % n)]

    def complete(self, s):
        if s == 0:
            self.load.wait()
        for copy in self.pending.pop(s):
            copy.wait_recv()

    def end(self):
        for s in sorted(self.pending):
            self.complete(s)
        for copy in self.sent:
            copy.wait_send()


class SlotWork:
    def __init__(self, own, small, position):
        self.own, self.small, self.position = own, small, position
        self.first = (lax.axis_index("dp") * own).astype(F32)
        self.length = position.shape[2]

    def count_with(self, earlier):
        self.earlier = earlier
        row = lax.broadcasted_iota(jnp.int32, earlier.shape, 0)
        col = lax.broadcasted_iota(jnp.int32, earlier.shape, 1)
        earlier[...] = jnp.where(row < col, 1.0, 0.0).astype(BF)

    def gate_with(self, router, gates, slot_gates):
        self.router, self.gates, self.slot_gates = router, gates, slot_gates

    def named(self, block, first, count):
        length = self.length
        routes = self.small[block, :, 0:length].astype(F32)
        expert = lax.broadcasted_iota(jnp.int32, (count, length), 0).astype(F32) + first
        found = routes[1:2, :] == expert
        for k in range(2, TOPK + 1):
            found = found | (routes[k : k + 1, :] == expert)
        return found

    def place(self, block):
        named = self.named(block, self.first, 8)
        count = dot(jnp.where(named, 1.0, 0.0).astype(BF), self.earlier[...])
        self.position[block] = jnp.where(named, count, -1.0)[0 : self.own, :]

    def pick(self, block):
        return pick_matrix(self.position[block], self.own)

    def gate(self, block, rows, pick):
        own = self.own
        logits = dot(rows, self.router[...])
        named = jnp.where(self.named(block, 0.0, LANES), 1.0, 0.0).T > 0.5
        top = jnp.max(jnp.where(named, logits, MASKED), axis=1, keepdims=True)
        powers = jnp.where(named, jnp.exp(jnp.minimum(logits - top, 0.0)), 0.0)
        gate = powers / jnp.sum(powers, axis=1, keepdims=True)
        self.gates[block] = gate
        of_slot = dot(pick, jnp.concatenate(two_parts(gate), axis=1))
        of_slot = of_slot[:, 0:LANES] + of_slot[:, LANES : 2 * LANES]
        row = lax.broadcasted_iota(jnp.int32, of_slot.shape, 0)
        col = lax.broadcasted_iota(jnp.int32, of_slot.shape, 1)
        mine = col - lax.axis_index("dp") * own == row // CAP
        of_slot = jnp.sum(jnp.where(mine, of_slot, 0.0), axis=1, keepdims=True)
        of_slot = jnp.broadcast_to(of_slot, (own * CAP, LANES)).reshape(own, CAP, LANES)
        for e in range(own):
            self.slot_gates[e, block] = of_slot[e]


class RowStream:
    def __init__(self, source, target, in_buf, out_buf, load_sem, store_sem):
        self.source, self.target, self.in_buf, self.out_buf = source, target, in_buf, out_buf
        self.load_sem, self.store_sem = load_sem, store_sem
        self.loads, self.stores = [], []

    def load(self, block):
        at = len(self.loads) % self.in_buf.shape[0]
        copy = pltpu.make_async_copy(self.source.at[block], self.in_buf.at[at], self.load_sem.at[at])
        copy.start()
        self.loads.append(copy)

    def take(self, i, wait=True):
        if wait:
            self.loads[i].wait()
        held = self.in_buf[i % self.in_buf.shape[0]]
        return held.reshape(-1, held.shape[-1])

    def give(self, i, block, picked):
        if i > 1:
            self.stores[i - 2].wait()
        self.out_buf[i % 2] = picked.astype(BF).reshape(self.out_buf.shape[1:])
        copy = pltpu.make_async_copy(
            self.out_buf.at[i % 2], self.target.at[:, block], self.store_sem.at[i % 2]
        )
        copy.start()
        self.stores.append(copy)

    def end(self):
        for copy in self.stores[-2:]:
            copy.wait()


def token_gather_kernel(
    n,
    both,
    own,
    units,
    x,
    position,
    small,
    weights,
    cot,
    out,
    x_rows,
    gates,
    slot_gates,
    block,
    act,
    d_mid,
    shared_res,
    shared_d,
    x_in,
    x_out,
    mid,
    stream_sem,
    *sems,
):
    inner = weights.shape[1] - 3 * units - LANES
    shared_in = pl.ds(inner, 2 * units)
    shared_out = pl.ds(inner + 2 * units, units)
    router = weights.at[:, pl.ds(inner + 3 * units, LANES)]
    gather = TokenGather(n, both, x, out, sems)
    work = SlotWork(own, small, position)
    work.gate_with(router, gates, slot_gates)
    x_stream = RowStream(out, x_rows, x_in, x_out, stream_sem.at[0], stream_sem.at[1])
    half = n // 2
    greet([gather.core, gather.chip, gather.nxt, gather.prv])
    gather.begin()
    tasks = []

    def shared(held):
        def first():
            block[...] = x_stream.take(held["at"])
            mid[...] = dot(block[...], weights[:, shared_in])

        def second():
            gate, up = mid[:, 0:units], mid[:, units : 2 * units]
            sig = jax.nn.sigmoid(gate)
            silu = gate * sig
            act[...] = (silu * up).astype(BF)
            d_act = dot(cot[...], weights[:, shared_out])
            slope = sig * (1.0 + gate * (1.0 - sig))
            d_mid[:, 0:units] = (d_act * up * slope).astype(BF)
            d_mid[:, units : 2 * units] = (d_act * silu).astype(BF)

        def third():
            shared_res[...] = dot(act[...], weights[:, shared_out], ((1,), (1,)))

        def fourth():
            shared_d[...] = dot(d_mid[...], weights[:, shared_in], ((1,), (1,)))

        return [first, second, third, fourth]

    def pick_x(s):
        blocks = gather.blocks(s)
        held = {}

        def start():
            gather.complete(s)
            held["at"] = len(x_stream.loads)
            for block in blocks:
                x_stream.load(block)

        found = [start]
        if s == 0:
            found += shared(held)
        for i, block in enumerate(blocks):

            def pick(i=i, block=block):
                held[i] = work.pick(block)
                rows = x_stream.take(held["at"] + i, s > 0)
                x_stream.give(held["at"] + i, block, dot(held[i], rows))

            def gate(i=i, block=block):
                work.gate(block, x_stream.take(held["at"] + i, False), held[i])

            found += [pick, gate]
        return found

    def between():
        for _ in range(1 if len(tasks) < 6 else 2):
            if tasks:
                tasks.pop(0)()

    gather.step(0)
    for s in range(1, half + 1):
        gather.step(s, between)
        gather.pass_on(s - 1)
        tasks += pick_x(s - 1)
    final = pick_x(half)
    while len(tasks) > 4:
        tasks.pop(0)()
    gather.pass_on(half)
    tasks.pop(0)()
    tasks.pop(0)()
    final.pop(0)()
    for task in tasks + final:
        task()
    gather.end()
    x_stream.end()


def gather_tokens(x, position, small, weights, cot, units, cid):
    n, own, tokens = position.shape
    quarter, model = x.shape
    both = quarter // 128 * 48
    return pl.pallas_call(
        partial(token_gather_kernel, n, both, own, units),
        out_shape=[
            jax.ShapeDtypeStruct((n, 4) + x.shape, x.dtype),
            jax.ShapeDtypeStruct((own, n, CAP, model), BF),
            jax.ShapeDtypeStruct((n, tokens, LANES), F32),
            jax.ShapeDtypeStruct((own, n, CAP, LANES), F32),
            jax.ShapeDtypeStruct((tokens, model), BF),
            jax.ShapeDtypeStruct((tokens, units), BF),
            jax.ShapeDtypeStruct((tokens, 2 * units), BF),
            jax.ShapeDtypeStruct((tokens, model), F32),
            jax.ShapeDtypeStruct((tokens, model), F32),
        ],
        in_specs=[ANY, VM, VM, VM, VM],
        out_specs=[ANY, ANY] + [VM] * 7,
        scratch_shapes=[
            pltpu.VMEM((3, 4, quarter, model), BF),
            pltpu.VMEM((2, own, CAP, model), BF),
            pltpu.VMEM((tokens, 2 * units), F32),
            pltpu.SemaphoreType.DMA((2, 3)),
        ]
        + TokenGather.scratch(n, quarter, both),
        compiler_params=pltpu.CompilerParams(
            collective_id=cid, has_side_effects=True, vmem_limit_bytes=56 * 1024 * 1024
        ),
    )(x, position, small, weights, cot)


def slots_kernel(own, y, small, y_rows, position, earlier):
    work = SlotWork(own, small, position)
    work.count_with(earlier)
    work.place(0)
    y_rows[...] = dot(work.pick(0), y[0]).astype(BF).reshape(y_rows.shape)


def slots_of(y, small, own):
    n, tokens, model = y.shape
    return pl.pallas_call(
        partial(slots_kernel, own),
        grid=(n,),
        out_shape=[
            jax.ShapeDtypeStruct((own, n, CAP, model), BF),
            jax.ShapeDtypeStruct((n, own, tokens), F32),
        ],
        in_specs=[token_spec(tokens, model), token_spec(small.shape[1], small.shape[2])],
        out_specs=[slot_spec(own, model), token_spec(own, tokens)],
        scratch_shapes=[pltpu.VMEM((tokens, tokens), BF)],
        compiler_params=BIG,
    )(y, small)


def first_kernel(n, k, *refs):
    ins, x = refs[:k], refs[k]
    outs, x_out = refs[k + 1 : 2 * k + 1], refs[2 * k + 1]
    ring = RingGather(n, ins, outs, refs[2 * k + 2 : 2 * k + 5])
    gather = TokenGather(n, 0, x, x_out, refs[2 * k + 5 :])
    greet([gather.core, gather.chip, gather.nxt, gather.prv])
    ring.begin()
    gather.begin()
    for s in range(n // 2 + 1):
        gather.step(s)
        ring.step(s)
        if s > 0:
            gather.pass_on(s - 1)
    gather.pass_on(n // 2)
    gather.end()
    ring.end()


def first_gather(arrays, x, cid):
    n, k = lax.axis_size("dp"), len(arrays)
    rows, cols = x.shape[0] // 4, x.shape[1]
    return pl.pallas_call(
        partial(first_kernel, n, k),
        out_shape=[jax.ShapeDtypeStruct((n,) + a.shape, a.dtype) for a in arrays]
        + [jax.ShapeDtypeStruct((n, 4, rows, cols), x.dtype)],
        in_specs=[ANY] * (k + 1),
        out_specs=[ANY] * (k + 1),
        scratch_shapes=RingGather.scratch(n, arrays) + TokenGather.scratch(n, rows, 0),
        compiler_params=pltpu.CompilerParams(collective_id=cid, has_side_effects=True),
    )(*arrays, x)


def token_scatter_kernel(
    n,
    x,
    out,
    from_core,
    slots,
    loads,
    far_loads,
    from_chip,
    to_chip,
    first,
    done,
    last_buf,
    load_sem,
    far_sem,
    core_send,
    core_recv,
    chip_send,
    chip_recv,
    send_sem,
    recv_sem,
    last_send,
    last_recv,
):
    m = lax.axis_index("mp")
    c, y = m % 2, m // 2
    core, chip = mp_partners(m)
    far = (m + 2) % 4
    beside = m + 1 - 2 * c
    p, nxt, prv = ring_neighbours(n)
    rows = out.shape[0]
    half, steps = rows // 2, n // 2
    greet([core, chip, nxt, prv])

    def block_of(i):
        s = (i + 1) // 2
        return ring_device(n, (p + steps - s) % n if i % 2 or i == 0 else (p + n - steps + s) % n)

    over, sent, loading, chips = {}, [], {}, {}
    loaded, summed = set(), set()
    upper, lower, whole = pl.ds(half, half), pl.ds(0, half), pl.ds(0, rows)

    def core_sends(i):
        if i >= n:
            return
        block = block_of(i)
        moves = [((beside + 2) % 4, 1 - y, upper), (beside, y, whole), ((beside + 2) % 4, 1 - y, lower)]
        for k, (theirs, piece, part) in enumerate(moves):
            copy = remote(
                x.at[block, theirs, part],
                from_core.at[block, piece, part],
                core_send.at[i, k],
                core_recv.at[i, k],
                core,
            )
            copy.start()
            over[i, k] = copy
            sent.append(copy)

    def start_pair(name, source, other, target, sems):
        loading[name] = []
        for k, ref in enumerate((source, other)):
            copy = pltpu.make_async_copy(ref, target.at[k], sems.at[k])
            copy.start()
            loading[name].append(copy)

    def load(i):
        if i >= n:
            return
        block = block_of(i)
        at = i % 4
        over[i, 1].wait_recv()
        start_pair(
            (i, 0), x.at[block, m], from_core.at[block, y], loads.at[at, :, whole], load_sem.at[at, 0]
        )
        over[i, 2].wait_recv()
        start_pair(
            (i, 1),
            x.at[block, far, lower],
            from_core.at[block, 1 - y, lower],
            loads.at[at, :, pl.ds(rows, half)],
            load_sem.at[at, 1],
        )

    def load_far(i):
        if i >= n:
            return
        block = block_of(i)
        over[i, 0].wait_recv()
        start_pair(
            (i, 2),
            x.at[block, far, upper],
            from_core.at[block, 1 - y, upper],
            far_loads.at[i % 2],
            far_sem.at[i % 2],
        )

    def to_other_chip(i):
        if i >= n:
            return
        for copy in loading[i, 2]:
            copy.wait()
        if i > 1:
            chips[i - 2].wait_send()
        add_rows(to_chip.at[i % 2], [far_loads.at[i % 2, 0], far_loads.at[i % 2, 1]], half, BF)
        copy = remote(to_chip.at[i % 2], from_chip.at[i], chip_send.at[i], chip_recv.at[i], chip)
        copy.start()
        chips[i] = copy

    chunks = chunk_rows(0, rows + half)
    count = len(chunks)
    order = [k for k in range(count) if chunks[k][0] >= rows]
    order += [k for k in range(count) if chunks[k][0] < rows]

    def pieces_of(i, k):
        start, size = chunks[k]
        area = pl.ds(start, size)
        if i not in loaded:
            loaded.add(i)
            for copy in loading[i, 0] + loading[i, 1]:
                copy.wait()
        found = [loads.at[i % 4, 0, area], loads.at[i % 4, 1, area]]
        if half <= start < rows:
            if i not in summed:
                summed.add(i)
                chips[i].wait_recv()
            found.append(from_chip.at[i, pl.ds(start - half, size)])
        return found

    for i in range(3):
        core_sends(i)
    load_far(0)
    load(0)
    load_far(1)
    to_other_chip(0)
    load_far(2)
    to_other_chip(1)
    core_sends(3)
    core_sends(4)
    load(1)
    to_other_chip(2)
    load(2)
    ring = {}
    for s in range(steps):
        for k, way in [(k, way) for k in order for way in range(2) if s > 0 or k % 2 == way]:
            start, size = chunks[k]
            area = pl.ds(start, size)
            if s == 0:
                target, pieces = first.at[area], pieces_of(0, k)
            else:
                target, pieces = slots.at[s - 1, way, area], pieces_of(2 * s - 1 + way, k)
                if (s - 1, k, way) in ring:
                    ring[s - 1, k, way].wait_recv()
                    pieces.append(target)
            add_rows(target, pieces, size, BF)
            copy = remote(
                target,
                slots.at[s, way, area],
                send_sem.at[s, k, way],
                recv_sem.at[s, k, way],
                nxt if way == 0 else prv,
            )
            copy.start()
            ring[s, k, way] = copy
        for i in (2 * s + 3, 2 * s + 4):
            load_far(i)
            core_sends(i + 2)
            to_other_chip(i)
            load(i)
    last = []
    for k in order:
        start, size = chunks[k]
        area = pl.ds(start, size)
        pieces = pieces_of(n - 1, k)
        for way in range(2):
            ring[steps - 1, k, way].wait_recv()
            pieces.append(slots.at[steps - 1, way, area])
        if start < rows:
            add_rows(out.at[area], pieces, size, F32)
            continue
        at = pl.ds(start - rows, size)
        add_rows(done.at[at], pieces, size, BF)
        copy = remote(done.at[at], last_buf.at[at], last_send.at[k], last_recv.at[k], chip)
        copy.start()
        last.append(copy)
    for copy in last:
        copy.wait_recv()
    add_rows(out.at[lower], [out.at[lower], last_buf], half, F32)
    for copy in sent + list(ring.values()) + last + [chips[n - 2], chips[n - 1]]:
        copy.wait_send()


def scatter_tokens(x, cid):
    n, _, rows, cols = x.shape
    half, steps = rows // 2, n // 2
    count = len(chunk_rows(0, rows + half))
    dma = pltpu.SemaphoreType.DMA
    out, _ = pl.pallas_call(
        partial(token_scatter_kernel, n),
        out_shape=[
            jax.ShapeDtypeStruct((rows, cols), F32),
            jax.ShapeDtypeStruct((n, 2, rows, cols), BF),
        ],
        in_specs=[ANY],
        out_specs=[VM, ANY],
        scratch_shapes=[
            pltpu.VMEM((steps, 2, rows + half, cols), BF),
            pltpu.VMEM((4, 2, rows + half, cols), BF),
            pltpu.VMEM((2, 2, half, cols), BF),
            pltpu.VMEM((n, half, cols), BF),
            pltpu.VMEM((2, half, cols), BF),
            pltpu.VMEM((rows + half, cols), BF),
            pltpu.VMEM((half, cols), BF),
            pltpu.VMEM((half, cols), BF),
            dma((4, 2, 2)),
            dma((2, 2)),
            dma((n, 3)),
            dma((n, 3)),
            dma((n,)),
            dma((n,)),
            dma((steps, count, 2)),
            dma((steps, count, 2)),
            dma((count,)),
            dma((count,)),
        ],
        compiler_params=pltpu.CompilerParams(
            collective_id=cid, has_side_effects=True, vmem_limit_bytes=56 * 1024 * 1024
        ),
    )(x)
    return out


def put_scatter_kernel(
    n,
    own,
    position,
    slot_a,
    slot_b,
    slot_c,
    shared_a,
    shared_b,
    out,
    from_core,
    made,
    in_a,
    in_b,
    in_c,
    slots,
    loads,
    far_loads,
    from_chip,
    to_chip,
    first,
    done,
    last_buf,
    slot_sem,
    load_sem,
    far_sem,
    core_send,
    core_recv,
    chip_send,
    chip_recv,
    send_sem,
    recv_sem,
    last_send,
    last_recv,
):
    m = lax.axis_index("mp")
    c, y = m % 2, m // 2
    core, chip = mp_partners(m)
    far = (m + 2) % 4
    beside = m + 1 - 2 * c
    p, nxt, prv = ring_neighbours(n)
    rows = out.shape[0]
    model = shared_a.shape[1]
    half, steps = rows // 2, n // 2

    def block_of(i):
        s = (i + 1) // 2
        return ring_device(n, (p + steps - s) % n if i % 2 or i == 0 else (p + n - steps + s) % n)

    over, sent, loading, chips, arriving = {}, [], {}, {}, {}
    loaded, summed = set(), set()
    upper, lower, whole = pl.ds(half, half), pl.ds(0, half), pl.ds(0, rows)

    def slot_load(i):
        if i >= n:
            return
        arriving[i] = []
        for k, (source, target) in enumerate(((slot_a, in_a), (slot_b, in_b), (slot_c, in_c))):
            copy = pltpu.make_async_copy(source.at[:, block_of(i)], target.at[i % 2], slot_sem.at[i % 2, k])
            copy.start()
            arriving[i].append(copy)

    def make(i):
        if i >= n:
            return
        slot_load(i + 1)
        if i >= 4:
            for k in range(3):
                over[i - 4, k].wait_send()
        pick = pick_matrix(position[block_of(i)], own)
        for copy in arriving[i]:
            copy.wait()
        start = 0
        for target, shared in ((in_a, shared_a), (in_b, shared_b), (in_c, None)):
            cols = target.shape[3]
            total = dot(pick, target[i % 2].reshape(own * CAP, cols), ((0,), (0,)))
            if i == n - 1 and shared is not None:
                total = total + shared[...]
            made[i % 4, :, :, start : start + cols] = total.astype(BF).reshape(4, rows, cols)
            start += cols

    def core_sends(i):
        if i >= n:
            return
        block = block_of(i)
        moves = [((beside + 2) % 4, 1 - y, upper), (beside, y, whole), ((beside + 2) % 4, 1 - y, lower)]
        for k, (theirs, piece, part) in enumerate(moves):
            copy = remote(
                made.at[i % 4, theirs, part],
                from_core.at[block, piece, part],
                core_send.at[i, k],
                core_recv.at[i, k],
                core,
            )
            copy.start()
            over[i, k] = copy
            if i >= n - 4:
                sent.append(copy)

    def load(i):
        if i >= n:
            return
        block = block_of(i)
        loading[i] = []
        for k, (piece, part, at) in enumerate(((y, whole, 0), (1 - y, lower, rows))):
            over[i, k + 1].wait_recv()
            copy = pltpu.make_async_copy(
                from_core.at[block, piece, part],
                loads.at[i % 4, pl.ds(at, rows if k == 0 else half)],
                load_sem.at[i % 4, k],
            )
            copy.start()
            loading[i].append(copy)

    def to_other_chip(i):
        if i >= n:
            return
        over[i, 0].wait_recv()
        copy = pltpu.make_async_copy(
            from_core.at[block_of(i), 1 - y, upper], far_loads.at[i % 2], far_sem.at[i % 2]
        )
        copy.start()
        load(i)
        if i > 1:
            chips[i - 2].wait_send()
        copy.wait()
        add_rows(to_chip.at[i % 2], [far_loads.at[i % 2], made.at[i % 4, far, upper]], half, BF)
        copy = remote(to_chip.at[i % 2], from_chip.at[i], chip_send.at[i], chip_recv.at[i], chip)
        copy.start()
        chips[i] = copy

    chunks = chunk_rows(0, rows + half)
    order = [k for k in range(len(chunks)) if chunks[k][0] >= rows]
    order += [k for k in range(len(chunks)) if chunks[k][0] < rows]

    def pieces_of(i, k):
        start, size = chunks[k]
        area = pl.ds(start, size)
        if i not in loaded:
            loaded.add(i)
            for copy in loading[i]:
                copy.wait()
        found = [loads.at[i % 4, area]]
        if start < rows:
            found.append(made.at[i % 4, m, area])
        else:
            found.append(made.at[i % 4, far, pl.ds(start - rows, size)])
        if half <= start < rows:
            if i not in summed:
                summed.add(i)
                chips[i].wait_recv()
            found.append(from_chip.at[i, pl.ds(start - half, size)])
        return found

    slot_load(0)
    make(0)
    greet([core, chip, nxt, prv])
    core_sends(0)
    make(1)
    core_sends(1)
    to_other_chip(0)
    ring = {}
    for s in range(steps):
        for k, way in [(k, way) for k in order for way in range(2) if s > 0 or k % 2 == way]:
            start, size = chunks[k]
            area = pl.ds(start, size)
            if s == 0:
                if start == half:
                    make(2)
                    core_sends(2)
                target, pieces = first.at[area], pieces_of(0, k)
            else:
                target, pieces = slots.at[s - 1, way, area], pieces_of(2 * s - 1 + way, k)
                if (s - 1, k, way) in ring:
                    ring[s - 1, k, way].wait_recv()
                    pieces.append(target)
            add_rows(target, pieces, size, BF)
            copy = remote(
                target,
                slots.at[s, way, area],
                send_sem.at[s, k, way],
                recv_sem.at[s, k, way],
                nxt if way == 0 else prv,
            )
            copy.start()
            ring[s, k, way] = copy
        if s == 0:
            to_other_chip(1)
            to_other_chip(2)
        for i in (2 * s + 3, 2 * s + 4):
            make(i)
            core_sends(i)
        for i in (2 * s + 3, 2 * s + 4):
            to_other_chip(i)
    last = []
    for k in order:
        start, size = chunks[k]
        area = pl.ds(start, size)
        pieces = pieces_of(n - 1, k)
        for way in range(2):
            ring[steps - 1, k, way].wait_recv()
            pieces.append(slots.at[steps - 1, way, area])
        if start < rows:
            add_rows(out.at[area], pieces, size, F32)
            continue
        at = pl.ds(start - rows, size)
        add_rows(done.at[at], pieces, size, BF)
        copy = remote(done.at[at], last_buf.at[at], last_send.at[k], last_recv.at[k], chip)
        copy.start()
        last.append(copy)
    for copy in last:
        copy.wait_recv()
    add_rows(out.at[lower], [out.at[lower], last_buf], half, F32)
    for copy in sent + list(ring.values()) + last + [chips[n - 2], chips[n - 1]]:
        copy.wait_send()


def put_scatter(position, rows_a, rows_b, rows_c, shared_a, shared_b, cid):
    n, own, tokens = position.shape
    model = shared_a.shape[1]
    quarter = tokens // 4
    cols = 2 * model + LANES
    half, steps = quarter // 2, n // 2
    count = len(chunk_rows(0, quarter + half))
    dma = pltpu.SemaphoreType.DMA
    out, _ = pl.pallas_call(
        partial(put_scatter_kernel, n, own),
        out_shape=[
            jax.ShapeDtypeStruct((quarter, cols), F32),
            jax.ShapeDtypeStruct((n, 2, quarter, cols), BF),
        ],
        in_specs=[VM, ANY, ANY, ANY, VM, VM],
        out_specs=[VM, ANY],
        scratch_shapes=[
            pltpu.VMEM((4, 4, quarter, cols), BF),
            pltpu.VMEM((2, own, CAP, model), BF),
            pltpu.VMEM((2, own, CAP, model), BF),
            pltpu.VMEM((2, own, CAP, LANES), BF),
            pltpu.VMEM((steps, 2, quarter + half, cols), BF),
            pltpu.VMEM((4, quarter + half, cols), BF),
            pltpu.VMEM((2, half, cols), BF),
            pltpu.VMEM((n, half, cols), BF),
            pltpu.VMEM((2, half, cols), BF),
            pltpu.VMEM((quarter + half, cols), BF),
            pltpu.VMEM((half, cols), BF),
            pltpu.VMEM((half, cols), BF),
            dma((2, 3)),
            dma((4, 2)),
            dma((2,)),
            dma((n, 3)),
            dma((n, 3)),
            dma((n,)),
            dma((n,)),
            dma((steps, count, 2)),
            dma((steps, count, 2)),
            dma((count,)),
            dma((count,)),
        ],
        compiler_params=pltpu.CompilerParams(
            collective_id=cid, has_side_effects=True, vmem_limit_bytes=60 * 1024 * 1024
        ),
    )(
        position,
        rows_a.reshape(own, n, CAP, model),
        rows_b.reshape(own, n, CAP, model),
        rows_c.reshape(own, n, CAP, LANES),
        shared_a,
        shared_b,
    )
    return out


def edge_kernel(n, part, slope, rim, total, ahead, mine, from_core, from_chip, edge, send_sem, recv_sem):
    d, m = lax.axis_index("dp"), lax.axis_index("mp")
    core, chip = mp_partners(m)
    before, after = {"dp": (d + n - 1) % n}, {"dp": (d + 1) % n}
    rows, cols = part.shape
    edge_rows, rim_cols = rim.shape
    greet([core, chip, before, after])

    def add(dst, pieces, dtype):
        add_rows(dst, pieces, rows, dtype)

    one = remote(part, from_core, send_sem.at[0], recv_sem.at[0], core)
    one.start()
    one.wait()
    add(mine, [part, from_core], BF)
    two = remote(mine, from_chip, send_sem.at[1], recv_sem.at[1], chip)
    two.start()
    two.wait_recv()
    add(total, [mine, from_chip], F32)
    edge[:, 0:rim_cols] = rim[...]
    edge[:, rim_cols : rim_cols + cols] = total[0:edge_rows, :] * slope[...]
    three = remote(edge, ahead, send_sem.at[2], recv_sem.at[2], before)

    @pl.when(d > 0)
    def _():
        three.start()

    @pl.when(d == n - 1)
    def _():
        ahead[...] = jnp.zeros_like(ahead)

    @pl.when(d < n - 1)
    def _():
        three.wait_recv()

    @pl.when(d > 0)
    def _():
        three.wait_send()

    two.wait_send()


def sum_and_edge(part, slope, rim, cid):
    rows, cols = part.shape
    edge_shape = (rim.shape[0], rim.shape[1] + cols)
    return pl.pallas_call(
        partial(edge_kernel, lax.axis_size("dp")),
        out_shape=[
            jax.ShapeDtypeStruct(part.shape, F32),
            jax.ShapeDtypeStruct(edge_shape, F32),
        ],
        in_specs=[VM] * 3,
        out_specs=[VM] * 2,
        scratch_shapes=[
            pltpu.VMEM((rows, cols), BF),
            pltpu.VMEM((rows, cols), F32),
            pltpu.VMEM((rows, cols), BF),
            pltpu.VMEM(edge_shape, F32),
            pltpu.SemaphoreType.DMA((3,)),
            pltpu.SemaphoreType.DMA((3,)),
        ],
        compiler_params=pltpu.CompilerParams(
            collective_id=cid, has_side_effects=True, vmem_limit_bytes=32 * 1024 * 1024
        ),
    )(part, slope, rim)


def head_pair(pair, first, second):
    lane = lax.broadcasted_iota(jnp.int32, first.shape, 1)
    return jnp.where(lane < LANES // 2, first, second)


def visible_pairs(seg_col, seg_row):
    length = seg_col.shape[0]
    row = lax.broadcasted_iota(jnp.int32, (length, length), 0)
    col = lax.broadcasted_iota(jnp.int32, (length, length), 1)
    return (row >= col) & (seg_col == seg_row)


def state_decay(entry, expand):
    last = entry[entry.shape[0] - 1 :, :]
    spread = jnp.broadcast_to(last, (LANES, LANES)).T
    return dot(expand, spread, ((0,), (0,)), HIGH)


def recur_kernel(
    pairs,
    values,
    write,
    read,
    cumul,
    cumul_t,
    step_t,
    entry,
    tail,
    seg_col,
    seg_row,
    expand,
    skip,
    start,
    out,
    kept,
    state,
):
    @pl.when(pl.program_id(0) == 0)
    def _():
        state[...] = start[...]

    held = state[...]
    kept[0] = held
    v, b, c = values[...], write[...], read[...]
    scores = dot(c, b, ((1,), (1,)), HIGH)
    visible = visible_pairs(seg_col[...], seg_row[...])
    entry_full = dot(entry[...], expand[...], precision=HIGH)
    tail_full = dot(tail[...], expand[...], precision=HIGH)
    carried = entry_full * dot(c, held, ((1,), (1,)), HIGH) + skip[...] * v
    cum, cum_t, st_t = cumul[...], cumul_t[...], step_t[...]
    for pair in range(pairs):
        cols = slice(pair * LANES, (pair + 1) * LANES)
        v2 = v[:, cols]
        found = []
        for h in (2 * pair, 2 * pair + 1):
            spread = jnp.where(visible, cum[:, h : h + 1] - cum_t[h : h + 1, :], MASKED)
            mixing = jnp.exp(spread) * (scores * st_t[h : h + 1, :])
            found.append(dot_three(mixing, v2, (1, 0)))
        out[:, cols] = head_pair(pair, found[0], found[1]) + carried[:, cols]
    state[...] = state_decay(entry[...], expand[...]) * held + dot(v * tail_full, b, ((0,), (0,)), HIGH)


def recur_specs(width, lengths):
    def rows(cols):
        return pl.BlockSpec((BLK, cols), lambda i: (lengths(i), 0))

    def flat(count):
        return pl.BlockSpec((count, BLK), lambda i: (0, lengths(i)))

    def whole(shape):
        return pl.BlockSpec(shape, lambda i: (0,) * len(shape))

    return rows, flat, whole


def recur_forward(v, b, c, cumul, cumul_t, step_t, entry, tail, seg_col, seg_row, expand, skip, start):
    total, width = v.shape
    blocks = total // BLK
    rows, flat, whole = recur_specs(width, lambda i: i)
    return pl.pallas_call(
        partial(recur_kernel, width // LANES),
        grid=(blocks,),
        out_shape=[
            jax.ShapeDtypeStruct((total, width), F32),
            jax.ShapeDtypeStruct((blocks, width, LANES), F32),
        ],
        in_specs=[
            rows(width),
            rows(LANES),
            rows(LANES),
            rows(LANES),
            flat(16),
            flat(16),
            rows(LANES),
            rows(LANES),
            rows(1),
            flat(1),
            whole((LANES, width)),
            whole((1, width)),
            whole((width, LANES)),
        ],
        out_specs=[
            rows(width),
            pl.BlockSpec((1, width, LANES), lambda i: (i, 0, 0)),
        ],
        scratch_shapes=[pltpu.VMEM((width, LANES), F32)],
        compiler_params=pltpu.CompilerParams(vmem_limit_bytes=48 * 1024 * 1024),
    )(v, b, c, cumul, cumul_t, step_t, entry, tail, seg_col, seg_row, expand, skip, start)


def adjoint_kernel(
    pairs,
    values,
    write,
    read,
    cumul,
    cumul_t,
    step_t,
    step,
    entry,
    tail_bare,
    seg_col,
    seg_row,
    expand,
    skip,
    kept,
    d_out,
    start,
    d_values,
    d_write,
    d_read,
    d_step,
    d_rate_step,
    d_skip,
    state,
    columns,
):
    @pl.when(pl.program_id(0) == 0)
    def _():
        state[...] = start[...]
        d_skip[...] = jnp.zeros_like(d_skip)
        columns[...] = jnp.zeros_like(columns)

    length = values.shape[0]
    lam, held = state[...], kept[0]
    v, b, c, dy = values[...], write[...], read[...], d_out[...]
    ex = expand[...]
    st = step[...]
    scores = dot(c, b, ((1,), (1,)), HIGH)
    visible = visible_pairs(seg_col[...], seg_row[...])
    entry_full = dot(entry[...], ex, precision=HIGH)
    tail = tail_bare[...] * st
    tail_full = dot(tail, ex, precision=HIGH)
    c_state = dot(c, held, ((1,), (1,)), HIGH)
    b_lam = dot(b, lam, ((1,), (1,)), HIGH)
    dy_in = dy * entry_full
    v_out = v * tail_full
    dc = dot(dy_in, held, precision=HIGH)
    db = dot(v_out, lam, precision=HIGH)
    reach = dot(dy_in * c_state, ex, ((1,), (1,)), HIGH)
    leave = dot(v * b_lam, ex, ((1,), (1,)), HIGH)
    d_skip[...] += jnp.sum(dy * v, axis=0, keepdims=True)
    dv_far = tail_full * b_lam + skip[...] * dy
    cum, cum_t, st_t = cumul[...], cumul_t[...], step_t[...]
    lane = lax.broadcasted_iota(jnp.int32, (length, LANES), 1)
    d_scores = jnp.zeros((length, length), F32)
    row_sums = jnp.zeros((length, LANES), F32)
    for pair in range(pairs):
        cols = slice(pair * LANES, (pair + 1) * LANES)
        v2, dy2 = v[:, cols], dy[:, cols]
        found = []
        for j in range(2):
            h = 2 * pair + j
            own = (lane < LANES // 2) if j == 0 else (lane >= LANES // 2)
            d_mix = dot_three(jnp.where(own, dy2, 0.0), v2, (1, 1))
            spread = jnp.where(visible, cum[:, h : h + 1] - cum_t[h : h + 1, :], MASKED)
            decay = jnp.exp(spread)
            decay_step = decay * st_t[h : h + 1, :]
            weighted = d_mix * scores * decay
            d_scores = d_scores + d_mix * decay_step
            columns[h : h + 1, :] = jnp.sum(weighted, axis=0, keepdims=True)
            per_row = jnp.sum(weighted * st_t[h : h + 1, :], axis=1, keepdims=True)
            row_sums = jnp.where(lane == h, per_row, row_sums)
            found.append(dot(scores * decay_step, dy2, ((0,), (0,))))
        d_values[:, cols] = head_pair(pair, found[0], found[1]) + dv_far[:, cols]
    d_read[...] = dc + dot(d_scores, b, precision=HIGH)
    d_write[...] = db + dot(d_scores, c, ((0,), (0,)), HIGH)
    col_sums = columns[...].T
    leave_step = tail * leave
    d_step[...] = col_sums + tail_bare[...] * leave
    d_cum = row_sums - st * col_sums + reach - leave_step
    row = lax.broadcasted_iota(jnp.int32, (length, length), 0)
    col = lax.broadcasted_iota(jnp.int32, (length, length), 1)
    upper = (col >= row).astype(F32)
    met = jnp.sum(dot(lam * held, ex, ((0,), (1,)), HIGH), axis=0, keepdims=True)
    at_end = jnp.sum(leave_step, axis=0, keepdims=True) + entry[length - 1 :, :] * met
    d_rate_step[...] = dot(upper, d_cum, precision=HIGH) + at_end
    state[...] = state_decay(entry[...], ex) * lam + dot(dy_in, c, ((0,), (0,)), HIGH)


def recur_backward(
    v, b, c, cumul, cumul_t, step_t, step, entry, tail_bare, seg_col, seg_row, expand, skip, kept, dy, start
):
    total, width = v.shape
    blocks = total // BLK
    rows, flat, whole = recur_specs(width, lambda i: blocks - 1 - i)
    return pl.pallas_call(
        partial(adjoint_kernel, width // LANES),
        grid=(blocks,),
        out_shape=[
            jax.ShapeDtypeStruct((total, width), F32),
            jax.ShapeDtypeStruct((total, LANES), F32),
            jax.ShapeDtypeStruct((total, LANES), F32),
            jax.ShapeDtypeStruct((total, LANES), F32),
            jax.ShapeDtypeStruct((total, LANES), F32),
            jax.ShapeDtypeStruct((1, width), F32),
        ],
        in_specs=[
            rows(width),
            rows(LANES),
            rows(LANES),
            rows(LANES),
            flat(16),
            flat(16),
            rows(LANES),
            rows(LANES),
            rows(LANES),
            rows(1),
            flat(1),
            whole((LANES, width)),
            whole((1, width)),
            pl.BlockSpec((1, width, LANES), lambda i: (blocks - 1 - i, 0, 0)),
            rows(width),
            whole((width, LANES)),
        ],
        out_specs=[
            rows(width),
            rows(LANES),
            rows(LANES),
            rows(LANES),
            rows(LANES),
            whole((1, width)),
        ],
        scratch_shapes=[pltpu.VMEM((width, LANES), F32), pltpu.VMEM((LANES, LANES), F32)],
        compiler_params=pltpu.CompilerParams(vmem_limit_bytes=48 * 1024 * 1024),
    )(v, b, c, cumul, cumul_t, step_t, step, entry, tail_bare, seg_col, seg_row, expand, skip, kept, dy, start)


def state_scan_kernel(n, own, *refs):
    reverse = own == 0
    if reverse:
        mine, decay, expand, out = refs[:4]
        refs = refs[4:]
    else:
        mine, decay, expand, y, small, out, y_rows, position = refs[:8]
        refs = refs[8:]
    first, second, got_first, got_second, half, got_half, send_sem, recv_sem = refs[:8]

    def work(blocks):
        pass

    if not reverse:
        earlier, y_in, y_out, stream_sem = refs[8:]
        slots = SlotWork(own, small, position)
        stream = RowStream(y, y_rows, y_in, y_out, stream_sem.at[0], stream_sem.at[1])
        stream.load(0)

        def work(blocks):
            for b in blocks:
                if b + 1 < n:
                    stream.load(b + 1)
                if b == 0:
                    slots.count_with(earlier)
                    for block in range(n):
                        slots.place(block)
                stream.give(b, b, dot(slots.pick(b), stream.take(b)))

    d = lax.axis_index("dp")
    q = n - 1 - d if reverse else d
    zq, xq = q // 2, q % 2
    depth = n // 2
    rows = mine.shape[0] // 2
    xf = xq.astype(F32)
    sent_type = first.dtype

    def device(logical):
        return {"dp": n - 1 - logical if reverse else logical}

    beside = device(2 * zq + 1 - xq)
    others = [device(2 * ((zq + k) % depth) + xq) for k in range(1, depth)]
    own_rows = pl.ds(pl.multiple_of(rows * xq, 16), rows)
    other_rows = pl.ds(pl.multiple_of(rows * (1 - xq), 16), rows)
    own_lanes = pl.ds(pl.multiple_of(rows * xq, LANES), rows)
    tail = pl.ds(rows, 16)
    body = pl.ds(0, rows)
    row = lax.broadcasted_iota(jnp.int32, (16, LANES), 0)

    def spread(values):
        square = jnp.broadcast_to(values, (LANES, LANES)).T
        return dot(expand[:, own_lanes], square, ((0,), (0,)), HIGH)

    def two_terms(values):
        high = values.astype(sent_type).astype(F32)
        wide = jnp.where(row == 0, high, jnp.where(row == 1, values - high, 0.0))
        return wide.astype(sent_type)

    def one_term(block):
        return block[0:1, :].astype(F32) + block[1:2, :].astype(F32)

    for k in range(1, depth):

        @pl.when(zq < k)
        def _():
            got_second[k - 1] = jnp.zeros(got_second.shape[1:], sent_type)

    own_decay = decay[0:1, :]
    first[body, :] = mine[other_rows, :].astype(sent_type)
    first[tail, :] = two_terms(own_decay)
    greet([beside] + others)
    one = remote(first, got_first, send_sem.at[0], recv_sem.at[0], beside)
    one.start()
    work(range(0, 2))
    one.wait_recv()
    own_part = mine[own_rows, :]
    got, got_decay = got_first[body, :].astype(F32), one_term(got_first[tail, :])
    early = own_part * (1.0 - xf) + got * xf
    early_decay = own_decay * (1.0 - xf) + got_decay * xf
    late = own_part * xf + got * (1.0 - xf)
    late_decay = own_decay * xf + got_decay * (1.0 - xf)
    second[body, :] = (spread(late_decay) * early + late).astype(sent_type)
    second[tail, :] = two_terms(early_decay * late_decay)
    sent = []
    for k in range(1, depth):
        copy = remote(
            second, got_second.at[k - 1], send_sem.at[k], recv_sem.at[k], device(2 * ((zq + k) % depth) + xq)
        )
        sent.append(copy)

        @pl.when(zq + k < depth)
        def _():
            copy.start()

    early_spread = spread(early_decay)
    work(range(2, n - 1))
    total = jnp.zeros((rows, LANES), F32)
    for k in range(depth - 1, 0, -1):

        @pl.when(zq >= k)
        def _():
            sent[k - 1].wait_recv()

        got_k = got_second.at[k - 1]
        total = spread(one_term(got_k[tail, :])) * total + got_k[body, :].astype(F32)
    after = early_spread * total + early
    half[...] = (total * xf + after * (1.0 - xf)).astype(sent_type)
    last = remote(half, got_half, send_sem.at[depth], recv_sem.at[depth], beside)
    last.start()
    out[own_rows, :] = total * (1.0 - xf) + after * xf
    work(range(n - 1, n))
    last.wait_recv()
    out[other_rows, :] = got_half[...].astype(F32)
    one.wait_send()
    last.wait_send()
    for k in range(1, depth):

        @pl.when(zq + k < depth)
        def _():
            sent[k - 1].wait_send()

    if not reverse:
        stream.end()


def state_scan(mine, decay, expand, cid, sent_type, y=None, small=None, own=0):
    n = lax.axis_size("dp")
    half = mine.shape[0] // 2
    depth = n // 2
    message = (half + 16, LANES)
    out_shape, out_specs = [jax.ShapeDtypeStruct(mine.shape, F32)], [VM]
    args, in_specs, more = [mine, decay, expand], [VM] * 3, []
    if own:
        tokens, model = y.shape[1:]
        args += [y, small]
        in_specs += [ANY, VM]
        out_shape += [
            jax.ShapeDtypeStruct((own, n, CAP, model), BF),
            jax.ShapeDtypeStruct((n, own, tokens), F32),
        ]
        out_specs += [ANY, VM]
        more = [
            pltpu.VMEM((tokens, tokens), BF),
            pltpu.VMEM((2, tokens, model), BF),
            pltpu.VMEM((2, own, CAP, model), BF),
            pltpu.SemaphoreType.DMA((2, 2)),
        ]
    return pl.pallas_call(
        partial(state_scan_kernel, n, own),
        out_shape=out_shape,
        in_specs=in_specs,
        out_specs=out_specs,
        scratch_shapes=[
            pltpu.VMEM(message, sent_type),
            pltpu.VMEM(message, sent_type),
            pltpu.VMEM(message, sent_type),
            pltpu.VMEM((depth - 1,) + message, sent_type),
            pltpu.VMEM((half, LANES), sent_type),
            pltpu.VMEM((half, LANES), sent_type),
            pltpu.SemaphoreType.DMA((depth + 1,)),
            pltpu.SemaphoreType.DMA((depth + 1,)),
        ]
        + more,
        compiler_params=pltpu.CompilerParams(
            collective_id=cid, has_side_effects=True, vmem_limit_bytes=48 * 1024 * 1024
        ),
    )(*args)


def pick_matrix(position, own):
    length = position.shape[1]
    slot = lax.broadcasted_iota(jnp.int32, (CAP, length), 0).astype(F32)
    parts = [
        jnp.where(position[e : e + 1, :] == slot, 1.0, 0.0).astype(BF) for e in range(own)
    ]
    return jnp.concatenate(parts, axis=0)


def slot_spec(own, cols):
    return pl.BlockSpec((own, 1, CAP, cols), lambda s: (0, s, 0, 0))


def token_spec(rows, cols):
    return pl.BlockSpec((1, rows, cols), lambda s: (s, 0, 0))


BIG = pltpu.CompilerParams(vmem_limit_bytes=56 * 1024 * 1024)


def expert_kernel(
    own, parts, rows, cot_rows, gate, w_in, w_out, grad_in, grad_out, d_rows, res, dots, wide, both
):
    e, part = pl.program_id(0), pl.program_id(1)
    model = rows.shape[2]
    units = w_out.shape[1]

    @pl.when(part == 0)
    def _():
        wide[...] = w_in[0].astype(F32)
        both[:, 0:units] = wide[pl.ds(0, model, stride=2), :].astype(BF)
        both[:, units : 2 * units] = wide[pl.ds(1, model, stride=2), :].astype(BF)
        if parts > 1:
            grad_in[...] = jnp.zeros_like(grad_in)
            grad_out[...] = jnp.zeros_like(grad_out)

    x, c, g = rows[0], cot_rows[0], gate[0]
    mid = dot(x, both[...])
    mid_gate, mid_up = mid[:, 0:units], mid[:, units : 2 * units]
    sig = jax.nn.sigmoid(mid_gate)
    mid_silu = mid_gate * sig
    act = (mid_silu * mid_up).astype(BF).astype(F32)
    back = dot(c, w_out[0], ((1,), (1,)))
    dot_sum = jnp.sum(act * back, axis=1, keepdims=True)
    lane = lax.broadcasted_iota(jnp.int32, g.shape, 1)
    dots[0] = jnp.where(lane == lax.axis_index("dp") * own + e, dot_sum, 0.0).astype(BF)
    gated = (act * g).astype(BF)
    d_act = back * g
    d_gate = (d_act * mid_up * (sig * (1.0 + mid_gate * (1.0 - sig)))).astype(BF)
    d_mid = jnp.concatenate([d_gate, (d_act * mid_silu).astype(BF)], axis=1)
    grads = dot(x, d_mid, ((0,), (0,)))
    grads_down = dot(gated, c, ((0,), (0,)))
    if parts > 1:
        grad_in[0, pl.ds(0, model, stride=2), :] += grads[:, 0:units]
        grad_in[0, pl.ds(1, model, stride=2), :] += grads[:, units : 2 * units]
        grad_out[0] += grads_down
    else:
        grad_in[0, pl.ds(0, model, stride=2), :] = grads[:, 0:units]
        grad_in[0, pl.ds(1, model, stride=2), :] = grads[:, units : 2 * units]
        grad_out[0] = grads_down
    d_rows[0] = dot(d_mid, both[...], ((1,), (1,))).astype(BF)
    res[0] = dot(gated, w_out[0]).astype(BF)


def run_experts(rows, cot_rows, gate, w_in, w_out):
    own, slots, model = rows.shape
    units = w_out.shape[1]
    part = min(slots, 512)

    def slot(cols):
        return pl.BlockSpec((1, part, cols), lambda e, j: (e, j, 0))

    def weight(a, b):
        return pl.BlockSpec((1, a, b), lambda e, j: (e, 0, 0))

    return pl.pallas_call(
        partial(expert_kernel, own, slots // part),
        grid=(own, slots // part),
        out_shape=[
            jax.ShapeDtypeStruct((own, 2 * model, units), F32),
            jax.ShapeDtypeStruct((own, units, model), F32),
            jax.ShapeDtypeStruct((own, slots, model), BF),
            jax.ShapeDtypeStruct((own, slots, model), BF),
            jax.ShapeDtypeStruct((own, slots, LANES), BF),
        ],
        in_specs=[slot(model), slot(model), slot(LANES), weight(2 * model, units), weight(units, model)],
        out_specs=[weight(2 * model, units), weight(units, model), slot(model), slot(model), slot(LANES)],
        scratch_shapes=[pltpu.VMEM((2 * model, units), F32), pltpu.VMEM((model, 2 * units), BF)],
        compiler_params=BIG,
    )(rows, cot_rows, gate, w_in, w_out)


def put_kernel(own, k, position, *refs):
    out = refs[-1]
    put = pick_matrix(position[0], own)
    here = jnp.where(pl.program_id(0) == lax.axis_index("dp"), 1.0, 0.0)
    start = 0
    for i in range(k):
        rows, shared = refs[2 * i], refs[2 * i + 1]
        cols = shared.shape[1]
        total = dot(put, rows[...].reshape(own * CAP, cols), ((0,), (0,)))
        out[0, :, start : start + cols] = (total + here * shared[...]).astype(BF)
        start += cols
    if len(refs) > 2 * k + 1:
        extra = refs[2 * k]
        out[0, :, start : start + LANES] = dot(
            put, extra[...].reshape(own * CAP, LANES), ((0,), (0,))
        ).astype(BF)


def put_rows(position, parts, extra=None):
    n, own, tokens = position.shape
    args, specs, cols = [], [], 0
    for rows, shared in parts:
        model = shared.shape[1]
        args += [rows.reshape(own, n, CAP, model), shared]
        specs += [slot_spec(own, model), pl.BlockSpec((tokens, model), lambda s: (0, 0))]
        cols += model
    if extra is not None:
        args.append(extra.reshape(own, n, CAP, LANES))
        specs.append(slot_spec(own, LANES))
        cols += LANES
    return pl.pallas_call(
        partial(put_kernel, own, len(parts)),
        grid=(n,),
        out_shape=jax.ShapeDtypeStruct((n, tokens, cols), BF),
        in_specs=[token_spec(own, tokens)] + specs,
        out_specs=token_spec(tokens, cols),
        compiler_params=BIG,
    )(position, *args)


def grads_kernel(k, *refs):
    lefts, rights, out = refs[:k], refs[k : 2 * k], refs[2 * k]
    start = 0
    for left, right in zip(lefts, rights):
        cols = right.shape[1]
        out[:, start : start + cols] = dot(left[...], right[...], ((0,), (0,))).astype(BF)
        start += cols


def weight_grads(pairs):
    k = len(pairs)
    tokens, model = pairs[1][0].shape
    block = 256
    cols = sum(right.shape[1] for _, right in pairs)
    return pl.pallas_call(
        partial(grads_kernel, k),
        grid=(model // block,),
        out_shape=jax.ShapeDtypeStruct((model, cols), BF),
        in_specs=[pl.BlockSpec((tokens, block), lambda i: (0, i)) for _ in pairs]
        + [pl.BlockSpec(right.shape, lambda i: (0, 0)) for _, right in pairs],
        out_specs=pl.BlockSpec((block, cols), lambda i: (i, 0)),
        compiler_params=BIG,
    )(*[left for left, _ in pairs], *[right for _, right in pairs])


def combine_states(states, decays, expand, reverse):
    n = states.shape[0]
    place = lax.axis_index("dp")
    wide = dot(decays, expand, precision=HIGH)
    state = jnp.zeros(states.shape[1:], F32)
    for j in range(n):
        source = n - 1 - j if reverse else j
        use = source > place if reverse else source < place
        fresh = wide[source][:, None] * state + states[source]
        state = jnp.where(use, fresh, state)
    return state


def ring_state(mine, decay, expand, reverse, cid):
    rows = jnp.pad(decay, ((0, 31), (0, 0)))
    (gathered,) = gather_dp([jnp.concatenate([mine, rows], axis=0)], cid)
    width = mine.shape[0]
    return combine_states(gathered[:, :width], gathered[:, width], expand, reverse)


def per_device(
    hidden,
    segment_ids,
    routes,
    norm_gain,
    mixer_in,
    state_in,
    step_in,
    conv_value,
    conv_value_bias,
    conv_state,
    conv_state_bias,
    head_params,
    gated_gain,
    mixer_out,
    ffn_gain,
    router,
    shared_in,
    shared_out,
    expert_in,
    expert_out,
    cotangent,
):
    n = lax.axis_size("dp")
    place, mp_place = lax.axis_index("dp"), lax.axis_index("mp")
    tokens, model = hidden.shape
    shard = model // n
    inner = mixer_in.shape[2]
    state_cols = state_in.shape[1]
    taps = conv_value.shape[0]
    heads = head_params.shape[1]
    width = inner // heads
    own_experts = expert_in.shape[0]
    hidden_units = shared_out.shape[0]
    quarter = tokens // 4

    misc_parts = [
        conv_value.reshape(-1),
        conv_value_bias.reshape(-1),
        gated_gain.reshape(-1),
        conv_state.reshape(-1),
        conv_state_bias,
        norm_gain,
        ffn_gain,
    ]
    misc = jnp.concatenate(misc_parts)
    small = jnp.concatenate(
        [
            jnp.pad(misc, (0, model - misc.shape[0]))[None],
            jnp.pad(routes.T.astype(BF), ((0, 0), (0, model - tokens))),
            hidden[tokens - 15 + TOPK :],
        ],
        axis=0,
    )
    pack_a = jnp.concatenate(
        [
            mixer_in.reshape(shard, 2 * inner),
            state_in,
            jnp.pad(step_in, ((0, 0), (0, LANES - heads))),
        ],
        axis=1,
    )
    pack_b = jnp.concatenate(
        [
            mixer_out.T,
            shared_in.reshape(shard, 2 * hidden_units),
            shared_out.T,
            jnp.pad(router, ((0, 0), (0, LANES - EXPERTS))),
        ],
        axis=1,
    )
    mine_cot = lax.dynamic_slice_in_dim(cotangent, mp_place * quarter, quarter, 0)
    weight_a, small_all, cot_all = first_gather([pack_a, small], cotangent, 0)
    weight_a = weight_a.reshape(model, -1)
    cot_all = cot_all.reshape(n, tokens, model)
    pack_b, small_all = lax.optimization_barrier((pack_b, small_all))
    weight_b = lax.all_gather(pack_b, "dp", axis=0, tiled=True)

    pieces = []
    start = 0
    for part in misc_parts:
        pieces.append(small_all[:, 0, start : start + part.shape[0]].astype(F32))
        start += part.shape[0]
    local_p = conv_value.shape[1]
    value_rows = jnp.concatenate(pieces[:3], axis=1).reshape(n, taps + 2, local_p, heads)
    value_rows = value_rows.transpose(1, 3, 0, 2).reshape(taps + 2, inner)
    state_rows = jnp.concatenate(pieces[3:5], axis=1).reshape(n, taps + 1, state_cols // n)
    state_rows = state_rows.transpose(1, 0, 2).reshape(taps + 1, state_cols)
    gain_first = pieces[5].reshape(1, model)
    gain_second = pieces[6].reshape(1, model)
    conv_taps = jnp.concatenate([value_rows[:taps], state_rows[:taps]], axis=1)
    conv_bias = jnp.concatenate([value_rows[taps], state_rows[taps]])[None]
    gated_row = value_rows[taps + 1][None]

    group_start = place * tokens
    seg_padded = jnp.concatenate([jnp.full((taps - 1,), -1, jnp.int32), segment_ids])
    seg_ext = lax.dynamic_slice_in_dim(seg_padded, group_start, tokens + taps - 1)
    segments = seg_ext[taps - 1 :]
    prev_seg = seg_ext[taps - 2]
    same = [
        (seg_ext[k : k + tokens] == segments).astype(F32)[:, None] for k in range(taps)
    ]
    blocks = tokens // BLK
    seg_blocks = segments.reshape(blocks, BLK)
    last_segs = seg_blocks[:, BLK - 1]
    prev_segs = jnp.concatenate([prev_seg[None], last_segs[:-1]])
    entry_ok = (seg_blocks == prev_segs[:, None]).astype(F32).reshape(tokens, 1)
    tail_ok = (seg_blocks == last_segs[:, None]).astype(F32).reshape(tokens, 1)
    group_entry_ok = (segments == prev_seg).astype(F32)[:, None]
    group_tail_ok = (segments == segments[tokens - 1]).astype(F32)[:, None]
    seg_f = segments.astype(F32)
    seg_col, seg_row = seg_f[:, None], seg_f[None, :]

    behind = lax.dynamic_index_in_dim(small_all, (place + n - 1) % n, 0, False)
    hidden_ext = jnp.concatenate([behind, hidden], axis=0).astype(F32)
    inv_ext = lax.rsqrt(jnp.mean(hidden_ext * hidden_ext, axis=1, keepdims=True) + EPS)
    normed_ext = (hidden_ext * inv_ext * gain_first).astype(BF)
    normed = normed_ext[16:]
    zx_ext = dot(normed_ext, weight_a)
    gate_z = zx_ext[16:, :inner]
    pre_ext = zx_ext[16 - taps + 1 :, inner : 2 * inner + state_cols]
    head_local = head_params.astype(F32)
    dt_lanes = zx_ext[16:, 2 * inner + state_cols :]
    conv = jnp.broadcast_to(conv_bias, (tokens, inner + state_cols))
    for k in range(taps):
        conv = conv + conv_taps[k][None] * pre_ext[k : k + tokens] * same[k]
    act = jax.nn.silu(conv)
    values = act[:, :inner]
    write = act[:, inner : inner + state_cols // 2]
    read = act[:, inner + state_cols // 2 :]

    live = (jnp.arange(LANES) < heads)[None]
    head_pad = jnp.pad(head_local, ((0, 0), (0, LANES - heads)))
    rate = jnp.where(live, -jnp.exp(head_pad[0:1]), 0.0)
    step = jnp.where(live, jax.nn.softplus(dt_lanes + head_pad[1:2]), 0.0)
    rated = (step * rate).reshape(blocks, BLK, LANES)
    lower = jnp.tril(jnp.ones((BLK, BLK), F32))
    cumul_b = jnp.einsum("ts,bsh->bth", lower, rated, precision=HIGH)
    totals = cumul_b[:, BLK - 1]
    zero_row = jnp.zeros((1, LANES), F32)
    before, after = [zero_row], [zero_row]
    for i in range(blocks - 1):
        before.append(before[-1] + totals[i][None])
        after.append(after[-1] + totals[blocks - 1 - i][None])
    before = jnp.stack(before)
    after = jnp.stack(after[::-1])
    cumul = cumul_b.reshape(tokens, LANES)
    to_end = totals[:, None] - cumul_b
    entry = jnp.exp(cumul) * entry_ok
    tail_bare = jnp.exp(to_end).reshape(tokens, LANES) * tail_ok
    tail = tail_bare * step
    group_entry = jnp.exp(cumul_b + before).reshape(tokens, LANES) * group_entry_ok
    group_tail = jnp.exp(to_end + after).reshape(tokens, LANES) * group_tail_ok * step
    cumul_t = cumul[:, :16].T
    step_t = step[:, :16].T
    expand = (jnp.arange(LANES)[:, None] == jnp.arange(inner)[None, :] // width).astype(F32)
    skip = dot(head_pad[2:3], expand, precision=HIGH)
    outgoing = dot(
        values * dot(group_tail, expand, precision=HIGH), write, ((0,), (0,)), HIGH
    )
    group_decay = group_entry[tokens - 1 :]
    if n == 8:
        incoming, cot_rows, position = state_scan(
            outgoing, jnp.broadcast_to(group_decay, (8, LANES)), expand, 1, F32, cot_all, small_all, own_experts
        )
    else:
        incoming = ring_state(outgoing, group_decay, expand, False, 1)
        cot_rows, position = slots_of(cot_all, small_all, own_experts)
    ssd, kept = recur_forward(
        values, write, read, cumul, cumul_t, step_t, entry, tail, seg_col, seg_row, expand, skip, incoming
    )

    gate_act = jax.nn.silu(gate_z)
    gated = ssd * gate_act
    scaled = (gated * gated_row).astype(BF)
    unit_first = hidden_ext[16:] * inv_ext[16:]
    mine_unit = lax.dynamic_slice_in_dim(unit_first, mp_place * quarter, quarter, 0)
    entry_wide = dot(group_entry, expand, precision=HIGH)
    unit_first, mine_unit, entry_wide, weight_b = lax.optimization_barrier(
        (unit_first, mine_unit, entry_wide, weight_b)
    )
    out_t = weight_b[:, :inner]
    router_w = weight_b[:, inner + 3 * hidden_units :]
    proj_part = dot(scaled, out_t, ((1,), (1,)))
    square_part = jnp.sum(gated * gated, axis=1, keepdims=True)
    proj_pack = jnp.concatenate([proj_part, jnp.broadcast_to(square_part, (tokens, LANES))], axis=1)
    proj_sum = scatter_mp(proj_pack.reshape(4, quarter, -1), 2)
    proj = proj_sum[:, :model]
    square = proj_sum[:, model : model + 1]
    inv_gated = lax.rsqrt(square / DI + EPS)
    mine_hidden = lax.dynamic_slice_in_dim(hidden, mp_place * quarter, quarter, 0).astype(F32)
    mixed = mine_hidden + proj * inv_gated
    inv_second = lax.rsqrt(jnp.mean(mixed * mixed, axis=1, keepdims=True) + EPS)
    unit_second = mixed * inv_second
    ffn_mine = (unit_second * gain_second).astype(BF)

    first_expert = place * own_experts
    (
        _,
        rows,
        gates,
        slot_gates,
        ffn_block,
        shared_act,
        d_shared_mid,
        shared_res,
        d_ffn_shared,
    ) = gather_tokens(ffn_mine, position, small_all, weight_b, cotangent, hidden_units, 3)

    slots = n * CAP
    grad_in_rows, grad_expert_out, d_rows, expert_res, slot_dots = run_experts(
        rows.reshape(own_experts, slots, model),
        cot_rows.reshape(own_experts, slots, model),
        slot_gates.reshape(own_experts, slots, LANES),
        expert_in.reshape(own_experts, 2 * model, -1),
        expert_out,
    )
    grad_expert_in = grad_in_rows.reshape(expert_in.shape)

    if n > 8:
        d_ffn_pack = put_rows(position, [(d_rows, d_ffn_shared)], slot_dots)
        d_ffn_sum = scatter_tokens(d_ffn_pack.reshape(n, 4, quarter, -1), 4)
        expert_res, d_ffn_sum = lax.optimization_barrier((expert_res, d_ffn_sum))
        res_pack = put_rows(position, [(expert_res, shared_res)])
        res_sum = scatter_tokens(res_pack.reshape(n, 4, quarter, model), 10)
    else:
        both_sums = put_scatter(position, expert_res, d_rows, slot_dots, shared_res, d_ffn_shared, 4)
        res_sum, d_ffn_sum = both_sums[:, :model], both_sums[:, model:]

    own_tokens_gates = lax.dynamic_slice(
        gates, (place, mp_place * quarter, 0), (1, quarter, LANES)
    ).reshape(quarter, LANES)
    dots = d_ffn_sum[:, model : model + LANES]
    share = jnp.sum(own_tokens_gates * dots, axis=1, keepdims=True)
    d_logits = (own_tokens_gates * (dots - share)).astype(BF)
    d_ffn = d_ffn_sum[:, :model] + dot(d_logits, router_w, ((1,), (1,)))
    mine_cot_f = mine_cot.astype(F32)
    grad_gain_second = jnp.sum(d_ffn * unit_second, axis=0)
    d_unit = d_ffn * gain_second
    d_mixed = mine_cot_f + inv_second * (
        d_unit - unit_second * jnp.mean(d_unit * unit_second, axis=1, keepdims=True)
    )
    d_proj_mine = (d_mixed * inv_gated).astype(BF)
    d_inv = jnp.sum(d_mixed * proj, axis=1, keepdims=True)
    d_square = d_inv * -0.5 * inv_gated * inv_gated * inv_gated / DI
    d_square_high = d_square.astype(BF)
    d_square_low = (d_square - d_square_high.astype(F32)).astype(BF)
    sent = jnp.concatenate(
        [
            d_proj_mine,
            d_logits[:, :EXPERTS],
            d_square_high,
            d_square_low,
            jnp.zeros((quarter, LANES - EXPERTS - 2), BF),
        ],
        axis=1,
    )
    (got,) = gather_mp([sent], 5)
    got = got.reshape(tokens, model + LANES)
    d_proj = got[:, :model]
    d_logits_all = jnp.pad(got[:, model : model + EXPERTS], ((0, 0), (0, LANES - EXPERTS)))
    d_square_all = got[:, model + EXPERTS : model + EXPERTS + 1].astype(F32) + got[
        :, model + EXPERTS + 1 : model + EXPERTS + 2
    ].astype(F32)

    rows0 = ((0,), (0,))
    grad_b = weight_grads(
        [
            (got, scaled),
            (ffn_block, d_shared_mid),
            (cotangent, shared_act),
            (ffn_block, d_logits_all),
        ]
    )
    grad_b, got = lax.optimization_barrier((grad_b, got))
    d_proj = got[:, :model]
    sum_b = lax.psum_scatter(grad_b, "dp", scatter_dimension=0, tiled=True)
    d_scaled = dot(d_proj, out_t)
    grad_gated_row = jnp.sum(d_scaled * gated, axis=0)
    d_gated = d_scaled * gated_row + 2.0 * gated * d_square_all
    d_ssd = d_gated * gate_act
    d_gate_z = d_gated * ssd * silu_slope(gate_z)

    direct = dot(d_ssd * entry_wide, read, rows0, HIGH)
    if n == 8:
        (state_grad,) = state_scan(direct, jnp.broadcast_to(group_decay, (8, LANES)), expand, 6, BF)
    else:
        state_grad = ring_state(direct, group_decay, expand, True, 6)
    d_values, d_write, d_read, d_step, d_rated, d_skip_row = recur_backward(
        values,
        write,
        read,
        cumul,
        cumul_t,
        step_t,
        step,
        entry,
        tail_bare,
        seg_col,
        seg_row,
        expand,
        skip,
        kept,
        d_ssd,
        state_grad,
    )
    d_rate = jnp.sum(d_rated * step, axis=0, keepdims=True)
    d_dt = jnp.where(
        live, (d_step + rate * d_rated) * jax.nn.sigmoid(dt_lanes + head_pad[1:2]), 0.0
    )
    d_skip = dot(d_skip_row, expand, ((1,), (1,)), HIGH)
    grad_head = jnp.concatenate(
        [d_rate * rate, jnp.sum(d_dt, axis=0, keepdims=True), d_skip], axis=0
    )[:, :heads]

    slope = silu_slope(conv)
    d_conv_values = d_values * slope[:, :inner]
    d_state_act, rim_ahead = sum_and_edge(
        jnp.concatenate([d_write, d_read], axis=1), slope[:16, inner:], d_conv_values[:16], 11
    )
    d_conv = jnp.concatenate([d_conv_values, d_state_act * slope[:, inner:]], axis=1)
    d_conv_ext = jnp.concatenate([d_conv, rim_ahead], axis=0)
    seg_after = lax.dynamic_slice_in_dim(
        jnp.concatenate([segment_ids, jnp.full((taps - 1,), -1, jnp.int32)]),
        group_start,
        tokens + taps - 1,
    )
    d_pre = jnp.zeros_like(d_conv)
    grad_rows = []
    for k in range(taps):
        ahead = taps - 1 - k
        ok = (seg_after[ahead : ahead + tokens] == segments).astype(F32)[:, None]
        d_pre = d_pre + conv_taps[k][None] * d_conv_ext[ahead : ahead + tokens] * ok
        grad_rows.append(jnp.sum(d_conv * pre_ext[k : k + tokens] * same[k], axis=0))
    grad_rows.append(jnp.sum(d_conv, axis=0))
    d_a = jnp.concatenate([d_gate_z, d_pre, d_dt], axis=1).astype(BF)

    d_state_mine = lax.dynamic_slice_in_dim(
        d_a[:, 2 * inner : 2 * inner + state_cols], mp_place * quarter, quarter, 0
    )
    d_normed_part = dot(d_a[:, : 2 * inner], weight_a[:, : 2 * inner], ((1,), (1,))) + dot(
        d_a[:, 2 * inner + state_cols :], weight_a[:, 2 * inner + state_cols :], ((1,), (1,))
    )
    d_state_rows = dot(
        d_state_mine, weight_a[:, 2 * inner : 2 * inner + state_cols], ((1,), (1,))
    )
    grad_a = dot(normed, d_a, rows0).astype(BF)
    grad_gain_first = jnp.sum(d_normed_part * unit_first, axis=0) + jnp.sum(
        d_state_rows * mine_unit, axis=0
    )

    value_grads = jnp.stack([g[:inner] for g in grad_rows] + [grad_gated_row])
    value_grads = value_grads.reshape(taps + 2, heads, n, local_p).transpose(2, 0, 3, 1)
    state_grads = jnp.stack([g[inner:] for g in grad_rows])
    state_grads = state_grads.reshape(taps + 1, n, state_cols // n).transpose(1, 0, 2)
    misc_grads = [
        value_grads.reshape(n, -1),
        state_grads.reshape(n, -1),
        jnp.broadcast_to(grad_head.reshape(1, -1), (n, 3 * heads)),
    ]
    sizes = [g.shape[1] for g in misc_grads]
    misc_grads = jnp.concatenate(misc_grads, axis=1)
    misc_grads = jnp.pad(misc_grads, ((0, 0), (0, 32 * LANES - misc_grads.shape[1])))
    gains = jnp.concatenate(
        [grad_gain_first.reshape(n, shard), grad_gain_second.reshape(n, shard)], axis=1
    )
    gains = jnp.pad(gains, ((0, 0), (0, 16 * LANES - 2 * shard)))
    mine_result = (mixed + res_sum).astype(BF)
    sum_zx, sum_state, sum_dt, misc_sum, gains_sum, hidden_all, result = last_exchange(
        grad_a.reshape(n, shard, -1),
        misc_grads.reshape(n, 32, LANES),
        gains.reshape(n, 16, LANES),
        d_normed_part.astype(BF).reshape(4, quarter, model),
        d_state_rows,
        d_mixed,
        mine_hidden,
        gain_first,
        mine_result,
        (2 * inner, state_cols, LANES),
        8,
    )
    result = result.reshape(tokens, model)
    misc_sum = misc_sum.reshape(-1)
    gains_sum = gains_sum.reshape(-1)
    cut = [0]
    for size in sizes:
        cut.append(cut[-1] + size)
    value_sum = misc_sum[: cut[1]].reshape(taps + 2, local_p, heads)
    state_sum = misc_sum[cut[1] : cut[2]].reshape(taps + 1, state_cols // n)
    head_sum = misc_sum[cut[2] : cut[3]].reshape(3, heads)

    b1, b2 = inner, inner + 2 * hidden_units
    b3 = b2 + hidden_units
    return (
        result,
        hidden_all.reshape(tokens, model).astype(F32),
        gains_sum[:shard],
        sum_zx.reshape(shard, 2, inner),
        sum_state,
        sum_dt[:, :heads],
        value_sum[:taps],
        value_sum[taps],
        state_sum[:taps],
        state_sum[taps],
        head_sum,
        value_sum[taps + 1],
        sum_b[:, :b1].T.astype(F32),
        gains_sum[shard : 2 * shard],
        sum_b[:, b3 : b3 + EXPERTS].astype(F32),
        sum_b[:, b1:b2].reshape(shard, 2, hidden_units).astype(F32),
        sum_b[:, b2:b3].T.astype(F32),
        grad_expert_in,
        grad_expert_out,
    )


def solution(mesh):
    placed = (
        P("dp", None),
        P(),
        P("dp", None),
        P("dp"),
        P("dp", None, "mp"),
        P("dp", None),
        P("dp", "mp"),
        P(None, "dp", "mp"),
        P("dp", "mp"),
        P(None, "dp"),
        P("dp"),
        P(None, "mp"),
        P("dp", "mp"),
        P("mp", "dp"),
        P("dp"),
        P("dp", None),
        P("dp", None, "mp"),
        P("mp", "dp"),
        P("dp", None, None, "mp"),
        P("dp", "mp", None),
        P("dp", None),
    )
    return jax.shard_map(
        per_device,
        mesh=mesh,
        in_specs=placed,
        out_specs=(
            P("dp", None),
            P("dp", None),
            P("dp"),
            P("dp", None, "mp"),
            P("dp", None),
            P("dp", "mp"),
            P(None, "dp", "mp"),
            P("dp", "mp"),
            P(None, "dp"),
            P("dp"),
            P(None, "mp"),
            P("dp", "mp"),
            P("mp", "dp"),
            P("dp"),
            P("dp", None),
            P("dp", None, "mp"),
            P("mp", "dp"),
            P("dp", None, None, "mp"),
            P("dp", "mp", None),
        ),
        check_vma=False,
    )
```

```python
from functools import partial

import jax
import jax.numpy as jnp
from jax import lax
from jax.experimental import pallas as pl
from jax.experimental.pallas import tpu as pltpu
from jax.sharding import PartitionSpec as P

MESH = pl.DeviceIdType.MESH
BLK = 128
EXPERTS = 64
TOPK = 6
DI = 3072
CAP = 64
LANES = 128

EPS = 1e-05
HIGH = lax.Precision.HIGHEST
MASKED = -1e30
BF = jnp.bfloat16
F32 = jnp.float32
ANY = pl.BlockSpec(memory_space=pl.ANY)
VM = pl.BlockSpec(memory_space=pltpu.VMEM)


def dot(a, b, dims=((1,), (0,)), precision=None):
    return lax.dot_general(
        a, b, (dims, ((), ())), precision=precision, preferred_element_type=F32
    )


def two_parts(a):
    high = a.astype(BF)
    return high, (a - high.astype(F32)).astype(BF)


def dot_three(a, b, over):
    a_high, a_low = two_parts(a)
    b_high, b_low = two_parts(b)
    left = jnp.concatenate([a_high, a_low, a_high], axis=over[0])
    right = jnp.concatenate([b_high, b_high, b_low], axis=over[1])
    return dot(left, right, ((over[0],), (over[1],)))


def silu_slope(argument):
    sigmoid_val = jax.nn.sigmoid(argument)
    return sigmoid_val * (1.0 + argument * (1.0 - sigmoid_val))


def chunk_rows(start, size):
    return [(start + i, min(32, size - i)) for i in range(0, size, 32)]


def ring_place(n, d):
    high, low = d // 2, d % 2
    return high * (1 - low) + (n - 1 - high) * low


def ring_device(n, p):
    back = p // (n // 2)
    return (2 * p) * (1 - back) + (2 * (n - 1 - p) + 1) * back


def greet(targets):
    barrier = pltpu.get_barrier_semaphore()
    for target in targets:
        pl.semaphore_signal(barrier, inc=1, device_id=target, device_id_type=MESH)
    pl.semaphore_wait(barrier, len(targets))


def remote(src, dst, send, recv, target):
    return pltpu.make_async_remote_copy(
        src_ref=src,
        dst_ref=dst,
        send_sem=send,
        recv_sem=recv,
        device_id=target,
        device_id_type=MESH,
    )


def mp_partners(m):
    return {"mp": m + 1 - 2 * (m % 2)}, {"mp": (m + 2) % 4}


def ring_neighbours(n):
    p = ring_place(n, lax.axis_index("dp"))
    nxt = {"dp": ring_device(n, (p + 1) % n)}
    prv = {"dp": ring_device(n, (p + n - 1) % n)}
    return p, nxt, prv


class RingGather:
    def __init__(self, n, ins, outs, sems):
        self.n, self.ins, self.outs = n, ins, outs
        self.local_sem, self.send_sem, self.recv_sem = sems
        self.p, self.nxt, self.prv = ring_neighbours(n)
        self.copies = {}

    @staticmethod
    def scratch(n, arrays):
        dma = pltpu.SemaphoreType.DMA
        most = max(len(chunk_rows(0, a.shape[0])) for a in arrays)
        shape = (n // 2, len(arrays), most, 2)
        return [dma((len(arrays),)), dma(shape), dma(shape)]

    def begin(self):
        d = lax.axis_index("dp")
        self.local = []
        for j, (a, out) in enumerate(zip(self.ins, self.outs)):
            copy = pltpu.make_async_copy(a, out.at[d], self.local_sem.at[j])
            copy.start()
            self.local.append(copy)

    def step(self, s):
        n, p = self.n, self.p
        for j, (a, out) in enumerate(zip(self.ins, self.outs)):
            for i, (start, rows) in enumerate(chunk_rows(0, a.shape[0])):
                part = pl.ds(start, rows)
                for way in range(2):
                    origin = ring_device(n, (p + n - s) % n if way == 0 else (p + s) % n)
                    if (s - 1, j, i, way) in self.copies:
                        self.copies[s - 1, j, i, way].wait_recv()
                    if s + 1 < n // 2 or (s + 1 == n // 2 and i % 2 == way):
                        copy = remote(
                            a.at[part] if s == 0 else out.at[origin, part],
                            out.at[origin, part],
                            self.send_sem.at[s, j, i, way],
                            self.recv_sem.at[s, j, i, way],
                            self.nxt if way == 0 else self.prv,
                        )
                        copy.start()
                        self.copies[s, j, i, way] = copy

    def end(self):
        for copy in self.copies.values():
            copy.wait_send()
        for copy in self.local:
            copy.wait()


def gather_kernel(n, k, *refs):
    ring = RingGather(n, refs[:k], refs[k : 2 * k], refs[2 * k :])
    greet([ring.nxt, ring.prv])
    ring.begin()
    for s in range(n // 2 + 1):
        ring.step(s)
    ring.end()


def gather_dp(arrays, cid):
    n, k = lax.axis_size("dp"), len(arrays)
    return pl.pallas_call(
        partial(gather_kernel, n, k),
        out_shape=[jax.ShapeDtypeStruct((n,) + a.shape, a.dtype) for a in arrays],
        in_specs=[ANY] * k,
        out_specs=[ANY] * k,
        scratch_shapes=RingGather.scratch(n, arrays),
        compiler_params=pltpu.CompilerParams(collective_id=cid, has_side_effects=True),
    )(*arrays)


def add_rows(dst, pieces, rows, dtype):
    def body(i, carry):
        sl = pl.ds(pl.multiple_of(i * 16, 16), 16)
        total = pieces[0][sl, :].astype(F32)
        for piece in pieces[1:]:
            total = total + piece[sl, :].astype(F32)
        dst[sl, :] = total.astype(dtype)
        return carry

    lax.fori_loop(0, rows // 16, body, 0)


class RingScatter:
    def __init__(self, n, ins, outs, slots, sems):
        self.n, self.ins, self.outs, self.slots = n, ins, outs, slots
        self.send_sem, self.recv_sem = sems
        self.p, self.nxt, self.prv = ring_neighbours(n)
        self.copies = {}

    @staticmethod
    def scratch(n, arrays):
        most = max(len(chunk_rows(0, a.shape[1])) for a in arrays)
        shape = (n // 2, len(arrays), most, 2)
        return [pltpu.VMEM((n // 2, 2) + a.shape[1:], a.dtype) for a in arrays] + [
            pltpu.SemaphoreType.DMA(shape),
            pltpu.SemaphoreType.DMA(shape),
        ]

    def step(self, s, j):
        n, p = self.n, self.p
        array, out, slots = self.ins[j], self.outs[j], self.slots[j]
        for i, (start, size) in enumerate(chunk_rows(0, array.shape[1])):
            part = pl.ds(start, size)
            if s == n // 2:
                for way in range(2):
                    self.copies[s - 1, j, i, way].wait_recv()
                start_col = 0
                for ref in out:
                    cols = pl.ds(start_col, ref.shape[1])
                    start_col += ref.shape[1]
                    pieces = [array.at[ring_device(n, p), part, cols]]
                    pieces += [slots.at[s - 1, way, part, cols] for way in range(2)]
                    add_rows(ref.at[part], pieces, size, F32)
                continue
            for way in range(2):
                if s == 0 and i % 2 != way:
                    continue
                away = n // 2 - s
                block = ring_device(n, (p + away) % n if way == 0 else (p + n - away) % n)
                source = array.at[block, part]
                if (s - 1, j, i, way) in self.copies:
                    self.copies[s - 1, j, i, way].wait_recv()
                    held = slots.at[s - 1, way, part]
                    add_rows(held, [held, source], size, array.dtype)
                    source = held
                copy = remote(
                    source,
                    slots.at[s, way, part],
                    self.send_sem.at[s, j, i, way],
                    self.recv_sem.at[s, j, i, way],
                    self.nxt if way == 0 else self.prv,
                )
                copy.start()
                self.copies[s, j, i, way] = copy

    def end(self):
        for copy in self.copies.values():
            copy.wait_send()


def last_kernel(
    n,
    grad_a,
    misc,
    gains,
    d_normed,
    extra,
    d_mixed,
    hidden,
    gain,
    result,
    out_zx,
    out_state,
    out_dt,
    out_misc,
    out_gains,
    all_hidden,
    all_result,
    gains_mine,
    gains_core,
    gains_chip,
    rows_core,
    rows_chip,
    rows_bf,
    slots_a,
    slots_misc,
    slots_gains,
    ring_send,
    ring_recv,
    mp_send,
    mp_recv,
    local_sem,
):
    m = lax.axis_index("mp")
    core, chip = mp_partners(m)
    far = (m + 2) % 4
    beside = m + 1 - 2 * (m % 2)
    ring = RingScatter(
        n,
        [grad_a, misc, gains_mine],
        [(out_zx, out_state, out_dt), (out_misc,), (out_gains,)],
        [slots_a, slots_misc, slots_gains],
        [ring_send, ring_recv],
    )
    greet([core, chip, ring.nxt, ring.prv])
    sent = []

    def over_mp(i, source, target, device):
        copy = remote(source, target, mp_send.at[i], mp_recv.at[i], device)
        copy.start()
        sent.append(copy)
        return copy

    ring.step(0, 0)
    ring.step(0, 1)
    gains_one = over_mp(0, gains, gains_core, core)
    rows_far = over_mp(1, d_normed.at[(beside + 2) % 4], rows_core.at[1], core)
    rows_near = over_mp(2, d_normed.at[beside], rows_core.at[0], core)
    own_result = pltpu.make_async_copy(result, all_result.at[m], local_sem.at[0])
    own_result.start()
    gains_one.wait_recv()
    for b in range(n):
        add_rows(gains_mine.at[b], [gains.at[b], gains_core.at[b]], 16, F32)
    gains_two = over_mp(3, gains_mine, gains_chip, chip)
    count = d_mixed.shape[0]
    rows_far.wait_recv()
    add_rows(rows_core.at[1], [rows_core.at[1], d_normed.at[far]], count, BF)
    rows_two = over_mp(4, rows_core.at[1], rows_chip, chip)
    result_chip = over_mp(5, result, all_result.at[m], chip)
    result_core = over_mp(6, result, all_result.at[m], core)
    ring.step(1, 0)
    ring.step(1, 1)
    gains_two.wait()
    for b in range(n):
        add_rows(gains_mine.at[b], [gains_mine.at[b], gains_chip.at[b]], 16, F32)
    ring.step(0, 2)
    rows_near.wait_recv()
    rows_two.wait_recv()

    def body(i, carry):
        sl = pl.ds(pl.multiple_of(i * 16, 16), 16)
        d_n = d_normed[m, sl, :].astype(F32) + rows_core[0, sl, :].astype(F32)
        d_n = d_n + rows_chip[sl, :].astype(F32) + extra[sl, :]
        x = hidden[sl, :].astype(F32)
        inv = lax.rsqrt(jnp.mean(x * x, axis=1, keepdims=True) + EPS)
        unit = x * inv
        d_unit = d_n * gain[...]
        mean = jnp.mean(d_unit * unit, axis=1, keepdims=True)
        rows_bf[sl, :] = (d_mixed[sl, :] + inv * (d_unit - unit * mean)).astype(BF)
        return carry

    lax.fori_loop(0, count // 16, body, 0)
    own_hidden = pltpu.make_async_copy(rows_bf, all_hidden.at[m], local_sem.at[1])
    own_hidden.start()
    hidden_chip = over_mp(7, rows_bf, all_hidden.at[m], chip)
    hidden_core = over_mp(8, rows_bf, all_hidden.at[m], core)
    arrive = []
    for s in range(2, n // 2 + 1):
        ring.step(s, 0)
        ring.step(s, 1)
        ring.step(s - 1, 2)
        if s == 2:
            result_chip.wait_recv()
            arrive.append(over_mp(9, all_result.at[far], all_result.at[far], core))
        if s == n // 2 - 1:
            hidden_chip.wait_recv()
            arrive.append(over_mp(10, all_hidden.at[far], all_hidden.at[far], core))
    ring.step(n // 2, 2)
    for copy in [result_core, hidden_core] + arrive:
        copy.wait_recv()
    own_result.wait()
    own_hidden.wait()
    for copy in sent:
        if copy is not gains_two:
            copy.wait_send()
    ring.end()


def last_exchange(grad_a, misc, gains, d_normed, extra, d_mixed, hidden, gain, result, cols, cid):
    n = lax.axis_size("dp")
    shard = grad_a.shape[1]
    rows, model = d_mixed.shape
    dma = pltpu.SemaphoreType.DMA
    every = jax.ShapeDtypeStruct((4, rows, model), BF)
    return pl.pallas_call(
        partial(last_kernel, n),
        out_shape=[jax.ShapeDtypeStruct((shard, c), F32) for c in cols]
        + [jax.ShapeDtypeStruct(a.shape[1:], F32) for a in (misc, gains)]
        + [every, every],
        in_specs=[VM] * 8 + [ANY],
        out_specs=[VM] * 5 + [ANY] * 2,
        scratch_shapes=[
            pltpu.VMEM(gains.shape, F32),
            pltpu.VMEM(gains.shape, F32),
            pltpu.VMEM(gains.shape, F32),
            pltpu.VMEM((2, rows, model), BF),
            pltpu.VMEM((rows, model), BF),
            pltpu.VMEM((rows, model), BF),
        ]
        + RingScatter.scratch(n, [grad_a, misc, gains])
        + [dma((11,)), dma((11,)), dma((2,))],
        compiler_params=pltpu.CompilerParams(
            collective_id=cid, has_side_effects=True, vmem_limit_bytes=56 * 1024 * 1024
        ),
    )(grad_a, misc, gains, d_normed, extra, d_mixed, hidden, gain, result)


def mp_scatter_kernel(x, out, from_core, from_chip, send_sem, recv_sem):
    m = lax.axis_index("mp")
    core, chip = mp_partners(m)
    mine, far = m, (m + 2) % 4
    beside = m + 1 - 2 * (m % 2)
    parts = [(pl.ds(start, size), size) for start, size in chunk_rows(0, out.shape[0])]
    greet([core, chip])
    first, last = [], []
    for slot, block in ((1, (beside + 2) % 4), (0, beside)):
        for i, (part, _) in enumerate(parts):
            copy = remote(
                x.at[block, part], from_core.at[slot, part], send_sem.at[slot, i], recv_sem.at[slot, i], core
            )
            copy.start()
            first.append(copy)
    for i, (part, size) in enumerate(parts):
        first[i].wait_recv()
        held = from_core.at[1, part]
        add_rows(held, [held, x.at[far, part]], size, x.dtype)
        copy = remote(held, from_chip.at[part], send_sem.at[2, i], recv_sem.at[2, i], chip)
        copy.start()
        last.append(copy)
    for i, (part, size) in enumerate(parts):
        first[len(parts) + i].wait_recv()
        last[i].wait_recv()
        add_rows(out.at[part], [x.at[mine, part], from_core.at[0, part], from_chip.at[part]], size, F32)
    for copy in first + last:
        copy.wait_send()


def scatter_mp(x, cid):
    rows, cols = x.shape[1:]
    count = len(chunk_rows(0, rows))
    return pl.pallas_call(
        mp_scatter_kernel,
        out_shape=jax.ShapeDtypeStruct((rows, cols), F32),
        in_specs=[VM],
        out_specs=VM,
        scratch_shapes=[
            pltpu.VMEM((2, rows, cols), x.dtype),
            pltpu.VMEM((rows, cols), x.dtype),
            pltpu.SemaphoreType.DMA((3, count)),
            pltpu.SemaphoreType.DMA((3, count)),
        ],
        compiler_params=pltpu.CompilerParams(
            collective_id=cid, has_side_effects=True, vmem_limit_bytes=32 * 1024 * 1024
        ),
    )(x)


def mp_gather_kernel(k, *refs):
    ins, outs = refs[:k], refs[k : 2 * k]
    local_sem, send_sem, recv_sem = refs[2 * k :]
    m = lax.axis_index("mp")
    core, chip = mp_partners(m)
    far = (m + 2) % 4
    greet([core, chip])
    copies, local, arrive = [], [], []
    for j in range(k):
        to_chip = remote(ins[j], outs[j].at[m], send_sem.at[0, j], recv_sem.at[0, j], chip)
        to_chip.start()
        to_core = remote(ins[j], outs[j].at[m], send_sem.at[1, j], recv_sem.at[1, j], core)
        to_core.start()
        own = pltpu.make_async_copy(ins[j], outs[j].at[m], local_sem.at[j])
        own.start()
        copies += [to_chip, to_core]
        arrive.append(to_chip)
        local.append(own)
    onward = []
    for j in range(k):
        arrive[j].wait_recv()
        copy = remote(outs[j].at[far], outs[j].at[far], send_sem.at[2, j], recv_sem.at[2, j], core)
        copy.start()
        onward.append(copy)
    for j in range(k):
        copies[2 * j + 1].wait_recv()
        onward[j].wait_recv()
        local[j].wait()
    for copy in copies + onward:
        copy.wait_send()


def gather_mp(arrays, cid):
    k = len(arrays)
    return pl.pallas_call(
        partial(mp_gather_kernel, k),
        out_shape=[jax.ShapeDtypeStruct((4,) + a.shape, a.dtype) for a in arrays],
        in_specs=[ANY] * k,
        out_specs=[ANY] * k,
        scratch_shapes=[
            pltpu.SemaphoreType.DMA((k,)),
            pltpu.SemaphoreType.DMA((3, k)),
            pltpu.SemaphoreType.DMA((3, k)),
        ],
        compiler_params=pltpu.CompilerParams(collective_id=cid, has_side_effects=True),
    )(*arrays)


class TokenGather:
    def __init__(self, n, both, x, out, sems):
        self.n, self.both, self.out = n, both, out
        self.local, self.ring_s, self.ring_r, self.core_s, self.core_r, self.chip_s, self.chip_r = sems
        self.d, self.m = lax.axis_index("dp"), lax.axis_index("mp")
        self.far = (self.m + 2) % 4
        self.core, self.chip = mp_partners(self.m)
        self.p, self.nxt, self.prv = ring_neighbours(n)
        rows = out.shape[2]
        base = pl.multiple_of(self.m * rows, rows) if x.shape[0] > rows else 0
        self.x = x.at[pl.ds(base, rows)]
        self.pieces = [(0,) + c for c in chunk_rows(0, both) + chunk_rows(both, rows - both)]
        self.pieces += [(1,) + c for c in chunk_rows(0, both)]
        self.sent, self.pending = [], {}
        self.ring, self.chips = {}, {}

    @staticmethod
    def scratch(n, rows, both):
        dma = pltpu.SemaphoreType.DMA
        far = len(chunk_rows(0, both))
        own = far + len(chunk_rows(both, rows - both))
        steps = n // 2
        return [
            dma((3,)),
            dma((steps, own + far, 2)),
            dma((steps, own + far, 2)),
            dma((steps + 1, 2 * own + far, 2)),
            dma((steps + 1, 2 * own + far, 2)),
            dma((steps + 1, own, 2)),
            dma((steps + 1, own, 2)),
        ]

    def send(self, source, place, s_sem, r_sem, target):
        copy = remote(source, place, s_sem, r_sem, target)
        copy.start()
        self.sent.append(copy)
        return copy

    def begin(self):
        own = self.out.at[self.d, self.m]
        self.load = pltpu.make_async_copy(self.x, own, self.local.at[0])
        self.load.start()
        self.first = None
        if self.both:
            part = pl.ds(0, self.both)
            self.first = remote(
                self.x.at[part], own.at[part], self.local.at[1], self.local.at[2], self.chip
            )
            self.first.start()
            self.sent.append(self.first)

    def step(self, s, between=None):
        n, p = self.n, self.p
        for k, (is_far, start, rows) in enumerate(self.pieces):
            if k > 0 and between is not None:
                between()
            for way in range(2):
                origin = ring_device(n, (p + n - s) % n if way == 0 else (p + s) % n)
                place = self.far if is_far else self.m
                region = self.out.at[origin, place, pl.ds(start, rows)]
                source = region if s > 0 or is_far else self.x.at[pl.ds(start, rows)]
                if (s - 1, k, way) in self.ring:
                    self.ring[s - 1, k, way].wait_recv()
                elif s > 0:
                    continue
                elif is_far and self.first is not None:
                    self.first.wait_recv()
                    self.first = None
                if s + 1 < n // 2 or (s + 1 == n // 2 and k % 2 == way):
                    self.ring[s, k, way] = self.send(
                        source,
                        region,
                        self.ring_s.at[s, k, way],
                        self.ring_r.at[s, k, way],
                        self.nxt if way == 0 else self.prv,
                    )
                if s == 0 and way == 1:
                    continue
                self.pending.setdefault(s, []).append(
                    self.send(source, region, self.core_s.at[s, k, way], self.core_r.at[s, k, way], self.core)
                )
                if not is_far and start >= self.both:
                    self.chips[s, k, way] = (
                        self.send(
                            source, region, self.chip_s.at[s, k, way], self.chip_r.at[s, k, way], self.chip
                        ),
                        self.out.at[origin, self.far, pl.ds(start, rows)],
                    )

    def pass_on(self, s):
        total = len(self.pieces)
        for k in range(total):
            for way in range(2):
                if (s, k, way) in self.chips:
                    copy, region = self.chips[s, k, way]
                    copy.wait_recv()
                    at = (s, total + k, way)
                    self.pending.setdefault(s, []).append(
                        self.send(region, region, self.core_s.at[at], self.core_r.at[at], self.core)
                    )

    def blocks(self, s):
        n, p = self.n, self.p
        if s in (0, n // 2):
            return [ring_device(n, (p + s) % n)]
        return [ring_device(n, (p + n - s) % n), ring_device(n, (p + s) % n)]

    def complete(self, s):
        if s == 0:
            self.load.wait()
        for copy in self.pending.pop(s):
            copy.wait_recv()

    def end(self):
        for s in sorted(self.pending):
            self.complete(s)
        for copy in self.sent:
            copy.wait_send()


class SlotWork:
    def __init__(self, own, small, position):
        self.own, self.small, self.position = own, small, position
        self.first = (lax.axis_index("dp") * own).astype(F32)
        self.length = position.shape[2]

    def count_with(self, earlier):
        self.earlier = earlier
        row = lax.broadcasted_iota(jnp.int32, earlier.shape, 0)
        col = lax.broadcasted_iota(jnp.int32, earlier.shape, 1)
        earlier[...] = jnp.where(row < col, 1.0, 0.0).astype(BF)

    def gate_with(self, router, gates, slot_gates):
        self.router, self.gates, self.slot_gates = router, gates, slot_gates

    def named(self, block, first, count):
        length = self.length
        routes = self.small[block, :, 0:length].astype(F32)
        expert = lax.broadcasted_iota(jnp.int32, (count, length), 0).astype(F32) + first
        found = routes[1:2, :] == expert
        for k in range(2, TOPK + 1):
            found = found | (routes[k : k + 1, :] == expert)
        return found

    def place(self, block):
        named = self.named(block, self.first, 8)
        count = dot(jnp.where(named, 1.0, 0.0).astype(BF), self.earlier[...])
        self.position[block] = jnp.where(named, count, -1.0)[0 : self.own, :]

    def pick(self, block):
        return pick_matrix(self.position[block], self.own)

    def gate(self, block, rows, pick):
        own = self.own
        logits = dot(rows, self.router[...])
        named = jnp.where(self.named(block, 0.0, LANES), 1.0, 0.0).T > 0.5
        top = jnp.max(jnp.where(named, logits, MASKED), axis=1, keepdims=True)
        powers = jnp.where(named, jnp.exp(jnp.minimum(logits - top, 0.0)), 0.0)
        gate = powers / jnp.sum(powers, axis=1, keepdims=True)
        self.gates[block] = gate
        of_slot = dot(pick, jnp.concatenate(two_parts(gate), axis=1))
        of_slot = of_slot[:, 0:LANES] + of_slot[:, LANES : 2 * LANES]
        row = lax.broadcasted_iota(jnp.int32, of_slot.shape, 0)
        col = lax.broadcasted_iota(jnp.int32, of_slot.shape, 1)
        mine = col - lax.axis_index("dp") * own == row // CAP
        of_slot = jnp.sum(jnp.where(mine, of_slot, 0.0), axis=1, keepdims=True)
        of_slot = jnp.broadcast_to(of_slot, (own * CAP, LANES)).reshape(own, CAP, LANES)
        for e in range(own):
            self.slot_gates[e, block] = of_slot[e]


class RowStream:
    def __init__(self, source, target, in_buf, out_buf, load_sem, store_sem):
        self.source, self.target, self.in_buf, self.out_buf = source, target, in_buf, out_buf
        self.load_sem, self.store_sem = load_sem, store_sem
        self.loads, self.stores = [], []

    def load(self, block):
        at = len(self.loads) % self.in_buf.shape[0]
        copy = pltpu.make_async_copy(self.source.at[block], self.in_buf.at[at], self.load_sem.at[at])
        copy.start()
        self.loads.append(copy)

    def take(self, i, wait=True):
        if wait:
            self.loads[i].wait()
        held = self.in_buf[i % self.in_buf.shape[0]]
        return held.reshape(-1, held.shape[-1])

    def give(self, i, block, picked):
        if i > 1:
            self.stores[i - 2].wait()
        self.out_buf[i % 2] = picked.astype(BF).reshape(self.out_buf.shape[1:])
        copy = pltpu.make_async_copy(
            self.out_buf.at[i % 2], self.target.at[:, block], self.store_sem.at[i % 2]
        )
        copy.start()
        self.stores.append(copy)

    def end(self):
        for copy in self.stores[-2:]:
            copy.wait()


def token_gather_kernel(
    n,
    both,
    own,
    units,
    x,
    position,
    small,
    weights,
    cot,
    out,
    x_rows,
    gates,
    slot_gates,
    block,
    act,
    d_mid,
    shared_res,
    shared_d,
    x_in,
    x_out,
    mid,
    stream_sem,
    *sems,
):
    inner = weights.shape[1] - 3 * units - LANES
    shared_in = pl.ds(inner, 2 * units)
    shared_out = pl.ds(inner + 2 * units, units)
    router = weights.at[:, pl.ds(inner + 3 * units, LANES)]
    gather = TokenGather(n, both, x, out, sems)
    work = SlotWork(own, small, position)
    work.gate_with(router, gates, slot_gates)
    x_stream = RowStream(out, x_rows, x_in, x_out, stream_sem.at[0], stream_sem.at[1])
    half = n // 2
    greet([gather.core, gather.chip, gather.nxt, gather.prv])
    gather.begin()
    tasks = []

    def shared(held):
        def first():
            block[...] = x_stream.take(held["at"])
            mid[...] = dot(block[...], weights[:, shared_in])

        def second():
            gate, up = mid[:, 0:units], mid[:, units : 2 * units]
            sig = jax.nn.sigmoid(gate)
            silu = gate * sig
            act[...] = (silu * up).astype(BF)
            d_act = dot(cot[...], weights[:, shared_out])
            slope = sig * (1.0 + gate * (1.0 - sig))
            d_mid[:, 0:units] = (d_act * up * slope).astype(BF)
            d_mid[:, units : 2 * units] = (d_act * silu).astype(BF)

        def third():
            shared_res[...] = dot(act[...], weights[:, shared_out], ((1,), (1,)))

        def fourth():
            shared_d[...] = dot(d_mid[...], weights[:, shared_in], ((1,), (1,)))

        return [first, second, third, fourth]

    def pick_x(s):
        blocks = gather.blocks(s)
        held = {}

        def start():
            gather.complete(s)
            held["at"] = len(x_stream.loads)
            for block in blocks:
                x_stream.load(block)

        found = [start]
        if s == 0:
            found += shared(held)
        for i, block in enumerate(blocks):

            def pick(i=i, block=block):
                held[i] = work.pick(block)
                rows = x_stream.take(held["at"] + i, s > 0)
                x_stream.give(held["at"] + i, block, dot(held[i], rows))

            def gate(i=i, block=block):
                work.gate(block, x_stream.take(held["at"] + i, False), held[i])

            found += [pick, gate]
        return found

    def between():
        for _ in range(1 if len(tasks) < 6 else 2):
            if tasks:
                tasks.pop(0)()

    gather.step(0)
    for s in range(1, half + 1):
        gather.step(s, between)
        gather.pass_on(s - 1)
        tasks += pick_x(s - 1)
    final = pick_x(half)
    while len(tasks) > 4:
        tasks.pop(0)()
    gather.pass_on(half)
    tasks.pop(0)()
    tasks.pop(0)()
    final.pop(0)()
    for task in tasks + final:
        task()
    gather.end()
    x_stream.end()


def gather_tokens(x, position, small, weights, cot, units, cid):
    n, own, tokens = position.shape
    quarter, model = x.shape
    both = quarter // 128 * 48
    return pl.pallas_call(
        partial(token_gather_kernel, n, both, own, units),
        out_shape=[
            jax.ShapeDtypeStruct((n, 4) + x.shape, x.dtype),
            jax.ShapeDtypeStruct((own, n, CAP, model), BF),
            jax.ShapeDtypeStruct((n, tokens, LANES), F32),
            jax.ShapeDtypeStruct((own, n, CAP, LANES), F32),
            jax.ShapeDtypeStruct((tokens, model), BF),
            jax.ShapeDtypeStruct((tokens, units), BF),
            jax.ShapeDtypeStruct((tokens, 2 * units), BF),
            jax.ShapeDtypeStruct((tokens, model), F32),
            jax.ShapeDtypeStruct((tokens, model), F32),
        ],
        in_specs=[ANY, VM, VM, VM, VM],
        out_specs=[ANY, ANY] + [VM] * 7,
        scratch_shapes=[
            pltpu.VMEM((3, 4, quarter, model), BF),
            pltpu.VMEM((2, own, CAP, model), BF),
            pltpu.VMEM((tokens, 2 * units), F32),
            pltpu.SemaphoreType.DMA((2, 3)),
        ]
        + TokenGather.scratch(n, quarter, both),
        compiler_params=pltpu.CompilerParams(
            collective_id=cid, has_side_effects=True, vmem_limit_bytes=56 * 1024 * 1024
        ),
    )(x, position, small, weights, cot)


def slots_kernel(own, y, small, y_rows, position, earlier):
    work = SlotWork(own, small, position)
    work.count_with(earlier)
    work.place(0)
    y_rows[...] = dot(work.pick(0), y[0]).astype(BF).reshape(y_rows.shape)


def slots_of(y, small, own):
    n, tokens, model = y.shape
    return pl.pallas_call(
        partial(slots_kernel, own),
        grid=(n,),
        out_shape=[
            jax.ShapeDtypeStruct((own, n, CAP, model), BF),
            jax.ShapeDtypeStruct((n, own, tokens), F32),
        ],
        in_specs=[token_spec(tokens, model), token_spec(small.shape[1], small.shape[2])],
        out_specs=[slot_spec(own, model), token_spec(own, tokens)],
        scratch_shapes=[pltpu.VMEM((tokens, tokens), BF)],
        compiler_params=BIG,
    )(y, small)


def first_kernel(n, k, *refs):
    ins, x = refs[:k], refs[k]
    outs, x_out = refs[k + 1 : 2 * k + 1], refs[2 * k + 1]
    ring = RingGather(n, ins, outs, refs[2 * k + 2 : 2 * k + 5])
    gather = TokenGather(n, 0, x, x_out, refs[2 * k + 5 :])
    greet([gather.core, gather.chip, gather.nxt, gather.prv])
    ring.begin()
    gather.begin()
    for s in range(n // 2 + 1):
        gather.step(s)
        ring.step(s)
        if s > 0:
            gather.pass_on(s - 1)
    gather.pass_on(n // 2)
    gather.end()
    ring.end()


def first_gather(arrays, x, cid):
    n, k = lax.axis_size("dp"), len(arrays)
    rows, cols = x.shape[0] // 4, x.shape[1]
    return pl.pallas_call(
        partial(first_kernel, n, k),
        out_shape=[jax.ShapeDtypeStruct((n,) + a.shape, a.dtype) for a in arrays]
        + [jax.ShapeDtypeStruct((n, 4, rows, cols), x.dtype)],
        in_specs=[ANY] * (k + 1),
        out_specs=[ANY] * (k + 1),
        scratch_shapes=RingGather.scratch(n, arrays) + TokenGather.scratch(n, rows, 0),
        compiler_params=pltpu.CompilerParams(collective_id=cid, has_side_effects=True),
    )(*arrays, x)


def token_scatter_kernel(
    n,
    x,
    out,
    from_core,
    slots,
    loads,
    far_loads,
    from_chip,
    to_chip,
    first,
    done,
    last_buf,
    load_sem,
    far_sem,
    core_send,
    core_recv,
    chip_send,
    chip_recv,
    send_sem,
    recv_sem,
    last_send,
    last_recv,
):
    m = lax.axis_index("mp")
    c, y = m % 2, m // 2
    core, chip = mp_partners(m)
    far = (m + 2) % 4
    beside = m + 1 - 2 * c
    p, nxt, prv = ring_neighbours(n)
    rows = out.shape[0]
    half, steps = rows // 2, n // 2
    greet([core, chip, nxt, prv])

    def block_of(i):
        s = (i + 1) // 2
        return ring_device(n, (p + steps - s) % n if i % 2 or i == 0 else (p + n - steps + s) % n)

    over, sent, loading, chips = {}, [], {}, {}
    loaded, summed = set(), set()
    upper, lower, whole = pl.ds(half, half), pl.ds(0, half), pl.ds(0, rows)

    def core_sends(i):
        if i >= n:
            return
        block = block_of(i)
        moves = [((beside + 2) % 4, 1 - y, upper), (beside, y, whole), ((beside + 2) % 4, 1 - y, lower)]
        for k, (theirs, piece, part) in enumerate(moves):
            copy = remote(
                x.at[block, theirs, part],
                from_core.at[block, piece, part],
                core_send.at[i, k],
                core_recv.at[i, k],
                core,
            )
            copy.start()
            over[i, k] = copy
            sent.append(copy)

    def start_pair(name, source, other, target, sems):
        loading[name] = []
        for k, ref in enumerate((source, other)):
            copy = pltpu.make_async_copy(ref, target.at[k], sems.at[k])
            copy.start()
            loading[name].append(copy)

    def load(i):
        if i >= n:
            return
        block = block_of(i)
        at = i % 4
        over[i, 1].wait_recv()
        start_pair(
            (i, 0), x.at[block, m], from_core.at[block, y], loads.at[at, :, whole], load_sem.at[at, 0]
        )
        over[i, 2].wait_recv()
        start_pair(
            (i, 1),
            x.at[block, far, lower],
            from_core.at[block, 1 - y, lower],
            loads.at[at, :, pl.ds(rows, half)],
            load_sem.at[at, 1],
        )

    def load_far(i):
        if i >= n:
            return
        block = block_of(i)
        over[i, 0].wait_recv()
        start_pair(
            (i, 2),
            x.at[block, far, upper],
            from_core.at[block, 1 - y, upper],
            far_loads.at[i % 2],
            far_sem.at[i % 2],
        )

    def to_other_chip(i):
        if i >= n:
            return
        for copy in loading[i, 2]:
            copy.wait()
        if i > 1:
            chips[i - 2].wait_send()
        add_rows(to_chip.at[i % 2], [far_loads.at[i % 2, 0], far_loads.at[i % 2, 1]], half, BF)
        copy = remote(to_chip.at[i % 2], from_chip.at[i], chip_send.at[i], chip_recv.at[i], chip)
        copy.start()
        chips[i] = copy

    chunks = chunk_rows(0, rows + half)
    count = len(chunks)
    order = [k for k in range(count) if chunks[k][0] >= rows]
    order += [k for k in range(count) if chunks[k][0] < rows]

    def pieces_of(i, k):
        start, size = chunks[k]
        area = pl.ds(start, size)
        if i not in loaded:
            loaded.add(i)
            for copy in loading[i, 0] + loading[i, 1]:
                copy.wait()
        found = [loads.at[i % 4, 0, area], loads.at[i % 4, 1, area]]
        if half <= start < rows:
            if i not in summed:
                summed.add(i)
                chips[i].wait_recv()
            found.append(from_chip.at[i, pl.ds(start - half, size)])
        return found

    for i in range(3):
        core_sends(i)
    load_far(0)
    load(0)
    load_far(1)
    to_other_chip(0)
    load_far(2)
    to_other_chip(1)
    core_sends(3)
    core_sends(4)
    load(1)
    to_other_chip(2)
    load(2)
    ring = {}
    for s in range(steps):
        for k, way in [(k, way) for k in order for way in range(2) if s > 0 or k % 2 == way]:
            start, size = chunks[k]
            area = pl.ds(start, size)
            if s == 0:
                target, pieces = first.at[area], pieces_of(0, k)
            else:
                target, pieces = slots.at[s - 1, way, area], pieces_of(2 * s - 1 + way, k)
                if (s - 1, k, way) in ring:
                    ring[s - 1, k, way].wait_recv()
                    pieces.append(target)
            add_rows(target, pieces, size, BF)
            copy = remote(
                target,
                slots.at[s, way, area],
                send_sem.at[s, k, way],
                recv_sem.at[s, k, way],
                nxt if way == 0 else prv,
            )
            copy.start()
            ring[s, k, way] = copy
        for i in (2 * s + 3, 2 * s + 4):
            load_far(i)
            core_sends(i + 2)
            to_other_chip(i)
            load(i)
    last = []
    for k in order:
        start, size = chunks[k]
        area = pl.ds(start, size)
        pieces = pieces_of(n - 1, k)
        for way in range(2):
            ring[steps - 1, k, way].wait_recv()
            pieces.append(slots.at[steps - 1, way, area])
        if start < rows:
            add_rows(out.at[area], pieces, size, F32)
            continue
        at = pl.ds(start - rows, size)
        add_rows(done.at[at], pieces, size, BF)
        copy = remote(done.at[at], last_buf.at[at], last_send.at[k], last_recv.at[k], chip)
        copy.start()
        last.append(copy)
    for copy in last:
        copy.wait_recv()
    add_rows(out.at[lower], [out.at[lower], last_buf], half, F32)
    for copy in sent + list(ring.values()) + last + [chips[n - 2], chips[n - 1]]:
        copy.wait_send()


def scatter_tokens(x, cid):
    n, _, rows, cols = x.shape
    half, steps = rows // 2, n // 2
    count = len(chunk_rows(0, rows + half))
    dma = pltpu.SemaphoreType.DMA
    out, _ = pl.pallas_call(
        partial(token_scatter_kernel, n),
        out_shape=[
            jax.ShapeDtypeStruct((rows, cols), F32),
            jax.ShapeDtypeStruct((n, 2, rows, cols), BF),
        ],
        in_specs=[ANY],
        out_specs=[VM, ANY],
        scratch_shapes=[
            pltpu.VMEM((steps, 2, rows + half, cols), BF),
            pltpu.VMEM((4, 2, rows + half, cols), BF),
            pltpu.VMEM((2, 2, half, cols), BF),
            pltpu.VMEM((n, half, cols), BF),
            pltpu.VMEM((2, half, cols), BF),
            pltpu.VMEM((rows + half, cols), BF),
            pltpu.VMEM((half, cols), BF),
            pltpu.VMEM((half, cols), BF),
            dma((4, 2, 2)),
            dma((2, 2)),
            dma((n, 3)),
            dma((n, 3)),
            dma((n,)),
            dma((n,)),
            dma((steps, count, 2)),
            dma((steps, count, 2)),
            dma((count,)),
            dma((count,)),
        ],
        compiler_params=pltpu.CompilerParams(
            collective_id=cid, has_side_effects=True, vmem_limit_bytes=56 * 1024 * 1024
        ),
    )(x)
    return out


def put_scatter_kernel(
    n,
    own,
    position,
    slot_a,
    slot_b,
    slot_c,
    shared_a,
    shared_b,
    out,
    from_core,
    made,
    in_a,
    in_b,
    in_c,
    slots,
    loads,
    far_loads,
    from_chip,
    to_chip,
    first,
    done,
    last_buf,
    slot_sem,
    load_sem,
    far_sem,
    core_send,
    core_recv,
    chip_send,
    chip_recv,
    send_sem,
    recv_sem,
    last_send,
    last_recv,
):
    m = lax.axis_index("mp")
    c, y = m % 2, m // 2
    core, chip = mp_partners(m)
    far = (m + 2) % 4
    beside = m + 1 - 2 * c
    p, nxt, prv = ring_neighbours(n)
    rows = out.shape[0]
    model = shared_a.shape[1]
    half, steps = rows // 2, n // 2

    def block_of(i):
        s = (i + 1) // 2
        return ring_device(n, (p + steps - s) % n if i % 2 or i == 0 else (p + n - steps + s) % n)

    over, sent, loading, chips, arriving = {}, [], {}, {}, {}
    loaded, summed = set(), set()
    upper, lower, whole = pl.ds(half, half), pl.ds(0, half), pl.ds(0, rows)

    def slot_load(i):
        if i >= n:
            return
        arriving[i] = []
        for k, (source, target) in enumerate(((slot_a, in_a), (slot_b, in_b), (slot_c, in_c))):
            copy = pltpu.make_async_copy(source.at[:, block_of(i)], target.at[i % 2], slot_sem.at[i % 2, k])
            copy.start()
            arriving[i].append(copy)

    def make(i):
        if i >= n:
            return
        slot_load(i + 1)
        if i >= 4:
            for k in range(3):
                over[i - 4, k].wait_send()
        pick = pick_matrix(position[block_of(i)], own)
        for copy in arriving[i]:
            copy.wait()
        start = 0
        for target, shared in ((in_a, shared_a), (in_b, shared_b), (in_c, None)):
            cols = target.shape[3]
            total = dot(pick, target[i % 2].reshape(own * CAP, cols), ((0,), (0,)))
            if i == n - 1 and shared is not None:
                total = total + shared[...]
            made[i % 4, :, :, start : start + cols] = total.astype(BF).reshape(4, rows, cols)
            start += cols

    def core_sends(i):
        if i >= n:
            return
        block = block_of(i)
        moves = [((beside + 2) % 4, 1 - y, upper), (beside, y, whole), ((beside + 2) % 4, 1 - y, lower)]
        for k, (theirs, piece, part) in enumerate(moves):
            copy = remote(
                made.at[i % 4, theirs, part],
                from_core.at[block, piece, part],
                core_send.at[i, k],
                core_recv.at[i, k],
                core,
            )
            copy.start()
            over[i, k] = copy
            if i >= n - 4:
                sent.append(copy)

    def load(i):
        if i >= n:
            return
        block = block_of(i)
        loading[i] = []
        for k, (piece, part, at) in enumerate(((y, whole, 0), (1 - y, lower, rows))):
            over[i, k + 1].wait_recv()
            copy = pltpu.make_async_copy(
                from_core.at[block, piece, part],
                loads.at[i % 4, pl.ds(at, rows if k == 0 else half)],
                load_sem.at[i % 4, k],
            )
            copy.start()
            loading[i].append(copy)

    def to_other_chip(i):
        if i >= n:
            return
        over[i, 0].wait_recv()
        copy = pltpu.make_async_copy(
            from_core.at[block_of(i), 1 - y, upper], far_loads.at[i % 2], far_sem.at[i % 2]
        )
        copy.start()
        load(i)
        if i > 1:
            chips[i - 2].wait_send()
        copy.wait()
        add_rows(to_chip.at[i % 2], [far_loads.at[i % 2], made.at[i % 4, far, upper]], half, BF)
        copy = remote(to_chip.at[i % 2], from_chip.at[i], chip_send.at[i], chip_recv.at[i], chip)
        copy.start()
        chips[i] = copy

    chunks = chunk_rows(0, rows + half)
    order = [k for k in range(len(chunks)) if chunks[k][0] >= rows]
    order += [k for k in range(len(chunks)) if chunks[k][0] < rows]

    def pieces_of(i, k):
        start, size = chunks[k]
        area = pl.ds(start, size)
        if i not in loaded:
            loaded.add(i)
            for copy in loading[i]:
                copy.wait()
        found = [loads.at[i % 4, area]]
        if start < rows:
            found.append(made.at[i % 4, m, area])
        else:
            found.append(made.at[i % 4, far, pl.ds(start - rows, size)])
        if half <= start < rows:
            if i not in summed:
                summed.add(i)
                chips[i].wait_recv()
            found.append(from_chip.at[i, pl.ds(start - half, size)])
        return found

    slot_load(0)
    make(0)
    greet([core, chip, nxt, prv])
    core_sends(0)
    make(1)
    core_sends(1)
    to_other_chip(0)
    ring = {}
    for s in range(steps):
        for k, way in [(k, way) for k in order for way in range(2) if s > 0 or k % 2 == way]:
            start, size = chunks[k]
            area = pl.ds(start, size)
            if s == 0:
                if start == half:
                    make(2)
                    core_sends(2)
                target, pieces = first.at[area], pieces_of(0, k)
            else:
                target, pieces = slots.at[s - 1, way, area], pieces_of(2 * s - 1 + way, k)
                if (s - 1, k, way) in ring:
                    ring[s - 1, k, way].wait_recv()
                    pieces.append(target)
            add_rows(target, pieces, size, BF)
            copy = remote(
                target,
                slots.at[s, way, area],
                send_sem.at[s, k, way],
                recv_sem.at[s, k, way],
                nxt if way == 0 else prv,
            )
            copy.start()
            ring[s, k, way] = copy
        if s == 0:
            to_other_chip(1)
            to_other_chip(2)
        for i in (2 * s + 3, 2 * s + 4):
            make(i)
            core_sends(i)
        for i in (2 * s + 3, 2 * s + 4):
            to_other_chip(i)
    last = []
    for k in order:
        start, size = chunks[k]
        area = pl.ds(start, size)
        pieces = pieces_of(n - 1, k)
        for way in range(2):
            ring[steps - 1, k, way].wait_recv()
            pieces.append(slots.at[steps - 1, way, area])
        if start < rows:
            add_rows(out.at[area], pieces, size, F32)
            continue
        at = pl.ds(start - rows, size)
        add_rows(done.at[at], pieces, size, BF)
        copy = remote(done.at[at], last_buf.at[at], last_send.at[k], last_recv.at[k], chip)
        copy.start()
        last.append(copy)
    for copy in last:
        copy.wait_recv()
    add_rows(out.at[lower], [out.at[lower], last_buf], half, F32)
    for copy in sent + list(ring.values()) + last + [chips[n - 2], chips[n - 1]]:
        copy.wait_send()


def put_scatter(position, rows_a, rows_b, rows_c, shared_a, shared_b, cid):
    n, own, tokens = position.shape
    model = shared_a.shape[1]
    quarter = tokens // 4
    cols = 2 * model + LANES
    half, steps = quarter // 2, n // 2
    count = len(chunk_rows(0, quarter + half))
    dma = pltpu.SemaphoreType.DMA
    out, _ = pl.pallas_call(
        partial(put_scatter_kernel, n, own),
        out_shape=[
            jax.ShapeDtypeStruct((quarter, cols), F32),
            jax.ShapeDtypeStruct((n, 2, quarter, cols), BF),
        ],
        in_specs=[VM, ANY, ANY, ANY, VM, VM],
        out_specs=[VM, ANY],
        scratch_shapes=[
            pltpu.VMEM((4, 4, quarter, cols), BF),
            pltpu.VMEM((2, own, CAP, model), BF),
            pltpu.VMEM((2, own, CAP, model), BF),
            pltpu.VMEM((2, own, CAP, LANES), BF),
            pltpu.VMEM((steps, 2, quarter + half, cols), BF),
            pltpu.VMEM((4, quarter + half, cols), BF),
            pltpu.VMEM((2, half, cols), BF),
            pltpu.VMEM((n, half, cols), BF),
            pltpu.VMEM((2, half, cols), BF),
            pltpu.VMEM((quarter + half, cols), BF),
            pltpu.VMEM((half, cols), BF),
            pltpu.VMEM((half, cols), BF),
            dma((2, 3)),
            dma((4, 2)),
            dma((2,)),
            dma((n, 3)),
            dma((n, 3)),
            dma((n,)),
            dma((n,)),
            dma((steps, count, 2)),
            dma((steps, count, 2)),
            dma((count,)),
            dma((count,)),
        ],
        compiler_params=pltpu.CompilerParams(
            collective_id=cid, has_side_effects=True, vmem_limit_bytes=60 * 1024 * 1024
        ),
    )(
        position,
        rows_a.reshape(own, n, CAP, model),
        rows_b.reshape(own, n, CAP, model),
        rows_c.reshape(own, n, CAP, LANES),
        shared_a,
        shared_b,
    )
    return out


def edge_kernel(n, part, slope, rim, total, ahead, mine, from_core, from_chip, edge, send_sem, recv_sem):
    d, m = lax.axis_index("dp"), lax.axis_index("mp")
    core, chip = mp_partners(m)
    before, after = {"dp": (d + n - 1) % n}, {"dp": (d + 1) % n}
    rows, cols = part.shape
    edge_rows, rim_cols = rim.shape
    greet([core, chip, before, after])

    def add(dst, pieces, dtype):
        add_rows(dst, pieces, rows, dtype)

    one = remote(part, from_core, send_sem.at[0], recv_sem.at[0], core)
    one.start()
    one.wait()
    add(mine, [part, from_core], BF)
    two = remote(mine, from_chip, send_sem.at[1], recv_sem.at[1], chip)
    two.start()
    two.wait_recv()
    add(total, [mine, from_chip], F32)
    edge[:, 0:rim_cols] = rim[...]
    edge[:, rim_cols : rim_cols + cols] = total[0:edge_rows, :] * slope[...]
    three = remote(edge, ahead, send_sem.at[2], recv_sem.at[2], before)

    @pl.when(d > 0)
    def _():
        three.start()

    @pl.when(d == n - 1)
    def _():
        ahead[...] = jnp.zeros_like(ahead)

    @pl.when(d < n - 1)
    def _():
        three.wait_recv()

    @pl.when(d > 0)
    def _():
        three.wait_send()

    two.wait_send()


def sum_and_edge(part, slope, rim, cid):
    rows, cols = part.shape
    edge_shape = (rim.shape[0], rim.shape[1] + cols)
    return pl.pallas_call(
        partial(edge_kernel, lax.axis_size("dp")),
        out_shape=[
            jax.ShapeDtypeStruct(part.shape, F32),
            jax.ShapeDtypeStruct(edge_shape, F32),
        ],
        in_specs=[VM] * 3,
        out_specs=[VM] * 2,
        scratch_shapes=[
            pltpu.VMEM((rows, cols), BF),
            pltpu.VMEM((rows, cols), F32),
            pltpu.VMEM((rows, cols), BF),
            pltpu.VMEM(edge_shape, F32),
            pltpu.SemaphoreType.DMA((3,)),
            pltpu.SemaphoreType.DMA((3,)),
        ],
        compiler_params=pltpu.CompilerParams(
            collective_id=cid, has_side_effects=True, vmem_limit_bytes=32 * 1024 * 1024
        ),
    )(part, slope, rim)


def head_pair(pair, first, second):
    lane = lax.broadcasted_iota(jnp.int32, first.shape, 1)
    return jnp.where(lane < LANES // 2, first, second)


def visible_pairs(seg_col, seg_row):
    length = seg_col.shape[0]
    row = lax.broadcasted_iota(jnp.int32, (length, length), 0)
    col = lax.broadcasted_iota(jnp.int32, (length, length), 1)
    return (row >= col) & (seg_col == seg_row)


def state_decay(entry, expand):
    last = entry[entry.shape[0] - 1 :, :]
    spread = jnp.broadcast_to(last, (LANES, LANES)).T
    return dot(expand, spread, ((0,), (0,)), HIGH)


def recur_kernel(
    pairs,
    values,
    write,
    read,
    cumul,
    cumul_t,
    step_t,
    entry,
    tail,
    seg_col,
    seg_row,
    expand,
    skip,
    start,
    out,
    kept,
    state,
):
    @pl.when(pl.program_id(0) == 0)
    def _():
        state[...] = start[...]

    held = state[...]
    kept[0] = held
    v, b, c = values[...], write[...], read[...]
    scores = dot(c, b, ((1,), (1,)), HIGH)
    visible = visible_pairs(seg_col[...], seg_row[...])
    entry_full = dot(entry[...], expand[...], precision=HIGH)
    tail_full = dot(tail[...], expand[...], precision=HIGH)
    carried = entry_full * dot(c, held, ((1,), (1,)), HIGH) + skip[...] * v
    cum, cum_t, st_t = cumul[...], cumul_t[...], step_t[...]
    for pair in range(pairs):
        cols = slice(pair * LANES, (pair + 1) * LANES)
        v2 = v[:, cols]
        found = []
        for h in (2 * pair, 2 * pair + 1):
            spread = jnp.where(visible, cum[:, h : h + 1] - cum_t[h : h + 1, :], MASKED)
            mixing = jnp.exp(spread) * (scores * st_t[h : h + 1, :])
            found.append(dot_three(mixing, v2, (1, 0)))
        out[:, cols] = head_pair(pair, found[0], found[1]) + carried[:, cols]
    state[...] = state_decay(entry[...], expand[...]) * held + dot(v * tail_full, b, ((0,), (0,)), HIGH)


def recur_specs(width, lengths):
    def rows(cols):
        return pl.BlockSpec((BLK, cols), lambda i: (lengths(i), 0))

    def flat(count):
        return pl.BlockSpec((count, BLK), lambda i: (0, lengths(i)))

    def whole(shape):
        return pl.BlockSpec(shape, lambda i: (0,) * len(shape))

    return rows, flat, whole


def recur_forward(v, b, c, cumul, cumul_t, step_t, entry, tail, seg_col, seg_row, expand, skip, start):
    total, width = v.shape
    blocks = total // BLK
    rows, flat, whole = recur_specs(width, lambda i: i)
    return pl.pallas_call(
        partial(recur_kernel, width // LANES),
        grid=(blocks,),
        out_shape=[
            jax.ShapeDtypeStruct((total, width), F32),
            jax.ShapeDtypeStruct((blocks, width, LANES), F32),
        ],
        in_specs=[
            rows(width),
            rows(LANES),
            rows(LANES),
            rows(LANES),
            flat(16),
            flat(16),
            rows(LANES),
            rows(LANES),
            rows(1),
            flat(1),
            whole((LANES, width)),
            whole((1, width)),
            whole((width, LANES)),
        ],
        out_specs=[
            rows(width),
            pl.BlockSpec((1, width, LANES), lambda i: (i, 0, 0)),
        ],
        scratch_shapes=[pltpu.VMEM((width, LANES), F32)],
        compiler_params=pltpu.CompilerParams(vmem_limit_bytes=48 * 1024 * 1024),
    )(v, b, c, cumul, cumul_t, step_t, entry, tail, seg_col, seg_row, expand, skip, start)


def adjoint_kernel(
    pairs,
    values,
    write,
    read,
    cumul,
    cumul_t,
    step_t,
    step,
    entry,
    tail_bare,
    seg_col,
    seg_row,
    expand,
    skip,
    kept,
    d_out,
    start,
    d_values,
    d_write,
    d_read,
    d_step,
    d_rate_step,
    d_skip,
    state,
    columns,
):
    @pl.when(pl.program_id(0) == 0)
    def _():
        state[...] = start[...]
        d_skip[...] = jnp.zeros_like(d_skip)
        columns[...] = jnp.zeros_like(columns)

    length = values.shape[0]
    lam, held = state[...], kept[0]
    v, b, c, dy = values[...], write[...], read[...], d_out[...]
    ex = expand[...]
    st = step[...]
    scores = dot(c, b, ((1,), (1,)), HIGH)
    visible = visible_pairs(seg_col[...], seg_row[...])
    entry_full = dot(entry[...], ex, precision=HIGH)
    tail = tail_bare[...] * st
    tail_full = dot(tail, ex, precision=HIGH)
    c_state = dot(c, held, ((1,), (1,)), HIGH)
    b_lam = dot(b, lam, ((1,), (1,)), HIGH)
    dy_in = dy * entry_full
    v_out = v * tail_full
    dc = dot(dy_in, held, precision=HIGH)
    db = dot(v_out, lam, precision=HIGH)
    reach = dot(dy_in * c_state, ex, ((1,), (1,)), HIGH)
    leave = dot(v * b_lam, ex, ((1,), (1,)), HIGH)
    d_skip[...] += jnp.sum(dy * v, axis=0, keepdims=True)
    dv_far = tail_full * b_lam + skip[...] * dy
    cum, cum_t, st_t = cumul[...], cumul_t[...], step_t[...]
    lane = lax.broadcasted_iota(jnp.int32, (length, LANES), 1)
    d_scores = jnp.zeros((length, length), F32)
    row_sums = jnp.zeros((length, LANES), F32)
    for pair in range(pairs):
        cols = slice(pair * LANES, (pair + 1) * LANES)
        v2, dy2 = v[:, cols], dy[:, cols]
        found = []
        for j in range(2):
            h = 2 * pair + j
            own = (lane < LANES // 2) if j == 0 else (lane >= LANES // 2)
            d_mix = dot_three(jnp.where(own, dy2, 0.0), v2, (1, 1))
            spread = jnp.where(visible, cum[:, h : h + 1] - cum_t[h : h + 1, :], MASKED)
            decay = jnp.exp(spread)
            decay_step = decay * st_t[h : h + 1, :]
            weighted = d_mix * scores * decay
            d_scores = d_scores + d_mix * decay_step
            columns[h : h + 1, :] = jnp.sum(weighted, axis=0, keepdims=True)
            per_row = jnp.sum(weighted * st_t[h : h + 1, :], axis=1, keepdims=True)
            row_sums = jnp.where(lane == h, per_row, row_sums)
            found.append(dot(scores * decay_step, dy2, ((0,), (0,))))
        d_values[:, cols] = head_pair(pair, found[0], found[1]) + dv_far[:, cols]
    d_read[...] = dc + dot(d_scores, b, precision=HIGH)
    d_write[...] = db + dot(d_scores, c, ((0,), (0,)), HIGH)
    col_sums = columns[...].T
    leave_step = tail * leave
    d_step[...] = col_sums + tail_bare[...] * leave
    d_cum = row_sums - st * col_sums + reach - leave_step
    row = lax.broadcasted_iota(jnp.int32, (length, length), 0)
    col = lax.broadcasted_iota(jnp.int32, (length, length), 1)
    upper = (col >= row).astype(F32)
    met = jnp.sum(dot(lam * held, ex, ((0,), (1,)), HIGH), axis=0, keepdims=True)
    at_end = jnp.sum(leave_step, axis=0, keepdims=True) + entry[length - 1 :, :] * met
    d_rate_step[...] = dot(upper, d_cum, precision=HIGH) + at_end
    state[...] = state_decay(entry[...], ex) * lam + dot(dy_in, c, ((0,), (0,)), HIGH)


def recur_backward(
    v, b, c, cumul, cumul_t, step_t, step, entry, tail_bare, seg_col, seg_row, expand, skip, kept, dy, start
):
    total, width = v.shape
    blocks = total // BLK
    rows, flat, whole = recur_specs(width, lambda i: blocks - 1 - i)
    return pl.pallas_call(
        partial(adjoint_kernel, width // LANES),
        grid=(blocks,),
        out_shape=[
            jax.ShapeDtypeStruct((total, width), F32),
            jax.ShapeDtypeStruct((total, LANES), F32),
            jax.ShapeDtypeStruct((total, LANES), F32),
            jax.ShapeDtypeStruct((total, LANES), F32),
            jax.ShapeDtypeStruct((total, LANES), F32),
            jax.ShapeDtypeStruct((1, width), F32),
        ],
        in_specs=[
            rows(width),
            rows(LANES),
            rows(LANES),
            rows(LANES),
            flat(16),
            flat(16),
            rows(LANES),
            rows(LANES),
            rows(LANES),
            rows(1),
            flat(1),
            whole((LANES, width)),
            whole((1, width)),
            pl.BlockSpec((1, width, LANES), lambda i: (blocks - 1 - i, 0, 0)),
            rows(width),
            whole((width, LANES)),
        ],
        out_specs=[
            rows(width),
            rows(LANES),
            rows(LANES),
            rows(LANES),
            rows(LANES),
            whole((1, width)),
        ],
        scratch_shapes=[pltpu.VMEM((width, LANES), F32), pltpu.VMEM((LANES, LANES), F32)],
        compiler_params=pltpu.CompilerParams(vmem_limit_bytes=48 * 1024 * 1024),
    )(v, b, c, cumul, cumul_t, step_t, step, entry, tail_bare, seg_col, seg_row, expand, skip, kept, dy, start)


def state_scan_kernel(n, own, *refs):
    reverse = own == 0
    if reverse:
        mine, decay, expand, out = refs[:4]
        refs = refs[4:]
    else:
        mine, decay, expand, y, small, out, y_rows, position = refs[:8]
        refs = refs[8:]
    first, second, got_first, got_second, half, got_half, send_sem, recv_sem = refs[:8]

    def work(blocks):
        pass

    if not reverse:
        earlier, y_in, y_out, stream_sem = refs[8:]
        slots = SlotWork(own, small, position)
        stream = RowStream(y, y_rows, y_in, y_out, stream_sem.at[0], stream_sem.at[1])
        stream.load(0)

        def work(blocks):
            for b in blocks:
                if b + 1 < n:
                    stream.load(b + 1)
                if b == 0:
                    slots.count_with(earlier)
                    for block in range(n):
                        slots.place(block)
                stream.give(b, b, dot(slots.pick(b), stream.take(b)))

    d = lax.axis_index("dp")
    q = n - 1 - d if reverse else d
    zq, xq = q // 2, q % 2
    depth = n // 2
    rows = mine.shape[0] // 2
    xf = xq.astype(F32)
    sent_type = first.dtype

    def device(logical):
        return {"dp": n - 1 - logical if reverse else logical}

    beside = device(2 * zq + 1 - xq)
    others = [device(2 * ((zq + k) % depth) + xq) for k in range(1, depth)]
    own_rows = pl.ds(pl.multiple_of(rows * xq, 16), rows)
    other_rows = pl.ds(pl.multiple_of(rows * (1 - xq), 16), rows)
    own_lanes = pl.ds(pl.multiple_of(rows * xq, LANES), rows)
    tail = pl.ds(rows, 16)
    body = pl.ds(0, rows)
    row = lax.broadcasted_iota(jnp.int32, (16, LANES), 0)

    def spread(values):
        square = jnp.broadcast_to(values, (LANES, LANES)).T
        return dot(expand[:, own_lanes], square, ((0,), (0,)), HIGH)

    def two_terms(values):
        high = values.astype(sent_type).astype(F32)
        wide = jnp.where(row == 0, high, jnp.where(row == 1, values - high, 0.0))
        return wide.astype(sent_type)

    def one_term(block):
        return block[0:1, :].astype(F32) + block[1:2, :].astype(F32)

    for k in range(1, depth):

        @pl.when(zq < k)
        def _():
            got_second[k - 1] = jnp.zeros(got_second.shape[1:], sent_type)

    own_decay = decay[0:1, :]
    first[body, :] = mine[other_rows, :].astype(sent_type)
    first[tail, :] = two_terms(own_decay)
    greet([beside] + others)
    one = remote(first, got_first, send_sem.at[0], recv_sem.at[0], beside)
    one.start()
    work(range(0, 2))
    one.wait_recv()
    own_part = mine[own_rows, :]
    got, got_decay = got_first[body, :].astype(F32), one_term(got_first[tail, :])
    early = own_part * (1.0 - xf) + got * xf
    early_decay = own_decay * (1.0 - xf) + got_decay * xf
    late = own_part * xf + got * (1.0 - xf)
    late_decay = own_decay * xf + got_decay * (1.0 - xf)
    second[body, :] = (spread(late_decay) * early + late).astype(sent_type)
    second[tail, :] = two_terms(early_decay * late_decay)
    sent = []
    for k in range(1, depth):
        copy = remote(
            second, got_second.at[k - 1], send_sem.at[k], recv_sem.at[k], device(2 * ((zq + k) % depth) + xq)
        )
        sent.append(copy)

        @pl.when(zq + k < depth)
        def _():
            copy.start()

    early_spread = spread(early_decay)
    work(range(2, n - 1))
    total = jnp.zeros((rows, LANES), F32)
    for k in range(depth - 1, 0, -1):

        @pl.when(zq >= k)
        def _():
            sent[k - 1].wait_recv()

        got_k = got_second.at[k - 1]
        total = spread(one_term(got_k[tail, :])) * total + got_k[body, :].astype(F32)
    after = early_spread * total + early
    half[...] = (total * xf + after * (1.0 - xf)).astype(sent_type)
    last = remote(half, got_half, send_sem.at[depth], recv_sem.at[depth], beside)
    last.start()
    out[own_rows, :] = total * (1.0 - xf) + after * xf
    work(range(n - 1, n))
    last.wait_recv()
    out[other_rows, :] = got_half[...].astype(F32)
    one.wait_send()
    last.wait_send()
    for k in range(1, depth):

        @pl.when(zq + k < depth)
        def _():
            sent[k - 1].wait_send()

    if not reverse:
        stream.end()


def state_scan(mine, decay, expand, cid, sent_type, y=None, small=None, own=0):
    n = lax.axis_size("dp")
    half = mine.shape[0] // 2
    depth = n // 2
    message = (half + 16, LANES)
    out_shape, out_specs = [jax.ShapeDtypeStruct(mine.shape, F32)], [VM]
    args, in_specs, more = [mine, decay, expand], [VM] * 3, []
    if own:
        tokens, model = y.shape[1:]
        args += [y, small]
        in_specs += [ANY, VM]
        out_shape += [
            jax.ShapeDtypeStruct((own, n, CAP, model), BF),
            jax.ShapeDtypeStruct((n, own, tokens), F32),
        ]
        out_specs += [ANY, VM]
        more = [
            pltpu.VMEM((tokens, tokens), BF),
            pltpu.VMEM((2, tokens, model), BF),
            pltpu.VMEM((2, own, CAP, model), BF),
            pltpu.SemaphoreType.DMA((2, 2)),
        ]
    return pl.pallas_call(
        partial(state_scan_kernel, n, own),
        out_shape=out_shape,
        in_specs=in_specs,
        out_specs=out_specs,
        scratch_shapes=[
            pltpu.VMEM(message, sent_type),
            pltpu.VMEM(message, sent_type),
            pltpu.VMEM(message, sent_type),
            pltpu.VMEM((depth - 1,) + message, sent_type),
            pltpu.VMEM((half, LANES), sent_type),
            pltpu.VMEM((half, LANES), sent_type),
            pltpu.SemaphoreType.DMA((depth + 1,)),
            pltpu.SemaphoreType.DMA((depth + 1,)),
        ]
        + more,
        compiler_params=pltpu.CompilerParams(
            collective_id=cid, has_side_effects=True, vmem_limit_bytes=48 * 1024 * 1024
        ),
    )(*args)


def pick_matrix(position, own):
    length = position.shape[1]
    slot = lax.broadcasted_iota(jnp.int32, (CAP, length), 0).astype(F32)
    parts = [
        jnp.where(position[e : e + 1, :] == slot, 1.0, 0.0).astype(BF) for e in range(own)
    ]
    return jnp.concatenate(parts, axis=0)


def slot_spec(own, cols):
    return pl.BlockSpec((own, 1, CAP, cols), lambda s: (0, s, 0, 0))


def token_spec(rows, cols):
    return pl.BlockSpec((1, rows, cols), lambda s: (s, 0, 0))


BIG = pltpu.CompilerParams(vmem_limit_bytes=56 * 1024 * 1024)


def expert_kernel(
    own, parts, rows, cot_rows, gate, w_in, w_out, grad_in, grad_out, d_rows, res, dots, wide, both
):
    e, part = pl.program_id(0), pl.program_id(1)
    model = rows.shape[2]
    units = w_out.shape[1]

    @pl.when(part == 0)
    def _():
        wide[...] = w_in[0].astype(F32)
        both[:, 0:units] = wide[pl.ds(0, model, stride=2), :].astype(BF)
        both[:, units : 2 * units] = wide[pl.ds(1, model, stride=2), :].astype(BF)
        if parts > 1:
            grad_in[...] = jnp.zeros_like(grad_in)
            grad_out[...] = jnp.zeros_like(grad_out)

    x, c, g = rows[0], cot_rows[0], gate[0]
    mid = dot(x, both[...])
    mid_gate, mid_up = mid[:, 0:units], mid[:, units : 2 * units]
    sig = jax.nn.sigmoid(mid_gate)
    mid_silu = mid_gate * sig
    act = (mid_silu * mid_up).astype(BF).astype(F32)
    back = dot(c, w_out[0], ((1,), (1,)))
    dot_sum = jnp.sum(act * back, axis=1, keepdims=True)
    lane = lax.broadcasted_iota(jnp.int32, g.shape, 1)
    dots[0] = jnp.where(lane == lax.axis_index("dp") * own + e, dot_sum, 0.0).astype(BF)
    gated = (act * g).astype(BF)
    d_act = back * g
    d_gate = (d_act * mid_up * (sig * (1.0 + mid_gate * (1.0 - sig)))).astype(BF)
    d_mid = jnp.concatenate([d_gate, (d_act * mid_silu).astype(BF)], axis=1)
    grads = dot(x, d_mid, ((0,), (0,)))
    grads_down = dot(gated, c, ((0,), (0,)))
    if parts > 1:
        grad_in[0, pl.ds(0, model, stride=2), :] += grads[:, 0:units]
        grad_in[0, pl.ds(1, model, stride=2), :] += grads[:, units : 2 * units]
        grad_out[0] += grads_down
    else:
        grad_in[0, pl.ds(0, model, stride=2), :] = grads[:, 0:units]
        grad_in[0, pl.ds(1, model, stride=2), :] = grads[:, units : 2 * units]
        grad_out[0] = grads_down
    d_rows[0] = dot(d_mid, both[...], ((1,), (1,))).astype(BF)
    res[0] = dot(gated, w_out[0]).astype(BF)


def run_experts(rows, cot_rows, gate, w_in, w_out):
    own, slots, model = rows.shape
    units = w_out.shape[1]
    part = min(slots, 512)

    def slot(cols):
        return pl.BlockSpec((1, part, cols), lambda e, j: (e, j, 0))

    def weight(a, b):
        return pl.BlockSpec((1, a, b), lambda e, j: (e, 0, 0))

    return pl.pallas_call(
        partial(expert_kernel, own, slots // part),
        grid=(own, slots // part),
        out_shape=[
            jax.ShapeDtypeStruct((own, 2 * model, units), F32),
            jax.ShapeDtypeStruct((own, units, model), F32),
            jax.ShapeDtypeStruct((own, slots, model), BF),
            jax.ShapeDtypeStruct((own, slots, model), BF),
            jax.ShapeDtypeStruct((own, slots, LANES), BF),
        ],
        in_specs=[slot(model), slot(model), slot(LANES), weight(2 * model, units), weight(units, model)],
        out_specs=[weight(2 * model, units), weight(units, model), slot(model), slot(model), slot(LANES)],
        scratch_shapes=[pltpu.VMEM((2 * model, units), F32), pltpu.VMEM((model, 2 * units), BF)],
        compiler_params=BIG,
    )(rows, cot_rows, gate, w_in, w_out)


def put_kernel(own, k, position, *refs):
    out = refs[-1]
    put = pick_matrix(position[0], own)
    here = jnp.where(pl.program_id(0) == lax.axis_index("dp"), 1.0, 0.0)
    start = 0
    for i in range(k):
        rows, shared = refs[2 * i], refs[2 * i + 1]
        cols = shared.shape[1]
        total = dot(put, rows[...].reshape(own * CAP, cols), ((0,), (0,)))
        out[0, :, start : start + cols] = (total + here * shared[...]).astype(BF)
        start += cols
    if len(refs) > 2 * k + 1:
        extra = refs[2 * k]
        out[0, :, start : start + LANES] = dot(
            put, extra[...].reshape(own * CAP, LANES), ((0,), (0,))
        ).astype(BF)


def put_rows(position, parts, extra=None):
    n, own, tokens = position.shape
    args, specs, cols = [], [], 0
    for rows, shared in parts:
        model = shared.shape[1]
        args += [rows.reshape(own, n, CAP, model), shared]
        specs += [slot_spec(own, model), pl.BlockSpec((tokens, model), lambda s: (0, 0))]
        cols += model
    if extra is not None:
        args.append(extra.reshape(own, n, CAP, LANES))
        specs.append(slot_spec(own, LANES))
        cols += LANES
    return pl.pallas_call(
        partial(put_kernel, own, len(parts)),
        grid=(n,),
        out_shape=jax.ShapeDtypeStruct((n, tokens, cols), BF),
        in_specs=[token_spec(own, tokens)] + specs,
        out_specs=token_spec(tokens, cols),
        compiler_params=BIG,
    )(position, *args)


def grads_kernel(k, *refs):
    lefts, rights, out = refs[:k], refs[k : 2 * k], refs[2 * k]
    start = 0
    for left, right in zip(lefts, rights):
        cols = right.shape[1]
        out[:, start : start + cols] = dot(left[...], right[...], ((0,), (0,))).astype(BF)
        start += cols


def weight_grads(pairs):
    k = len(pairs)
    tokens, model = pairs[1][0].shape
    block = 256
    cols = sum(right.shape[1] for _, right in pairs)
    return pl.pallas_call(
        partial(grads_kernel, k),
        grid=(model // block,),
        out_shape=jax.ShapeDtypeStruct((model, cols), BF),
        in_specs=[pl.BlockSpec((tokens, block), lambda i: (0, i)) for _ in pairs]
        + [pl.BlockSpec(right.shape, lambda i: (0, 0)) for _, right in pairs],
        out_specs=pl.BlockSpec((block, cols), lambda i: (i, 0)),
        compiler_params=BIG,
    )(*[left for left, _ in pairs], *[right for _, right in pairs])


def combine_states(states, decays, expand, reverse):
    n = states.shape[0]
    place = lax.axis_index("dp")
    wide = dot(decays, expand, precision=HIGH)
    state = jnp.zeros(states.shape[1:], F32)
    for j in range(n):
        source = n - 1 - j if reverse else j
        use = source > place if reverse else source < place
        fresh = wide[source][:, None] * state + states[source]
        state = jnp.where(use, fresh, state)
    return state


def ring_state(mine, decay, expand, reverse, cid):
    rows = jnp.pad(decay, ((0, 31), (0, 0)))
    (gathered,) = gather_dp([jnp.concatenate([mine, rows], axis=0)], cid)
    width = mine.shape[0]
    return combine_states(gathered[:, :width], gathered[:, width], expand, reverse)


def per_device(
    hidden,
    segment_ids,
    routes,
    norm_gain,
    mixer_in,
    state_in,
    step_in,
    conv_value,
    conv_value_bias,
    conv_state,
    conv_state_bias,
    head_params,
    gated_gain,
    mixer_out,
    ffn_gain,
    router,
    shared_in,
    shared_out,
    expert_in,
    expert_out,
    cotangent,
):
    n = lax.axis_size("dp")
    place, mp_place = lax.axis_index("dp"), lax.axis_index("mp")
    tokens, model = hidden.shape
    shard = model // n
    inner = mixer_in.shape[2]
    state_cols = state_in.shape[1]
    taps = conv_value.shape[0]
    heads = head_params.shape[1]
    width = inner // heads
    own_experts = expert_in.shape[0]
    hidden_units = shared_out.shape[0]
    quarter = tokens // 4

    misc_parts = [
        conv_value.reshape(-1),
        conv_value_bias.reshape(-1),
        gated_gain.reshape(-1),
        conv_state.reshape(-1),
        conv_state_bias,
        norm_gain,
        ffn_gain,
    ]
    misc = jnp.concatenate(misc_parts)
    small = jnp.concatenate(
        [
            jnp.pad(misc, (0, model - misc.shape[0]))[None],
            jnp.pad(routes.T.astype(BF), ((0, 0), (0, model - tokens))),
            hidden[tokens - 15 + TOPK :],
        ],
        axis=0,
    )
    pack_a = jnp.concatenate(
        [
            mixer_in.reshape(shard, 2 * inner),
            state_in,
            jnp.pad(step_in, ((0, 0), (0, LANES - heads))),
        ],
        axis=1,
    )
    pack_b = jnp.concatenate(
        [
            mixer_out.T,
            shared_in.reshape(shard, 2 * hidden_units),
            shared_out.T,
            jnp.pad(router, ((0, 0), (0, LANES - EXPERTS))),
        ],
        axis=1,
    )
    mine_cot = lax.dynamic_slice_in_dim(cotangent, mp_place * quarter, quarter, 0)
    weight_a, small_all, cot_all = first_gather([pack_a, small], cotangent, 0)
    weight_a = weight_a.reshape(model, -1)
    cot_all = cot_all.reshape(n, tokens, model)
    pack_b, small_all = lax.optimization_barrier((pack_b, small_all))
    weight_b = lax.all_gather(pack_b, "dp", axis=0, tiled=True)

    pieces = []
    start = 0
    for part in misc_parts:
        pieces.append(small_all[:, 0, start : start + part.shape[0]].astype(F32))
        start += part.shape[0]
    local_p = conv_value.shape[1]
    value_rows = jnp.concatenate(pieces[:3], axis=1).reshape(n, taps + 2, local_p, heads)
    value_rows = value_rows.transpose(1, 3, 0, 2).reshape(taps + 2, inner)
    state_rows = jnp.concatenate(pieces[3:5], axis=1).reshape(n, taps + 1, state_cols // n)
    state_rows = state_rows.transpose(1, 0, 2).reshape(taps + 1, state_cols)
    gain_first = pieces[5].reshape(1, model)
    gain_second = pieces[6].reshape(1, model)
    conv_taps = jnp.concatenate([value_rows[:taps], state_rows[:taps]], axis=1)
    conv_bias = jnp.concatenate([value_rows[taps], state_rows[taps]])[None]
    gated_row = value_rows[taps + 1][None]

    group_start = place * tokens
    seg_padded = jnp.concatenate([jnp.full((taps - 1,), -1, jnp.int32), segment_ids])
    seg_ext = lax.dynamic_slice_in_dim(seg_padded, group_start, tokens + taps - 1)
    segments = seg_ext[taps - 1 :]
    prev_seg = seg_ext[taps - 2]
    same = [
        (seg_ext[k : k + tokens] == segments).astype(F32)[:, None] for k in range(taps)
    ]
    blocks = tokens // BLK
    seg_blocks = segments.reshape(blocks, BLK)
    last_segs = seg_blocks[:, BLK - 1]
    prev_segs = jnp.concatenate([prev_seg[None], last_segs[:-1]])
    entry_ok = (seg_blocks == prev_segs[:, None]).astype(F32).reshape(tokens, 1)
    tail_ok = (seg_blocks == last_segs[:, None]).astype(F32).reshape(tokens, 1)
    group_entry_ok = (segments == prev_seg).astype(F32)[:, None]
    group_tail_ok = (segments == segments[tokens - 1]).astype(F32)[:, None]
    seg_f = segments.astype(F32)
    seg_col, seg_row = seg_f[:, None], seg_f[None, :]

    behind = lax.dynamic_index_in_dim(small_all, (place + n - 1) % n, 0, False)
    hidden_ext = jnp.concatenate([behind, hidden], axis=0).astype(F32)
    inv_ext = lax.rsqrt(jnp.mean(hidden_ext * hidden_ext, axis=1, keepdims=True) + EPS)
    normed_ext = (hidden_ext * inv_ext * gain_first).astype(BF)
    normed = normed_ext[16:]
    zx_ext = dot(normed_ext, weight_a)
    gate_z = zx_ext[16:, :inner]
    pre_ext = zx_ext[16 - taps + 1 :, inner : 2 * inner + state_cols]
    head_local = head_params.astype(F32)
    dt_lanes = zx_ext[16:, 2 * inner + state_cols :]
    conv = jnp.broadcast_to(conv_bias, (tokens, inner + state_cols))
    for k in range(taps):
        conv = conv + conv_taps[k][None] * pre_ext[k : k + tokens] * same[k]
    act = jax.nn.silu(conv)
    values = act[:, :inner]
    write = act[:, inner : inner + state_cols // 2]
    read = act[:, inner + state_cols // 2 :]

    live = (jnp.arange(LANES) < heads)[None]
    head_pad = jnp.pad(head_local, ((0, 0), (0, LANES - heads)))
    rate = jnp.where(live, -jnp.exp(head_pad[0:1]), 0.0)
    step = jnp.where(live, jax.nn.softplus(dt_lanes + head_pad[1:2]), 0.0)
    rated = (step * rate).reshape(blocks, BLK, LANES)
    lower = jnp.tril(jnp.ones((BLK, BLK), F32))
    cumul_b = jnp.einsum("ts,bsh->bth", lower, rated, precision=HIGH)
    totals = cumul_b[:, BLK - 1]
    zero_row = jnp.zeros((1, LANES), F32)
    before, after = [zero_row], [zero_row]
    for i in range(blocks - 1):
        before.append(before[-1] + totals[i][None])
        after.append(after[-1] + totals[blocks - 1 - i][None])
    before = jnp.stack(before)
    after = jnp.stack(after[::-1])
    cumul = cumul_b.reshape(tokens, LANES)
    to_end = totals[:, None] - cumul_b
    entry = jnp.exp(cumul) * entry_ok
    tail_bare = jnp.exp(to_end).reshape(tokens, LANES) * tail_ok
    tail = tail_bare * step
    group_entry = jnp.exp(cumul_b + before).reshape(tokens, LANES) * group_entry_ok
    group_tail = jnp.exp(to_end + after).reshape(tokens, LANES) * group_tail_ok * step
    cumul_t = cumul[:, :16].T
    step_t = step[:, :16].T
    expand = (jnp.arange(LANES)[:, None] == jnp.arange(inner)[None, :] // width).astype(F32)
    skip = dot(head_pad[2:3], expand, precision=HIGH)
    outgoing = dot(
        values * dot(group_tail, expand, precision=HIGH), write, ((0,), (0,)), HIGH
    )
    group_decay = group_entry[tokens - 1 :]
    if n == 8:
        incoming, cot_rows, position = state_scan(
            outgoing, jnp.broadcast_to(group_decay, (8, LANES)), expand, 1, F32, cot_all, small_all, own_experts
        )
    else:
        incoming = ring_state(outgoing, group_decay, expand, False, 1)
        cot_rows, position = slots_of(cot_all, small_all, own_experts)
    ssd, kept = recur_forward(
        values, write, read, cumul, cumul_t, step_t, entry, tail, seg_col, seg_row, expand, skip, incoming
    )

    gate_act = jax.nn.silu(gate_z)
    gated = ssd * gate_act
    scaled = (gated * gated_row).astype(BF)
    unit_first = hidden_ext[16:] * inv_ext[16:]
    mine_unit = lax.dynamic_slice_in_dim(unit_first, mp_place * quarter, quarter, 0)
    entry_wide = dot(group_entry, expand, precision=HIGH)
    unit_first, mine_unit, entry_wide, weight_b = lax.optimization_barrier(
        (unit_first, mine_unit, entry_wide, weight_b)
    )
    out_t = weight_b[:, :inner]
    router_w = weight_b[:, inner + 3 * hidden_units :]
    proj_part = dot(scaled, out_t, ((1,), (1,)))
    square_part = jnp.sum(gated * gated, axis=1, keepdims=True)
    proj_pack = jnp.concatenate([proj_part, jnp.broadcast_to(square_part, (tokens, LANES))], axis=1)
    proj_sum = scatter_mp(proj_pack.reshape(4, quarter, -1), 2)
    proj = proj_sum[:, :model]
    square = proj_sum[:, model : model + 1]
    inv_gated = lax.rsqrt(square / DI + EPS)
    mine_hidden = lax.dynamic_slice_in_dim(hidden, mp_place * quarter, quarter, 0).astype(F32)
    mixed = mine_hidden + proj * inv_gated
    inv_second = lax.rsqrt(jnp.mean(mixed * mixed, axis=1, keepdims=True) + EPS)
    unit_second = mixed * inv_second
    ffn_mine = (unit_second * gain_second).astype(BF)

    first_expert = place * own_experts
    (
        _,
        rows,
        gates,
        slot_gates,
        ffn_block,
        shared_act,
        d_shared_mid,
        shared_res,
        d_ffn_shared,
    ) = gather_tokens(ffn_mine, position, small_all, weight_b, cotangent, hidden_units, 3)

    slots = n * CAP
    grad_in_rows, grad_expert_out, d_rows, expert_res, slot_dots = run_experts(
        rows.reshape(own_experts, slots, model),
        cot_rows.reshape(own_experts, slots, model),
        slot_gates.reshape(own_experts, slots, LANES),
        expert_in.reshape(own_experts, 2 * model, -1),
        expert_out,
    )
    grad_expert_in = grad_in_rows.reshape(expert_in.shape)

    if n > 8:
        d_ffn_pack = put_rows(position, [(d_rows, d_ffn_shared)], slot_dots)
        d_ffn_sum = scatter_tokens(d_ffn_pack.reshape(n, 4, quarter, -1), 4)
        expert_res, d_ffn_sum = lax.optimization_barrier((expert_res, d_ffn_sum))
        res_pack = put_rows(position, [(expert_res, shared_res)])
        res_sum = scatter_tokens(res_pack.reshape(n, 4, quarter, model), 10)
    else:
        both_sums = put_scatter(position, expert_res, d_rows, slot_dots, shared_res, d_ffn_shared, 4)
        res_sum, d_ffn_sum = both_sums[:, :model], both_sums[:, model:]

    own_tokens_gates = lax.dynamic_slice(
        gates, (place, mp_place * quarter, 0), (1, quarter, LANES)
    ).reshape(quarter, LANES)
    dots = d_ffn_sum[:, model : model + LANES]
    share = jnp.sum(own_tokens_gates * dots, axis=1, keepdims=True)
    d_logits = (own_tokens_gates * (dots - share)).astype(BF)
    d_ffn = d_ffn_sum[:, :model] + dot(d_logits, router_w, ((1,), (1,)))
    mine_cot_f = mine_cot.astype(F32)
    grad_gain_second = jnp.sum(d_ffn * unit_second, axis=0)
    d_unit = d_ffn * gain_second
    d_mixed = mine_cot_f + inv_second * (
        d_unit - unit_second * jnp.mean(d_unit * unit_second, axis=1, keepdims=True)
    )
    d_proj_mine = (d_mixed * inv_gated).astype(BF)
    d_inv = jnp.sum(d_mixed * proj, axis=1, keepdims=True)
    d_square = d_inv * -0.5 * inv_gated * inv_gated * inv_gated / DI
    d_square_high = d_square.astype(BF)
    d_square_low = (d_square - d_square_high.astype(F32)).astype(BF)
    side = jnp.concatenate(
        [
            d_logits[:, :EXPERTS],
            d_square_high,
            d_square_low,
            jnp.zeros((quarter, LANES - EXPERTS - 2), BF),
        ],
        axis=1,
    )
    d_proj, side = gather_mp([d_proj_mine, side], 5)
    d_proj = d_proj.reshape(tokens, model)
    side = side.reshape(tokens, LANES)
    d_square_all = side[:, EXPERTS : EXPERTS + 1].astype(F32) + side[:, EXPERTS + 1 : EXPERTS + 2].astype(F32)

    rows0 = ((0,), (0,))
    grad_b = weight_grads(
        [
            (d_proj, scaled),
            (ffn_block, d_shared_mid),
            (cotangent, shared_act),
            (ffn_block, side),
        ]
    )
    grad_b, d_proj = lax.optimization_barrier((grad_b, d_proj))
    sum_b = lax.psum_scatter(grad_b, "dp", scatter_dimension=0, tiled=True).astype(F32)
    d_scaled = dot(d_proj, out_t)
    grad_gated_row = jnp.sum(d_scaled * gated, axis=0)
    d_gated = d_scaled * gated_row + 2.0 * gated * d_square_all
    d_ssd = d_gated * gate_act
    d_gate_z = d_gated * ssd * silu_slope(gate_z)

    direct = dot(d_ssd * entry_wide, read, rows0, HIGH)
    if n == 8:
        (state_grad,) = state_scan(direct, jnp.broadcast_to(group_decay, (8, LANES)), expand, 6, BF)
    else:
        state_grad = ring_state(direct, group_decay, expand, True, 6)
    d_values, d_write, d_read, d_step, d_rated, d_skip_row = recur_backward(
        values,
        write,
        read,
        cumul,
        cumul_t,
        step_t,
        step,
        entry,
        tail_bare,
        seg_col,
        seg_row,
        expand,
        skip,
        kept,
        d_ssd,
        state_grad,
    )
    d_rate = jnp.sum(d_rated * step, axis=0, keepdims=True)
    d_dt = jnp.where(
        live, (d_step + rate * d_rated) * jax.nn.sigmoid(dt_lanes + head_pad[1:2]), 0.0
    )
    d_skip = dot(d_skip_row, expand, ((1,), (1,)), HIGH)
    grad_head = jnp.concatenate(
        [d_rate * rate, jnp.sum(d_dt, axis=0, keepdims=True), d_skip], axis=0
    )[:, :heads]

    slope = silu_slope(conv)
    d_conv_values = d_values * slope[:, :inner]
    d_state_act, rim_ahead = sum_and_edge(
        jnp.concatenate([d_write, d_read], axis=1), slope[:16, inner:], d_conv_values[:16], 11
    )
    d_conv = jnp.concatenate([d_conv_values, d_state_act * slope[:, inner:]], axis=1)
    d_conv_ext = jnp.concatenate([d_conv, rim_ahead], axis=0)
    seg_after = lax.dynamic_slice_in_dim(
        jnp.concatenate([segment_ids, jnp.full((taps - 1,), -1, jnp.int32)]),
        group_start,
        tokens + taps - 1,
    )
    d_pre = jnp.zeros_like(d_conv)
    grad_rows = []
    for k in range(taps):
        ahead = taps - 1 - k
        ok = (seg_after[ahead : ahead + tokens] == segments).astype(F32)[:, None]
        d_pre = d_pre + conv_taps[k][None] * d_conv_ext[ahead : ahead + tokens] * ok
        grad_rows.append(jnp.sum(d_conv * pre_ext[k : k + tokens] * same[k], axis=0))
    grad_rows.append(jnp.sum(d_conv, axis=0))
    d_a = jnp.concatenate([d_gate_z, d_pre, d_dt], axis=1).astype(BF)

    d_state_mine = lax.dynamic_slice_in_dim(
        d_a[:, 2 * inner : 2 * inner + state_cols], mp_place * quarter, quarter, 0
    )
    d_normed_part = dot(d_a[:, : 2 * inner], weight_a[:, : 2 * inner], ((1,), (1,))) + dot(
        d_a[:, 2 * inner + state_cols :], weight_a[:, 2 * inner + state_cols :], ((1,), (1,))
    )
    d_state_rows = dot(
        d_state_mine, weight_a[:, 2 * inner : 2 * inner + state_cols], ((1,), (1,))
    )
    grad_a = dot(normed, d_a, rows0).astype(BF)
    grad_gain_first = jnp.sum(d_normed_part * unit_first, axis=0) + jnp.sum(
        d_state_rows * mine_unit, axis=0
    )

    value_grads = jnp.stack([g[:inner] for g in grad_rows] + [grad_gated_row])
    value_grads = value_grads.reshape(taps + 2, heads, n, local_p).transpose(2, 0, 3, 1)
    state_grads = jnp.stack([g[inner:] for g in grad_rows])
    state_grads = state_grads.reshape(taps + 1, n, state_cols // n).transpose(1, 0, 2)
    misc_grads = [
        value_grads.reshape(n, -1),
        state_grads.reshape(n, -1),
        jnp.broadcast_to(grad_head.reshape(1, -1), (n, 3 * heads)),
    ]
    sizes = [g.shape[1] for g in misc_grads]
    misc_grads = jnp.concatenate(misc_grads, axis=1)
    misc_grads = jnp.pad(misc_grads, ((0, 0), (0, 32 * LANES - misc_grads.shape[1])))
    gains = jnp.concatenate(
        [grad_gain_first.reshape(n, shard), grad_gain_second.reshape(n, shard)], axis=1
    )
    gains = jnp.pad(gains, ((0, 0), (0, 16 * LANES - 2 * shard)))
    mine_result = (mixed + res_sum).astype(BF)
    sum_zx, sum_state, sum_dt, misc_sum, gains_sum, hidden_all, result = last_exchange(
        grad_a.reshape(n, shard, -1),
        misc_grads.reshape(n, 32, LANES),
        gains.reshape(n, 16, LANES),
        d_normed_part.astype(BF).reshape(4, quarter, model),
        d_state_rows,
        d_mixed,
        mine_hidden,
        gain_first,
        mine_result,
        (2 * inner, state_cols, LANES),
        8,
    )
    result = result.reshape(tokens, model)
    misc_sum = misc_sum.reshape(-1)
    gains_sum = gains_sum.reshape(-1)
    cut = [0]
    for size in sizes:
        cut.append(cut[-1] + size)
    value_sum = misc_sum[: cut[1]].reshape(taps + 2, local_p, heads)
    state_sum = misc_sum[cut[1] : cut[2]].reshape(taps + 1, state_cols // n)
    head_sum = misc_sum[cut[2] : cut[3]].reshape(3, heads)

    b1, b2 = inner, inner + 2 * hidden_units
    b3 = b2 + hidden_units
    return (
        result,
        hidden_all.reshape(tokens, model).astype(F32),
        gains_sum[:shard],
        sum_zx.reshape(shard, 2, inner),
        sum_state,
        sum_dt[:, :heads],
        value_sum[:taps],
        value_sum[taps],
        state_sum[:taps],
        state_sum[taps],
        head_sum,
        value_sum[taps + 1],
        sum_b[:, :b1].T,
        gains_sum[shard : 2 * shard],
        sum_b[:, b3 : b3 + EXPERTS],
        sum_b[:, b1:b2].reshape(shard, 2, hidden_units),
        sum_b[:, b2:b3].T,
        grad_expert_in,
        grad_expert_out,
    )


def solution(mesh):
    placed = (
        P("dp", None),
        P(),
        P("dp", None),
        P("dp"),
        P("dp", None, "mp"),
        P("dp", None),
        P("dp", "mp"),
        P(None, "dp", "mp"),
        P("dp", "mp"),
        P(None, "dp"),
        P("dp"),
        P(None, "mp"),
        P("dp", "mp"),
        P("mp", "dp"),
        P("dp"),
        P("dp", None),
        P("dp", None, "mp"),
        P("mp", "dp"),
        P("dp", None, None, "mp"),
        P("dp", "mp", None),
        P("dp", None),
    )
    return jax.shard_map(
        per_device,
        mesh=mesh,
        in_specs=placed,
        out_specs=(
            P("dp", None),
            P("dp", None),
            P("dp"),
            P("dp", None, "mp"),
            P("dp", None),
            P("dp", "mp"),
            P(None, "dp", "mp"),
            P("dp", "mp"),
            P(None, "dp"),
            P("dp"),
            P(None, "mp"),
            P("dp", "mp"),
            P("mp", "dp"),
            P("dp"),
            P("dp", None),
            P("dp", None, "mp"),
            P("mp", "dp"),
            P("dp", None, None, "mp"),
            P("dp", "mp", None),
        ),
        check_vma=False,
    )
```
